32 devices in a mesh: groups: 2 (over x), domain: 4 (over y, core), band: 4 (over z).
Axes of the slice: x: 2, y: 2, z: 4, core: 2. Of those that a mesh axis runs over, the one named last changes fastest.
Arguments:
- orbitals: bfloat16 [256, 8, 128, 128], P('band', ('groups', 'domain')), parts along dimension 1, may hold values from -8 to 8
- potential: float32 [8, 128, 128], P(('groups', 'domain')), parts along dimension 0, may hold values from -3 to 0.5
- projectors: bfloat16 [3072, 16, 128], P(('groups', 'domain')), parts along dimension 0, may hold values from -0.5 to 0.5
- tile_atom: int32 [3072], P(('groups', 'domain')), parts along dimension 0, may hold values from 0 to 255, as said below
- tile_line: int32 [3072], P(('groups', 'domain')), parts along dimension 0, may hold values from 0 to 127
- tile_count: int32 [8], P(('groups', 'domain')), parts along dimension 0, may hold values from 96 to 384, as said below
- energies: float32 [512, 16], P('groups'), parts along dimension 0, may hold values from -1.5 to 1.5
Outputs:
- applied: bfloat16 [256, 8, 128, 128], P('band', ('groups', 'domain')), parts along dimension 1
- subspace: float32 [2, 512, 256], P(None, ('groups', 'band'), 'domain'), parts along dimension 1
The draws below stay inside these ranges and needn't reach their ends.
There are 2 independent parts, one for each index of `groups`. The reference program is written for one: setup_inputs(seed, part) draws one part's arguments, and reference() takes and returns one part's arrays. A program takes and returns all parts, laid end to end along the dimension named above; each array names one. Nothing has to cross between parts.
Inputs may be any that keep to these rules, and one draw needn't show every extreme that they name: `tile_count`: each subdomain's number of live tile slots; one subdomain has exactly 384 in every draw. `tile_atom`: an atom number for every slot, live or not; subdomain e owns atoms e * 64 to (e + 1) * 64 - 1, and a slot of subdomain d names an atom owned by d, d - 1 or d + 1 (no wrap-round at the slab's ends).
All inputs are finite; a program needn't handle non-finite values.
Results may differ from the reference program's by a relative error of at most 0.0075.
Values may be sent and summed in bfloat16 or wider, within the bound.
No kernel may reach another device: no remote copies, remote signals or barrier semaphores. Data moves between devices by JAX's collectives and lax.ppermute only.
A program may use at most 192 MiB of HBM per device.

```python
import jax
import jax.numpy as jnp
from jax import lax

NS = 256
NPROJ = 16
CX = 1
NY = 128
NZ = 128
TCAP = 384
ATOMS_DEV = 64
NX = 4
NATOMS = 256
TILES = 1536
N_DOMAIN = 4


def draw_orbitals(key, part):
    key = jax.random.fold_in(key, 11)
    key_noise, key_state, key_cell = jax.random.split(key, 3)
    shape = (NS, NX, NY, NZ)
    state_part = jax.random.normal(key_state, (NS, 1, 1, 1), jnp.float32)
    cell_part = jax.random.normal(key_cell, (1, NX, NY, NZ), jnp.float32)
    noise = jax.random.normal(key_noise, shape, jnp.float32)
    values = noise + 0.6 * state_part * cell_part
    return jnp.clip(values, -8.0, 8.0).astype(jnp.bfloat16)


def draw_tile_atom(key, part):
    key = jax.random.fold_in(key, 12)
    key_off, key_inner = jax.random.split(key)
    domain_of = jnp.arange(N_DOMAIN * TCAP, dtype=jnp.int32) // TCAP
    offset = jax.random.randint(key_off, (N_DOMAIN * TCAP,), -1, 2, jnp.int32)
    inner = jax.random.randint(key_inner, (N_DOMAIN * TCAP,), 0, ATOMS_DEV, jnp.int32)
    home = jnp.clip(domain_of + offset, 0, N_DOMAIN - 1)
    return (home * ATOMS_DEV + inner).astype(jnp.int32)


def draw_tile_count(key, part):
    key = jax.random.fold_in(key, 13)
    key_count, key_full = jax.random.split(key)
    counts = jax.random.randint(key_count, (N_DOMAIN,), TCAP // 4, TCAP + 1, jnp.int32)
    fullest = jax.random.randint(key_full, (), 0, N_DOMAIN, jnp.int32)
    return counts.at[fullest].set(TCAP).astype(jnp.int32)


def touch_ends(values, own_key, smallest, high):
    shape = values.shape
    index_at = [jax.random.randint(jax.random.fold_in(own_key, axis), (), 0, shape[axis]) for axis in range(len(shape))]
    values = values.at[tuple(index_at)].set(smallest)
    longest = shape.index(max(shape))
    index_at[longest] = (index_at[longest] + 1) % shape[longest]
    return values.at[tuple(index_at)].set(high)


def block_levels(key, dims, cuts, smallest, largest):
    factor_of = 1.0
    for axis_at, parts in cuts:
        draws = jax.random.uniform(jax.random.fold_in(jax.random.fold_in(key, 6), axis_at), (parts,), jnp.float32, smallest / len(cuts), largest / len(cuts))
        factor_of = factor_of * jnp.repeat(jnp.exp(draws), dims[axis_at] // parts).reshape((-1,) + (1,) * (len(dims) - 1 - axis_at))
    return factor_of


def normal_values(stream_key, dims, spread, most, cuts=(), kind=jnp.bfloat16):
    entries = jax.random.normal(stream_key, dims, jnp.float32) * spread
    if len(cuts) > 0:
        entries = block_levels(stream_key, dims, cuts, -0.22, 0.18) * entries
    return jnp.clip(entries, min=-most, max=most).astype(kind)


def setup_inputs(seed: int = 0, part: int = 0) -> dict:
    key_of = jax.random.split(jax.random.key(seed), 8)
    part_splits = jax.random.split(jax.random.fold_in(key_of[7], part), 8)
    return {
        "orbitals": draw_orbitals(jax.random.fold_in(jax.random.fold_in(key_of[7], part), 71), part),
        "potential": jnp.clip(-3.0 + 3.5 * jax.random.uniform(part_splits[1], (NX, NY, NZ), jnp.float32) ** block_levels(part_splits[1], (NX, NY, NZ), ((0, 4),), -0.2, 0.2), -3.0, 0.5),
        "projectors": normal_values(part_splits[2], (TILES, NPROJ, NZ), NZ ** -0.5, 0.5, ((0, 4),)),
        "tile_atom": draw_tile_atom(jax.random.fold_in(jax.random.fold_in(key_of[7], part), 71), part),
        "tile_line": touch_ends(jax.random.randint(part_splits[4], (TILES,), 0, CX * NY), jax.random.fold_in(part_splits[4], 1), 0, (CX * NY) - 1).astype(jnp.int32),
        "tile_count": draw_tile_count(jax.random.fold_in(jax.random.fold_in(key_of[7], part), 71), part),
        "energies": jnp.clip(jax.random.uniform(part_splits[6], (NATOMS, NPROJ), jnp.float32, -1.5, 1.5), -1.5, 1.5),
    }


kinetic_weight = 0.5


def reference(orbitals, potential, projectors, tile_atom, tile_line, tile_count, energies):
    states, planes, rows_y, cols_z = orbitals.shape
    slots = projectors.shape[0]
    slot_ids = jnp.arange(slots, dtype=jnp.int32)
    domain_of = slot_ids // TCAP
    live = (slot_ids % TCAP < tile_count[domain_of]).astype(jnp.bfloat16)
    live_proj = projectors * live[:, None, None]
    global_line = (domain_of * (CX * NY) + tile_line).astype(jnp.int32)
    blocks = orbitals.reshape(states // 32, 32, planes, rows_y, cols_z)

    def one_block(block):
        flat = block.reshape(32, planes * rows_y, cols_z)
        lines = flat[:, global_line, :]
        part = jnp.einsum('tpz,stz->tps', live_proj.astype(jnp.float32), lines.astype(jnp.float32))
        proj = jax.ops.segment_sum(part, tile_atom, num_segments=NATOMS)
        scaled = (proj * energies[:, :, None]).astype(jnp.bfloat16)
        back = jnp.einsum('tps,tpz->stz', scaled[tile_atom].astype(jnp.float32), live_proj.astype(jnp.float32))
        nonlocal_part = jnp.zeros((32, planes * rows_y, cols_z), jnp.float32).at[:, global_line, :].add(back)
        field = block.astype(jnp.float32)
        padded = jnp.pad(field, ((0, 0), (1, 1), (0, 0), (0, 0)))
        beside_all = padded[:, 2:] + padded[:, :-2]
        beside_all = beside_all + jnp.roll(field, 1, axis=2) + jnp.roll(field, -1, axis=2)
        beside_all = beside_all + jnp.roll(field, 1, axis=3) + jnp.roll(field, -1, axis=3)
        total = kinetic_weight * (6.0 * field - beside_all) + potential[None] * field
        total = total + nonlocal_part.reshape(32, planes, rows_y, cols_z)
        return total.astype(jnp.bfloat16)

    applied = lax.map(one_block, blocks).reshape(states, planes, rows_y, cols_z)
    scale = 1.0 / (planes * rows_y * cols_z)
    orb_flat = orbitals.reshape(states, -1)
    app_flat = applied.reshape(states, -1)
    gram = jnp.dot(orb_flat, orb_flat.T, preferred_element_type=jnp.float32) * scale
    hamil = jnp.dot(app_flat, orb_flat.T, preferred_element_type=jnp.float32) * scale
    return applied, jnp.stack([gram, hamil])
```

```python
import functools

import jax
import jax.numpy as jnp
from jax import lax
from jax.experimental import pallas as pl
from jax.experimental.pallas import tpu as pltpu
from jax.sharding import PartitionSpec as P

F32 = jnp.float32
BF16 = jnp.bfloat16
LANES = 128
VMEM_BYTES = 48 * 1024 * 1024
NT = (((1,), (1,)), ((), ()))


def call(kernel, outs, ins, scratch=(), flops=0, moved=0):
    spaces = [pltpu.SMEM if kind == "smem" else pltpu.VMEM for kind, _ in ins]
    return pl.pallas_call(
        kernel,
        out_shape=[jax.ShapeDtypeStruct(shape, kind) for shape, kind in outs],
        in_specs=[pl.BlockSpec(memory_space=space) for space in spaces],
        out_specs=[pl.BlockSpec(memory_space=pltpu.VMEM)] * len(outs),
        scratch_shapes=list(scratch),
        compiler_params=pltpu.CompilerParams(vmem_limit_bytes=VMEM_BYTES),
        cost_estimate=pl.CostEstimate(flops=flops, bytes_accessed=moved, transcendentals=0),
    )(*[value for _, value in ins])


def pack_kernel(bands, first, ids_ref, x_ref, xt_ref, *piece_refs):
    states, lines, _ = x_ref.shape
    share = lines // bands
    step = 16

    def rows(i, carry):
        y0 = pl.multiple_of(i * step, step)
        for s0 in range(0, states, step):
            block = x_ref[s0 : s0 + step, pl.ds(y0, step), :].astype(F32)
            turned = jnp.swapaxes(block, 0, 1).astype(BF16)
            xt_ref[pl.ds(y0, step), s0 : s0 + step, :] = turned
        return carry

    lax.fori_loop(0, lines // step, rows, 0)
    band = ids_ref[1]
    later, early = piece_refs[:bands], piece_refs[bands:]
    for k in range(bands):
        start = (band ^ k) * share
        for i in range(share - first + 1):
            later[k][i] = xt_ref[lax.rem(start + first + i, lines)]
        for i in range(first):
            early[k][i] = xt_ref[start + i]


def spread(tile, place, count):
    nothing = jnp.zeros_like(tile)
    return jnp.concatenate([jnp.where(place == k, tile, nothing) for k in range(count)], axis=0)


def project_kernel(words_ref, xt_ref, p_ref, below_ref, own_ref, above_ref, total):
    slots, proj_count, _ = p_ref.shape
    per_group = LANES // proj_count
    groups = own_ref.shape[0]
    total[...] = jnp.zeros_like(total)
    unroll = 8

    def body(i, carry):
        for u in range(unroll):
            t = i * unroll + u
            word = words_ref[t]
            line, group, place = word >> 16, (word >> 4) & 0xFFF, word & 0xF
            tile = spread(p_ref[t], place, per_group)
            total[group] += lax.dot_general(xt_ref[line], tile, NT, preferred_element_type=F32)
        return carry

    lax.fori_loop(0, slots // unroll, body, 0)
    below_ref[...] = total[:groups].astype(BF16)
    own_ref[...] = total[groups : 2 * groups]
    above_ref[...] = total[2 * groups :].astype(BF16)


def owner_kernel(bands, ids_ref, own_ref, left_ref, right_ref, energy_ref, scaled_ref, *piece_refs):
    groups = own_ref.shape[0]
    share = groups // bands
    first = ids_ref[0] * groups
    for g in range(groups):
        whole = own_ref[g] + left_ref[g].astype(F32) + right_ref[g].astype(F32)
        scaled_ref[g] = (whole * energy_ref[pl.ds(first + g, 1), :]).astype(BF16)
        piece_refs[-1][g] = whole.astype(BF16)
    for k in range(bands):
        for i in range(share):
            piece_refs[k][i] = piece_refs[-1][(ids_ref[1] ^ k) * share + i]


def apply_kernel(
    words_ref, xt_ref, p_ref, below_ref, above_ref, low_ref, own_ref, high_ref, pot_ref, out_ref, total, scaled
):
    slots, proj_count, _ = p_ref.shape
    lines, states, _ = xt_ref.shape
    groups = own_ref.shape[0]
    per_group = LANES // proj_count
    total[...] = jnp.zeros_like(total)
    unroll = 8

    scaled[:groups] = low_ref[...]
    scaled[groups : 2 * groups] = own_ref[...]
    scaled[2 * groups :] = high_ref[...]

    def body(i, carry):
        for u in range(unroll):
            t = i * unroll + u
            word = words_ref[t]
            line, group, place = word >> 16, (word >> 4) & 0xFFF, word & 0xF
            tile = spread(p_ref[t], place, per_group)
            total[line] += jnp.dot(scaled[group], tile, preferred_element_type=F32)
        return carry

    lax.fori_loop(0, slots // unroll, body, 0)

    step = 16

    def rows(i, carry):
        y0 = pl.multiple_of(i * step, step)
        results = []
        for j in range(step):
            y = y0 + j
            x = xt_ref[y].astype(F32)
            beside = xt_ref[lax.rem(y + 1, lines)].astype(F32) + xt_ref[lax.rem(y + lines - 1, lines)].astype(F32)
            beside += below_ref[y].astype(F32) + above_ref[y].astype(F32)
            beside += pltpu.roll(x, 1, 1) + pltpu.roll(x, x.shape[1] - 1, 1)
            value = (3.0 + pot_ref[pl.ds(y, 1), :]) * x - 0.5 * beside + total[y]
            results.append(value)
        turned = jnp.swapaxes(jnp.stack(results, axis=0), 0, 1)
        out_ref[:, pl.ds(y0, step), :] = turned.astype(BF16)
        return carry

    lax.fori_loop(0, lines // step, rows, 0)


def assemble_kernel(bands, ids_ref, *refs):
    pieces, outs = refs[:bands], refs[bands:]
    states = pieces[0].shape[1]
    band = ids_ref[1]
    at = 0
    for out in outs:
        for i in range(out.shape[0]):
            for k in range(bands):
                row = pl.multiple_of((band ^ k) * states, states)
                out[i, pl.ds(row, states), :] = pieces[k][at + i]
        at += out.shape[0]


def add_products(first, ids_ref, low_ref, high_ref, next_ref, low_beside, high_beside, pot_ref, share, acc):
    half = low_ref.shape[0]
    row = ids_ref[1] * share + first
    for part, ref, beside in ((0, low_ref, low_beside), (1, high_ref, high_beside)):
        xs, ys = [], []
        for i in range(half):
            here = ref[i]
            x = here.astype(F32)
            if i + 1 < half:
                after = ref[i + 1]
            else:
                after = high_ref[0] if part == 0 else next_ref[0]
            pot = pot_ref[pl.ds(row + part * half + i, 1), :]
            y = (3.0 + pot) * x - pltpu.roll(x, x.shape[1] - 1, 1)
            y = y - after.astype(F32) - beside[i].astype(F32)
            xs.append(here)
            ys.append(y.astype(BF16))
            if len(xs) == 4 or i + 1 == half:
                flat_x = jnp.concatenate(xs, axis=1)
                flat_y = jnp.concatenate(ys, axis=1)
                acc[0] += lax.dot_general(flat_x, flat_x, NT, preferred_element_type=F32)
                acc[1] += lax.dot_general(flat_y, flat_x, NT, preferred_element_type=F32)
                xs, ys = [], []


def gram_kernel(first, share, ids_ref, low, high, after, low_beside, high_beside, pot_ref, acc):
    acc[...] = jnp.zeros_like(acc)
    add_products(first, ids_ref, low, high, after, low_beside, high_beside, pot_ref, share, acc)


def final_kernel(
    bands, domains, share, ids_ref, low, high, after, low_beside, high_beside, pot_ref, begun, energy_ref, *refs
):
    pieces, out_ref, acc, projs = refs[:bands], refs[bands], refs[bands + 1], refs[bands + 2]
    acc[...] = begun[...]
    add_products(0, ids_ref, low, high, after, low_beside, high_beside, pot_ref, share, acc)
    groups, states = pieces[0].shape[:2]
    band = ids_ref[1]
    for k in range(bands):
        row = pl.multiple_of((band ^ k) * states, states)
        for g in range(groups):
            projs[g, pl.ds(row, states), :] = pieces[k][g]
    first = ids_ref[0] * groups * bands + band * groups
    for g in range(groups):
        here = projs[g]
        scaled = (here.astype(F32) * energy_ref[pl.ds(first + g, 1), :]).astype(BF16)
        acc[1] += lax.dot_general(scaled, here, NT, preferred_element_type=F32)
    gram = acc[0]
    hamil = 0.5 * (acc[1] + acc[1].T)
    total = gram.shape[0]
    rows, cols = total // bands, total // domains
    for r in range(bands):
        for c in range(domains):
            r0, c0 = r * rows, c * cols
            out_ref[r * domains + c, :, :cols] = gram[r0 : r0 + rows, c0 : c0 + cols].astype(BF16)
            out_ref[r * domains + c, :, cols:] = hamil[r0 : r0 + rows, c0 : c0 + cols].astype(BF16)


def local(orbitals, potential, projectors, tile_atom, tile_line, tile_count, energies):
    states, _, lines, cols_z = orbitals.shape
    slots, proj_count, _ = projectors.shape
    atom_total = energies.shape[0]
    domains, bands = lax.axis_size("domain"), lax.axis_size("band")
    domain, band = lax.axis_index("domain"), lax.axis_index("band")
    total_states = states * bands
    atoms_here = atom_total // domains
    per_group = LANES // proj_count
    groups = atoms_here // per_group
    share = lines // bands
    first = share // 4
    rest = share - first

    up = [(i, i + 1) for i in range(domains - 1)]
    down = [(i + 1, i) for i in range(domains - 1)]

    def swap(value, k):
        return lax.ppermute(value, "band", [(i, i ^ k) for i in range(bands)])

    ids = jnp.stack([domain, band]).astype(jnp.int32)
    near = jnp.clip(tile_atom - (domain - 1) * atoms_here, 0, 3 * atoms_here - 1)
    live = jnp.arange(slots, dtype=jnp.int32) < tile_count[0]
    place = jnp.where(live, near % per_group, per_group)
    words = (tile_line << 16) | ((near // per_group) << 4) | place
    field = orbitals.reshape(states, lines, cols_z)
    pot = potential.reshape(lines, cols_z)
    energy = energies.reshape(atom_total // per_group, LANES)

    packed = call(
        functools.partial(pack_kernel, bands, first),
        [((lines, states, cols_z), BF16)]
        + [((rest + 1, states, cols_z), BF16)] * bands
        + [((first, states, cols_z), BF16)] * bands,
        [("smem", ids), ("vmem", field)],
        moved=3 * field.size * 2,
    )
    xt, later, early = packed[0], packed[1 : 1 + bands], packed[1 + bands :]
    later = [later[0]] + [swap(later[k], k) for k in range(1, bands)]
    below = lax.ppermute(xt, "domain", up)
    above = lax.ppermute(xt, "domain", down)
    early = [early[0]] + [swap(early[k], k) for k in range(1, bands)]

    to_below, own, to_above = call(
        project_kernel,
        [((groups, states, LANES), BF16), ((groups, states, LANES), F32), ((groups, states, LANES), BF16)],
        [("smem", words), ("vmem", xt), ("vmem", projectors)],
        [pltpu.VMEM((3 * groups, states, LANES), F32)],
        flops=2 * slots * states * LANES * LANES * 4,
        moved=field.size * 4,
    )
    from_left = lax.ppermute(to_above, "domain", up)
    from_right = lax.ppermute(to_below, "domain", down)
    mine = call(
        functools.partial(owner_kernel, bands),
        [((groups, states, LANES), BF16)]
        + [((groups // bands, states, LANES), BF16)] * bands
        + [((groups, states, LANES), BF16)],
        [("smem", ids), ("vmem", own), ("vmem", from_left), ("vmem", from_right), ("vmem", energy)],
        moved=own.size * 12,
    )
    scaled, shares = mine[0], mine[1 : 1 + bands]
    low = lax.ppermute(scaled, "domain", up)
    high = lax.ppermute(scaled, "domain", down)
    shares = [shares[0]] + [swap(shares[k], k) for k in range(1, bands)]

    (applied,) = call(
        apply_kernel,
        [((states, lines, cols_z), BF16)],
        [
            ("smem", words), ("vmem", xt), ("vmem", projectors), ("vmem", below), ("vmem", above),
            ("vmem", low), ("vmem", scaled), ("vmem", high), ("vmem", pot),
        ],
        [pltpu.VMEM((lines, states, cols_z), F32), pltpu.VMEM((3 * groups, states, LANES), BF16)],
        flops=2 * slots * states * LANES * LANES * 4,
        moved=field.size * 10,
    )

    def gathered(pieces, counts):
        return call(
            functools.partial(assemble_kernel, bands),
            [((count, total_states, cols_z), BF16) for count in counts],
            [("smem", ids)] + [("vmem", piece) for piece in pieces],
            moved=sum(counts) * total_states * cols_z * 4,
        )

    def passed(halves):
        return lax.ppermute(halves[0], "domain", up), lax.ppermute(halves[1], "domain", down)

    late = gathered(later, (rest // 2, rest // 2, 1))
    late_beside = passed(late)
    (begun,) = call(
        functools.partial(gram_kernel, first, share),
        [((2, total_states, total_states), F32)],
        [("smem", ids)] + [("vmem", v) for v in (*late, *late_beside, pot)],
        flops=4 * total_states * total_states * rest * cols_z,
        moved=2 * rest * total_states * cols_z * 2,
    )
    soon = gathered(early, (first // 2, first // 2))
    soon_beside = passed(soon)
    (blocks,) = call(
        functools.partial(final_kernel, bands, domains, share),
        [((bands * domains, states, 2 * total_states // domains), BF16)],
        [("smem", ids)] + [("vmem", v) for v in (*soon, late[0], *soon_beside, pot, begun, energy, *shares)],
        [
            pltpu.VMEM((2, total_states, total_states), F32),
            pltpu.VMEM((groups // bands, total_states, LANES), BF16),
        ],
        flops=4 * total_states * total_states * first * cols_z,
        moved=2 * first * total_states * cols_z * 2,
    )
    landed = lax.all_to_all(blocks, ("band", "domain"), split_axis=0, concat_axis=0, tiled=True)
    scale = 1.0 / (lines * cols_z * domains)
    whole = jnp.sum(landed.astype(F32), axis=0) * scale
    cols = total_states // domains
    subspace = jnp.stack([whole[:, :cols], whole[:, cols:]])
    return applied.reshape(orbitals.shape), subspace


def solution(mesh):
    in_specs = (
        P("band", ("groups", "domain"), None, None),
        P(("groups", "domain"), None, None),
        P(("groups", "domain"), None, None),
        P(("groups", "domain")),
        P(("groups", "domain")),
        P(("groups", "domain")),
        P("groups", None),
    )
    out_specs = (P("band", ("groups", "domain"), None, None), P(None, ("groups", "band"), "domain"))
    return jax.shard_map(local, mesh=mesh, in_specs=in_specs, out_specs=out_specs, check_vma=False)
```

```python
import functools

import jax
import jax.numpy as jnp
from jax import lax
from jax.experimental import pallas as pl
from jax.experimental.pallas import tpu as pltpu
from jax.sharding import PartitionSpec as P

F32 = jnp.float32
BF16 = jnp.bfloat16
LANES = 128
ROWS = 16
VMEM_BYTES = 48 * 1024 * 1024
NT = (((1,), (1,)), ((), ()))
WHOLE = pl.BlockSpec(memory_space=pltpu.VMEM)
SCALARS = pl.BlockSpec(memory_space=pltpu.SMEM)
UNREAD = pl.BlockSpec(memory_space=pl.ANY)


def call(kernel, grid, in_specs, out_specs, outs, scratch, args, micros):
    return pl.pallas_call(
        kernel,
        grid=grid,
        out_shape=[jax.ShapeDtypeStruct(shape, kind) for shape, kind in outs],
        in_specs=in_specs,
        out_specs=out_specs,
        scratch_shapes=scratch,
        compiler_params=pltpu.CompilerParams(vmem_limit_bytes=VMEM_BYTES),
        cost_estimate=pl.CostEstimate(flops=int(micros * 1.1e9), bytes_accessed=1 << 20, transcendentals=0),
    )(*args)


def line_at(index, states):
    return pl.ds(pl.multiple_of(index * states, states), states)


def pack_kernel(share, x_hbm, pot_ref, xt_hbm, msg_hbm, x, xt, pots, in_sems, out_sems, msg_sems):
    states, lines, _ = x.shape
    parts = lines // share
    chunks = in_sems.shape[0]
    size = lines // chunks
    loads = []
    for c in range(chunks):
        where = (slice(None), pl.ds(c * size, size), slice(None))
        loads.append(pltpu.make_async_copy(x_hbm.at[where], x.at[where], in_sems.at[c]))
        loads[-1].start()

    here = pot_ref[...]
    high = here.astype(BF16)
    rest = (here - high.astype(F32)).astype(BF16)
    pots[...] = jnp.zeros_like(pots)
    for j in range(parts):
        both = jnp.concatenate([high[j * share : (j + 1) * share], rest[j * share : (j + 1) * share]], axis=0)
        pots[j, : 2 * share, :] = both
    span = (share + 1) * states
    tail = pltpu.make_async_copy(pots, msg_hbm.at[:, pl.ds(span, pots.shape[1]), :], msg_sems.at[parts + 1])
    tail.start()

    sends = []

    def send(j):
        last = j == parts - 1
        count = share * states if last else span
        sends.append(
            pltpu.make_async_copy(
                xt.at[pl.ds(j * share * states, count)], msg_hbm.at[j, pl.ds(0, count), :], msg_sems.at[j]
            )
        )
        sends[-1].start()
        if last:
            sends.append(
                pltpu.make_async_copy(
                    xt.at[pl.ds(0, states)], msg_hbm.at[j, pl.ds(count, states), :], msg_sems.at[parts]
                )
            )
            sends[-1].start()

    sent = 0
    for c in range(chunks):
        loads[c].wait()
        for y0 in range(c * size, (c + 1) * size, ROWS):
            for s0 in range(0, states, ROWS):
                block = x[s0 : s0 + ROWS, y0 : y0 + ROWS, :].astype(F32)
                turned = jnp.swapaxes(block, 0, 1).astype(BF16)
                for i in range(ROWS):
                    xt[(y0 + i) * states + s0 : (y0 + i) * states + s0 + ROWS, :] = turned[i]
        while sent < parts - 1 and (sent + 1) * share + 1 <= (c + 1) * size:
            send(sent)
            sent += 1
        where = pl.ds(c * size * states, size * states)
        sends.append(pltpu.make_async_copy(xt.at[where], xt_hbm.at[where], out_sems.at[c]))
        sends[-1].start()
    while sent < parts:
        send(sent)
        sent += 1
    for copy in sends:
        copy.wait()
    tail.wait()


def project_kernel(words_ref, ids_ref, xt_ref, p_ref, core_ref, own_ref, link_ref, total):
    slots, proj_count, _ = p_ref.shape
    groups, states, _ = own_ref.shape
    per_group = LANES // proj_count
    unroll = 16

    def clear(i, carry):
        for u in range(per_group):
            total[i * per_group + u] = jnp.zeros_like(total[0])
        return carry

    lax.fori_loop(0, 3 * groups, clear, 0)

    def body(i, carry):
        for u in range(unroll):
            t = i * unroll + u
            word = words_ref[t]
            line, atom = word >> 16, word & 0xFFFF
            total[atom] += lax.dot_general(
                p_ref[t], xt_ref[line_at(line, states), :], NT, preferred_element_type=F32
            )
        return carry

    lax.fori_loop(0, slots // unroll, body, 0)
    odd = ids_ref[0] & 1
    core_first, link_first = (1 - odd) * 2 * groups, odd * 2 * groups

    def turned(group):
        tiles = [total[group * per_group + u] for u in range(per_group)]
        return jnp.concatenate(tiles, axis=0).T

    for g in range(groups):
        core_ref[g] = turned(core_first + g).astype(BF16)
        link_ref[g] = turned(link_first + g).astype(BF16)
        own_ref[g] = turned(groups + g)


def owner_kernel(ids_ref, own_ref, core_ref, link_ref, energy_ref, scaled_ref, whole_ref):
    groups = own_ref.shape[0]
    first = ids_ref[0] * groups
    for g in range(groups):
        whole = own_ref[g] + core_ref[g].astype(F32) + link_ref[g].astype(F32)
        scaled_ref[g] = (whole * energy_ref[pl.ds(first + g, 1), :]).astype(BF16)
        whole_ref[g] = whole.astype(BF16)


def nonlocal_kernel(words_ref, ids_ref, p_ref, core_ref, own_ref, link_ref, out_ref, atoms):
    slots, proj_count, _ = p_ref.shape
    groups, states, _ = own_ref.shape
    per_group = LANES // proj_count
    lines = out_ref.shape[0] // states
    unroll = 16

    def clear(i, carry):
        out_ref[line_at(i, states), :] = jnp.zeros((states, LANES), F32)
        return carry

    lax.fori_loop(0, lines, clear, 0)
    odd = ids_ref[0] & 1
    for first, ref in (((1 - odd) * 2 * groups, core_ref), (groups, own_ref), (odd * 2 * groups, link_ref)):
        for g in range(groups):
            tile = ref[g]
            for u in range(per_group):
                atoms[(first + g) * per_group + u] = tile[:, u * proj_count : (u + 1) * proj_count]

    def body(i, carry):
        for u in range(unroll):
            t = i * unroll + u
            word = words_ref[t]
            line, atom = word >> 16, word & 0xFFFF
            out_ref[line_at(line, states), :] += jnp.dot(atoms[atom], p_ref[t], preferred_element_type=F32)
        return carry

    lax.fori_loop(0, slots // unroll, body, 0)


def stencil_kernel(xt_ref, before_ref, after_ref, core_ref, link_ref, nonlocal_ref, pot_ref, unread, out_ref):
    states, lines, _ = out_ref.shape

    def line(i):
        if i < 0:
            return before_ref[...].astype(F32)
        if i == lines:
            return after_ref[...].astype(F32)
        return xt_ref[i * states : (i + 1) * states, :].astype(F32)

    results = []
    for i in range(lines):
        rows = slice(i * states, (i + 1) * states)
        x = line(i)
        beside = line(i - 1) + line(i + 1)
        beside += core_ref[rows, :].astype(F32) + link_ref[rows, :].astype(F32)
        beside += pltpu.roll(x, 1, 1) + pltpu.roll(x, x.shape[1] - 1, 1)
        results.append((3.0 + pot_ref[i : i + 1, :]) * x - 0.5 * beside + nonlocal_ref[rows, :])
    out_ref[...] = jnp.swapaxes(jnp.stack(results, axis=0), 0, 1).astype(BF16)


def gram_kernel(
    bands, domains, states, share, ids_ref, here_ref, next_ref, proj_ref, energy_ref, unread, out_ref, acc
):
    plane = pl.program_id(0)

    @pl.when(plane == 0)
    def _():
        acc[...] = jnp.zeros_like(acc)

    keep = jnp.where(plane < domains - 1, 1.0, 0.0).astype(F32)

    def line(ref, i):
        return jnp.concatenate([ref[b, i * states : (i + 1) * states, :] for b in range(bands)], axis=0)

    span = (share + 1) * states
    pots = here_ref[0, span : span + 2 * share + (-2 * share) % ROWS, :].astype(F32)
    group = 4
    for i0 in range(0, share, group):
        xs, ys = [], []
        for i in range(i0, min(i0 + group, share)):
            cell = line(here_ref, i)
            x = cell.astype(F32)
            pot = pots[i : i + 1] + pots[share + i : share + i + 1]
            y = (3.0 + pot) * x - pltpu.roll(x, x.shape[1] - 1, 1)
            y = y - line(here_ref, i + 1).astype(F32) - keep * line(next_ref, i).astype(F32)
            xs.append(cell)
            ys.append(y.astype(BF16))
        flat_x = jnp.concatenate(xs, axis=1)
        flat_y = jnp.concatenate(ys, axis=1)
        acc[0] += lax.dot_general(flat_x, flat_x, NT, preferred_element_type=F32)
        acc[1] += lax.dot_general(flat_y, flat_x, NT, preferred_element_type=F32)

    @pl.when(plane == domains - 1)
    def _():
        groups = proj_ref.shape[0] // bands
        first = (ids_ref[0] * bands + ids_ref[1]) * groups
        for g in range(groups):
            here = jnp.concatenate([proj_ref[b * groups + g] for b in range(bands)], axis=0)
            scaled = (here.astype(F32) * energy_ref[pl.ds(first + g, 1), :]).astype(BF16)
            acc[1] += lax.dot_general(scaled, here, NT, preferred_element_type=F32)
        gram = acc[0]
        hamil = 0.5 * (acc[1] + acc[1].T)
        cols = gram.shape[0] // domains
        for c in range(domains):
            for r in range(bands):
                r0, c0 = r * states, c * cols
                out_ref[c * bands + r, :, :cols] = gram[r0 : r0 + states, c0 : c0 + cols].astype(BF16)
                out_ref[c * bands + r, :, cols:] = hamil[r0 : r0 + states, c0 : c0 + cols].astype(BF16)


def local(orbitals, potential, projectors, tile_atom, tile_line, tile_count, energies):
    states, _, lines, cols_z = orbitals.shape
    slots, proj_count, _ = projectors.shape
    atom_total = energies.shape[0]
    domains, bands = lax.axis_size("domain"), lax.axis_size("band")
    domain, band = lax.axis_index("domain"), lax.axis_index("band")
    total_states = states * bands
    atoms_here = atom_total // domains
    per_group = LANES // proj_count
    groups = atoms_here // per_group
    parts = domains * bands
    share = lines // parts
    pot_rows = 2 * share + (-2 * share) % ROWS
    message = (share + 1) * states + pot_rows

    core_pairs = [(i, i ^ 1) for i in range(domains) if i ^ 1 < domains]
    link_pairs = [(i, (i + 1 ^ 1) - 1) for i in range(1, domains) if (i + 1 ^ 1) - 1 < domains]

    ids = jnp.stack([domain, band]).astype(jnp.int32)
    near = jnp.clip(tile_atom - (domain - 1) * atoms_here, 0, 3 * atoms_here - 1)
    live = jnp.arange(slots, dtype=jnp.int32) < tile_count[0]
    project_words = (tile_line << 16) | jnp.where(live, near, 3 * atoms_here)
    nonlocal_words = (jnp.where(live, tile_line, lines) << 16) | near
    field = orbitals.reshape(states, lines, cols_z)
    pot = potential.reshape(lines, cols_z)
    energy = energies.reshape(atom_total // per_group, LANES)

    chunks = 4
    xt, msg = call(
        functools.partial(pack_kernel, share),
        (),
        [UNREAD, WHOLE],
        [UNREAD, UNREAD],
        [((lines * states, cols_z), BF16), ((parts, message, cols_z), BF16)],
        [
            pltpu.VMEM((states, lines, cols_z), BF16),
            pltpu.VMEM((lines * states, cols_z), BF16),
            pltpu.VMEM((parts, pot_rows, cols_z), BF16),
            pltpu.SemaphoreType.DMA((chunks,)),
            pltpu.SemaphoreType.DMA((chunks,)),
            pltpu.SemaphoreType.DMA((parts + 2,)),
        ],
        (field, pot),
        4,
    )
    landed = lax.all_to_all(msg, ("domain", "band"), split_axis=0, concat_axis=0, tiled=True)
    link_field = lax.ppermute(xt, "domain", link_pairs)
    core_field = lax.ppermute(xt, "domain", core_pairs)

    group_shape = (groups, states, LANES)
    to_core, own, to_link = call(
        project_kernel,
        (),
        [SCALARS, SCALARS, WHOLE, WHOLE],
        [WHOLE] * 3,
        [(group_shape, BF16), (group_shape, F32), (group_shape, BF16)],
        [pltpu.VMEM((3 * atoms_here + 1, proj_count, states), F32)],
        (project_words, ids, xt, projectors),
        9,
    )
    from_link = lax.ppermute(to_link, "domain", link_pairs)
    from_core = lax.ppermute(to_core, "domain", core_pairs)
    scaled, whole = call(
        owner_kernel,
        (),
        [SCALARS] + [WHOLE] * 4,
        [WHOLE] * 2,
        [(group_shape, BF16), (group_shape, BF16)],
        [],
        (ids, own, from_core, from_link, energy),
        1,
    )
    link_scaled = lax.ppermute(scaled, "domain", link_pairs)
    core_scaled = lax.ppermute(scaled, "domain", core_pairs)
    shares = lax.all_to_all(whole, "band", split_axis=0, concat_axis=0, tiled=True)

    (added,) = call(
        nonlocal_kernel,
        (),
        [SCALARS, SCALARS] + [WHOLE] * 4,
        [WHOLE],
        [(((lines + 1) * states, cols_z), F32)],
        [pltpu.VMEM((3 * atoms_here, states, proj_count), BF16)],
        (nonlocal_words, ids, projectors, core_scaled, scaled, link_scaled),
        9,
    )

    (blocks,) = call(
        functools.partial(gram_kernel, bands, domains, states, share),
        (domains,),
        [
            SCALARS,
            pl.BlockSpec((bands, message, cols_z), lambda d: (d, 0, 0)),
            pl.BlockSpec((bands, message, cols_z), lambda d: (jnp.minimum(d + 1, domains - 1), 0, 0)),
            WHOLE,
            WHOLE,
            UNREAD,
        ],
        [WHOLE],
        [((parts, states, 2 * total_states // domains), BF16)],
        [pltpu.VMEM((2, total_states, total_states), F32)],
        (ids, landed, landed, shares, energy, added),
        4,
    )
    summed = lax.all_to_all(blocks, ("domain", "band"), split_axis=0, concat_axis=0, tiled=True)

    steps = lines // ROWS
    rows = ROWS * states
    block = pl.BlockSpec((rows, cols_z), lambda i: (i, 0))
    (applied,) = call(
        stencil_kernel,
        (steps,),
        [
            block,
            pl.BlockSpec((states, cols_z), lambda i: (lax.rem(i * ROWS + lines - 1, lines), 0)),
            pl.BlockSpec((states, cols_z), lambda i: (lax.rem(i * ROWS + ROWS, lines), 0)),
            block,
            block,
            block,
            pl.BlockSpec((ROWS, cols_z), lambda i: (i, 0)),
            UNREAD,
        ],
        [pl.BlockSpec((states, ROWS, cols_z), lambda i: (0, i, 0))],
        [((states, lines, cols_z), BF16)],
        [],
        (xt, xt, xt, core_field, link_field, added, pot, blocks),
        7,
    )
    scale = 1.0 / (lines * cols_z * domains)
    result = jnp.sum(summed.astype(F32), axis=0) * scale
    cols = total_states // domains
    subspace = jnp.stack([result[:, :cols], result[:, cols:]])
    return applied.reshape(orbitals.shape), subspace


def solution(mesh):
    in_specs = (
        P("band", ("groups", "domain"), None, None),
        P(("groups", "domain"), None, None),
        P(("groups", "domain"), None, None),
        P(("groups", "domain")),
        P(("groups", "domain")),
        P(("groups", "domain")),
        P("groups", None),
    )
    out_specs = (P("band", ("groups", "domain"), None, None), P(None, ("groups", "band"), "domain"))
    return jax.shard_map(local, mesh=mesh, in_specs=in_specs, out_specs=out_specs, check_vma=False)
```

```python
import functools

import jax
import jax.numpy as jnp
from jax import lax
from jax.experimental import pallas as pl
from jax.experimental.pallas import tpu as pltpu
from jax.sharding import PartitionSpec as P

F32 = jnp.float32
BF16 = jnp.bfloat16
LANES = 128
ROWS = 16
VMEM_BYTES = 32 * 1024 * 1024
NT = (((1,), (1,)), ((), ()))
WHOLE = pl.BlockSpec(memory_space=pltpu.VMEM)
SCALARS = pl.BlockSpec(memory_space=pltpu.SMEM)
FAR = pl.BlockSpec(memory_space=pltpu.HBM)
UNREAD = pl.BlockSpec(memory_space=pl.ANY)
copies = pltpu.SemaphoreType.DMA


def call(kernel, grid, in_specs, out_specs, outs, scratch, args, micros, aliases=None):
    return pl.pallas_call(
        kernel,
        grid=grid,
        out_shape=[jax.ShapeDtypeStruct(shape, kind) for shape, kind in outs],
        in_specs=in_specs,
        out_specs=out_specs,
        scratch_shapes=scratch,
        input_output_aliases=aliases or {},
        compiler_params=pltpu.CompilerParams(vmem_limit_bytes=VMEM_BYTES),
        cost_estimate=pl.CostEstimate(flops=int(micros * 1.1e9), bytes_accessed=1 << 20, transcendentals=0),
    )(*args)


def start(copy):
    copy.start()
    return copy


def pack_kernel(bands, first, ids_ref, x_hbm, xt, xt_hbm, *refs):
    halves, pieces, (x, in_sems, out_sems) = refs[:2], refs[2 : 1 + bands], refs[1 + bands :]
    states, lines, _ = x.shape
    share = lines // bands
    band = ids_ref[1]
    chunks = in_sems.shape[0]
    size = lines // chunks
    loads = []
    for c in range(chunks):
        where = (slice(None), pl.ds(c * size, size), slice(None))
        loads.append(start(pltpu.make_async_copy(x_hbm.at[where], x.at[where], in_sems.at[c])))

    for c in range(chunks):
        loads[c].wait()
        for y0 in range(c * size, (c + 1) * size, ROWS):
            for s0 in range(0, states, ROWS):
                block = x[s0 : s0 + ROWS, y0 : y0 + ROWS, :].astype(F32)
                turned = jnp.swapaxes(block, 0, 1).astype(BF16)
                xt[y0 : y0 + ROWS, s0 : s0 + ROWS, :] = turned

    sends = []

    def send(source, target):
        sends.append(start(pltpu.make_async_copy(source, target, out_sems.at[len(sends)])))

    for k in range(1, bands):
        begin = (band ^ k) * share
        count = share - first
        send(xt.at[pl.ds(begin + first, count)], pieces[k - 1].at[pl.ds(0, count)])
        send(xt.at[pl.ds(lax.rem(begin + share, lines), 1)], pieces[k - 1].at[pl.ds(count, 1)])
    send(xt.at[pl.ds(0, lines // 2)], halves[0])
    send(xt.at[pl.ds(lines // 2, lines // 2)], halves[1])
    send(xt, xt_hbm)
    for copy in sends:
        copy.wait()


def project_kernel(words_ref, ids_ref, xt_ref, p_hbm, core_ref, own_ref, link_ref, total, p_ref, sems):
    slots, proj_count, _ = p_ref.shape
    groups, states, _ = own_ref.shape
    per_group = LANES // proj_count
    chunks = sems.shape[0]
    size = slots // chunks
    unroll = 16
    loads = []
    for c in range(chunks):
        where = pl.ds(c * size, size)
        loads.append(start(pltpu.make_async_copy(p_hbm.at[where], p_ref.at[where], sems.at[c])))

    def clear(i, carry):
        for u in range(per_group):
            total[i * per_group + u] = jnp.zeros_like(total[0])
        return carry

    lax.fori_loop(0, 3 * groups, clear, 0)

    def body(i, carry):
        for u in range(unroll):
            t = i * unroll + u
            word = words_ref[t]
            line, atom = word >> 16, word & 0xFFFF
            total[atom] += lax.dot_general(p_ref[t], xt_ref[line], NT, preferred_element_type=F32)
        return carry

    for c in range(chunks):
        loads[c].wait()
        lax.fori_loop(c * size // unroll, (c + 1) * size // unroll, body, 0)
    odd = ids_ref[0] & 1
    core_first, link_first = (1 - odd) * 2 * groups, odd * 2 * groups

    def turned(group):
        tiles = [total[group * per_group + u] for u in range(per_group)]
        return jnp.concatenate(tiles, axis=0).T

    for g in range(groups):
        core_ref[g] = turned(core_first + g).astype(BF16)
        link_ref[g] = turned(link_first + g).astype(BF16)
        own_ref[g] = turned(groups + g)


def owner_kernel(bands, first, ids_ref, xt_ref, own_ref, core_hbm, link_hbm, energy_ref, half_in, *refs):
    half_out, scaled_ref, scaled_hbm, whole_ref = refs[:4]
    messages, (core_ref, link_ref, in_sems, out_sems) = refs[4 : 3 + bands], refs[3 + bands :]
    lines = xt_ref.shape[0]
    share = lines // bands
    band = ids_ref[1]
    groups = own_ref.shape[0]
    group_share = groups // bands
    loads = [
        start(pltpu.make_async_copy(core_hbm, core_ref, in_sems.at[0])),
        start(pltpu.make_async_copy(link_hbm, link_ref, in_sems.at[1])),
    ]
    sends = []

    def send(source, target):
        sends.append(start(pltpu.make_async_copy(source, target, out_sems.at[len(sends)])))

    for k in range(1, bands):
        send(xt_ref.at[pl.ds((band ^ k) * share, first)], messages[k - 1].at[pl.ds(0, first)])
    for copy in loads:
        copy.wait()
    row = ids_ref[0] * groups
    for g in range(groups):
        whole = own_ref[g] + core_ref[g].astype(F32) + link_ref[g].astype(F32)
        scaled_ref[g] = (whole * energy_ref[pl.ds(row + g, 1), :]).astype(BF16)
        whole_ref[g] = whole.astype(BF16)
    send(scaled_ref, scaled_hbm)
    for k in range(1, bands):
        send(whole_ref.at[pl.ds((band ^ k) * group_share, group_share)], messages[k - 1].at[pl.ds(first, group_share)])
    for copy in sends:
        copy.wait()


def nonlocal_kernel(words_ref, ids_ref, p_hbm, core_hbm, own_ref, link_hbm, out_ref, atoms, p_ref, core_ref, link_ref, sems):
    slots, proj_count, _ = p_ref.shape
    groups, states, _ = own_ref.shape
    per_group = LANES // proj_count
    lines = out_ref.shape[0]
    unroll = 16
    pairs = ((core_hbm, core_ref), (link_hbm, link_ref), (p_hbm, p_ref))
    loads = [start(pltpu.make_async_copy(far, near, sems.at[i])) for i, (far, near) in enumerate(pairs)]

    def clear(i, carry):
        out_ref[i] = jnp.zeros((states, LANES), F32)
        return carry

    lax.fori_loop(0, lines, clear, 0)
    odd = ids_ref[0] & 1

    def spread(first, ref):
        for g in range(groups):
            tile = ref[g]
            for u in range(per_group):
                atoms[(first + g) * per_group + u] = tile[:, u * proj_count : (u + 1) * proj_count]

    spread(groups, own_ref)
    loads[0].wait()
    spread((1 - odd) * 2 * groups, core_ref)
    loads[1].wait()
    spread(odd * 2 * groups, link_ref)
    loads[2].wait()

    def body(i, carry):
        for u in range(unroll):
            t = i * unroll + u
            word = words_ref[t]
            line, atom = word >> 16, word & 0xFFFF
            out_ref[line] += jnp.dot(atoms[atom], p_ref[t], preferred_element_type=F32)
        return carry

    lax.fori_loop(0, slots // unroll, body, 0)


def stencil_kernel(xt_ref, core_ref, early_ref, late_ref, added_ref, pot_ref, ring_ref, unread, out_ref):
    states, here, _ = out_ref.shape
    lines = xt_ref.shape[0]
    step = pl.program_id(0)
    y0 = step * here
    early = step < pl.num_programs(0) // 2
    for s0 in range(0, states, ROWS):
        rows = slice(s0, s0 + ROWS)
        results = []
        cells = jnp.concatenate([xt_ref[y0 + i, rows, :] for i in range(here)], axis=0)
        along = jnp.dot(cells, ring_ref[...], preferred_element_type=F32)
        before = xt_ref[lax.rem(y0 + lines - 1, lines), rows, :].astype(F32)
        x = xt_ref[y0, rows, :].astype(F32)
        for i in range(here):
            after = xt_ref[lax.rem(y0 + i + 1, lines), rows, :].astype(F32)
            link = jnp.where(early, early_ref[i, rows, :].astype(F32), late_ref[i, rows, :].astype(F32))
            beside = (before + after) + (core_ref[i, rows, :].astype(F32) + link)
            value = along[i * ROWS : (i + 1) * ROWS] + pot_ref[i : i + 1, :] * x
            results.append(value + added_ref[y0 + i, rows, :] - 0.5 * beside)
            before, x = x, after
        out_ref[rows, :, :] = jnp.swapaxes(jnp.stack(results, axis=0), 0, 1).astype(BF16)


def gather_kernel(bands, first, share, ids_ref, xt_ref, shares_ref, after_hbm, unread, *refs):
    pieces, outs = refs[: bands - 1], refs[bands - 1 :]
    later = after_hbm is None
    all_ref, pass_hbm = outs[:2]
    projs_ref = None if later else outs[2]
    sems, pass_sem = outs[-2:]
    lines, states, _ = xt_ref.shape
    band = ids_ref[1]
    begin = band * share + first
    count = all_ref.shape[0] - 1
    loads = []

    def load(source, target):
        loads.append(start(pltpu.make_async_copy(source, target, sems.at[len(loads)])))

    def at(k):
        return pl.ds(pl.multiple_of((band ^ k) * states, states), states)

    brought = count + 1 if later else count
    load(xt_ref.at[pl.ds(begin, count)], all_ref.at[pl.ds(0, count), at(0), :])
    for k in range(1, bands):
        load(pieces[k - 1].at[pl.ds(0, brought)], all_ref.at[pl.ds(0, brought), at(k), :])
    if later:
        load(xt_ref.at[pl.ds(lax.rem(begin + count, lines), 1)], all_ref.at[pl.ds(count, 1), at(0), :])
    else:
        load(after_hbm.at[pl.ds(0, 1)], all_ref.at[pl.ds(count, 1)])
        held = projs_ref.shape[0]
        load(shares_ref.at[pl.ds(band * held, held)], projs_ref.at[:, at(0), :])
        for k in range(1, bands):
            load(pieces[k - 1].at[pl.ds(count, held)], projs_ref.at[:, at(k), :])
    for copy in loads:
        copy.wait()
    half = count // 2
    passed = pltpu.make_async_copy(all_ref.at[pl.ds((1 - (ids_ref[0] & 1)) * half, half)], pass_hbm, pass_sem)
    passed.start()
    passed.wait()


def add_products(row, ids_ref, all_ref, core_ref, link_ref, pot_ref, acc):
    half = core_ref.shape[0]
    group = 4
    mine = (ids_ref[0] & 1) * half
    for part, base in ((0, mine), (1, half - mine)):
        for i0 in range(0, half, group):
            xs, ys = [], []
            for i in range(i0, min(i0 + group, half)):
                cell = all_ref[base + i]
                x = cell.astype(F32)
                y = (3.0 + pot_ref[pl.ds(row + base + i, 1), :]) * x - pltpu.roll(x, x.shape[1] - 1, 1)
                y = y - all_ref[base + i + 1].astype(F32)
                if part == 0:
                    y = y - core_ref[i].astype(F32) - link_ref[i].astype(F32)
                xs.append(cell)
                ys.append(y.astype(BF16))
            flat_x = jnp.concatenate(xs, axis=1)
            flat_y = jnp.concatenate(ys, axis=1)
            acc[0] += lax.dot_general(flat_x, flat_x, NT, preferred_element_type=F32)
            acc[1] += lax.dot_general(flat_y, flat_x, NT, preferred_element_type=F32)


def gram_kernel(first, share, ids_ref, all_ref, core_ref, link_ref, pot_ref, unread, acc):
    acc[...] = jnp.zeros_like(acc)
    add_products(ids_ref[1] * share + first, ids_ref, all_ref, core_ref, link_ref, pot_ref, acc)


def final_kernel(
    bands, domains, share, ids_ref, all_ref, core_ref, link_ref, pot_ref, begun_ref, proj_ref, energy_ref, out_ref, acc
):
    acc[...] = begun_ref[...]
    add_products(ids_ref[1] * share, ids_ref, all_ref, core_ref, link_ref, pot_ref, acc)
    groups = proj_ref.shape[0]
    first = (ids_ref[0] * bands + ids_ref[1]) * groups
    for g in range(groups):
        here = proj_ref[g]
        scaled = (here.astype(F32) * energy_ref[pl.ds(first + g, 1), :]).astype(BF16)
        acc[1] += lax.dot_general(scaled, here, NT, preferred_element_type=F32)
    gram = acc[0]
    hamil = 0.5 * (acc[1] + acc[1].T)
    rows, cols = gram.shape[0] // bands, gram.shape[0] // domains
    for c in range(domains):
        for r in range(bands):
            r0, c0 = r * rows, c * cols
            out_ref[c * bands + r, :, :cols] = gram[r0 : r0 + rows, c0 : c0 + cols].astype(BF16)
            out_ref[c * bands + r, :, cols:] = hamil[r0 : r0 + rows, c0 : c0 + cols].astype(BF16)


def local(orbitals, potential, projectors, tile_atom, tile_line, tile_count, energies):
    states, _, lines, cols_z = orbitals.shape
    slots, proj_count, _ = projectors.shape
    atom_total = energies.shape[0]
    domains, bands = lax.axis_size("domain"), lax.axis_size("band")
    domain, band = lax.axis_index("domain"), lax.axis_index("band")
    total_states = states * bands
    atoms_here = atom_total // domains
    per_group = LANES // proj_count
    groups = atoms_here // per_group
    group_share = groups // bands
    parts = domains * bands
    share = lines // bands
    first = share // 4
    rest = share - first

    core_pairs = [(i, i ^ 1) for i in range(domains) if i ^ 1 < domains]
    link_pairs = [(i, ((i + 1) ^ 1) - 1) for i in range(1, domains) if ((i + 1) ^ 1) - 1 < domains]
    band_pairs = [[(i, i ^ k) for i in range(bands)] for k in range(bands)]
    far_first = sorted(range(1, bands), key=lambda k: -k)

    def swapped(values):
        got = {k: lax.ppermute(values[k - 1], "band", band_pairs[k]) for k in far_first}
        return [got[k] for k in range(1, bands)]

    ids = jnp.stack([domain, band]).astype(jnp.int32)
    near = jnp.clip(tile_atom - (domain - 1) * atoms_here, 0, 3 * atoms_here - 1)
    live = jnp.arange(slots, dtype=jnp.int32) < tile_count[0]
    project_words = (tile_line << 16) | jnp.where(live, near, 3 * atoms_here)
    nonlocal_words = (jnp.where(live, tile_line, lines) << 16) | near
    field = orbitals.reshape(states, lines, cols_z)
    pot = potential.reshape(lines, cols_z)
    energy = energies.reshape(atom_total // per_group, LANES)
    eye = jnp.eye(cols_z, dtype=F32)
    ring = (3.0 * eye - 0.5 * (jnp.roll(eye, 1, axis=0) + jnp.roll(eye, -1, axis=0))).astype(BF16)

    chunks = 4
    line_shape, half_shape = (lines, states, cols_z), (lines // 2, states, cols_z)
    packed = call(
        functools.partial(pack_kernel, bands, first),
        (),
        [SCALARS, FAR],
        [WHOLE] + [FAR] * (2 + bands),
        [(line_shape, BF16), (line_shape, BF16), (half_shape, BF16), (half_shape, BF16)]
        + [((rest + 1, states, cols_z), BF16)] * (bands - 1),
        [pltpu.VMEM((states, lines, cols_z), BF16), copies((chunks,)), copies((2 * bands + 1,))],
        (ids, field),
        3,
    )
    xt, xt_far, early_half, late_half = packed[:4]
    later = swapped(packed[4:])
    link_early = lax.ppermute(early_half, "domain", link_pairs)
    core_field = lax.ppermute(xt_far, "domain", core_pairs)

    group_shape = (groups, states, LANES)
    to_core, own, to_link = call(
        project_kernel,
        (),
        [SCALARS, SCALARS, WHOLE, FAR],
        [WHOLE] * 3,
        [(group_shape, BF16), (group_shape, F32), (group_shape, BF16)],
        [
            pltpu.VMEM((3 * atoms_here + 1, proj_count, states), F32),
            pltpu.VMEM(projectors.shape, BF16),
            copies((4,)),
        ],
        (project_words, ids, xt, projectors),
        8,
    )
    from_link = lax.ppermute(to_link, "domain", link_pairs)
    from_core = lax.ppermute(to_core, "domain", core_pairs)
    owned = call(
        functools.partial(owner_kernel, bands, first),
        (),
        [SCALARS, WHOLE, WHOLE, FAR, FAR, WHOLE, FAR],
        [FAR, WHOLE, FAR, WHOLE] + [FAR] * (bands - 1),
        [(half_shape, BF16)]
        + [(group_shape, BF16)] * 3
        + [((first + group_share, states, cols_z), BF16)] * (bands - 1),
        [pltpu.VMEM(group_shape, BF16), pltpu.VMEM(group_shape, BF16), copies((2,)), copies((2 * bands - 1,))],
        (ids, xt, own, from_core, from_link, energy, late_half),
        1,
        aliases={6: 0},
    )
    late_half, scaled, scaled_far, whole = owned[:4]
    link_scaled = lax.ppermute(scaled_far, "domain", link_pairs)
    core_scaled = lax.ppermute(scaled_far, "domain", core_pairs)
    link_late = lax.ppermute(late_half, "domain", link_pairs)
    early = swapped(owned[4:])

    (added,) = call(
        nonlocal_kernel,
        (),
        [SCALARS, SCALARS, FAR, FAR, WHOLE, FAR],
        [WHOLE],
        [((lines + 1, states, cols_z), F32)],
        [
            pltpu.VMEM((3 * atoms_here, states, proj_count), BF16),
            pltpu.VMEM(projectors.shape, BF16),
            pltpu.VMEM(group_shape, BF16),
            pltpu.VMEM(group_shape, BF16),
            copies((3,)),
        ],
        (nonlocal_words, ids, projectors, core_scaled, scaled, link_scaled),
        9,
    )

    def later_kernel(ids_ref, xt_ref, unread, *refs):
        gather_kernel(bands, first, share, ids_ref, xt_ref, None, None, unread, *refs)

    later_all, later_pass = call(
        later_kernel,
        (),
        [SCALARS, WHOLE, UNREAD] + [FAR] * (bands - 1),
        [WHOLE, FAR],
        [((rest + 1, total_states, cols_z), BF16), ((rest // 2, total_states, cols_z), BF16)],
        [copies((bands + 1,)), copies],
        (ids, xt, added, *later),
        2,
    )
    later_link = lax.ppermute(later_pass, "domain", link_pairs)
    later_core = lax.ppermute(later_pass, "domain", core_pairs)

    steps = lines // ROWS
    block = pl.BlockSpec((ROWS, states, cols_z), lambda i: (i, 0, 0))
    (applied,) = call(
        stencil_kernel,
        (steps,),
        [
            WHOLE,
            block,
            pl.BlockSpec((ROWS, states, cols_z), lambda i: (jnp.minimum(i, steps // 2 - 1), 0, 0)),
            pl.BlockSpec((ROWS, states, cols_z), lambda i: (jnp.maximum(i - steps // 2, 0), 0, 0)),
            WHOLE,
            pl.BlockSpec((ROWS, cols_z), lambda i: (i, 0)),
            WHOLE,
            UNREAD,
        ],
        [pl.BlockSpec((states, ROWS, cols_z), lambda i: (0, i, 0))],
        [((states, lines, cols_z), BF16)],
        [],
        (xt, core_field, link_early, link_late, added, pot, ring, later_all),
        6,
    )

    def early_kernel(ids_ref, xt_ref, shares_ref, after_ref, unread, *refs):
        gather_kernel(bands, 0, share, ids_ref, xt_ref, shares_ref, after_ref, unread, *refs)

    early_all, early_pass, projs = call(
        early_kernel,
        (),
        [SCALARS, WHOLE, WHOLE, WHOLE, UNREAD] + [FAR] * (bands - 1),
        [WHOLE, FAR, WHOLE],
        [
            ((first + 1, total_states, cols_z), BF16),
            ((first // 2, total_states, cols_z), BF16),
            ((group_share, total_states, LANES), BF16),
        ],
        [copies((2 * bands + 1,)), copies],
        (ids, xt, whole, later_all, applied, *early),
        1,
    )
    early_link = lax.ppermute(early_pass, "domain", link_pairs)
    early_core = lax.ppermute(early_pass, "domain", core_pairs)
    (begun,) = call(
        functools.partial(gram_kernel, first, share),
        (),
        [SCALARS, WHOLE, WHOLE, WHOLE, WHOLE, UNREAD],
        [WHOLE],
        [((2, total_states, total_states), F32)],
        [],
        (ids, later_all, later_core, later_link, pot, early_all),
        2,
    )
    (blocks,) = call(
        functools.partial(final_kernel, bands, domains, share),
        (),
        [SCALARS] + [WHOLE] * 7,
        [WHOLE],
        [((parts, states, 2 * total_states // domains), BF16)],
        [pltpu.VMEM((2, total_states, total_states), F32)],
        (ids, early_all, early_core, early_link, pot, begun, projs, energy),
        2,
    )
    summed = lax.all_to_all(blocks, ("domain", "band"), split_axis=0, concat_axis=0, tiled=True)
    scale = 1.0 / (lines * cols_z * domains)
    result = jnp.sum(summed.astype(F32), axis=0) * scale
    cols = total_states // domains
    subspace = jnp.stack([result[:, :cols], result[:, cols:]])
    return applied.reshape(orbitals.shape), subspace


def solution(mesh):
    in_specs = (
        P("band", ("groups", "domain"), None, None),
        P(("groups", "domain"), None, None),
        P(("groups", "domain"), None, None),
        P(("groups", "domain")),
        P(("groups", "domain")),
        P(("groups", "domain")),
        P("groups", None),
    )
    out_specs = (P("band", ("groups", "domain"), None, None), P(None, ("groups", "band"), "domain"))
    return jax.shard_map(local, mesh=mesh, in_specs=in_specs, out_specs=out_specs, check_vma=False)
```

```python
import functools

import jax
import jax.numpy as jnp
import numpy as np
from jax import lax
from jax.experimental import pallas as pl
from jax.experimental.pallas import tpu as pltpu
from jax.sharding import PartitionSpec as P

F32 = jnp.float32
BF16 = jnp.bfloat16
LANES = 128
ROWS = 16
VMEM_BYTES = 50 * 1024 * 1024
NT = (((1,), (1,)), ((), ()))
WHOLE = pl.BlockSpec(memory_space=pltpu.VMEM)
NEAR = pl.BlockSpec(memory_space=pltpu.VMEM)
SCALARS = pl.BlockSpec(memory_space=pltpu.SMEM)
FAR = pl.BlockSpec(memory_space=pltpu.HBM)
UNREAD = pl.BlockSpec(memory_space=pl.ANY)
copies = pltpu.SemaphoreType.DMA


def call(kernel, grid, in_specs, out_specs, outs, scratch, args, aliases=None):
    def place(spec):
        return pltpu.VMEM if spec is NEAR else None

    args = [
        pltpu.with_memory_space_constraint(arg, place(spec)) if place(spec) else arg
        for spec, arg in zip(in_specs, args)
    ]
    shapes = [(place(spec) or jax.ShapeDtypeStruct)(shape, kind) for spec, (shape, kind) in zip(out_specs, outs)]
    return pl.pallas_call(
        kernel,
        grid=grid,
        out_shape=shapes,
        in_specs=in_specs,
        out_specs=out_specs,
        scratch_shapes=scratch,
        input_output_aliases=aliases or {},
        compiler_params=pltpu.CompilerParams(vmem_limit_bytes=VMEM_BYTES),
        cost_estimate=pl.CostEstimate(flops=1 << 20, bytes_accessed=1 << 10, transcendentals=0),
    )(*args)


def start(copy):
    copy.start()
    return copy


def pack_kernel(first, x_hbm, xt, xt_hbm, early_half, late_half, message, x, in_sems, out_sems):
    states, lines, _ = x.shape
    bands = in_sems.shape[0]
    share = lines // bands
    count = share - first
    loads, sends = [], []
    for c in range(bands):
        where = (slice(None), pl.ds(c * share, share), slice(None))
        loads.append(start(pltpu.make_async_copy(x_hbm.at[where], x.at[where], in_sems.at[c])))

    def send(line, number, target, at):
        copy = pltpu.make_async_copy(
            xt.at[pl.ds(line, number)], target.at[pl.ds(at, number)], out_sems.at[len(sends)]
        )
        sends.append(start(copy))

    for c in range(bands):
        loads[c].wait()
        for y0 in range(c * share, (c + 1) * share, ROWS):
            for s0 in range(0, states, ROWS):
                block = x[s0 : s0 + ROWS, y0 : y0 + ROWS, :].astype(F32)
                turned = jnp.swapaxes(block, 0, 1).astype(BF16)
                xt[y0 : y0 + ROWS, s0 : s0 + ROWS, :] = turned
        send(c * share + first, count, message, c * (count + 1))
        send(c * share, 1, message, (c + bands - 1) % bands * (count + 1) + count)
        if c == bands // 2 - 1:
            send(0, lines // 2, early_half, 0)
    send(lines // 2, lines // 2, late_half, 0)
    send(0, lines, xt_hbm, 0)
    for copy in sends:
        copy.wait()


def project_kernel(words_ref, ids_ref, xt_ref, p_hbm, core_ref, own_ref, link_ref, total, p_ref, sems):
    slots, proj_count, _ = p_ref.shape
    groups, states, _ = own_ref.shape
    per_group = LANES // proj_count
    chunks = sems.shape[0]
    size = slots // chunks
    unroll = 16
    loads = []
    for c in range(chunks):
        where = pl.ds(c * size, size)
        loads.append(start(pltpu.make_async_copy(p_hbm.at[where], p_ref.at[where], sems.at[c])))

    def clear(i, carry):
        for u in range(per_group):
            total[i * per_group + u] = jnp.zeros_like(total[0])
        return carry

    lax.fori_loop(0, 3 * groups, clear, 0)

    def body(i, carry):
        for u in range(unroll):
            t = i * unroll + u
            word = words_ref[t]
            line, atom = word >> 16, word & 0xFFFF
            total[atom] += lax.dot_general(p_ref[t], xt_ref[line], NT, preferred_element_type=F32)
        return carry

    for c in range(chunks):
        loads[c].wait()
        lax.fori_loop(c * size // unroll, (c + 1) * size // unroll, body, 0)
    odd = ids_ref[0] & 1
    core_first, link_first = (1 - odd) * 2 * groups, odd * 2 * groups

    def turned(group):
        tiles = [total[group * per_group + u] for u in range(per_group)]
        return jnp.concatenate(tiles, axis=0).T

    for g in range(groups):
        core_ref[g] = turned(core_first + g).astype(BF16)
        link_ref[g] = turned(link_first + g).astype(BF16)
        own_ref[g] = turned(groups + g)


def owner_kernel(bands, first, ids_ref, xt_ref, own_ref, core_hbm, link_hbm, energy_ref, half_in, *refs):
    half_out, scaled_ref, scaled_hbm, whole_ref = refs[:4]
    messages, (core_ref, link_ref, in_sems, out_sems) = refs[4 : 3 + bands], refs[3 + bands :]
    lines = xt_ref.shape[0]
    share = lines // bands
    band = ids_ref[1]
    groups = own_ref.shape[0]
    group_share = groups // bands
    loads = [
        start(pltpu.make_async_copy(core_hbm, core_ref, in_sems.at[0])),
        start(pltpu.make_async_copy(link_hbm, link_ref, in_sems.at[1])),
    ]
    sends = []

    def send(source, target):
        sends.append(start(pltpu.make_async_copy(source, target, out_sems.at[len(sends)])))

    for k in range(1, bands):
        send(xt_ref.at[pl.ds((band ^ k) * share, first)], messages[k - 1].at[pl.ds(0, first)])
    for copy in loads:
        copy.wait()
    row = ids_ref[0] * groups
    for g in range(groups):
        whole = own_ref[g] + core_ref[g].astype(F32) + link_ref[g].astype(F32)
        scaled_ref[g] = (whole * energy_ref[pl.ds(row + g, 1), :]).astype(BF16)
        whole_ref[g] = whole.astype(BF16)
    send(scaled_ref, scaled_hbm)
    for k in range(1, bands):
        send(whole_ref.at[pl.ds((band ^ k) * group_share, group_share)], messages[k - 1].at[pl.ds(first, group_share)])
    for copy in sends:
        copy.wait()


def nonlocal_kernel(words_ref, ids_ref, p_hbm, core_hbm, own_ref, link_hbm, out_ref, atoms, p_ref, core_ref, link_ref, sems):
    slots, proj_count, _ = p_ref.shape
    groups, states, _ = own_ref.shape
    per_group = LANES // proj_count
    lines = out_ref.shape[0]
    unroll = 16
    pairs = ((core_hbm, core_ref), (link_hbm, link_ref), (p_hbm, p_ref))
    loads = [start(pltpu.make_async_copy(far, near, sems.at[i])) for i, (far, near) in enumerate(pairs)]

    def clear(i, carry):
        out_ref[i] = jnp.zeros((states, LANES), F32)
        return carry

    lax.fori_loop(0, lines, clear, 0)
    odd = ids_ref[0] & 1

    def spread(first, ref):
        for g in range(groups):
            tile = ref[g]
            for u in range(per_group):
                atoms[(first + g) * per_group + u] = tile[:, u * proj_count : (u + 1) * proj_count]

    spread(groups, own_ref)
    loads[0].wait()
    spread((1 - odd) * 2 * groups, core_ref)
    loads[1].wait()
    spread(odd * 2 * groups, link_ref)
    loads[2].wait()

    def body(i, carry):
        for u in range(unroll):
            t = i * unroll + u
            word = words_ref[t]
            line, atom = word >> 16, word & 0xFFFF
            out_ref[line] += jnp.dot(atoms[atom], p_ref[t], preferred_element_type=F32)
        return carry

    lax.fori_loop(0, slots // unroll, body, 0)


def stencil_kernel(xt_ref, core_ref, early_ref, late_ref, added_ref, pot_ref, ring_ref, unread, out_ref, done_ref):
    states, here, _ = out_ref.shape
    lines = xt_ref.shape[0]
    done_ref[...] = jnp.zeros_like(done_ref)
    step = pl.program_id(0)
    y0 = step * here
    early = step < pl.num_programs(0) // 2
    for s0 in range(0, states, ROWS):
        rows = slice(s0, s0 + ROWS)
        results = []
        cells = jnp.concatenate([xt_ref[y0 + i, rows, :] for i in range(here)], axis=0)
        along = jnp.dot(cells, ring_ref[...], preferred_element_type=F32)
        before = xt_ref[lax.rem(y0 + lines - 1, lines), rows, :].astype(F32)
        x = xt_ref[y0, rows, :].astype(F32)
        for i in range(here):
            after = xt_ref[lax.rem(y0 + i + 1, lines), rows, :].astype(F32)
            link = jnp.where(early, early_ref[i, rows, :].astype(F32), late_ref[i, rows, :].astype(F32))
            beside = (before + after) + (core_ref[i, rows, :].astype(F32) + link)
            value = along[i * ROWS : (i + 1) * ROWS] + pot_ref[i : i + 1, :] * x
            results.append(value + added_ref[y0 + i, rows, :] - 0.5 * beside)
            before, x = x, after
        out_ref[rows, :, :] = jnp.swapaxes(jnp.stack(results, axis=0), 0, 1).astype(BF16)


def pass_half(ids_ref, all_ref, pass_hbm, sem):
    half = pass_hbm.shape[0]
    copy = start(pltpu.make_async_copy(all_ref.at[pl.ds((1 - (ids_ref[0] & 1)) * half, half)], pass_hbm, sem))
    copy.wait()


def later_kernel(bands, ids_ref, landed, unread, all_ref, pass_hbm, sems, pass_sem):
    count, states = all_ref.shape[0], landed.shape[1]
    loads = [
        start(
            pltpu.make_async_copy(
                landed.at[pl.ds(b * count, count)], all_ref.at[:, pl.ds(b * states, states), :], sems.at[b]
            )
        )
        for b in range(bands)
    ]
    for copy in loads:
        copy.wait()
    pass_half(ids_ref, all_ref, pass_hbm, pass_sem)


def early_kernel(bands, share, ids_ref, xt_ref, whole_ref, after_ref, unread, *refs):
    pieces, (all_ref, pass_hbm, projs_ref, sems, pass_sem) = refs[: bands - 1], refs[bands - 1 :]
    states = xt_ref.shape[1]
    band = ids_ref[1]
    count, held = all_ref.shape[0] - 1, projs_ref.shape[0]
    loads = []

    def load(source, target):
        loads.append(start(pltpu.make_async_copy(source, target, sems.at[len(loads)])))

    for k in range(bands):
        at = pl.ds(pl.multiple_of((band ^ k) * states, states), states)
        if k == 0:
            load(xt_ref.at[pl.ds(band * share, count)], all_ref.at[pl.ds(0, count), at, :])
            load(whole_ref.at[pl.ds(band * held, held)], projs_ref.at[:, at, :])
        else:
            load(pieces[k - 1].at[pl.ds(0, count)], all_ref.at[pl.ds(0, count), at, :])
            load(pieces[k - 1].at[pl.ds(count, held)], projs_ref.at[:, at, :])
    load(after_ref.at[pl.ds(0, 1)], all_ref.at[pl.ds(count, 1)])
    for copy in loads:
        copy.wait()
    pass_half(ids_ref, all_ref, pass_hbm, pass_sem)


def add_products(row, ids_ref, all_ref, core_ref, link_ref, pot_ref, acc):
    half = core_ref.shape[0]
    group = 4
    mine = (ids_ref[0] & 1) * half
    for part, base in ((0, mine), (1, half - mine)):
        for i0 in range(0, half, group):
            xs, ys = [], []
            for i in range(i0, min(i0 + group, half)):
                cell = all_ref[base + i]
                x = cell.astype(F32)
                y = (3.0 + pot_ref[pl.ds(row + base + i, 1), :]) * x - pltpu.roll(x, x.shape[1] - 1, 1)
                y = y - all_ref[base + i + 1].astype(F32)
                if part == 0:
                    y = y - core_ref[i].astype(F32) - link_ref[i].astype(F32)
                xs.append(cell)
                ys.append(y.astype(BF16))
            flat_x = jnp.concatenate(xs, axis=1)
            flat_y = jnp.concatenate(ys, axis=1)
            acc[0] += lax.dot_general(flat_x, flat_x, NT, preferred_element_type=F32)
            acc[1] += lax.dot_general(flat_y, flat_x, NT, preferred_element_type=F32)


def gram_kernel(first, share, ids_ref, all_ref, core_ref, link_ref, pot_ref, unread, acc):
    acc[...] = jnp.zeros_like(acc)
    add_products(ids_ref[1] * share + first, ids_ref, all_ref, core_ref, link_ref, pot_ref, acc)


def final_kernel(
    bands, share, ids_ref, all_ref, core_ref, link_ref, pot_ref, begun_ref, proj_ref, energy_ref, *refs
):
    out_refs, (acc, blocks) = refs[:-2], refs[-2:]
    acc[...] = begun_ref[...]
    add_products(ids_ref[1] * share, ids_ref, all_ref, core_ref, link_ref, pot_ref, acc)
    groups = proj_ref.shape[0]
    first = (ids_ref[0] * bands + ids_ref[1]) * groups
    for g in range(groups):
        here = proj_ref[g]
        scaled = (here.astype(F32) * energy_ref[pl.ds(first + g, 1), :]).astype(BF16)
        acc[1] += lax.dot_general(scaled, here, NT, preferred_element_type=F32)
    hamil = 0.5 * (acc[1] + acc[1].T)
    cols = blocks.shape[2] // 2
    for c in range(blocks.shape[0]):
        blocks[c, :, :cols] = acc[0, :, c * cols : (c + 1) * cols].astype(BF16)
        blocks[c, :, cols:] = hamil[:, c * cols : (c + 1) * cols].astype(BF16)
    for k, out_ref in enumerate(out_refs):
        out_ref[...] = blocks[ids_ref[0] ^ k]


def load_all(sources, slots, sems):
    copies_in = [start(pltpu.make_async_copy(far, slots.at[i], sems.at[i])) for i, far in enumerate(sources)]
    for copy in copies_in:
        copy.wait()


def rows_kernel(domains, ids_ref, own_ref, *refs):
    landed, (own_out, *outs, slots, total, sems) = refs[: domains - 1], refs[domains - 1 :]
    load_all(landed, slots, sems)
    rows = own_out.shape[0]
    total[...] = own_ref[...].astype(F32) + jnp.sum(slots[...].astype(F32), axis=0)
    for k, out_ref in enumerate((own_out, *outs)):
        begin = pl.multiple_of((ids_ref[1] ^ k) * rows, rows)
        out_ref[...] = total[pl.ds(begin, rows), :].astype(out_ref.dtype)


def result_kernel(bands, scale, own_ref, *refs):
    landed, (out_ref, slots, sems) = refs[: bands - 1], refs[bands - 1 :]
    load_all(landed, slots, sems)
    total = (own_ref[...] + jnp.sum(slots[...].astype(F32), axis=0)) * scale
    cols = out_ref.shape[2]
    out_ref[0] = total[:, :cols]
    out_ref[1] = total[:, cols:]


def local(orbitals, potential, projectors, tile_atom, tile_line, tile_count, energies):
    states, _, lines, cols_z = orbitals.shape
    slots, proj_count, _ = projectors.shape
    atom_total = energies.shape[0]
    domains, bands = lax.axis_size("domain"), lax.axis_size("band")
    domain, band = lax.axis_index("domain"), lax.axis_index("band")
    total_states = states * bands
    atoms_here = atom_total // domains
    per_group = LANES // proj_count
    groups = atoms_here // per_group
    group_share = groups // bands
    share = lines // bands
    first = share // 4
    rest = share - first

    core_pairs = [(i, i ^ 1) for i in range(domains) if i ^ 1 < domains]
    link_pairs = [(i, ((i + 1) ^ 1) - 1) for i in range(1, domains) if ((i + 1) ^ 1) - 1 < domains]

    def swapped(values, axis):
        size = lax.axis_size(axis)
        got = {k: lax.ppermute(values[k - 1], axis, [(i, i ^ k) for i in range(size)]) for k in range(size - 1, 0, -1)}
        return [got[k] for k in range(1, size)]

    ids = jnp.stack([domain, band]).astype(jnp.int32)
    near = jnp.clip(tile_atom - (domain - 1) * atoms_here, 0, 3 * atoms_here - 1)
    live = jnp.arange(slots, dtype=jnp.int32) < tile_count[0]
    project_words = (tile_line << 16) | jnp.where(live, near, 3 * atoms_here)
    nonlocal_words = (jnp.where(live, tile_line, lines) << 16) | near
    field = orbitals.reshape(states, lines, cols_z)
    pot = potential.reshape(lines, cols_z)
    energy = energies.reshape(atom_total // per_group, LANES)
    eye = np.eye(cols_z, dtype=np.float32)
    ring = jnp.asarray(3.0 * eye - 0.5 * (np.roll(eye, 1, axis=0) + np.roll(eye, -1, axis=0)), dtype=BF16)

    line_shape, half_shape = (lines, states, cols_z), (lines // 2, states, cols_z)
    xt, xt_far, early_half, late_half, message = call(
        functools.partial(pack_kernel, first),
        (),
        [FAR],
        [NEAR, FAR, FAR, FAR, FAR],
        [
            (line_shape, BF16),
            (line_shape, BF16),
            (half_shape, BF16),
            (half_shape, BF16),
            ((bands * (rest + 1), states, cols_z), BF16),
        ],
        [pltpu.VMEM((states, lines, cols_z), BF16), copies((bands,)), copies((2 * bands + 3,))],
        (field,),
    )
    landed = lax.all_to_all(message, "band", split_axis=0, concat_axis=0, tiled=True)
    link_early = lax.ppermute(early_half, "domain", link_pairs)
    core_field = lax.ppermute(xt_far, "domain", core_pairs)

    group_shape = (groups, states, LANES)
    to_core, own, to_link = call(
        project_kernel,
        (),
        [SCALARS, SCALARS, NEAR, FAR],
        [WHOLE, NEAR, WHOLE],
        [(group_shape, BF16), (group_shape, F32), (group_shape, BF16)],
        [
            pltpu.VMEM((3 * atoms_here + 1, proj_count, states), F32),
            pltpu.VMEM(projectors.shape, BF16),
            copies((4,)),
        ],
        (project_words, ids, xt, projectors),
    )
    from_link = lax.ppermute(to_link, "domain", link_pairs)
    from_core = lax.ppermute(to_core, "domain", core_pairs)
    late_half, scaled, scaled_far, whole, *messages = call(
        functools.partial(owner_kernel, bands, first),
        (),
        [SCALARS, NEAR, NEAR, FAR, FAR, WHOLE, FAR],
        [FAR, NEAR, FAR, NEAR] + [FAR] * (bands - 1),
        [(half_shape, BF16)]
        + [(group_shape, BF16)] * 3
        + [((first + group_share, states, cols_z), BF16)] * (bands - 1),
        [pltpu.VMEM(group_shape, BF16), pltpu.VMEM(group_shape, BF16), copies((2,)), copies((2 * bands - 1,))],
        (ids, xt, own, from_core, from_link, energy, late_half),
        aliases={6: 0},
    )
    link_scaled = lax.ppermute(scaled_far, "domain", link_pairs)
    core_scaled = lax.ppermute(scaled_far, "domain", core_pairs)
    link_late = lax.ppermute(late_half, "domain", link_pairs)
    early = swapped(messages, "band")

    (added,) = call(
        nonlocal_kernel,
        (),
        [SCALARS, SCALARS, FAR, FAR, NEAR, FAR],
        [NEAR],
        [((lines + 1, states, cols_z), F32)],
        [
            pltpu.VMEM((3 * atoms_here, states, proj_count), BF16),
            pltpu.VMEM(projectors.shape, BF16),
            pltpu.VMEM(group_shape, BF16),
            pltpu.VMEM(group_shape, BF16),
            copies((3,)),
        ],
        (nonlocal_words, ids, projectors, core_scaled, scaled, link_scaled),
    )

    later_all, later_pass = call(
        functools.partial(later_kernel, bands),
        (),
        [SCALARS, FAR, NEAR],
        [NEAR, FAR],
        [((rest + 1, total_states, cols_z), BF16), ((rest // 2, total_states, cols_z), BF16)],
        [copies((bands,)), copies],
        (ids, landed, added),
    )
    later_link = lax.ppermute(later_pass, "domain", link_pairs)
    later_core = lax.ppermute(later_pass, "domain", core_pairs)

    steps = lines // ROWS
    block = pl.BlockSpec((ROWS, states, cols_z), lambda i: (i, 0, 0))
    applied, done = call(
        stencil_kernel,
        (steps,),
        [
            NEAR,
            block,
            pl.BlockSpec((ROWS, states, cols_z), lambda i: (jnp.minimum(i, steps // 2 - 1), 0, 0)),
            pl.BlockSpec((ROWS, states, cols_z), lambda i: (jnp.maximum(i - steps // 2, 0), 0, 0)),
            NEAR,
            pl.BlockSpec((ROWS, cols_z), lambda i: (i, 0)),
            WHOLE,
            NEAR,
        ],
        [pl.BlockSpec((states, ROWS, cols_z), lambda i: (0, i, 0)), WHOLE],
        [((states, lines, cols_z), BF16), ((8, LANES), F32)],
        [],
        (xt, core_field, link_early, link_late, added, pot, ring, later_all),
    )

    early_all, early_pass, projs = call(
        functools.partial(early_kernel, bands, share),
        (),
        [SCALARS, NEAR, NEAR, NEAR, WHOLE] + [FAR] * (bands - 1),
        [NEAR, FAR, NEAR],
        [
            ((first + 1, total_states, cols_z), BF16),
            ((first // 2, total_states, cols_z), BF16),
            ((group_share, total_states, LANES), BF16),
        ],
        [copies((2 * bands + 1,)), copies],
        (ids, xt, whole, later_all, done, *early),
    )
    early_link = lax.ppermute(early_pass, "domain", link_pairs)
    early_core = lax.ppermute(early_pass, "domain", core_pairs)
    (begun,) = call(
        functools.partial(gram_kernel, first, share),
        (),
        [SCALARS, NEAR, WHOLE, WHOLE, WHOLE, NEAR],
        [NEAR],
        [((2, total_states, total_states), F32)],
        [],
        (ids, later_all, later_core, later_link, pot, early_all),
    )
    columns = (total_states, 2 * total_states // domains)
    own_columns, *far_columns = call(
        functools.partial(final_kernel, bands, share),
        (),
        [SCALARS, NEAR, WHOLE, WHOLE, WHOLE, NEAR, NEAR, WHOLE],
        [NEAR] + [WHOLE] * (domains - 1),
        [(columns, BF16)] * domains,
        [pltpu.VMEM((2, total_states, total_states), F32), pltpu.VMEM((domains, *columns), BF16)],
        (ids, early_all, early_core, early_link, pot, begun, projs, energy),
    )
    piece = (states, columns[1])
    own_rows, *far_rows = call(
        functools.partial(rows_kernel, domains),
        (),
        [SCALARS, NEAR] + [FAR] * (domains - 1),
        [NEAR] + [WHOLE] * (bands - 1),
        [(piece, F32)] + [(piece, BF16)] * (bands - 1),
        [pltpu.VMEM((domains - 1, *columns), BF16), pltpu.VMEM(columns, F32), copies((domains - 1,))],
        (ids, own_columns, *swapped(far_columns, "domain")),
    )
    (subspace,) = call(
        functools.partial(result_kernel, bands, 1.0 / (lines * cols_z * domains)),
        (),
        [NEAR] + [FAR] * (bands - 1),
        [WHOLE],
        [((2, states, total_states // domains), F32)],
        [pltpu.VMEM((bands - 1, *piece), BF16), copies((bands - 1,))],
        (own_rows, *swapped(far_rows, "band")),
    )
    return applied.reshape(orbitals.shape), subspace


def solution(mesh):
    in_specs = (
        P("band", ("groups", "domain"), None, None),
        P(("groups", "domain"), None, None),
        P(("groups", "domain"), None, None),
        P(("groups", "domain")),
        P(("groups", "domain")),
        P(("groups", "domain")),
        P("groups", None),
    )
    out_specs = (P("band", ("groups", "domain"), None, None), P(None, ("groups", "band"), "domain"))
    return jax.shard_map(local, mesh=mesh, in_specs=in_specs, out_specs=out_specs, check_vma=False)
```

```python
import functools

import jax
import jax.numpy as jnp
import numpy as np
from jax import lax
from jax.experimental import pallas as pl
from jax.experimental.pallas import tpu as pltpu
from jax.sharding import PartitionSpec as P

F32 = jnp.float32
BF16 = jnp.bfloat16
LANES = 128
ROWS = 16
NT = (((1,), (1,)), ((), ()))
WHOLE = pl.BlockSpec(memory_space=pltpu.VMEM)
NEAR = pl.BlockSpec(memory_space=pltpu.VMEM)
SCALARS = pl.BlockSpec(memory_space=pltpu.SMEM)
FAR = pl.BlockSpec(memory_space=pltpu.HBM)
UNREAD = pl.BlockSpec(memory_space=pl.ANY)
copies = pltpu.SemaphoreType.DMA


def call(room, kernel, grid, in_specs, out_specs, outs, scratch, args, aliases=None, micros=0.001):
    def place(spec):
        return pltpu.VMEM if spec is NEAR else None

    args = [
        pltpu.with_memory_space_constraint(arg, place(spec)) if place(spec) else arg
        for spec, arg in zip(in_specs, args)
    ]
    shapes = [(place(spec) or jax.ShapeDtypeStruct)(shape, kind) for spec, (shape, kind) in zip(out_specs, outs)]
    return pl.pallas_call(
        kernel,
        grid=grid,
        out_shape=shapes,
        in_specs=in_specs,
        out_specs=out_specs,
        scratch_shapes=scratch,
        input_output_aliases=aliases or {},
        compiler_params=pltpu.CompilerParams(vmem_limit_bytes=room << 20),
        cost_estimate=pl.CostEstimate(flops=int(micros * 1.1e9), bytes_accessed=1 << 10, transcendentals=0),
    )(*args)


def start(copy):
    copy.start()
    return copy


def pack_kernel(first, x_hbm, xt, xt_hbm, early_half, late_half, message, x, in_sems, out_sems):
    states, lines, _ = x.shape
    bands = in_sems.shape[0]
    share = lines // bands
    count = share - first
    loads, sends = [], []
    for c in range(bands):
        where = (slice(None), pl.ds(c * share, share), slice(None))
        loads.append(start(pltpu.make_async_copy(x_hbm.at[where], x.at[where], in_sems.at[c])))

    def send(line, number, target, at):
        copy = pltpu.make_async_copy(
            xt.at[pl.ds(line, number)], target.at[pl.ds(at, number)], out_sems.at[len(sends)]
        )
        sends.append(start(copy))

    for c in range(bands):
        loads[c].wait()
        for y0 in range(c * share, (c + 1) * share, ROWS):
            for s0 in range(0, states, ROWS):
                block = x[s0 : s0 + ROWS, y0 : y0 + ROWS, :].astype(F32)
                turned = jnp.swapaxes(block, 0, 1).astype(BF16)
                xt[y0 : y0 + ROWS, s0 : s0 + ROWS, :] = turned
        send(c * share + first, count, message, c * (count + 1))
        send(c * share, 1, message, (c + bands - 1) % bands * (count + 1) + count)
        if c == bands // 2 - 1:
            send(0, lines // 2, early_half, 0)
    send(lines // 2, lines // 2, late_half, 0)
    send(0, lines, xt_hbm, 0)
    for copy in sends:
        copy.wait()


def project_kernel(words_ref, ids_ref, xt_ref, p_hbm, core_ref, own_ref, link_ref, total, p_ref, sems):
    slots, proj_count, _ = p_ref.shape
    groups, states, _ = own_ref.shape
    per_group = LANES // proj_count
    chunks = sems.shape[0]
    size = slots // chunks
    unroll = 16
    loads = []
    for c in range(chunks):
        where = pl.ds(c * size, size)
        loads.append(start(pltpu.make_async_copy(p_hbm.at[where], p_ref.at[where], sems.at[c])))

    def clear(i, carry):
        for u in range(per_group):
            total[i * per_group + u] = jnp.zeros_like(total[0])
        return carry

    lax.fori_loop(0, 3 * groups, clear, 0)

    def body(i, carry):
        for u in range(unroll):
            t = i * unroll + u
            word = words_ref[t]
            line, atom = word >> 16, word & 0xFFFF
            total[atom] += lax.dot_general(p_ref[t], xt_ref[line], NT, preferred_element_type=F32)
        return carry

    for c in range(chunks):
        loads[c].wait()
        lax.fori_loop(c * size // unroll, (c + 1) * size // unroll, body, 0)
    odd = ids_ref[0] & 1
    core_first, link_first = (1 - odd) * 2 * groups, odd * 2 * groups

    def turned(group):
        tiles = [total[group * per_group + u] for u in range(per_group)]
        return jnp.concatenate(tiles, axis=0).T

    for g in range(groups):
        core_ref[g] = turned(core_first + g).astype(BF16)
        link_ref[g] = turned(link_first + g).astype(BF16)
        own_ref[g] = turned(groups + g)


def hand_on(value, unread, same):
    pass


def owner_kernel(bands, first, ids_ref, xt_ref, own_ref, core_hbm, link_hbm, energy_ref, unread, unread_too, *refs):
    scaled_ref, scaled_hbm, whole_ref = refs[:3]
    messages, (core_ref, link_ref, in_sems, out_sems) = refs[3 : 2 + bands], refs[2 + bands :]
    lines = xt_ref.shape[0]
    share = lines // bands
    band = ids_ref[1]
    groups = own_ref.shape[0]
    group_share = groups // bands
    loads = [
        start(pltpu.make_async_copy(core_hbm, core_ref, in_sems.at[0])),
        start(pltpu.make_async_copy(link_hbm, link_ref, in_sems.at[1])),
    ]
    sends = []

    def send(source, target):
        sends.append(start(pltpu.make_async_copy(source, target, out_sems.at[len(sends)])))

    for k in range(1, bands):
        send(xt_ref.at[pl.ds((band ^ k) * share, first)], messages[k - 1].at[pl.ds(0, first)])
    for copy in loads:
        copy.wait()
    row = ids_ref[0] * groups
    for g in range(groups):
        whole = own_ref[g] + core_ref[g].astype(F32) + link_ref[g].astype(F32)
        scaled_ref[g] = (whole * energy_ref[pl.ds(row + g, 1), :]).astype(BF16)
        whole_ref[g] = whole.astype(BF16)
    send(scaled_ref, scaled_hbm)
    for k in range(1, bands):
        send(whole_ref.at[pl.ds((band ^ k) * group_share, group_share)], messages[k - 1].at[pl.ds(first, group_share)])
    for copy in sends:
        copy.wait()


def nonlocal_kernel(words_ref, ids_ref, p_hbm, core_hbm, own_ref, link_hbm, out_ref, atoms, p_ref, core_ref, link_ref, sems):
    slots, proj_count, _ = p_ref.shape
    groups, states, _ = own_ref.shape
    per_group = LANES // proj_count
    lines = out_ref.shape[0]
    unroll = 16
    pairs = ((core_hbm, core_ref), (link_hbm, link_ref), (p_hbm, p_ref))
    loads = [start(pltpu.make_async_copy(far, near, sems.at[i])) for i, (far, near) in enumerate(pairs)]

    def clear(i, carry):
        out_ref[i] = jnp.zeros((states, LANES), F32)
        return carry

    lax.fori_loop(0, lines, clear, 0)
    odd = ids_ref[0] & 1

    def spread(first, ref):
        for g in range(groups):
            tile = ref[g]
            for u in range(per_group):
                atoms[(first + g) * per_group + u] = tile[:, u * proj_count : (u + 1) * proj_count]

    spread(groups, own_ref)
    loads[0].wait()
    spread((1 - odd) * 2 * groups, core_ref)
    loads[1].wait()
    spread(odd * 2 * groups, link_ref)
    loads[2].wait()

    def body(i, carry):
        for u in range(unroll):
            t = i * unroll + u
            word = words_ref[t]
            line, atom = word >> 16, word & 0xFFFF
            out_ref[line] += jnp.dot(atoms[atom], p_ref[t], preferred_element_type=F32)
        return carry

    lax.fori_loop(0, slots // unroll, body, 0)


def stencil_kernel(xt_ref, core_ref, early_ref, late_ref, added_ref, pot_ref, ring_ref, unread, out_ref):
    states, here, _ = out_ref.shape
    lines = xt_ref.shape[0]
    step = pl.program_id(0)
    y0 = step * here
    early = step < pl.num_programs(0) // 2
    for s0 in range(0, states, ROWS):
        rows = slice(s0, s0 + ROWS)
        results = []
        cells = jnp.concatenate([xt_ref[y0 + i, rows, :] for i in range(here)], axis=0)
        along = jnp.dot(cells, ring_ref[...], preferred_element_type=F32)
        before = xt_ref[lax.rem(y0 + lines - 1, lines), rows, :].astype(F32)
        x = xt_ref[y0, rows, :].astype(F32)
        for i in range(here):
            after = xt_ref[lax.rem(y0 + i + 1, lines), rows, :].astype(F32)
            link = jnp.where(early, early_ref[i, rows, :].astype(F32), late_ref[i, rows, :].astype(F32))
            beside = (before + after) + (core_ref[i, rows, :].astype(F32) + link)
            value = along[i * ROWS : (i + 1) * ROWS] + pot_ref[i : i + 1, :] * x
            results.append(value + added_ref[y0 + i, rows, :] - 0.5 * beside)
            before, x = x, after
        out_ref[rows, :, :] = jnp.swapaxes(jnp.stack(results, axis=0), 0, 1).astype(BF16)


def pass_half(ids_ref, all_ref, pass_hbm, sem):
    half = pass_hbm.shape[0]
    copy = start(pltpu.make_async_copy(all_ref.at[pl.ds((1 - (ids_ref[0] & 1)) * half, half)], pass_hbm, sem))
    copy.wait()


def later_kernel(bands, ids_ref, landed, unread, unread_too, all_ref, pass_hbm, sems, pass_sem):
    count, states = all_ref.shape[0], landed.shape[1]
    loads = [
        start(
            pltpu.make_async_copy(
                landed.at[pl.ds(b * count, count)], all_ref.at[:, pl.ds(b * states, states), :], sems.at[b]
            )
        )
        for b in range(bands)
    ]
    for copy in loads:
        copy.wait()
    pass_half(ids_ref, all_ref, pass_hbm, pass_sem)


def early_kernel(bands, share, ids_ref, xt_ref, whole_ref, after_ref, *refs):
    pieces, (all_ref, pass_hbm, projs_ref, sems, pass_sem) = refs[: bands - 1], refs[bands - 1 :]
    states = xt_ref.shape[1]
    band = ids_ref[1]
    count, held = all_ref.shape[0] - 1, projs_ref.shape[0]
    loads = []

    def load(source, target):
        loads.append(start(pltpu.make_async_copy(source, target, sems.at[len(loads)])))

    for k in range(bands):
        at = pl.ds(pl.multiple_of((band ^ k) * states, states), states)
        if k == 0:
            load(xt_ref.at[pl.ds(band * share, count)], all_ref.at[pl.ds(0, count), at, :])
            load(whole_ref.at[pl.ds(band * held, held)], projs_ref.at[:, at, :])
        else:
            load(pieces[k - 1].at[pl.ds(0, count)], all_ref.at[pl.ds(0, count), at, :])
            load(pieces[k - 1].at[pl.ds(count, held)], projs_ref.at[:, at, :])
    load(after_ref.at[pl.ds(0, 1)], all_ref.at[pl.ds(count, 1)])
    for copy in loads:
        copy.wait()
    pass_half(ids_ref, all_ref, pass_hbm, pass_sem)


def add_products(row, ids_ref, all_ref, core_ref, link_ref, pot_ref, acc):
    half = core_ref.shape[0]
    group = 4
    mine = (ids_ref[0] & 1) * half
    for part, base in ((0, mine), (1, half - mine)):
        for i0 in range(0, half, group):
            xs, ys = [], []
            for i in range(i0, min(i0 + group, half)):
                cell = all_ref[base + i]
                x = cell.astype(F32)
                y = (3.0 + pot_ref[pl.ds(row + base + i, 1), :]) * x - pltpu.roll(x, x.shape[1] - 1, 1)
                y = y - all_ref[base + i + 1].astype(F32)
                if part == 0:
                    y = y - core_ref[i].astype(F32) - link_ref[i].astype(F32)
                xs.append(cell)
                ys.append(y.astype(BF16))
            flat_x = jnp.concatenate(xs, axis=1)
            flat_y = jnp.concatenate(ys, axis=1)
            acc[0] += lax.dot_general(flat_x, flat_x, NT, preferred_element_type=F32)
            acc[1] += lax.dot_general(flat_y, flat_x, NT, preferred_element_type=F32)


def gram_kernel(first, share, ids_ref, all_ref, core_ref, link_ref, pot_ref, unread, acc):
    acc[...] = jnp.zeros_like(acc)
    add_products(ids_ref[1] * share + first, ids_ref, all_ref, core_ref, link_ref, pot_ref, acc)


def final_kernel(
    bands, share, ids_ref, all_ref, core_ref, link_ref, pot_ref, begun_ref, proj_ref, energy_ref, out_ref, acc
):
    acc[...] = begun_ref[...]
    add_products(ids_ref[1] * share, ids_ref, all_ref, core_ref, link_ref, pot_ref, acc)
    groups = proj_ref.shape[0]
    first = (ids_ref[0] * bands + ids_ref[1]) * groups
    for g in range(groups):
        here = proj_ref[g]
        scaled = (here.astype(F32) * energy_ref[pl.ds(first + g, 1), :]).astype(BF16)
        acc[1] += lax.dot_general(scaled, here, NT, preferred_element_type=F32)
    hamil = 0.5 * (acc[1] + acc[1].T)
    domains = out_ref.shape[0] // bands
    rows, cols = out_ref.shape[1], out_ref.shape[2] // 2
    for c in range(domains):
        for r in range(bands):
            r0, c0 = r * rows, c * cols
            out_ref[c * bands + r, :, :cols] = acc[0, r0 : r0 + rows, c0 : c0 + cols].astype(BF16)
            out_ref[c * bands + r, :, cols:] = hamil[r0 : r0 + rows, c0 : c0 + cols].astype(BF16)


def result_kernel(scale, parts_ref, out_ref):
    total = jnp.sum(parts_ref[...].astype(F32), axis=0) * scale
    cols = out_ref.shape[2]
    out_ref[0] = total[:, :cols]
    out_ref[1] = total[:, cols:]


def local(orbitals, potential, projectors, tile_atom, tile_line, tile_count, energies):
    states, _, lines, cols_z = orbitals.shape
    slots, proj_count, _ = projectors.shape
    atom_total = energies.shape[0]
    domains, bands = lax.axis_size("domain"), lax.axis_size("band")
    domain, band = lax.axis_index("domain"), lax.axis_index("band")
    total_states = states * bands
    atoms_here = atom_total // domains
    per_group = LANES // proj_count
    groups = atoms_here // per_group
    group_share = groups // bands
    share = lines // bands
    first = share // 4
    rest = share - first

    core_pairs = [(i, i ^ 1) for i in range(domains) if i ^ 1 < domains]
    link_pairs = [(i, ((i + 1) ^ 1) - 1) for i in range(1, domains) if ((i + 1) ^ 1) - 1 < domains]

    def swapped(values, axis):
        size = lax.axis_size(axis)
        got = {k: lax.ppermute(values[k - 1], axis, [(i, i ^ k) for i in range(size)]) for k in range(size - 1, 0, -1)}
        return [got[k] for k in range(1, size)]

    ids = jnp.stack([domain, band]).astype(jnp.int32)
    near = jnp.clip(tile_atom - (domain - 1) * atoms_here, 0, 3 * atoms_here - 1)
    live = jnp.arange(slots, dtype=jnp.int32) < tile_count[0]
    project_words = (tile_line << 16) | jnp.where(live, near, 3 * atoms_here)
    nonlocal_words = (jnp.where(live, tile_line, lines) << 16) | near
    field = orbitals.reshape(states, lines, cols_z)
    pot = potential.reshape(lines, cols_z)
    energy = energies.reshape(atom_total // per_group, LANES)
    eye = np.eye(cols_z, dtype=np.float32)
    ring = jnp.asarray(3.0 * eye - 0.5 * (np.roll(eye, 1, axis=0) + np.roll(eye, -1, axis=0)), dtype=BF16)

    line_shape, half_shape = (lines, states, cols_z), (lines // 2, states, cols_z)
    xt, xt_far, early_half, late_half, message = call(
        58,
        functools.partial(pack_kernel, first),
        (),
        [FAR],
        [NEAR, FAR, FAR, FAR, FAR],
        [
            (line_shape, BF16),
            (line_shape, BF16),
            (half_shape, BF16),
            (half_shape, BF16),
            ((bands * (rest + 1), states, cols_z), BF16),
        ],
        [pltpu.VMEM((states, lines, cols_z), BF16), copies((bands,)), copies((2 * bands + 3,))],
        (field,),
    )
    landed = lax.all_to_all(message, "band", split_axis=0, concat_axis=0, tiled=True)
    link_early = lax.ppermute(early_half, "domain", link_pairs)
    core_field = lax.ppermute(xt_far, "domain", core_pairs)

    group_shape = (groups, states, LANES)
    to_core, own, to_link = call(
        50,
        project_kernel,
        (),
        [SCALARS, SCALARS, NEAR, FAR],
        [WHOLE, NEAR, WHOLE],
        [(group_shape, BF16), (group_shape, F32), (group_shape, BF16)],
        [
            pltpu.VMEM((3 * atoms_here + 1, proj_count, states), F32),
            pltpu.VMEM(projectors.shape, BF16),
            copies((4,)),
        ],
        (project_words, ids, xt, projectors),
    )
    from_link = lax.ppermute(to_link, "domain", link_pairs)
    from_core = lax.ppermute(to_core, "domain", core_pairs)
    scaled, scaled_far, whole, *messages = call(
        59,
        functools.partial(owner_kernel, bands, first),
        (),
        [SCALARS, NEAR, NEAR, FAR, FAR, WHOLE, UNREAD, UNREAD],
        [NEAR, FAR, NEAR] + [FAR] * (bands - 1),
        [(group_shape, BF16)] * 3
        + [((first + group_share, states, cols_z), BF16)] * (bands - 1),
        [pltpu.VMEM(group_shape, BF16), pltpu.VMEM(group_shape, BF16), copies((2,)), copies((2 * bands - 1,))],
        (ids, xt, own, from_core, from_link, energy, link_early, core_field),
    )
    link_scaled = lax.ppermute(scaled_far, "domain", link_pairs)
    core_scaled = lax.ppermute(scaled_far, "domain", core_pairs)
    (late_half,) = call(
        59, hand_on, (), [UNREAD, UNREAD], [UNREAD], [(half_shape, BF16)], [], (late_half, link_scaled), aliases={0: 0}
    )
    link_late = lax.ppermute(late_half, "domain", link_pairs)
    early = swapped(messages, "band")

    (added,) = call(
        40,
        nonlocal_kernel,
        (),
        [SCALARS, SCALARS, FAR, FAR, NEAR, FAR],
        [WHOLE],
        [((lines + 1, states, cols_z), F32)],
        [
            pltpu.VMEM((3 * atoms_here, states, proj_count), BF16),
            pltpu.VMEM(projectors.shape, BF16),
            pltpu.VMEM(group_shape, BF16),
            pltpu.VMEM(group_shape, BF16),
            copies((3,)),
        ],
        (nonlocal_words, ids, projectors, core_scaled, scaled, link_scaled),
    )

    later_all, later_pass = call(
        40,
        functools.partial(later_kernel, bands),
        (),
        [SCALARS, FAR, UNREAD, UNREAD],
        [NEAR, FAR],
        [((rest + 1, total_states, cols_z), BF16), ((rest // 2, total_states, cols_z), BF16)],
        [copies((bands,)), copies],
        (ids, landed, added, link_late),
    )
    later_link = lax.ppermute(later_pass, "domain", link_pairs)
    later_core = lax.ppermute(later_pass, "domain", core_pairs)

    early_all, early_pass, projs = call(
        40,
        functools.partial(early_kernel, bands, share),
        (),
        [SCALARS, NEAR, NEAR, NEAR] + [FAR] * (bands - 1),
        [NEAR, FAR, NEAR],
        [
            ((first + 1, total_states, cols_z), BF16),
            ((first // 2, total_states, cols_z), BF16),
            ((group_share, total_states, LANES), BF16),
        ],
        [copies((2 * bands + 1,)), copies],
        (ids, xt, whole, later_all, *early),
        micros=30,
    )
    early_link = lax.ppermute(early_pass, "domain", link_pairs)
    early_core = lax.ppermute(early_pass, "domain", core_pairs)
    (begun,) = call(
        40,
        functools.partial(gram_kernel, first, share),
        (),
        [SCALARS, NEAR, WHOLE, WHOLE, WHOLE, NEAR],
        [NEAR],
        [((2, total_states, total_states), F32)],
        [],
        (ids, later_all, later_core, later_link, pot, early_all),
    )
    parts = domains * bands
    (blocks,) = call(
        40,
        functools.partial(final_kernel, bands, share),
        (),
        [SCALARS, NEAR, WHOLE, WHOLE, WHOLE, NEAR, NEAR, WHOLE],
        [WHOLE],
        [((parts, states, 2 * total_states // domains), BF16)],
        [pltpu.VMEM((2, total_states, total_states), F32)],
        (ids, early_all, early_core, early_link, pot, begun, projs, energy),
    )
    summed = lax.all_to_all(blocks, ("domain", "band"), split_axis=0, concat_axis=0, tiled=True)
    steps = lines // ROWS
    block = pl.BlockSpec((ROWS, states, cols_z), lambda i: (i, 0, 0))
    (applied,) = call(
        40,
        stencil_kernel,
        (steps,),
        [
            NEAR,
            block,
            pl.BlockSpec((ROWS, states, cols_z), lambda i: (jnp.minimum(i, steps // 2 - 1), 0, 0)),
            pl.BlockSpec((ROWS, states, cols_z), lambda i: (jnp.maximum(i - steps // 2, 0), 0, 0)),
            WHOLE,
            pl.BlockSpec((ROWS, cols_z), lambda i: (i, 0)),
            WHOLE,
            UNREAD,
        ],
        [pl.BlockSpec((states, ROWS, cols_z), lambda i: (0, i, 0))],
        [((states, lines, cols_z), BF16)],
        [],
        (xt, core_field, link_early, link_late, added, pot, ring, blocks),
    )

    (subspace,) = call(
        40,
        functools.partial(result_kernel, 1.0 / (lines * cols_z * domains)),
        (),
        [WHOLE],
        [WHOLE],
        [((2, states, total_states // domains), F32)],
        [],
        (summed,),
    )
    return applied.reshape(orbitals.shape), subspace


def solution(mesh):
    in_specs = (
        P("band", ("groups", "domain"), None, None),
        P(("groups", "domain"), None, None),
        P(("groups", "domain"), None, None),
        P(("groups", "domain")),
        P(("groups", "domain")),
        P(("groups", "domain")),
        P("groups", None),
    )
    out_specs = (P("band", ("groups", "domain"), None, None), P(None, ("groups", "band"), "domain"))
    return jax.shard_map(local, mesh=mesh, in_specs=in_specs, out_specs=out_specs, check_vma=False)
```

```python
import functools

import jax
import jax.numpy as jnp
import numpy as np
from jax import lax
from jax.experimental import pallas as pl
from jax.experimental.pallas import tpu as pltpu
from jax.sharding import PartitionSpec as P

F32 = jnp.float32
BF16 = jnp.bfloat16
LANES = 128
ROWS = 16
NT = (((1,), (1,)), ((), ()))
WHOLE = pl.BlockSpec(memory_space=pltpu.VMEM)
NEAR = pl.BlockSpec(memory_space=pltpu.VMEM)
SCALARS = pl.BlockSpec(memory_space=pltpu.SMEM)
FAR = pl.BlockSpec(memory_space=pltpu.HBM)
UNREAD = pl.BlockSpec(memory_space=pl.ANY)
copies = pltpu.SemaphoreType.DMA


def call(room, kernel, grid, in_specs, out_specs, outs, scratch, args, aliases=None, micros=0.001):
    def place(spec):
        return pltpu.VMEM if spec is NEAR else None

    args = [
        pltpu.with_memory_space_constraint(arg, place(spec)) if place(spec) else arg
        for spec, arg in zip(in_specs, args)
    ]
    shapes = [(place(spec) or jax.ShapeDtypeStruct)(shape, kind) for spec, (shape, kind) in zip(out_specs, outs)]
    return pl.pallas_call(
        kernel,
        grid=grid,
        out_shape=shapes,
        in_specs=in_specs,
        out_specs=out_specs,
        scratch_shapes=scratch,
        input_output_aliases=aliases or {},
        compiler_params=pltpu.CompilerParams(vmem_limit_bytes=room << 20),
        cost_estimate=pl.CostEstimate(flops=int(micros * 1.1e9), bytes_accessed=1 << 10, transcendentals=0),
    )(*args)


def start(copy):
    copy.start()
    return copy


def pack_kernel(first, x_hbm, xt, xt_hbm, early_half, late_half, message, x, in_sems, out_sems):
    states, lines, _ = x.shape
    bands = in_sems.shape[0]
    share = lines // bands
    count = share - first
    loads, sends = [], []
    for c in range(bands):
        where = (slice(None), pl.ds(c * share, share), slice(None))
        loads.append(start(pltpu.make_async_copy(x_hbm.at[where], x.at[where], in_sems.at[c])))

    def send(line, number, target, at):
        copy = pltpu.make_async_copy(
            xt.at[pl.ds(line, number)], target.at[pl.ds(at, number)], out_sems.at[len(sends)]
        )
        sends.append(start(copy))

    for c in range(bands):
        loads[c].wait()
        for y0 in range(c * share, (c + 1) * share, ROWS):
            for s0 in range(0, states, ROWS):
                block = x[s0 : s0 + ROWS, y0 : y0 + ROWS, :].astype(F32)
                turned = jnp.swapaxes(block, 0, 1).astype(BF16)
                xt[y0 : y0 + ROWS, s0 : s0 + ROWS, :] = turned
        send(c * share + first, count, message, c * (count + 1))
        send(c * share, 1, message, (c + bands - 1) % bands * (count + 1) + count)
        if c == bands // 2 - 1:
            send(0, lines // 2, early_half, 0)
    send(lines // 2, lines // 2, late_half, 0)
    send(0, lines, xt_hbm, 0)
    for copy in sends:
        copy.wait()


def project_kernel(words_ref, ids_ref, xt_ref, p_hbm, core_ref, own_ref, link_ref, total, p_ref, sems):
    slots, proj_count, _ = p_ref.shape
    groups, states, _ = own_ref.shape
    per_group = LANES // proj_count
    chunks = sems.shape[0]
    size = slots // chunks
    unroll = 16
    loads = []
    for c in range(chunks):
        where = pl.ds(c * size, size)
        loads.append(start(pltpu.make_async_copy(p_hbm.at[where], p_ref.at[where], sems.at[c])))

    def clear(i, carry):
        for u in range(per_group):
            total[i * per_group + u] = jnp.zeros_like(total[0])
        return carry

    lax.fori_loop(0, 3 * groups, clear, 0)

    def body(i, carry):
        for u in range(unroll):
            t = i * unroll + u
            word = words_ref[t]
            line, atom = word >> 16, word & 0xFFFF
            total[atom] += lax.dot_general(p_ref[t], xt_ref[line], NT, preferred_element_type=F32)
        return carry

    for c in range(chunks):
        loads[c].wait()
        lax.fori_loop(c * size // unroll, (c + 1) * size // unroll, body, 0)
    odd = ids_ref[0] & 1
    core_first, link_first = (1 - odd) * 2 * groups, odd * 2 * groups

    def turned(group):
        tiles = [total[group * per_group + u] for u in range(per_group)]
        return jnp.concatenate(tiles, axis=0).T

    for g in range(groups):
        core_ref[g] = turned(core_first + g).astype(BF16)
        link_ref[g] = turned(link_first + g).astype(BF16)
        own_ref[g] = turned(groups + g)


def hand_on(value, unread, unread_too, same):
    pass


def owner_kernel(
    first, ids_ref, xt_ref, own_ref, core_ref, link_ref, energy_ref, unread, unread_too, scaled_ref, whole_ref, *messages
):
    share = xt_ref.shape[0] // (len(messages) + 1)
    groups = own_ref.shape[0]
    held = messages[0].shape[0] - first
    row = ids_ref[0] * groups
    for g in range(groups):
        whole = own_ref[g] + core_ref[g].astype(F32) + link_ref[g].astype(F32)
        scaled_ref[g] = (whole * energy_ref[pl.ds(row + g, 1), :]).astype(BF16)
        whole_ref[g] = whole.astype(BF16)
    for k, message in enumerate(messages, 1):
        to = ids_ref[1] ^ k
        for i in range(first):
            message[i] = xt_ref[to * share + i]
        for i in range(held):
            message[first + i] = whole_ref[to * held + i]


def nonlocal_kernel(words_ref, ids_ref, p_hbm, core_ref, own_ref, link_ref, out_ref, atoms, p_ref, sem):
    slots, proj_count, _ = p_ref.shape
    groups, states, _ = own_ref.shape
    per_group = LANES // proj_count
    lines = out_ref.shape[0]
    unroll = 16
    load = start(pltpu.make_async_copy(p_hbm, p_ref, sem))

    def clear(i, carry):
        out_ref[i] = jnp.zeros((states, LANES), F32)
        return carry

    lax.fori_loop(0, lines, clear, 0)
    odd = ids_ref[0] & 1

    for first, ref in (((1 - odd) * 2 * groups, core_ref), (groups, own_ref), (odd * 2 * groups, link_ref)):
        for g in range(groups):
            tile = ref[g]
            for u in range(per_group):
                atoms[(first + g) * per_group + u] = tile[:, u * proj_count : (u + 1) * proj_count]
    load.wait()

    def body(i, carry):
        for u in range(unroll):
            t = i * unroll + u
            word = words_ref[t]
            line, atom = word >> 16, word & 0xFFFF
            out_ref[line] += jnp.dot(atoms[atom], p_ref[t], preferred_element_type=F32)
        return carry

    lax.fori_loop(0, slots // unroll, body, 0)


def stencil_kernel(xt_ref, core_ref, early_ref, late_ref, added_ref, pot_ref, ring_ref, unread, out_ref, done_ref):
    states, here, _ = out_ref.shape
    lines = xt_ref.shape[0]
    done_ref[...] = jnp.zeros_like(done_ref)
    step = pl.program_id(0)
    y0 = step * here
    early = step < pl.num_programs(0) // 2
    for s0 in range(0, states, ROWS):
        rows = slice(s0, s0 + ROWS)
        results = []
        cells = jnp.concatenate([xt_ref[y0 + i, rows, :] for i in range(here)], axis=0)
        along = jnp.dot(cells, ring_ref[...], preferred_element_type=F32)
        before = xt_ref[lax.rem(y0 + lines - 1, lines), rows, :].astype(F32)
        x = xt_ref[y0, rows, :].astype(F32)
        for i in range(here):
            after = xt_ref[lax.rem(y0 + i + 1, lines), rows, :].astype(F32)
            link = jnp.where(early, early_ref[i, rows, :].astype(F32), late_ref[i, rows, :].astype(F32))
            beside = (before + after) + (core_ref[i, rows, :].astype(F32) + link)
            value = along[i * ROWS : (i + 1) * ROWS] + pot_ref[i : i + 1, :] * x
            results.append(value + added_ref[y0 + i, rows, :] - 0.5 * beside)
            before, x = x, after
        out_ref[rows, :, :] = jnp.swapaxes(jnp.stack(results, axis=0), 0, 1).astype(BF16)


def pass_half(ids_ref, all_ref, pass_hbm, sem):
    half = pass_hbm.shape[0]
    copy = start(pltpu.make_async_copy(all_ref.at[pl.ds((1 - (ids_ref[0] & 1)) * half, half)], pass_hbm, sem))
    copy.wait()


def later_kernel(bands, ids_ref, landed, unread, unread_too, all_ref, pass_hbm, sems, pass_sem):
    count, states = all_ref.shape[0], landed.shape[1]
    loads = [
        start(
            pltpu.make_async_copy(
                landed.at[pl.ds(b * count, count)], all_ref.at[:, pl.ds(b * states, states), :], sems.at[b]
            )
        )
        for b in range(bands)
    ]
    for copy in loads:
        copy.wait()
    pass_half(ids_ref, all_ref, pass_hbm, pass_sem)


def early_kernel(bands, share, ids_ref, xt_ref, whole_ref, after_ref, unread, *refs):
    pieces, (all_ref, pass_hbm, projs_ref, sems, pass_sem) = refs[: bands - 1], refs[bands - 1 :]
    states = xt_ref.shape[1]
    band = ids_ref[1]
    count, held = all_ref.shape[0] - 1, projs_ref.shape[0]
    loads = []

    def load(source, target):
        loads.append(start(pltpu.make_async_copy(source, target, sems.at[len(loads)])))

    for k in range(bands):
        at = pl.ds(pl.multiple_of((band ^ k) * states, states), states)
        if k == 0:
            load(xt_ref.at[pl.ds(band * share, count)], all_ref.at[pl.ds(0, count), at, :])
            load(whole_ref.at[pl.ds(band * held, held)], projs_ref.at[:, at, :])
        else:
            load(pieces[k - 1].at[pl.ds(0, count)], all_ref.at[pl.ds(0, count), at, :])
            load(pieces[k - 1].at[pl.ds(count, held)], projs_ref.at[:, at, :])
    load(after_ref.at[pl.ds(0, 1)], all_ref.at[pl.ds(count, 1)])
    for copy in loads:
        copy.wait()
    pass_half(ids_ref, all_ref, pass_hbm, pass_sem)


def add_products(row, ids_ref, all_ref, core_ref, link_ref, pot_ref, acc):
    half = core_ref.shape[0]
    group = 4
    mine = (ids_ref[0] & 1) * half
    for part, base in ((0, mine), (1, half - mine)):
        for i0 in range(0, half, group):
            xs, ys = [], []
            for i in range(i0, min(i0 + group, half)):
                cell = all_ref[base + i]
                x = cell.astype(F32)
                y = (3.0 + pot_ref[pl.ds(row + base + i, 1), :]) * x - pltpu.roll(x, x.shape[1] - 1, 1)
                y = y - all_ref[base + i + 1].astype(F32)
                if part == 0:
                    y = y - core_ref[i].astype(F32) - link_ref[i].astype(F32)
                xs.append(cell)
                ys.append(y.astype(BF16))
            flat_x = jnp.concatenate(xs, axis=1)
            flat_y = jnp.concatenate(ys, axis=1)
            acc[0] += lax.dot_general(flat_x, flat_x, NT, preferred_element_type=F32)
            acc[1] += lax.dot_general(flat_y, flat_x, NT, preferred_element_type=F32)


def gram_kernel(first, share, ids_ref, all_ref, core_ref, link_ref, pot_ref, unread, acc):
    acc[...] = jnp.zeros_like(acc)
    add_products(ids_ref[1] * share + first, ids_ref, all_ref, core_ref, link_ref, pot_ref, acc)


def final_kernel(
    bands, share, ids_ref, all_ref, core_ref, link_ref, pot_ref, begun_ref, proj_ref, energy_ref, out_ref, acc
):
    acc[...] = begun_ref[...]
    add_products(ids_ref[1] * share, ids_ref, all_ref, core_ref, link_ref, pot_ref, acc)
    groups = proj_ref.shape[0]
    first = (ids_ref[0] * bands + ids_ref[1]) * groups
    for g in range(groups):
        here = proj_ref[g]
        scaled = (here.astype(F32) * energy_ref[pl.ds(first + g, 1), :]).astype(BF16)
        acc[1] += lax.dot_general(scaled, here, NT, preferred_element_type=F32)
    hamil = 0.5 * (acc[1] + acc[1].T)
    domains = out_ref.shape[0] // bands
    rows, cols = out_ref.shape[1], out_ref.shape[2] // 2
    for c in range(domains):
        for r in range(bands):
            r0, c0 = r * rows, c * cols
            out_ref[c * bands + r, :, :cols] = acc[0, r0 : r0 + rows, c0 : c0 + cols].astype(BF16)
            out_ref[c * bands + r, :, cols:] = hamil[r0 : r0 + rows, c0 : c0 + cols].astype(BF16)


def result_kernel(scale, parts_ref, out_ref):
    total = jnp.sum(parts_ref[...].astype(F32), axis=0) * scale
    cols = out_ref.shape[2]
    out_ref[0] = total[:, :cols]
    out_ref[1] = total[:, cols:]


def local(orbitals, potential, projectors, tile_atom, tile_line, tile_count, energies):
    states, _, lines, cols_z = orbitals.shape
    slots, proj_count, _ = projectors.shape
    atom_total = energies.shape[0]
    domains, bands = lax.axis_size("domain"), lax.axis_size("band")
    domain, band = lax.axis_index("domain"), lax.axis_index("band")
    total_states = states * bands
    atoms_here = atom_total // domains
    per_group = LANES // proj_count
    groups = atoms_here // per_group
    group_share = groups // bands
    share = lines // bands
    first = share // 4
    rest = share - first

    core_pairs = [(i, i ^ 1) for i in range(domains) if i ^ 1 < domains]
    link_pairs = [(i, ((i + 1) ^ 1) - 1) for i in range(1, domains) if ((i + 1) ^ 1) - 1 < domains]

    def swapped(values, axis):
        size = lax.axis_size(axis)
        got = {k: lax.ppermute(values[k - 1], axis, [(i, i ^ k) for i in range(size)]) for k in range(size - 1, 0, -1)}
        return [got[k] for k in range(1, size)]

    ids = jnp.stack([domain, band]).astype(jnp.int32)
    near = jnp.clip(tile_atom - (domain - 1) * atoms_here, 0, 3 * atoms_here - 1)
    live = jnp.arange(slots, dtype=jnp.int32) < tile_count[0]
    project_words = (tile_line << 16) | jnp.where(live, near, 3 * atoms_here)
    nonlocal_words = (jnp.where(live, tile_line, lines) << 16) | near
    field = orbitals.reshape(states, lines, cols_z)
    pot = potential.reshape(lines, cols_z)
    energy = energies.reshape(atom_total // per_group, LANES)
    eye = np.eye(cols_z, dtype=np.float32)
    ring = jnp.asarray(3.0 * eye - 0.5 * (np.roll(eye, 1, axis=0) + np.roll(eye, -1, axis=0)), dtype=BF16)

    line_shape, half_shape = (lines, states, cols_z), (lines // 2, states, cols_z)
    xt, xt_far, early_half, late_half, message = call(
        58,
        functools.partial(pack_kernel, first),
        (),
        [FAR],
        [NEAR, FAR, FAR, FAR, FAR],
        [
            (line_shape, BF16),
            (line_shape, BF16),
            (half_shape, BF16),
            (half_shape, BF16),
            ((bands * (rest + 1), states, cols_z), BF16),
        ],
        [pltpu.VMEM((states, lines, cols_z), BF16), copies((bands,)), copies((2 * bands + 3,))],
        (field,),
    )
    landed = lax.all_to_all(message, "band", split_axis=0, concat_axis=0, tiled=True)
    link_early = lax.ppermute(early_half, "domain", link_pairs)
    core_field = lax.ppermute(xt_far, "domain", core_pairs)

    group_shape = (groups, states, LANES)
    to_core, own, to_link = call(
        50,
        project_kernel,
        (),
        [SCALARS, SCALARS, NEAR, FAR],
        [WHOLE, NEAR, WHOLE],
        [(group_shape, BF16), (group_shape, F32), (group_shape, BF16)],
        [
            pltpu.VMEM((3 * atoms_here + 1, proj_count, states), F32),
            pltpu.VMEM(projectors.shape, BF16),
            copies((4,)),
        ],
        (project_words, ids, xt, projectors),
    )
    from_link = lax.ppermute(to_link, "domain", link_pairs)
    from_core = lax.ppermute(to_core, "domain", core_pairs)
    scaled, whole, *messages = call(
        59,
        functools.partial(owner_kernel, first),
        (),
        [SCALARS, NEAR, NEAR, WHOLE, WHOLE, WHOLE, UNREAD, UNREAD],
        [WHOLE, NEAR] + [WHOLE] * (bands - 1),
        [(group_shape, BF16)] * 2 + [((first + group_share, states, cols_z), BF16)] * (bands - 1),
        [],
        (ids, xt, own, from_core, from_link, energy, link_early, core_field),
    )
    link_scaled = lax.ppermute(scaled, "domain", link_pairs)
    core_scaled = lax.ppermute(scaled, "domain", core_pairs)
    (late_half,) = call(
        59,
        hand_on,
        (),
        [UNREAD] * 3,
        [UNREAD],
        [(half_shape, BF16)],
        [],
        (late_half, link_scaled, core_scaled),
        aliases={0: 0},
    )
    link_late = lax.ppermute(late_half, "domain", link_pairs)
    early = swapped(messages, "band")

    (added,) = call(
        32,
        nonlocal_kernel,
        (),
        [SCALARS, SCALARS, FAR, WHOLE, WHOLE, WHOLE],
        [WHOLE],
        [((lines + 1, states, cols_z), F32)],
        [
            pltpu.VMEM((3 * atoms_here, states, proj_count), BF16),
            pltpu.VMEM(projectors.shape, BF16),
            copies,
        ],
        (nonlocal_words, ids, projectors, core_scaled, scaled, link_scaled),
    )

    later_all, later_pass = call(
        32,
        functools.partial(later_kernel, bands),
        (),
        [SCALARS, FAR, UNREAD, UNREAD],
        [NEAR, FAR],
        [((rest + 1, total_states, cols_z), BF16), ((rest // 2, total_states, cols_z), BF16)],
        [copies((bands,)), copies],
        (ids, landed, added, link_late),
    )
    later_link = lax.ppermute(later_pass, "domain", link_pairs)
    later_core = lax.ppermute(later_pass, "domain", core_pairs)

    steps = lines // ROWS
    block = pl.BlockSpec((ROWS, states, cols_z), lambda i: (i, 0, 0))
    applied, done = call(
        32,
        stencil_kernel,
        (steps,),
        [
            NEAR,
            block,
            pl.BlockSpec((ROWS, states, cols_z), lambda i: (jnp.minimum(i, steps // 2 - 1), 0, 0)),
            pl.BlockSpec((ROWS, states, cols_z), lambda i: (jnp.maximum(i - steps // 2, 0), 0, 0)),
            WHOLE,
            pl.BlockSpec((ROWS, cols_z), lambda i: (i, 0)),
            WHOLE,
            UNREAD,
        ],
        [pl.BlockSpec((states, ROWS, cols_z), lambda i: (0, i, 0)), WHOLE],
        [((states, lines, cols_z), BF16), ((8, LANES), F32)],
        [],
        (xt, core_field, link_early, link_late, added, pot, ring, later_all),
    )

    early_all, early_pass, projs = call(
        32,
        functools.partial(early_kernel, bands, share),
        (),
        [SCALARS, NEAR, NEAR, NEAR, WHOLE] + [FAR] * (bands - 1),
        [NEAR, FAR, NEAR],
        [
            ((first + 1, total_states, cols_z), BF16),
            ((first // 2, total_states, cols_z), BF16),
            ((group_share, total_states, LANES), BF16),
        ],
        [copies((2 * bands + 1,)), copies],
        (ids, xt, whole, later_all, done, *early),
        micros=30,
    )
    early_link = lax.ppermute(early_pass, "domain", link_pairs)
    early_core = lax.ppermute(early_pass, "domain", core_pairs)
    (begun,) = call(
        32,
        functools.partial(gram_kernel, first, share),
        (),
        [SCALARS, NEAR, WHOLE, WHOLE, WHOLE, NEAR],
        [NEAR],
        [((2, total_states, total_states), F32)],
        [],
        (ids, later_all, later_core, later_link, pot, early_all),
    )
    parts = domains * bands
    (blocks,) = call(
        32,
        functools.partial(final_kernel, bands, share),
        (),
        [SCALARS, NEAR, WHOLE, WHOLE, WHOLE, NEAR, NEAR, WHOLE],
        [WHOLE],
        [((parts, states, 2 * total_states // domains), BF16)],
        [pltpu.VMEM((2, total_states, total_states), F32)],
        (ids, early_all, early_core, early_link, pot, begun, projs, energy),
    )
    summed = lax.all_to_all(blocks, ("domain", "band"), split_axis=0, concat_axis=0, tiled=True)
    (subspace,) = call(
        32,
        functools.partial(result_kernel, 1.0 / (lines * cols_z * domains)),
        (),
        [WHOLE],
        [WHOLE],
        [((2, states, total_states // domains), F32)],
        [],
        (summed,),
    )
    return applied.reshape(orbitals.shape), subspace


def solution(mesh):
    in_specs = (
        P("band", ("groups", "domain"), None, None),
        P(("groups", "domain"), None, None),
        P(("groups", "domain"), None, None),
        P(("groups", "domain")),
        P(("groups", "domain")),
        P(("groups", "domain")),
        P("groups", None),
    )
    out_specs = (P("band", ("groups", "domain"), None, None), P(None, ("groups", "band"), "domain"))
    return jax.shard_map(local, mesh=mesh, in_specs=in_specs, out_specs=out_specs, check_vma=False)
```

```python
import functools

import jax
import jax.numpy as jnp
import numpy as np
from jax import lax
from jax.experimental import pallas as pl
from jax.experimental.pallas import tpu as pltpu
from jax.sharding import PartitionSpec as P

F32 = jnp.float32
BF16 = jnp.bfloat16
LANES = 128
ROWS = 16
NT = (((1,), (1,)), ((), ()))
WHOLE = pl.BlockSpec(memory_space=pltpu.VMEM)
NEAR = pl.BlockSpec(memory_space=pltpu.VMEM)
SCALARS = pl.BlockSpec(memory_space=pltpu.SMEM)
FAR = pl.BlockSpec(memory_space=pltpu.HBM)
UNREAD = pl.BlockSpec(memory_space=pl.ANY)
copies = pltpu.SemaphoreType.DMA


def call(room, kernel, grid, in_specs, out_specs, outs, scratch, args, aliases=None, micros=0.001):
    def place(spec):
        return pltpu.VMEM if spec is NEAR else None

    args = [
        pltpu.with_memory_space_constraint(arg, place(spec)) if place(spec) else arg
        for spec, arg in zip(in_specs, args)
    ]
    shapes = [(place(spec) or jax.ShapeDtypeStruct)(shape, kind) for spec, (shape, kind) in zip(out_specs, outs)]
    return pl.pallas_call(
        kernel,
        grid=grid,
        out_shape=shapes,
        in_specs=in_specs,
        out_specs=out_specs,
        scratch_shapes=scratch,
        input_output_aliases=aliases or {},
        compiler_params=pltpu.CompilerParams(vmem_limit_bytes=room << 20),
        cost_estimate=pl.CostEstimate(flops=int(micros * 1.1e9), bytes_accessed=1 << 10, transcendentals=0),
    )(*args)


def start(copy):
    copy.start()
    return copy


def pack_kernel(first, x_hbm, xt, xt_hbm, early, late, message, x, in_sems, out_sems):
    states, lines, _ = x.shape
    bands = in_sems.shape[0]
    share = lines // bands
    count = share - first
    loads, sends = [], []
    for c in range(bands):
        where = (slice(None), pl.ds(c * share, share), slice(None))
        loads.append(start(pltpu.make_async_copy(x_hbm.at[where], x.at[where], in_sems.at[c])))

    def send(line, number, target, at):
        copy = pltpu.make_async_copy(
            xt.at[pl.ds(line, number)], target.at[pl.ds(at, number)], out_sems.at[len(sends)]
        )
        sends.append(start(copy))

    for c in range(bands):
        loads[c].wait()
        for y0 in range(c * share, (c + 1) * share, ROWS):
            for s0 in range(0, states, ROWS):
                block = x[s0 : s0 + ROWS, y0 : y0 + ROWS, :].astype(F32)
                turned = jnp.swapaxes(block, 0, 1).astype(BF16)
                xt[y0 : y0 + ROWS, s0 : s0 + ROWS, :] = turned
        send(c * share + first, count, message, c * (count + 1))
        send(c * share, 1, message, (c + bands - 1) % bands * (count + 1) + count)
        if (c + 1) * share == early.shape[0]:
            send(0, early.shape[0], early, 0)
    send(early.shape[0], late.shape[0], late, 0)
    send(0, lines, xt_hbm, 0)
    for copy in sends:
        copy.wait()


def bases(ids_ref, groups):
    odd, upper = ids_ref[0] & 1, (ids_ref[0] >> 1) & 1
    return [2 * groups * side for side in (1 - odd, odd, 1 - upper, upper)]


def project_kernel(words_ref, ids_ref, xt_ref, p_hbm, mine_ref, core_ref, link_ref, *refs):
    far_refs, (total, p_ref, sems) = refs[:-3], refs[-3:]
    slots, proj_count, _ = p_ref.shape
    groups, states = mine_ref.shape[0] // 3, mine_ref.shape[1]
    per_group = LANES // proj_count
    chunks = sems.shape[0]
    size = slots // chunks
    unroll = 16
    loads = []
    for c in range(chunks):
        where = pl.ds(c * size, size)
        loads.append(start(pltpu.make_async_copy(p_hbm.at[where], p_ref.at[where], sems.at[c])))

    def clear(i, carry):
        for u in range(per_group):
            total[i * per_group + u] = jnp.zeros_like(total[0])
        return carry

    lax.fori_loop(0, 3 * groups, clear, 0)

    def body(i, carry):
        for u in range(unroll):
            t = i * unroll + u
            word = words_ref[t]
            line, atom = word >> 16, word & 0xFFFF
            total[atom] += lax.dot_general(p_ref[t], xt_ref[line], NT, preferred_element_type=F32)
        return carry

    for c in range(chunks):
        loads[c].wait()
        lax.fori_loop(c * size // unroll, (c + 1) * size // unroll, body, 0)

    for g in range(3 * groups):
        tiles = [total[g * per_group + u] for u in range(per_group)]
        mine_ref[g] = jnp.concatenate(tiles, axis=0).T
    sides = bases(ids_ref, groups)
    for g in range(groups):
        own = mine_ref[groups + g].astype(BF16)
        for side, ref in zip(sides[:2], (core_ref, link_ref)):
            ref[g] = mine_ref[side + g].astype(BF16)
            ref[groups + g] = own
        for side, ref in zip(sides[2:], far_refs):
            ref[g] = mine_ref[side + g].astype(BF16)


def nonlocal_kernel(first, fars, words_ref, ids_ref, xt_ref, p_hbm, energy_ref, mine_ref, core_ref, link_ref, *refs):
    far_refs, (_, _, _, out_ref, whole_ref, done_ref, _, *messages, total, atoms, p_ref, sem) = refs[:fars], refs[fars:]
    slots, proj_count, _ = p_ref.shape
    groups, states = mine_ref.shape[0] // 3, mine_ref.shape[1]
    per_group = LANES // proj_count
    lines = out_ref.shape[0]
    unroll = 16
    load = start(pltpu.make_async_copy(p_hbm, p_ref, sem))
    done_ref[...] = jnp.zeros_like(done_ref)

    def clear(i, carry):
        out_ref[i] = jnp.zeros((states, LANES), F32)
        return carry

    lax.fori_loop(0, lines, clear, 0)
    total[...] = mine_ref[...]
    sides = bases(ids_ref, groups)
    for g in range(groups):
        total[groups + g] += core_ref[g].astype(F32) + link_ref[g].astype(F32)
        for side, ref in zip(sides[:2], (core_ref, link_ref)):
            total[side + g] += ref[groups + g].astype(F32)
        for side, ref in zip(sides[2:], far_refs):
            total[side + g] += ref[g].astype(F32)
    last = energy_ref.shape[0] - 1
    for g in range(3 * groups):
        row = jnp.clip((ids_ref[0] - 1) * groups + g, 0, last)
        tile = (total[g] * energy_ref[pl.ds(row, 1), :]).astype(BF16)
        for u in range(per_group):
            atoms[g * per_group + u] = tile[:, u * proj_count : (u + 1) * proj_count]
    for g in range(groups):
        whole_ref[g] = total[groups + g].astype(BF16)
    share = xt_ref.shape[0] // (len(messages) + 1)
    held = groups // (len(messages) + 1)
    for k, message in enumerate(messages, 1):
        to = ids_ref[1] ^ k
        for i in range(first):
            message[i] = xt_ref[to * share + i]
        for i in range(held):
            message[first + i] = whole_ref[to * held + i]
    load.wait()

    def body(i, carry):
        for u in range(unroll):
            t = i * unroll + u
            word = words_ref[t]
            line, atom = word >> 16, word & 0xFFFF
            out_ref[line] += jnp.dot(atoms[atom], p_ref[t], preferred_element_type=F32)
        return carry

    lax.fori_loop(0, slots // unroll, body, 0)


def stencil_kernel(early_steps, xt_ref, core_ref, early_ref, late_ref, added_ref, pot_ref, ring_ref, unread, out_ref, done_ref):
    states, here, _ = out_ref.shape
    lines = xt_ref.shape[0]
    done_ref[...] = jnp.zeros_like(done_ref)
    step = pl.program_id(0)
    y0 = step * here
    early = step < early_steps
    for s0 in range(0, states, ROWS):
        rows = slice(s0, s0 + ROWS)
        results = []
        cells = jnp.concatenate([xt_ref[y0 + i, rows, :] for i in range(here)], axis=0)
        along = jnp.dot(cells, ring_ref[...], preferred_element_type=F32)
        before = xt_ref[lax.rem(y0 + lines - 1, lines), rows, :].astype(F32)
        x = xt_ref[y0, rows, :].astype(F32)
        for i in range(here):
            after = xt_ref[lax.rem(y0 + i + 1, lines), rows, :].astype(F32)
            link = jnp.where(early, early_ref[i, rows, :].astype(F32), late_ref[i, rows, :].astype(F32))
            beside = (before + after) + (core_ref[i, rows, :].astype(F32) + link)
            value = along[i * ROWS : (i + 1) * ROWS] + pot_ref[i : i + 1, :] * x
            results.append(value + added_ref[y0 + i, rows, :] - 0.5 * beside)
            before, x = x, after
        out_ref[rows, :, :] = jnp.swapaxes(jnp.stack(results, axis=0), 0, 1).astype(BF16)


def pass_half(ids_ref, all_ref, pass_hbm, sem):
    half = pass_hbm.shape[0]
    copy = start(pltpu.make_async_copy(all_ref.at[pl.ds((1 - (ids_ref[0] & 1)) * half, half)], pass_hbm, sem))
    copy.wait()


def later_kernel(bands, ids_ref, landed, unread, all_ref, pass_hbm, sems, pass_sem):
    count, states = all_ref.shape[0], landed.shape[1]
    loads = [
        start(
            pltpu.make_async_copy(
                landed.at[pl.ds(b * count, count)], all_ref.at[:, pl.ds(b * states, states), :], sems.at[b]
            )
        )
        for b in range(bands)
    ]
    for copy in loads:
        copy.wait()
    pass_half(ids_ref, all_ref, pass_hbm, pass_sem)


def early_kernel(bands, share, ids_ref, xt_ref, whole_ref, after_ref, unread, *refs):
    pieces, (all_ref, pass_hbm, projs_ref, sems, pass_sem) = refs[: bands - 1], refs[bands - 1 :]
    states = xt_ref.shape[1]
    band = ids_ref[1]
    count, held = all_ref.shape[0] - 1, projs_ref.shape[0]
    loads = []

    def load(source, target):
        loads.append(start(pltpu.make_async_copy(source, target, sems.at[len(loads)])))

    for k in range(bands):
        at = pl.ds(pl.multiple_of((band ^ k) * states, states), states)
        if k == 0:
            load(xt_ref.at[pl.ds(band * share, count)], all_ref.at[pl.ds(0, count), at, :])
            load(whole_ref.at[pl.ds(band * held, held)], projs_ref.at[:, at, :])
        else:
            load(pieces[k - 1].at[pl.ds(0, count)], all_ref.at[pl.ds(0, count), at, :])
            load(pieces[k - 1].at[pl.ds(count, held)], projs_ref.at[:, at, :])
    load(after_ref.at[pl.ds(0, 1)], all_ref.at[pl.ds(count, 1)])
    for copy in loads:
        copy.wait()
    pass_half(ids_ref, all_ref, pass_hbm, pass_sem)


def add_products(row, ids_ref, all_ref, core_ref, link_ref, pot_ref, acc):
    half = core_ref.shape[0]
    group = 4
    mine = (ids_ref[0] & 1) * half
    for part, base in ((0, mine), (1, half - mine)):
        for i0 in range(0, half, group):
            xs, ys = [], []
            for i in range(i0, min(i0 + group, half)):
                cell = all_ref[base + i]
                x = cell.astype(F32)
                y = (3.0 + pot_ref[pl.ds(row + base + i, 1), :]) * x - pltpu.roll(x, x.shape[1] - 1, 1)
                y = y - all_ref[base + i + 1].astype(F32)
                if part == 0:
                    y = y - core_ref[i].astype(F32) - link_ref[i].astype(F32)
                xs.append(cell)
                ys.append(y.astype(BF16))
            flat_x = jnp.concatenate(xs, axis=1)
            flat_y = jnp.concatenate(ys, axis=1)
            acc[0] += lax.dot_general(flat_x, flat_x, NT, preferred_element_type=F32)
            acc[1] += lax.dot_general(flat_y, flat_x, NT, preferred_element_type=F32)


def gram_kernel(first, share, ids_ref, all_ref, core_ref, link_ref, pot_ref, unread, acc):
    acc[...] = jnp.zeros_like(acc)
    add_products(ids_ref[1] * share + first, ids_ref, all_ref, core_ref, link_ref, pot_ref, acc)


def final_kernel(
    bands, share, ids_ref, all_ref, core_ref, link_ref, pot_ref, begun_ref, proj_ref, energy_ref, out_ref, acc
):
    acc[...] = begun_ref[...]
    add_products(ids_ref[1] * share, ids_ref, all_ref, core_ref, link_ref, pot_ref, acc)
    groups = proj_ref.shape[0]
    first = (ids_ref[0] * bands + ids_ref[1]) * groups
    for g in range(groups):
        here = proj_ref[g]
        scaled = (here.astype(F32) * energy_ref[pl.ds(first + g, 1), :]).astype(BF16)
        acc[1] += lax.dot_general(scaled, here, NT, preferred_element_type=F32)
    hamil = 0.5 * (acc[1] + acc[1].T)
    domains = out_ref.shape[0] // bands
    rows, cols = out_ref.shape[1], out_ref.shape[2] // 2
    for c in range(domains):
        for r in range(bands):
            r0, c0 = r * rows, c * cols
            out_ref[c * bands + r, :, :cols] = acc[0, r0 : r0 + rows, c0 : c0 + cols].astype(BF16)
            out_ref[c * bands + r, :, cols:] = hamil[r0 : r0 + rows, c0 : c0 + cols].astype(BF16)


def result_kernel(scale, parts_ref, out_ref):
    total = jnp.sum(parts_ref[...].astype(F32), axis=0) * scale
    cols = out_ref.shape[2]
    out_ref[0] = total[:, :cols]
    out_ref[1] = total[:, cols:]


def local(orbitals, potential, projectors, tile_atom, tile_line, tile_count, energies):
    states, _, lines, cols_z = orbitals.shape
    slots, proj_count, _ = projectors.shape
    atom_total = energies.shape[0]
    domains, bands = lax.axis_size("domain"), lax.axis_size("band")
    domain, band = lax.axis_index("domain"), lax.axis_index("band")
    total_states = states * bands
    atoms_here = atom_total // domains
    per_group = LANES // proj_count
    groups = atoms_here // per_group
    group_share = groups // bands
    share = lines // bands
    first = share // 4
    rest = share - first

    core_pairs = [(i, i ^ 1) for i in range(domains) if i ^ 1 < domains]
    link_pairs = [(i, ((i + 1) ^ 1) - 1) for i in range(1, domains) if ((i + 1) ^ 1) - 1 < domains]
    near_far = [(i, i ^ 2) for i in range(domains) if i ^ 2 < domains]
    next_far = [(i, ((i + 2) ^ 2) - 2) for i in range(2, domains) if ((i + 2) ^ 2) - 2 < domains]
    far_pairs = [pairs for pairs in (near_far, next_far) if pairs]

    def swapped(values, axis):
        size = lax.axis_size(axis)
        got = {k: lax.ppermute(values[k - 1], axis, [(i, i ^ k) for i in range(size)]) for k in range(size - 1, 0, -1)}
        return [got[k] for k in range(1, size)]

    ids = jnp.stack([domain, band]).astype(jnp.int32)
    near = jnp.clip(tile_atom - (domain - 1) * atoms_here, 0, 3 * atoms_here - 1)
    live = jnp.arange(slots, dtype=jnp.int32) < tile_count[0]
    project_words = (tile_line << 16) | jnp.where(live, near, 3 * atoms_here)
    nonlocal_words = (jnp.where(live, tile_line, lines) << 16) | near
    field = orbitals.reshape(states, lines, cols_z)
    pot = potential.reshape(lines, cols_z)
    energy = energies.reshape(atom_total // per_group, LANES)
    eye = np.eye(cols_z, dtype=np.float32)
    ring = jnp.asarray(3.0 * eye - 0.5 * (np.roll(eye, 1, axis=0) + np.roll(eye, -1, axis=0)), dtype=BF16)

    late_lines = lines // 4
    line_shape, late_shape = (lines, states, cols_z), (late_lines, states, cols_z)
    xt, xt_far, early_part, late_part, message = call(
        58,
        functools.partial(pack_kernel, first),
        (),
        [FAR],
        [NEAR, FAR, FAR, FAR, FAR],
        [
            (line_shape, BF16),
            (line_shape, BF16),
            ((lines - late_lines, states, cols_z), BF16),
            (late_shape, BF16),
            ((bands * (rest + 1), states, cols_z), BF16),
        ],
        [pltpu.VMEM((states, lines, cols_z), BF16), copies((bands,)), copies((2 * bands + 3,))],
        (field,),
    )
    landed = lax.all_to_all(message, "band", split_axis=0, concat_axis=0, tiled=True)
    link_early = lax.ppermute(early_part, "domain", link_pairs)
    core_field = lax.ppermute(xt_far, "domain", core_pairs)

    group_shape = (groups, states, LANES)
    mine, to_core, to_link, *to_far = call(
        50,
        project_kernel,
        (),
        [SCALARS, SCALARS, NEAR, FAR],
        [NEAR] + [WHOLE] * (2 + len(far_pairs)),
        [((3 * groups, states, LANES), F32)]
        + [((2 * groups, states, LANES), BF16)] * 2
        + [(group_shape, BF16)] * len(far_pairs),
        [
            pltpu.VMEM((3 * atoms_here + 1, proj_count, states), F32),
            pltpu.VMEM(projectors.shape, BF16),
            copies((4,)),
        ],
        (project_words, ids, xt, projectors),
    )
    from_link = lax.ppermute(to_link, "domain", link_pairs)
    from_far = [lax.ppermute(value, "domain", pairs) for value, pairs in zip(to_far, far_pairs)]
    from_core = lax.ppermute(to_core, "domain", core_pairs)
    added, whole, summed_up, late_part, *messages = call(
        32,
        functools.partial(nonlocal_kernel, first, len(far_pairs)),
        (),
        [SCALARS, SCALARS, NEAR, FAR, WHOLE, NEAR, WHOLE, WHOLE] + [WHOLE] * len(far_pairs) + [UNREAD] * 3,
        [WHOLE, NEAR, WHOLE, UNREAD] + [WHOLE] * (bands - 1),
        [((lines + 1, states, cols_z), F32), (group_shape, BF16), ((8, LANES), F32), (late_shape, BF16)]
        + [((first + group_share, states, cols_z), BF16)] * (bands - 1),
        [
            pltpu.VMEM((3 * groups, states, LANES), F32),
            pltpu.VMEM((3 * atoms_here, states, proj_count), BF16),
            pltpu.VMEM(projectors.shape, BF16),
            copies,
        ],
        (
            nonlocal_words, ids, xt, projectors, energy, mine, from_core, from_link, *from_far,
            link_early[0, :ROWS], core_field[0, :ROWS], late_part,
        ),
        aliases={10 + len(far_pairs): 3},
        micros=30,
    )
    link_late = lax.ppermute(late_part, "domain", link_pairs)
    early = swapped(messages, "band")

    later_all, later_pass = call(
        32,
        functools.partial(later_kernel, bands),
        (),
        [SCALARS, FAR, UNREAD],
        [NEAR, FAR],
        [((rest + 1, total_states, cols_z), BF16), ((rest // 2, total_states, cols_z), BF16)],
        [copies((bands,)), copies],
        (ids, landed, summed_up),
        micros=10,
    )
    later_link = lax.ppermute(later_pass, "domain", link_pairs)
    later_core = lax.ppermute(later_pass, "domain", core_pairs)

    steps, early_steps = lines // ROWS, (lines - late_lines) // ROWS
    block = pl.BlockSpec((ROWS, states, cols_z), lambda i: (i, 0, 0))
    applied, done = call(
        32,
        functools.partial(stencil_kernel, early_steps),
        (steps,),
        [
            NEAR,
            block,
            pl.BlockSpec((ROWS, states, cols_z), lambda i: (jnp.minimum(i, early_steps - 1), 0, 0)),
            pl.BlockSpec((ROWS, states, cols_z), lambda i: (jnp.maximum(i - early_steps, 0), 0, 0)),
            WHOLE,
            pl.BlockSpec((ROWS, cols_z), lambda i: (i, 0)),
            WHOLE,
            UNREAD,
        ],
        [pl.BlockSpec((states, ROWS, cols_z), lambda i: (0, i, 0)), WHOLE],
        [((states, lines, cols_z), BF16), ((8, LANES), F32)],
        [],
        (xt, core_field, link_early, link_late, added, pot, ring, later_all),
    )

    early_all, early_pass, projs = call(
        32,
        functools.partial(early_kernel, bands, share),
        (),
        [SCALARS, NEAR, NEAR, NEAR, WHOLE] + [FAR] * (bands - 1),
        [NEAR, FAR, NEAR],
        [
            ((first + 1, total_states, cols_z), BF16),
            ((first // 2, total_states, cols_z), BF16),
            ((group_share, total_states, LANES), BF16),
        ],
        [copies((2 * bands + 1,)), copies],
        (ids, xt, whole, later_all, done, *early),
        micros=30,
    )
    early_link = lax.ppermute(early_pass, "domain", link_pairs)
    early_core = lax.ppermute(early_pass, "domain", core_pairs)
    (begun,) = call(
        32,
        functools.partial(gram_kernel, first, share),
        (),
        [SCALARS, NEAR, WHOLE, WHOLE, WHOLE, NEAR],
        [NEAR],
        [((2, total_states, total_states), F32)],
        [],
        (ids, later_all, later_core, later_link, pot, early_all),
    )
    parts = domains * bands
    (blocks,) = call(
        32,
        functools.partial(final_kernel, bands, share),
        (),
        [SCALARS, NEAR, WHOLE, WHOLE, WHOLE, NEAR, NEAR, WHOLE],
        [WHOLE],
        [((parts, states, 2 * total_states // domains), BF16)],
        [pltpu.VMEM((2, total_states, total_states), F32)],
        (ids, early_all, early_core, early_link, pot, begun, projs, energy),
    )
    summed = lax.all_to_all(blocks, ("domain", "band"), split_axis=0, concat_axis=0, tiled=True)
    (subspace,) = call(
        32,
        functools.partial(result_kernel, 1.0 / (lines * cols_z * domains)),
        (),
        [WHOLE],
        [WHOLE],
        [((2, states, total_states // domains), F32)],
        [],
        (summed,),
    )
    return applied.reshape(orbitals.shape), subspace


def solution(mesh):
    in_specs = (
        P("band", ("groups", "domain"), None, None),
        P(("groups", "domain"), None, None),
        P(("groups", "domain"), None, None),
        P(("groups", "domain")),
        P(("groups", "domain")),
        P(("groups", "domain")),
        P("groups", None),
    )
    out_specs = (P("band", ("groups", "domain"), None, None), P(None, ("groups", "band"), "domain"))
    return jax.shard_map(local, mesh=mesh, in_specs=in_specs, out_specs=out_specs, check_vma=False)
```

```python
import functools

import jax
import jax.numpy as jnp
import numpy as np
from jax import lax
from jax.experimental import pallas as pl
from jax.experimental.pallas import tpu as pltpu
from jax.sharding import PartitionSpec as P

F32 = jnp.float32
BF16 = jnp.bfloat16
LANES = 128
ROWS = 16
NT = (((1,), (1,)), ((), ()))
WHOLE = pl.BlockSpec(memory_space=pltpu.VMEM)
NEAR = pl.BlockSpec(memory_space=pltpu.VMEM)
SCALARS = pl.BlockSpec(memory_space=pltpu.SMEM)
FAR = pl.BlockSpec(memory_space=pltpu.HBM)
UNREAD = pl.BlockSpec(memory_space=pl.ANY)
copies = pltpu.SemaphoreType.DMA


def call(room, kernel, grid, in_specs, out_specs, outs, scratch, args, aliases=None, micros=0.001):
    def place(spec):
        return pltpu.VMEM if spec is NEAR else None

    args = [
        pltpu.with_memory_space_constraint(arg, place(spec)) if place(spec) else arg
        for spec, arg in zip(in_specs, args)
    ]
    shapes = [(place(spec) or jax.ShapeDtypeStruct)(shape, kind) for spec, (shape, kind) in zip(out_specs, outs)]
    return pl.pallas_call(
        kernel,
        grid=grid,
        out_shape=shapes,
        in_specs=in_specs,
        out_specs=out_specs,
        scratch_shapes=scratch,
        input_output_aliases=aliases or {},
        compiler_params=pltpu.CompilerParams(vmem_limit_bytes=room << 20),
        cost_estimate=pl.CostEstimate(flops=int(micros * 1.1e9), bytes_accessed=1 << 10, transcendentals=0),
    )(*args)


def start(copy):
    copy.start()
    return copy


def pack_kernel(first, x_hbm, xt, xt_hbm, early, late, message, x, in_sems, out_sems):
    states, lines, _ = x.shape
    bands = in_sems.shape[0]
    share = lines // bands
    count = share - first
    loads, sends = [], []
    for c in range(bands):
        where = (slice(None), pl.ds(c * share, share), slice(None))
        loads.append(start(pltpu.make_async_copy(x_hbm.at[where], x.at[where], in_sems.at[c])))

    def send(line, number, target, at):
        copy = pltpu.make_async_copy(
            xt.at[pl.ds(line, number)], target.at[pl.ds(at, number)], out_sems.at[len(sends)]
        )
        sends.append(start(copy))

    for c in range(bands):
        loads[c].wait()
        for y0 in range(c * share, (c + 1) * share, ROWS):
            for s0 in range(0, states, ROWS):
                block = x[s0 : s0 + ROWS, y0 : y0 + ROWS, :].astype(F32)
                turned = jnp.swapaxes(block, 0, 1).astype(BF16)
                xt[y0 : y0 + ROWS, s0 : s0 + ROWS, :] = turned
        send(c * share + first, count, message, c * (count + 1))
        send(c * share, 1, message, (c + bands - 1) % bands * (count + 1) + count)
        if (c + 1) * share == early.shape[0]:
            send(0, early.shape[0], early, 0)
    send(early.shape[0], late.shape[0], late, 0)
    send(0, lines, xt_hbm, 0)
    for copy in sends:
        copy.wait()


def bases(ids_ref, groups):
    odd, upper = ids_ref[0] & 1, (ids_ref[0] >> 1) & 1
    return [2 * groups * side for side in (1 - odd, odd, 1 - upper, upper)]


def project_kernel(words_ref, ids_ref, xt_ref, p_hbm, handed, p_ref, mine_ref, same, core_ref, link_ref, *refs):
    far_refs, (total, sems) = refs[:-2], refs[-2:]
    slots, proj_count, _ = p_ref.shape
    groups, states = mine_ref.shape[0] // 3, mine_ref.shape[1]
    per_group = LANES // proj_count
    chunks = sems.shape[0]
    size = slots // chunks
    unroll = 16
    loads = []
    for c in range(chunks):
        where = pl.ds(c * size, size)
        loads.append(start(pltpu.make_async_copy(p_hbm.at[where], p_ref.at[where], sems.at[c])))

    def clear(i, carry):
        for u in range(per_group):
            total[i * per_group + u] = jnp.zeros_like(total[0])
        return carry

    lax.fori_loop(0, 3 * groups, clear, 0)

    def body(i, carry):
        for u in range(unroll):
            t = i * unroll + u
            word = words_ref[t]
            line, atom = word >> 16, word & 0xFFFF
            total[atom] += lax.dot_general(p_ref[t], xt_ref[line], NT, preferred_element_type=F32)
        return carry

    for c in range(chunks):
        loads[c].wait()
        lax.fori_loop(c * size // unroll, (c + 1) * size // unroll, body, 0)

    for g in range(3 * groups):
        tiles = [total[g * per_group + u] for u in range(per_group)]
        mine_ref[g] = jnp.concatenate(tiles, axis=0).T
    sides = bases(ids_ref, groups)
    for g in range(groups):
        own = mine_ref[groups + g].astype(BF16)
        for side, ref in zip(sides[:2], (core_ref, link_ref)):
            ref[g] = mine_ref[side + g].astype(BF16)
            ref[groups + g] = own
        for side, ref in zip(sides[2:], far_refs):
            ref[g] = mine_ref[side + g].astype(BF16)


def nonlocal_kernel(first, fars, words_ref, ids_ref, xt_ref, p_ref, energy_ref, mine_ref, core_ref, link_ref, *refs):
    far_refs, (_, _, out_ref, whole_ref, *messages, total, atoms) = refs[:fars], refs[fars:]
    slots, proj_count, _ = p_ref.shape
    groups, states = mine_ref.shape[0] // 3, mine_ref.shape[1]
    per_group = LANES // proj_count
    lines = out_ref.shape[0]
    unroll = 16

    def clear(i, carry):
        out_ref[i] = jnp.zeros((states, LANES), F32)
        return carry

    lax.fori_loop(0, lines, clear, 0)
    total[...] = mine_ref[...]
    sides = bases(ids_ref, groups)
    for g in range(groups):
        total[groups + g] += core_ref[g].astype(F32) + link_ref[g].astype(F32)
        for side, ref in zip(sides[:2], (core_ref, link_ref)):
            total[side + g] += ref[groups + g].astype(F32)
        for side, ref in zip(sides[2:], far_refs):
            total[side + g] += ref[g].astype(F32)
    last = energy_ref.shape[0] - 1
    for g in range(3 * groups):
        row = jnp.clip((ids_ref[0] - 1) * groups + g, 0, last)
        tile = (total[g] * energy_ref[pl.ds(row, 1), :]).astype(BF16)
        for u in range(per_group):
            atoms[g * per_group + u] = tile[:, u * proj_count : (u + 1) * proj_count]
    for g in range(groups):
        whole_ref[g] = total[groups + g].astype(BF16)
    share = xt_ref.shape[0] // (len(messages) + 1)
    held = groups // (len(messages) + 1)
    for k, message in enumerate(messages, 1):
        to = ids_ref[1] ^ k
        for i in range(first):
            message[i] = xt_ref[to * share + i]
        for i in range(held):
            message[first + i] = whole_ref[to * held + i]

    def body(i, carry):
        for u in range(unroll):
            t = i * unroll + u
            word = words_ref[t]
            line, atom = word >> 16, word & 0xFFFF
            out_ref[line] += jnp.dot(atoms[atom], p_ref[t], preferred_element_type=F32)
        return carry

    lax.fori_loop(0, slots // unroll, body, 0)


def stencil_kernel(early_steps, xt_ref, core_ref, early_ref, late_ref, added_ref, pot_ref, ring_ref, out_ref, done_ref):
    states, here, _ = out_ref.shape
    lines = xt_ref.shape[0]
    done_ref[...] = jnp.zeros_like(done_ref)
    step = pl.program_id(0)
    y0 = step * here
    early = step < early_steps
    for s0 in range(0, states, ROWS):
        rows = slice(s0, s0 + ROWS)
        results = []
        cells = jnp.concatenate([xt_ref[y0 + i, rows, :] for i in range(here)], axis=0)
        along = jnp.dot(cells, ring_ref[...], preferred_element_type=F32)
        before = xt_ref[lax.rem(y0 + lines - 1, lines), rows, :].astype(F32)
        x = xt_ref[y0, rows, :].astype(F32)
        for i in range(here):
            after = xt_ref[lax.rem(y0 + i + 1, lines), rows, :].astype(F32)
            link = jnp.where(early, early_ref[i, rows, :].astype(F32), late_ref[i, rows, :].astype(F32))
            beside = (before + after) + (core_ref[i, rows, :].astype(F32) + link)
            value = along[i * ROWS : (i + 1) * ROWS] + pot_ref[i : i + 1, :] * x
            results.append(value + added_ref[y0 + i, rows, :] - 0.5 * beside)
            before, x = x, after
        out_ref[rows, :, :] = jnp.swapaxes(jnp.stack(results, axis=0), 0, 1).astype(BF16)


def pass_half(ids_ref, all_ref, pass_hbm, sem):
    half = pass_hbm.shape[0]
    copy = start(pltpu.make_async_copy(all_ref.at[pl.ds((1 - (ids_ref[0] & 1)) * half, half)], pass_hbm, sem))
    copy.wait()


def later_kernel(bands, ids_ref, landed, unread, all_ref, pass_hbm, sems, pass_sem):
    count, states = all_ref.shape[0], landed.shape[1]
    loads = [
        start(
            pltpu.make_async_copy(
                landed.at[pl.ds(b * count, count)], all_ref.at[:, pl.ds(b * states, states), :], sems.at[b]
            )
        )
        for b in range(bands)
    ]
    for copy in loads:
        copy.wait()
    pass_half(ids_ref, all_ref, pass_hbm, pass_sem)


def early_kernel(bands, share, ids_ref, xt_ref, whole_ref, after_ref, *refs):
    pieces, (all_ref, pass_hbm, projs_ref, sems, pass_sem) = refs[: bands - 1], refs[bands - 1 :]
    states = xt_ref.shape[1]
    band = ids_ref[1]
    count, held = all_ref.shape[0] - 1, projs_ref.shape[0]
    loads = []

    def load(source, target):
        loads.append(start(pltpu.make_async_copy(source, target, sems.at[len(loads)])))

    for k in range(bands):
        at = pl.ds(pl.multiple_of((band ^ k) * states, states), states)
        if k == 0:
            load(xt_ref.at[pl.ds(band * share, count)], all_ref.at[pl.ds(0, count), at, :])
            load(whole_ref.at[pl.ds(band * held, held)], projs_ref.at[:, at, :])
        else:
            load(pieces[k - 1].at[pl.ds(0, count)], all_ref.at[pl.ds(0, count), at, :])
            load(pieces[k - 1].at[pl.ds(count, held)], projs_ref.at[:, at, :])
    load(after_ref.at[pl.ds(0, 1)], all_ref.at[pl.ds(count, 1)])
    for copy in loads:
        copy.wait()
    pass_half(ids_ref, all_ref, pass_hbm, pass_sem)


def add_products(row, ids_ref, all_ref, core_ref, link_ref, pot_ref, acc):
    half = core_ref.shape[0]
    group = 4
    mine = (ids_ref[0] & 1) * half
    for part, base in ((0, mine), (1, half - mine)):
        for i0 in range(0, half, group):
            xs, ys = [], []
            for i in range(i0, min(i0 + group, half)):
                cell = all_ref[base + i]
                x = cell.astype(F32)
                y = (3.0 + pot_ref[pl.ds(row + base + i, 1), :]) * x - pltpu.roll(x, x.shape[1] - 1, 1)
                y = y - all_ref[base + i + 1].astype(F32)
                if part == 0:
                    y = y - core_ref[i].astype(F32) - link_ref[i].astype(F32)
                xs.append(cell)
                ys.append(y.astype(BF16))
            flat_x = jnp.concatenate(xs, axis=1)
            flat_y = jnp.concatenate(ys, axis=1)
            acc[0] += lax.dot_general(flat_x, flat_x, NT, preferred_element_type=F32)
            acc[1] += lax.dot_general(flat_y, flat_x, NT, preferred_element_type=F32)


def gram_kernel(first, share, ids_ref, all_ref, core_ref, link_ref, pot_ref, unread, acc):
    acc[...] = jnp.zeros_like(acc)
    add_products(ids_ref[1] * share + first, ids_ref, all_ref, core_ref, link_ref, pot_ref, acc)


def final_kernel(
    bands, share, ids_ref, all_ref, core_ref, link_ref, pot_ref, begun_ref, proj_ref, energy_ref, out_ref, acc
):
    acc[...] = begun_ref[...]
    add_products(ids_ref[1] * share, ids_ref, all_ref, core_ref, link_ref, pot_ref, acc)
    groups = proj_ref.shape[0]
    first = (ids_ref[0] * bands + ids_ref[1]) * groups
    for g in range(groups):
        here = proj_ref[g]
        scaled = (here.astype(F32) * energy_ref[pl.ds(first + g, 1), :]).astype(BF16)
        acc[1] += lax.dot_general(scaled, here, NT, preferred_element_type=F32)
    hamil = 0.5 * (acc[1] + acc[1].T)
    domains = out_ref.shape[0] // bands
    rows, cols = out_ref.shape[1], out_ref.shape[2] // 2
    for c in range(domains):
        for r in range(bands):
            r0, c0 = r * rows, c * cols
            out_ref[c * bands + r, :, :cols] = acc[0, r0 : r0 + rows, c0 : c0 + cols].astype(BF16)
            out_ref[c * bands + r, :, cols:] = hamil[r0 : r0 + rows, c0 : c0 + cols].astype(BF16)


def result_kernel(scale, parts_ref, out_ref):
    total = jnp.sum(parts_ref[...].astype(F32), axis=0) * scale
    cols = out_ref.shape[2]
    out_ref[0] = total[:, :cols]
    out_ref[1] = total[:, cols:]


def local(orbitals, potential, projectors, tile_atom, tile_line, tile_count, energies):
    states, _, lines, cols_z = orbitals.shape
    slots, proj_count, _ = projectors.shape
    atom_total = energies.shape[0]
    domains, bands = lax.axis_size("domain"), lax.axis_size("band")
    domain, band = lax.axis_index("domain"), lax.axis_index("band")
    total_states = states * bands
    atoms_here = atom_total // domains
    per_group = LANES // proj_count
    groups = atoms_here // per_group
    group_share = groups // bands
    share = lines // bands
    first = share // 4
    rest = share - first

    core_pairs = [(i, i ^ 1) for i in range(domains) if i ^ 1 < domains]
    link_pairs = [(i, ((i + 1) ^ 1) - 1) for i in range(1, domains) if ((i + 1) ^ 1) - 1 < domains]
    near_far = [(i, i ^ 2) for i in range(domains) if i ^ 2 < domains]
    next_far = [(i, ((i + 2) ^ 2) - 2) for i in range(2, domains) if ((i + 2) ^ 2) - 2 < domains]
    far_pairs = [pairs for pairs in (near_far, next_far) if pairs]

    def swapped(values, axis):
        size = lax.axis_size(axis)
        got = {k: lax.ppermute(values[k - 1], axis, [(i, i ^ k) for i in range(size)]) for k in range(size - 1, 0, -1)}
        return [got[k] for k in range(1, size)]

    ids = jnp.stack([domain, band]).astype(jnp.int32)
    near = jnp.clip(tile_atom - (domain - 1) * atoms_here, 0, 3 * atoms_here - 1)
    live = jnp.arange(slots, dtype=jnp.int32) < tile_count[0]
    project_words = (tile_line << 16) | jnp.where(live, near, 3 * atoms_here)
    nonlocal_words = (jnp.where(live, tile_line, lines) << 16) | near
    field = orbitals.reshape(states, lines, cols_z)
    pot = potential.reshape(lines, cols_z)
    energy = energies.reshape(atom_total // per_group, LANES)
    eye = np.eye(cols_z, dtype=np.float32)
    ring = jnp.asarray(3.0 * eye - 0.5 * (np.roll(eye, 1, axis=0) + np.roll(eye, -1, axis=0)), dtype=BF16)

    late_lines = lines // 2
    line_shape, late_shape = (lines, states, cols_z), (late_lines, states, cols_z)
    xt, xt_far, early_part, late_part, message = call(
        58,
        functools.partial(pack_kernel, first),
        (),
        [FAR],
        [NEAR, FAR, FAR, FAR, FAR],
        [
            (line_shape, BF16),
            (line_shape, BF16),
            ((lines - late_lines, states, cols_z), BF16),
            (late_shape, BF16),
            ((bands * (rest + 1), states, cols_z), BF16),
        ],
        [pltpu.VMEM((states, lines, cols_z), BF16), copies((bands,)), copies((2 * bands + 3,))],
        (field,),
    )
    landed = lax.all_to_all(message, "band", split_axis=0, concat_axis=0, tiled=True)
    link_early = lax.ppermute(early_part, "domain", link_pairs)
    core_field = lax.ppermute(xt_far, "domain", core_pairs)

    group_shape = (groups, states, LANES)
    near_projectors, mine, late_part, to_core, to_link, *to_far = call(
        50,
        project_kernel,
        (),
        [SCALARS, SCALARS, NEAR, FAR, UNREAD],
        [NEAR, NEAR, UNREAD] + [WHOLE] * (2 + len(far_pairs)),
        [(projectors.shape, BF16), ((3 * groups, states, LANES), F32), (late_shape, BF16)]
        + [((2 * groups, states, LANES), BF16)] * 2
        + [(group_shape, BF16)] * len(far_pairs),
        [
            pltpu.VMEM((3 * atoms_here + 1, proj_count, states), F32),
            copies((4,)),
        ],
        (project_words, ids, xt, projectors, late_part),
        aliases={4: 2},
        micros=10,
    )
    from_link = lax.ppermute(to_link, "domain", link_pairs)
    from_far = [lax.ppermute(value, "domain", pairs) for value, pairs in zip(to_far, far_pairs)]
    from_core = lax.ppermute(to_core, "domain", core_pairs)
    link_late = lax.ppermute(late_part, "domain", link_pairs)
    added, whole, *messages = call(
        32,
        functools.partial(nonlocal_kernel, first, len(far_pairs)),
        (),
        [SCALARS, SCALARS, NEAR, NEAR, WHOLE, NEAR, WHOLE, WHOLE] + [WHOLE] * len(far_pairs) + [UNREAD] * 2,
        [WHOLE, NEAR] + [WHOLE] * (bands - 1),
        [((lines + 1, states, cols_z), F32), (group_shape, BF16)]
        + [((first + group_share, states, cols_z), BF16)] * (bands - 1),
        [
            pltpu.VMEM((3 * groups, states, LANES), F32),
            pltpu.VMEM((3 * atoms_here, states, proj_count), BF16),
        ],
        (
            nonlocal_words, ids, xt, near_projectors, energy, mine, from_core, from_link, *from_far,
            link_early[0, :ROWS], core_field[0, :ROWS],
        ),
        micros=30,
    )
    early = swapped(messages, "band")

    steps, early_steps = lines // ROWS, (lines - late_lines) // ROWS
    block = pl.BlockSpec((ROWS, states, cols_z), lambda i: (i, 0, 0))
    applied, done = call(
        32,
        functools.partial(stencil_kernel, early_steps),
        (steps,),
        [
            NEAR,
            block,
            pl.BlockSpec((ROWS, states, cols_z), lambda i: (jnp.minimum(i, early_steps - 1), 0, 0)),
            pl.BlockSpec((ROWS, states, cols_z), lambda i: (jnp.maximum(i - early_steps, 0), 0, 0)),
            WHOLE,
            pl.BlockSpec((ROWS, cols_z), lambda i: (i, 0)),
            WHOLE,
        ],
        [pl.BlockSpec((states, ROWS, cols_z), lambda i: (0, i, 0)), WHOLE],
        [((states, lines, cols_z), BF16), ((8, LANES), F32)],
        [],
        (xt, core_field, link_early, link_late, added, pot, ring),
        micros=10,
    )

    later_all, later_pass = call(
        32,
        functools.partial(later_kernel, bands),
        (),
        [SCALARS, FAR, UNREAD],
        [NEAR, FAR],
        [((rest + 1, total_states, cols_z), BF16), ((rest // 2, total_states, cols_z), BF16)],
        [copies((bands,)), copies],
        (ids, landed, done),
    )
    later_link = lax.ppermute(later_pass, "domain", link_pairs)
    later_core = lax.ppermute(later_pass, "domain", core_pairs)

    early_all, early_pass, projs = call(
        32,
        functools.partial(early_kernel, bands, share),
        (),
        [SCALARS, NEAR, NEAR, NEAR] + [FAR] * (bands - 1),
        [NEAR, FAR, NEAR],
        [
            ((first + 1, total_states, cols_z), BF16),
            ((first // 2, total_states, cols_z), BF16),
            ((group_share, total_states, LANES), BF16),
        ],
        [copies((2 * bands + 1,)), copies],
        (ids, xt, whole, later_all, *early),
        micros=30,
    )
    early_link = lax.ppermute(early_pass, "domain", link_pairs)
    early_core = lax.ppermute(early_pass, "domain", core_pairs)
    (begun,) = call(
        32,
        functools.partial(gram_kernel, first, share),
        (),
        [SCALARS, NEAR, WHOLE, WHOLE, WHOLE, NEAR],
        [NEAR],
        [((2, total_states, total_states), F32)],
        [],
        (ids, later_all, later_core, later_link, pot, early_all),
    )
    parts = domains * bands
    (blocks,) = call(
        32,
        functools.partial(final_kernel, bands, share),
        (),
        [SCALARS, NEAR, WHOLE, WHOLE, WHOLE, NEAR, NEAR, WHOLE],
        [WHOLE],
        [((parts, states, 2 * total_states // domains), BF16)],
        [pltpu.VMEM((2, total_states, total_states), F32)],
        (ids, early_all, early_core, early_link, pot, begun, projs, energy),
    )
    summed = lax.all_to_all(blocks, ("domain", "band"), split_axis=0, concat_axis=0, tiled=True)
    (subspace,) = call(
        32,
        functools.partial(result_kernel, 1.0 / (lines * cols_z * domains)),
        (),
        [WHOLE],
        [WHOLE],
        [((2, states, total_states // domains), F32)],
        [],
        (summed,),
    )
    return applied.reshape(orbitals.shape), subspace


def solution(mesh):
    in_specs = (
        P("band", ("groups", "domain"), None, None),
        P(("groups", "domain"), None, None),
        P(("groups", "domain"), None, None),
        P(("groups", "domain")),
        P(("groups", "domain")),
        P(("groups", "domain")),
        P("groups", None),
    )
    out_specs = (P("band", ("groups", "domain"), None, None), P(None, ("groups", "band"), "domain"))
    return jax.shard_map(local, mesh=mesh, in_specs=in_specs, out_specs=out_specs, check_vma=False)
```

```python
import functools

import jax
import jax.numpy as jnp
import numpy as np
from jax import lax
from jax.experimental import pallas as pl
from jax.experimental.pallas import tpu as pltpu
from jax.sharding import PartitionSpec as P

F32 = jnp.float32
BF16 = jnp.bfloat16
LANES = 128
VMEM_BYTES = 63 << 20
ROWS = 16
NT = (((1,), (1,)), ((), ()))
WHOLE = pl.BlockSpec(memory_space=pltpu.VMEM)
SCALARS = pl.BlockSpec(memory_space=pltpu.SMEM)
FAR = pl.BlockSpec(memory_space=pltpu.HBM)
UNREAD = pl.BlockSpec(memory_space=pl.ANY)
copies = pltpu.SemaphoreType.DMA


def call(kernel, grid, in_specs, out_specs, outs, scratch, args, aliases=None, micros=0.001):
    return pl.pallas_call(
        kernel,
        grid=grid,
        out_shape=[jax.ShapeDtypeStruct(shape, kind) for shape, kind in outs],
        in_specs=in_specs,
        out_specs=out_specs,
        scratch_shapes=scratch,
        input_output_aliases=aliases or {},
        compiler_params=pltpu.CompilerParams(vmem_limit_bytes=VMEM_BYTES),
        cost_estimate=pl.CostEstimate(flops=int(micros * 1.1e9), bytes_accessed=1 << 10, transcendentals=0),
    )(*args)


def start(copy):
    copy.start()
    return copy


def load_all(pairs, sems):
    return [start(pltpu.make_async_copy(far, near, sems.at[i])) for i, (far, near) in enumerate(pairs)]


def wait_all(started):
    for copy in started:
        copy.wait()


def pack_kernel(first, x_hbm, xt_hbm, early, late, message, x, xt, in_sems, out_sems):
    states, lines, _ = x.shape
    bands = in_sems.shape[0]
    share = lines // bands
    count = share - first
    loads, sends = [], []
    for c in range(bands):
        where = (slice(None), pl.ds(c * share, share), slice(None))
        loads.append(start(pltpu.make_async_copy(x_hbm.at[where], x.at[where], in_sems.at[c])))

    def send(line, number, target, at):
        copy = pltpu.make_async_copy(
            xt.at[pl.ds(line, number)], target.at[pl.ds(at, number)], out_sems.at[len(sends)]
        )
        sends.append(start(copy))

    for c in range(bands):
        loads[c].wait()
        for y0 in range(c * share, (c + 1) * share, ROWS):
            for s0 in range(0, states, ROWS):
                block = x[s0 : s0 + ROWS, y0 : y0 + ROWS, :].astype(F32)
                turned = jnp.swapaxes(block, 0, 1).astype(BF16)
                xt[y0 : y0 + ROWS, s0 : s0 + ROWS, :] = turned
        send(c * share + first, count, message, c * (count + 1))
        send(c * share, 1, message, (c + bands - 1) % bands * (count + 1) + count)
        if (c + 1) * share == early.shape[0]:
            send(0, early.shape[0], early, 0)
    send(early.shape[0], late.shape[0], late, 0)
    send(0, lines, xt_hbm, 0)
    wait_all(sends)


def bases(ids_ref, groups):
    odd, upper = ids_ref[0] & 1, (ids_ref[0] >> 1) & 1
    return [2 * groups * side for side in (1 - odd, odd, 1 - upper, upper)]


def project_kernel(words_ref, ids_ref, xt_hbm, p_hbm, handed, mine_hbm, same, core_ref, link_ref, *refs):
    far_refs, (total, mine, xt, p_ref, sems, mine_sem) = refs[:-6], refs[-6:]
    slots, proj_count, _ = p_ref.shape
    groups, states = mine.shape[0] // 3, mine.shape[1]
    per_group = LANES // proj_count
    chunks = sems.shape[0] - 1
    size = slots // chunks
    unroll = 16
    pairs = [(p_hbm.at[pl.ds(c * size, size)], p_ref.at[pl.ds(c * size, size)]) for c in range(chunks)]
    xt_load, *loads = load_all([(xt_hbm, xt), *pairs], sems)

    def clear(i, carry):
        for u in range(per_group):
            total[i * per_group + u] = jnp.zeros_like(total[0])
        return carry

    lax.fori_loop(0, 3 * groups, clear, 0)

    def body(i, carry):
        for u0 in range(0, unroll, 8):
            ts = [i * unroll + u0 + u for u in range(8)]
            words = [words_ref[t] for t in ts]
            parts = [
                lax.dot_general(p_ref[t], xt[word >> 16], NT, preferred_element_type=F32)
                for t, word in zip(ts, words)
            ]
            for word, part in zip(words, parts):
                total[word & 0xFFFF] += part
        return carry

    xt_load.wait()
    for c in range(chunks):
        loads[c].wait()
        lax.fori_loop(c * size // unroll, (c + 1) * size // unroll, body, 0)

    for g in range(3 * groups):
        tiles = [total[g * per_group + u] for u in range(per_group)]
        mine[g] = jnp.concatenate(tiles, axis=0).T
    send = start(pltpu.make_async_copy(mine, mine_hbm, mine_sem))
    sides = bases(ids_ref, groups)
    for g in range(groups):
        own = mine[groups + g].astype(BF16)
        for side, ref in zip(sides[:2], (core_ref, link_ref)):
            ref[g] = mine[side + g].astype(BF16)
            ref[groups + g] = own
        for side, ref in zip(sides[2:], far_refs):
            ref[g] = mine[side + g].astype(BF16)
    send.wait()


def nonlocal_kernel(
    first, fars, words_ref, ids_ref, xt_hbm, p_hbm, energy_ref, pot_ref, ring_ref, mine_hbm, core_hbm, link_hbm, *refs
):
    far_hbms, rest = refs[:fars], refs[fars:]
    _, _, out_hbm, whole_ref, *messages, lines_sum, total, atoms, p_ref, xt_ref, pair_refs, far_refs, sems, out_sems = rest
    slots, proj_count, _ = p_ref.shape
    groups, states = total.shape[0] // 3, total.shape[1]
    per_group = LANES // proj_count
    lines = xt_ref.shape[0]
    unroll = 16
    fars_here = [(far, far_refs.at[i]) for i, far in enumerate(far_hbms)]
    pairs = [(mine_hbm, total), (core_hbm, pair_refs.at[0]), (link_hbm, pair_refs.at[1]), *fars_here]
    loads = load_all([*pairs, (xt_hbm, xt_ref), (p_hbm, p_ref)], sems)

    def clear(i, carry):
        lines_sum[i] = jnp.zeros((states, LANES), F32)
        return carry

    lax.fori_loop(0, lines + 1, clear, 0)
    wait_all(loads[:-2])
    sides = bases(ids_ref, groups)
    for g in range(groups):
        total[groups + g] += pair_refs[0, g].astype(F32) + pair_refs[1, g].astype(F32)
        for i in range(2):
            total[sides[i] + g] += pair_refs[i, groups + g].astype(F32)
        for i in range(fars):
            total[sides[2 + i] + g] += far_refs[i, g].astype(F32)
    last = energy_ref.shape[0] - 1
    for g in range(3 * groups):
        row = jnp.clip((ids_ref[0] - 1) * groups + g, 0, last)
        tile = (total[g] * energy_ref[pl.ds(row, 1), :]).astype(BF16)
        for u in range(per_group):
            atoms[g * per_group + u] = tile[:, u * proj_count : (u + 1) * proj_count]
    for g in range(groups):
        whole_ref[g] = total[groups + g].astype(BF16)
    wait_all(loads[-2:])
    share = xt_ref.shape[0] // (len(messages) + 1)
    held = groups // (len(messages) + 1)
    for k, message in enumerate(messages, 1):
        to = ids_ref[1] ^ k
        for i in range(first):
            message[i] = xt_ref[to * share + i]
        for i in range(held):
            message[first + i] = whole_ref[to * held + i]

    def body(i, carry):
        for u0 in range(0, unroll, 4):
            ts = [i * unroll + u0 + u for u in range(4)]
            words = [words_ref[t] for t in ts]
            parts = [
                jnp.dot(atoms[word & 0xFFFF], p_ref[t], preferred_element_type=F32) for t, word in zip(ts, words)
            ]
            for word, part in zip(words, parts):
                lines_sum[word >> 16] += part
        return carry

    lax.fori_loop(0, slots // unroll, body, 0)
    blocks = out_sems.shape[0]
    size = lines // blocks
    step = 8

    def in_plane(i, carry):
        y0 = i * step
        cells = xt_ref[pl.ds(y0, step)].reshape(step * states, LANES)
        along = jnp.dot(cells, ring_ref[...], preferred_element_type=F32)
        before = xt_ref[lax.rem(y0 + lines - 1, lines)].astype(F32)
        x = xt_ref[y0].astype(F32)
        for j in range(step):
            after = xt_ref[lax.rem(y0 + j + 1, lines)].astype(F32)
            value = along[j * states : (j + 1) * states] + pot_ref[pl.ds(y0 + j, 1), :] * x
            lines_sum[y0 + j] += value - 0.5 * (before + after)
            before, x = x, after
        return carry

    sends = []
    for c in range(blocks):
        lax.fori_loop(c * size // step, (c + 1) * size // step, in_plane, 0)
        where = pl.ds(c * size, size)
        sends.append(start(pltpu.make_async_copy(lines_sum.at[where], out_hbm.at[where], out_sems.at[c])))
    wait_all(sends)


def beside_kernel(early_steps, sum_ref, core_ref, early_ref, late_ref, unread, out_ref, done_ref):
    states, here, _ = out_ref.shape
    done_ref[...] = jnp.zeros_like(done_ref)
    early = pl.program_id(0) < early_steps
    for s0 in range(0, states, ROWS):
        rows = slice(s0, s0 + ROWS)
        results = []
        for i in range(here):
            link = jnp.where(early, early_ref[i, rows, :], late_ref[i, rows, :]).astype(F32)
            results.append(sum_ref[i, rows, :] - 0.5 * (core_ref[i, rows, :].astype(F32) + link))
        out_ref[rows, :, :] = jnp.swapaxes(jnp.stack(results, axis=0), 0, 1).astype(BF16)


def later_kernel(bands, ids_ref, landed, unread, pass_hbm, done_ref, sems):
    done_ref[...] = jnp.zeros_like(done_ref)
    half, states = pass_hbm.shape[0], landed.shape[1]
    count = landed.shape[0] // bands
    begin = (1 - (ids_ref[0] & 1)) * half
    wait_all(
        load_all(
            [
                (landed.at[pl.ds(b * count + begin, half)], pass_hbm.at[:, pl.ds(b * states, states), :])
                for b in range(bands)
            ],
            sems,
        )
    )


def early_kernel(share, ids_ref, xt_hbm, unread, *refs):
    pieces, (pass_hbm, done_ref, sems) = refs[:-3], refs[-3:]
    done_ref[...] = jnp.zeros_like(done_ref)
    half, states = pass_hbm.shape[0], xt_hbm.shape[1]
    band = ids_ref[1]
    begin = (1 - (ids_ref[0] & 1)) * half
    pairs = []
    for k in range(len(pieces) + 1):
        at = pl.ds(pl.multiple_of((band ^ k) * states, states), states)
        source = xt_hbm.at[pl.ds(band * share + begin, half)] if k == 0 else pieces[k - 1].at[pl.ds(begin, half)]
        pairs.append((source, pass_hbm.at[:, at, :]))
    wait_all(load_all(pairs, sems))


def add_products(row, ids_ref, line, beside, pot_ref, acc):
    half = beside.shape[1]
    group = 4
    mine = (ids_ref[0] & 1) * half
    for part, base in ((0, mine), (1, half - mine)):
        for i0 in range(0, half, group):
            xs, ys = [], []
            for i in range(i0, min(i0 + group, half)):
                cell = line(base + i)
                x = cell.astype(F32)
                y = (3.0 + pot_ref[pl.ds(row + base + i, 1), :]) * x - pltpu.roll(x, x.shape[1] - 1, 1)
                y = y - line(base + i + 1).astype(F32)
                if part == 0:
                    y = y - beside[0, i].astype(F32) - beside[1, i].astype(F32)
                xs.append(cell)
                ys.append(y.astype(BF16))
            flat_x = jnp.concatenate(xs, axis=1)
            flat_y = jnp.concatenate(ys, axis=1)
            acc[0] += lax.dot_general(flat_x, flat_x, NT, preferred_element_type=F32)
            acc[1] += lax.dot_general(flat_y, flat_x, NT, preferred_element_type=F32)


def gram_kernel(bands, first, share, ids_ref, landed_hbm, core_hbm, link_hbm, pot_ref, unread, acc, landed, beside, sems):
    loads = load_all([(landed_hbm, landed), (core_hbm, beside.at[0]), (link_hbm, beside.at[1])], sems)
    acc[...] = jnp.zeros_like(acc)
    count = landed.shape[0] // bands
    wait_all(loads)

    def line(i):
        return jnp.concatenate([landed[b * count + i] for b in range(bands)], axis=0)

    add_products(ids_ref[1] * share + first, ids_ref, line, beside, pot_ref, acc)


def final_kernel(
    bands, share, ids_ref, xt_hbm, whole_ref, landed_hbm, core_hbm, link_hbm, begun_hbm, pot_ref, energy_ref, *refs
):
    pieces, (out_ref, lines_ref, projs, beside, acc, sems) = refs[: bands - 1], refs[bands - 1 :]
    states = xt_hbm.shape[1]
    band = ids_ref[1]
    first, held = lines_ref.shape[0] - 1, projs.shape[0]
    count = landed_hbm.shape[0] // bands
    pairs = [(begun_hbm, acc), (core_hbm, beside.at[0]), (link_hbm, beside.at[1])]
    for b in range(bands):
        at = pl.ds(b * states, states)
        pairs.append((landed_hbm.at[pl.ds(b * count, 1)], lines_ref.at[pl.ds(first, 1), at, :]))
    for k in range(bands):
        at = pl.ds(pl.multiple_of((band ^ k) * states, states), states)
        if k == 0:
            pairs.append((xt_hbm.at[pl.ds(band * share, first)], lines_ref.at[pl.ds(0, first), at, :]))
            for g in range(held):
                projs[g, at, :] = whole_ref[band * held + g]
        else:
            pairs.append((pieces[k - 1].at[pl.ds(0, first)], lines_ref.at[pl.ds(0, first), at, :]))
            pairs.append((pieces[k - 1].at[pl.ds(first, held)], projs.at[:, at, :]))
    wait_all(load_all(pairs, sems))
    add_products(band * share, ids_ref, lambda i: lines_ref[i], beside, pot_ref, acc)
    row = (ids_ref[0] * bands + band) * held
    for g in range(held):
        here = projs[g]
        scaled = (here.astype(F32) * energy_ref[pl.ds(row + g, 1), :]).astype(BF16)
        acc[1] += lax.dot_general(scaled, here, NT, preferred_element_type=F32)
    hamil = 0.5 * (acc[1] + acc[1].T)
    domains = out_ref.shape[0] // bands
    rows, cols = out_ref.shape[1], out_ref.shape[2] // 2
    for c in range(domains):
        for r in range(bands):
            r0, c0 = r * rows, c * cols
            out_ref[c * bands + r, :, :cols] = acc[0, r0 : r0 + rows, c0 : c0 + cols].astype(BF16)
            out_ref[c * bands + r, :, cols:] = hamil[r0 : r0 + rows, c0 : c0 + cols].astype(BF16)


def result_kernel(scale, parts_ref, out_ref):
    total = jnp.sum(parts_ref[...].astype(F32), axis=0) * scale
    cols = out_ref.shape[2]
    out_ref[0] = total[:, :cols]
    out_ref[1] = total[:, cols:]


def local(orbitals, potential, projectors, tile_atom, tile_line, tile_count, energies):
    states, _, lines, cols_z = orbitals.shape
    slots, proj_count, _ = projectors.shape
    atom_total = energies.shape[0]
    domains, bands = lax.axis_size("domain"), lax.axis_size("band")
    domain, band = lax.axis_index("domain"), lax.axis_index("band")
    total_states = states * bands
    atoms_here = atom_total // domains
    per_group = LANES // proj_count
    groups = atoms_here // per_group
    group_share = groups // bands
    share = lines // bands
    first = share // 4
    rest = share - first

    core_pairs = [(i, i ^ 1) for i in range(domains) if i ^ 1 < domains]
    link_pairs = [(i, ((i + 1) ^ 1) - 1) for i in range(1, domains) if ((i + 1) ^ 1) - 1 < domains]
    near_far = [(i, i ^ 2) for i in range(domains) if i ^ 2 < domains]
    next_far = [(i, ((i + 2) ^ 2) - 2) for i in range(2, domains) if ((i + 2) ^ 2) - 2 < domains]
    far_pairs = [pairs for pairs in (near_far, next_far) if pairs]

    def swapped(values, axis):
        size = lax.axis_size(axis)
        got = {k: lax.ppermute(values[k - 1], axis, [(i, i ^ k) for i in range(size)]) for k in range(size - 1, 0, -1)}
        return [got[k] for k in range(1, size)]

    ids = jnp.stack([domain, band]).astype(jnp.int32)
    near = jnp.clip(tile_atom - (domain - 1) * atoms_here, 0, 3 * atoms_here - 1)
    live = jnp.arange(slots, dtype=jnp.int32) < tile_count[0]
    project_words = (tile_line << 16) | jnp.where(live, near, 3 * atoms_here)
    nonlocal_words = (jnp.where(live, tile_line, lines) << 16) | near
    field = orbitals.reshape(states, lines, cols_z)
    pot = potential.reshape(lines, cols_z)
    energy = energies.reshape(atom_total // per_group, LANES)
    eye = np.eye(cols_z, dtype=np.float32)
    ring = jnp.asarray(3.0 * eye - 0.5 * (np.roll(eye, 1, axis=0) + np.roll(eye, -1, axis=0)), dtype=BF16)

    late_lines = lines // 2
    line_shape, late_shape = (lines, states, cols_z), (late_lines, states, cols_z)
    xt, early_part, late_part, message = call(
        functools.partial(pack_kernel, first),
        (),
        [FAR],
        [FAR] * 4,
        [
            (line_shape, BF16),
            ((lines - late_lines, states, cols_z), BF16),
            (late_shape, BF16),
            ((bands * (rest + 1), states, cols_z), BF16),
        ],
        [
            pltpu.VMEM((states, lines, cols_z), BF16),
            pltpu.VMEM(line_shape, BF16),
            copies((bands,)),
            copies((2 * bands + 3,)),
        ],
        (field,),
    )
    landed = lax.all_to_all(message, "band", split_axis=0, concat_axis=0, tiled=True)
    link_early = lax.ppermute(early_part, "domain", link_pairs)
    core_field = lax.ppermute(xt, "domain", core_pairs)

    group_shape = (groups, states, LANES)
    mine, late_part, to_core, to_link, *to_far = call(
        project_kernel,
        (),
        [SCALARS, SCALARS, FAR, FAR, UNREAD],
        [FAR, UNREAD] + [WHOLE] * (2 + len(far_pairs)),
        [((3 * groups, states, LANES), F32), (late_shape, BF16)]
        + [((2 * groups, states, LANES), BF16)] * 2
        + [(group_shape, BF16)] * len(far_pairs),
        [
            pltpu.VMEM((3 * atoms_here + 1, proj_count, states), F32),
            pltpu.VMEM((3 * groups, states, LANES), F32),
            pltpu.VMEM(line_shape, BF16),
            pltpu.VMEM(projectors.shape, BF16),
            copies((5,)),
            copies,
        ],
        (project_words, ids, xt, projectors, late_part),
        aliases={4: 1},
        micros=10,
    )
    from_link = lax.ppermute(to_link, "domain", link_pairs)
    from_far = [lax.ppermute(value, "domain", pairs) for value, pairs in zip(to_far, far_pairs)]
    from_core = lax.ppermute(to_core, "domain", core_pairs)
    link_late = lax.ppermute(late_part, "domain", link_pairs)
    added, whole, *messages = call(
        functools.partial(nonlocal_kernel, first, len(far_pairs)),
        (),
        [SCALARS, SCALARS, FAR, FAR, WHOLE, WHOLE, WHOLE] + [FAR] * (3 + len(far_pairs)) + [UNREAD] * 2,
        [FAR, WHOLE] + [WHOLE] * (bands - 1),
        [(line_shape, F32), (group_shape, BF16)]
        + [((first + group_share, states, cols_z), BF16)] * (bands - 1),
        [
            pltpu.VMEM((lines + 1, states, cols_z), F32),
            pltpu.VMEM((3 * groups, states, LANES), F32),
            pltpu.VMEM((3 * atoms_here, states, proj_count), BF16),
            pltpu.VMEM(projectors.shape, BF16),
            pltpu.VMEM(line_shape, BF16),
            pltpu.VMEM((2, 2 * groups, states, LANES), BF16),
            pltpu.VMEM((2, *group_shape), BF16),
            copies((5 + len(far_pairs),)),
            copies((4,)),
        ],
        (
            nonlocal_words, ids, xt, projectors, energy, pot, ring, mine, from_core, from_link, *from_far,
            link_early[0, :ROWS], core_field[0, :ROWS],
        ),
        micros=30,
    )
    early = swapped(messages, "band")

    later_pass, later_token = call(
        functools.partial(later_kernel, bands),
        (),
        [SCALARS, FAR, UNREAD],
        [FAR, WHOLE],
        [((rest // 2, total_states, cols_z), BF16), ((8, LANES), F32)],
        [copies((bands,))],
        (ids, landed, whole),
    )
    later_link = lax.ppermute(later_pass, "domain", link_pairs)
    later_core = lax.ppermute(later_pass, "domain", core_pairs)

    steps, early_steps = lines // ROWS, (lines - late_lines) // ROWS
    block = pl.BlockSpec((ROWS, states, cols_z), lambda i: (i, 0, 0))
    applied, beside_token = call(
        functools.partial(beside_kernel, early_steps),
        (steps,),
        [
            block,
            block,
            pl.BlockSpec((ROWS, states, cols_z), lambda i: (jnp.minimum(i, early_steps - 1), 0, 0)),
            pl.BlockSpec((ROWS, states, cols_z), lambda i: (jnp.maximum(i - early_steps, 0), 0, 0)),
            UNREAD,
        ],
        [pl.BlockSpec((states, ROWS, cols_z), lambda i: (0, i, 0)), WHOLE],
        [((states, lines, cols_z), BF16), ((8, LANES), F32)],
        [],
        (added, core_field, link_early, link_late, later_token),
    )

    early_pass, early_token = call(
        functools.partial(early_kernel, share),
        (),
        [SCALARS, FAR, UNREAD] + [FAR] * (bands - 1),
        [FAR, WHOLE],
        [((first // 2, total_states, cols_z), BF16), ((8, LANES), F32)],
        [copies((bands,))],
        (ids, xt, beside_token, *early),
        micros=30,
    )
    early_link = lax.ppermute(early_pass, "domain", link_pairs)
    early_core = lax.ppermute(early_pass, "domain", core_pairs)
    squares = (2, total_states, total_states)
    (begun,) = call(
        functools.partial(gram_kernel, bands, first, share),
        (),
        [SCALARS, FAR, FAR, FAR, WHOLE, UNREAD],
        [WHOLE],
        [(squares, F32)],
        [
            pltpu.VMEM((bands * (rest + 1), states, cols_z), BF16),
            pltpu.VMEM((2, rest // 2, total_states, cols_z), BF16),
            copies((3,)),
        ],
        (ids, landed, later_core, later_link, pot, early_token),
    )
    parts = domains * bands
    (blocks,) = call(
        functools.partial(final_kernel, bands, share),
        (),
        [SCALARS, FAR, WHOLE, FAR, FAR, FAR, FAR, WHOLE, WHOLE] + [FAR] * (bands - 1),
        [WHOLE],
        [((parts, states, 2 * total_states // domains), BF16)],
        [
            pltpu.VMEM((first + 1, total_states, cols_z), BF16),
            pltpu.VMEM((group_share, total_states, LANES), BF16),
            pltpu.VMEM((2, first // 2, total_states, cols_z), BF16),
            pltpu.VMEM(squares, F32),
            copies((3 * bands + 2,)),
        ],
        (ids, xt, whole, landed, early_core, early_link, begun, pot, energy, *early),
    )
    summed = lax.all_to_all(blocks, ("domain", "band"), split_axis=0, concat_axis=0, tiled=True)
    (subspace,) = call(
        functools.partial(result_kernel, 1.0 / (lines * cols_z * domains)),
        (),
        [WHOLE],
        [WHOLE],
        [((2, states, total_states // domains), F32)],
        [],
        (summed,),
    )
    return applied.reshape(orbitals.shape), subspace


def solution(mesh):
    in_specs = (
        P("band", ("groups", "domain"), None, None),
        P(("groups", "domain"), None, None),
        P(("groups", "domain"), None, None),
        P(("groups", "domain")),
        P(("groups", "domain")),
        P(("groups", "domain")),
        P("groups", None),
    )
    out_specs = (P("band", ("groups", "domain"), None, None), P(None, ("groups", "band"), "domain"))
    return jax.shard_map(local, mesh=mesh, in_specs=in_specs, out_specs=out_specs, check_vma=False)
```

```python
import functools

import jax
import jax.numpy as jnp
import numpy as np
from jax import lax
from jax.experimental import pallas as pl
from jax.experimental.pallas import tpu as pltpu
from jax.sharding import PartitionSpec as P

F32 = jnp.float32
BF16 = jnp.bfloat16
LANES = 128
ROWS = 16
NT = (((1,), (1,)), ((), ()))
WHOLE = pl.BlockSpec(memory_space=pltpu.VMEM)
NEAR = pl.BlockSpec(memory_space=pltpu.VMEM)
SCALARS = pl.BlockSpec(memory_space=pltpu.SMEM)
FAR = pl.BlockSpec(memory_space=pltpu.HBM)
PINNED = pl.BlockSpec(memory_space=pltpu.HBM)
UNREAD = pl.BlockSpec(memory_space=pl.ANY)
copies = pltpu.SemaphoreType.DMA


def call(room, kernel, grid, in_specs, out_specs, outs, scratch, args, aliases=None, micros=0.001):
    def place(spec):
        return {id(NEAR): pltpu.VMEM, id(PINNED): pltpu.HBM}.get(id(spec))

    args = [
        pltpu.with_memory_space_constraint(arg, place(spec)) if place(spec) else arg
        for spec, arg in zip(in_specs, args)
    ]
    shapes = [(place(spec) or jax.ShapeDtypeStruct)(shape, kind) for spec, (shape, kind) in zip(out_specs, outs)]
    return pl.pallas_call(
        kernel,
        grid=grid,
        out_shape=shapes,
        in_specs=in_specs,
        out_specs=out_specs,
        scratch_shapes=scratch,
        input_output_aliases=aliases or {},
        compiler_params=pltpu.CompilerParams(vmem_limit_bytes=room << 20),
        cost_estimate=pl.CostEstimate(flops=int(micros * 1.1e9), bytes_accessed=1 << 10, transcendentals=0),
    )(*args)


def start(copy):
    copy.start()
    return copy


def pack_kernel(first, x_hbm, xt, xt_hbm, early, late, message, x, in_sems, out_sems):
    states, lines, _ = x.shape
    bands = in_sems.shape[0]
    share = lines // bands
    count = share - first
    loads, sends = [], []
    for c in range(bands):
        where = (slice(None), pl.ds(c * share, share), slice(None))
        loads.append(start(pltpu.make_async_copy(x_hbm.at[where], x.at[where], in_sems.at[c])))

    def send(line, number, target, at):
        copy = pltpu.make_async_copy(
            xt.at[pl.ds(line, number)], target.at[pl.ds(at, number)], out_sems.at[len(sends)]
        )
        sends.append(start(copy))

    for c in range(bands):
        loads[c].wait()
        for y0 in range(c * share, (c + 1) * share, ROWS):
            for s0 in range(0, states, ROWS):
                block = x[s0 : s0 + ROWS, y0 : y0 + ROWS, :].astype(F32)
                turned = jnp.swapaxes(block, 0, 1).astype(BF16)
                xt[y0 : y0 + ROWS, s0 : s0 + ROWS, :] = turned
        send(c * share + first, count, message, c * (count + 1))
        send(c * share, 1, message, (c + bands - 1) % bands * (count + 1) + count)
        if (c + 1) * share == early.shape[0]:
            send(0, early.shape[0], early, 0)
    send(early.shape[0], late.shape[0], late, 0)
    send(0, lines, xt_hbm, 0)
    for copy in sends:
        copy.wait()


def bases(groups):
    domain = lax.axis_index("domain")
    odd, upper = domain & 1, (domain >> 1) & 1
    return [2 * groups * side for side in (1 - odd, odd, 1 - upper, upper)]


def slot_at(t, atom_ref, line_ref, count_ref, atoms_here):
    first = (lax.axis_index("domain") - 1) * atoms_here
    atom = jnp.clip(atom_ref[t] - first, 0, 3 * atoms_here - 1)
    return line_ref[t], atom, t < count_ref[0]


def project_kernel(atom_ref, line_ref, count_ref, xt_ref, p_hbm, handed, mine_ref, same, core_ref, link_ref, *refs):
    far_refs, (total, p_ref, sems) = refs[:-3], refs[-3:]
    slots, proj_count, _ = p_ref.shape
    groups, states = mine_ref.shape[0] // 3, mine_ref.shape[1]
    per_group = LANES // proj_count
    chunks = sems.shape[0]
    size = slots // chunks
    unroll = 16
    loads = []
    for c in range(chunks):
        where = pl.ds(c * size, size)
        loads.append(start(pltpu.make_async_copy(p_hbm.at[where], p_ref.at[where], sems.at[c])))

    def clear(i, carry):
        for u in range(per_group):
            total[i * per_group + u] = jnp.zeros_like(total[0])
        return carry

    lax.fori_loop(0, 3 * groups, clear, 0)

    def body(i, carry):
        for u in range(unroll):
            t = i * unroll + u
            line, atom, live = slot_at(t, atom_ref, line_ref, count_ref, groups * per_group)
            part = lax.dot_general(p_ref[t], xt_ref[line], NT, preferred_element_type=F32)
            total[jnp.where(live, atom, 3 * groups * per_group)] += part
        return carry

    for c in range(chunks):
        loads[c].wait()
        lax.fori_loop(c * size // unroll, (c + 1) * size // unroll, body, 0)

    for g in range(3 * groups):
        tiles = [total[g * per_group + u] for u in range(per_group)]
        mine_ref[g] = jnp.concatenate(tiles, axis=0).T
    sides = bases(groups)
    for g in range(groups):
        own = mine_ref[groups + g].astype(BF16)
        for side, ref in zip(sides[:2], (core_ref, link_ref)):
            ref[g] = mine_ref[side + g].astype(BF16)
            ref[groups + g] = own
        for side, ref in zip(sides[2:], far_refs):
            ref[g] = mine_ref[side + g].astype(BF16)


def nonlocal_kernel(
    first, fars, atom_ref, line_ref, count_ref, xt_ref, p_hbm, energy_ref, mine_ref, core_ref, link_ref, *refs
):
    far_refs, (_, _, out_hbm, whole_hbm, done_ref, *messages, lines_sum, whole_ref, total, atoms, p_ref, sems) = (
        refs[:fars],
        refs[fars:],
    )
    slots, proj_count, _ = p_ref.shape
    groups, states = mine_ref.shape[0] // 3, mine_ref.shape[1]
    per_group = LANES // proj_count
    lines = xt_ref.shape[0]
    unroll = 16
    load = start(pltpu.make_async_copy(p_hbm, p_ref, sems.at[0]))
    done_ref[...] = jnp.zeros_like(done_ref)

    def clear(i, carry):
        lines_sum[i] = jnp.zeros((states, LANES), F32)
        return carry

    lax.fori_loop(0, lines + 1, clear, 0)
    total[...] = mine_ref[...]
    sides = bases(groups)
    for g in range(groups):
        total[groups + g] += core_ref[g].astype(F32) + link_ref[g].astype(F32)
        for side, ref in zip(sides[:2], (core_ref, link_ref)):
            total[side + g] += ref[groups + g].astype(F32)
        for side, ref in zip(sides[2:], far_refs):
            total[side + g] += ref[g].astype(F32)
    last = energy_ref.shape[0] - 1
    for g in range(3 * groups):
        row = jnp.clip((lax.axis_index("domain") - 1) * groups + g, 0, last)
        tile = (total[g] * energy_ref[pl.ds(row, 1), :]).astype(BF16)
        for u in range(per_group):
            atoms[g * per_group + u] = tile[:, u * proj_count : (u + 1) * proj_count]
    for g in range(groups):
        whole_ref[g] = total[groups + g].astype(BF16)
    send_whole = start(pltpu.make_async_copy(whole_ref, whole_hbm, sems.at[1]))
    share = xt_ref.shape[0] // (len(messages) + 1)
    held = groups // (len(messages) + 1)
    for k, message in enumerate(messages, 1):
        to = lax.axis_index("band") ^ k
        for i in range(first):
            message[i] = xt_ref[to * share + i]
        for i in range(held):
            message[first + i] = whole_ref[to * held + i]
    load.wait()

    def body(i, carry):
        for u in range(unroll):
            t = i * unroll + u
            line, atom, live = slot_at(t, atom_ref, line_ref, count_ref, groups * per_group)
            part = jnp.dot(atoms[atom], p_ref[t], preferred_element_type=F32)
            lines_sum[jnp.where(live, line, lines)] += part
        return carry

    lax.fori_loop(0, slots // unroll, body, 0)
    send = start(pltpu.make_async_copy(lines_sum.at[pl.ds(0, lines)], out_hbm, sems.at[2]))
    send_whole.wait()
    send.wait()


def stencil_kernel(early_steps, xt_ref, core_ref, early_ref, late_ref, added_ref, pot_ref, ring_ref, unread, out_ref, done_ref):
    states, here, _ = out_ref.shape
    lines = xt_ref.shape[0]
    done_ref[...] = jnp.zeros_like(done_ref)
    step = pl.program_id(0)
    early = step < early_steps
    for part in range(0, here, ROWS):
        y0 = step * here + part
        for s0 in range(0, states, ROWS):
            rows = slice(s0, s0 + ROWS)
            results = []
            cells = jnp.concatenate([xt_ref[y0 + i, rows, :] for i in range(ROWS)], axis=0)
            along = jnp.dot(cells, ring_ref[...], preferred_element_type=F32)
            before = xt_ref[lax.rem(y0 + lines - 1, lines), rows, :].astype(F32)
            x = xt_ref[y0, rows, :].astype(F32)
            for i in range(ROWS):
                after = xt_ref[lax.rem(y0 + i + 1, lines), rows, :].astype(F32)
                link = jnp.where(early, early_ref[part + i, rows, :], late_ref[part + i, rows, :]).astype(F32)
                beside = (before + after) + (core_ref[part + i, rows, :].astype(F32) + link)
                value = along[i * ROWS : (i + 1) * ROWS] + pot_ref[part + i : part + i + 1, :] * x
                results.append(value + added_ref[part + i, rows, :] - 0.5 * beside)
                before, x = x, after
            turned = jnp.swapaxes(jnp.stack(results, axis=0), 0, 1).astype(BF16)
            out_ref[rows, part : part + ROWS, :] = turned


def pass_half(all_ref, pass_hbm, sem):
    half = pass_hbm.shape[0]
    copy = start(pltpu.make_async_copy(all_ref.at[pl.ds((1 - (lax.axis_index("domain") & 1)) * half, half)], pass_hbm, sem))
    copy.wait()


def later_kernel(bands, landed, unread, all_ref, pass_hbm, done_ref, sems, pass_sem):
    done_ref[...] = jnp.zeros_like(done_ref)
    count, states = all_ref.shape[0], landed.shape[1]
    loads = [
        start(
            pltpu.make_async_copy(
                landed.at[pl.ds(b * count, count)], all_ref.at[:, pl.ds(b * states, states), :], sems.at[b]
            )
        )
        for b in range(bands)
    ]
    for copy in loads:
        copy.wait()
    pass_half(all_ref, pass_hbm, pass_sem)


def early_kernel(bands, share, xt_ref, whole_ref, after_ref, unread, *refs):
    pieces, (all_ref, pass_hbm, projs_ref, done_ref, sems, pass_sem) = refs[: bands - 1], refs[bands - 1 :]
    done_ref[...] = jnp.zeros_like(done_ref)
    states = xt_ref.shape[1]
    band = lax.axis_index("band")
    count, held = all_ref.shape[0] - 1, projs_ref.shape[0]
    loads = []

    def load(source, target):
        loads.append(start(pltpu.make_async_copy(source, target, sems.at[len(loads)])))

    for k in range(bands):
        at = pl.ds(pl.multiple_of((band ^ k) * states, states), states)
        if k == 0:
            load(xt_ref.at[pl.ds(band * share, count)], all_ref.at[pl.ds(0, count), at, :])
            load(whole_ref.at[pl.ds(band * held, held)], projs_ref.at[:, at, :])
        else:
            load(pieces[k - 1].at[pl.ds(0, count)], all_ref.at[pl.ds(0, count), at, :])
            load(pieces[k - 1].at[pl.ds(count, held)], projs_ref.at[:, at, :])
    load(after_ref.at[pl.ds(0, 1)], all_ref.at[pl.ds(count, 1)])
    for copy in loads:
        copy.wait()
    pass_half(all_ref, pass_hbm, pass_sem)


def add_products(row, all_ref, core_ref, link_ref, pot_ref, acc):
    half = core_ref.shape[0]
    group = 4
    mine = (lax.axis_index("domain") & 1) * half
    for part, base in ((0, mine), (1, half - mine)):
        for i0 in range(0, half, group):
            xs, ys = [], []
            for i in range(i0, min(i0 + group, half)):
                cell = all_ref[base + i]
                x = cell.astype(F32)
                y = (3.0 + pot_ref[pl.ds(row + base + i, 1), :]) * x - pltpu.roll(x, x.shape[1] - 1, 1)
                y = y - all_ref[base + i + 1].astype(F32)
                if part == 0:
                    y = y - core_ref[i].astype(F32) - link_ref[i].astype(F32)
                xs.append(cell)
                ys.append(y.astype(BF16))
            flat_x = jnp.concatenate(xs, axis=1)
            flat_y = jnp.concatenate(ys, axis=1)
            acc[0] += lax.dot_general(flat_x, flat_x, NT, preferred_element_type=F32)
            acc[1] += lax.dot_general(flat_y, flat_x, NT, preferred_element_type=F32)


def gram_kernel(first, share, all_ref, core_ref, link_ref, pot_ref, unread, acc):
    acc[...] = jnp.zeros_like(acc)
    add_products(lax.axis_index("band") * share + first, all_ref, core_ref, link_ref, pot_ref, acc)


def final_kernel(
    bands, share, all_ref, core_ref, link_ref, pot_ref, begun_ref, proj_ref, energy_ref, out_ref, acc
):
    acc[...] = begun_ref[...]
    add_products(lax.axis_index("band") * share, all_ref, core_ref, link_ref, pot_ref, acc)
    groups = proj_ref.shape[0]
    first = (lax.axis_index("domain") * bands + lax.axis_index("band")) * groups
    for g in range(groups):
        here = proj_ref[g]
        scaled = (here.astype(F32) * energy_ref[pl.ds(first + g, 1), :]).astype(BF16)
        acc[1] += lax.dot_general(scaled, here, NT, preferred_element_type=F32)
    hamil = 0.5 * (acc[1] + acc[1].T)
    domains = out_ref.shape[0] // bands
    rows, cols = out_ref.shape[1], out_ref.shape[2] // 2
    for c in range(domains):
        for r in range(bands):
            r0, c0 = r * rows, c * cols
            out_ref[c * bands + r, :, :cols] = acc[0, r0 : r0 + rows, c0 : c0 + cols].astype(BF16)
            out_ref[c * bands + r, :, cols:] = hamil[r0 : r0 + rows, c0 : c0 + cols].astype(BF16)


def result_kernel(scale, parts_ref, out_ref):
    total = jnp.sum(parts_ref[...].astype(F32), axis=0) * scale
    cols = out_ref.shape[2]
    out_ref[0] = total[:, :cols]
    out_ref[1] = total[:, cols:]


def local(orbitals, potential, projectors, tile_atom, tile_line, tile_count, energies):
    states, _, lines, cols_z = orbitals.shape
    slots, proj_count, _ = projectors.shape
    atom_total = energies.shape[0]
    domains, bands = lax.axis_size("domain"), lax.axis_size("band")
    total_states = states * bands
    atoms_here = atom_total // domains
    per_group = LANES // proj_count
    groups = atoms_here // per_group
    group_share = groups // bands
    share = lines // bands
    first = share // 4
    rest = share - first

    core_pairs = [(i, i ^ 1) for i in range(domains) if i ^ 1 < domains]
    link_pairs = [(i, ((i + 1) ^ 1) - 1) for i in range(1, domains) if ((i + 1) ^ 1) - 1 < domains]
    near_far = [(i, i ^ 2) for i in range(domains) if i ^ 2 < domains]
    next_far = [(i, ((i + 2) ^ 2) - 2) for i in range(2, domains) if ((i + 2) ^ 2) - 2 < domains]
    far_pairs = [pairs for pairs in (near_far, next_far) if pairs]

    def swapped(values, axis):
        size = lax.axis_size(axis)
        got = {k: lax.ppermute(values[k - 1], axis, [(i, i ^ k) for i in range(size)]) for k in range(size - 1, 0, -1)}
        return [got[k] for k in range(1, size)]

    field = orbitals.reshape(states, lines, cols_z)
    pot = potential.reshape(lines, cols_z)
    energy = energies.reshape(atom_total // per_group, LANES)
    eye = np.eye(cols_z, dtype=np.float32)
    ring = jnp.asarray(3.0 * eye - 0.5 * (np.roll(eye, 1, axis=0) + np.roll(eye, -1, axis=0)), dtype=BF16)

    late_lines = lines // 2
    line_shape, late_shape = (lines, states, cols_z), (late_lines, states, cols_z)
    xt, xt_far, early_part, late_part, message = call(
        58,
        functools.partial(pack_kernel, first),
        (),
        [FAR],
        [NEAR, FAR, FAR, FAR, FAR],
        [
            (line_shape, BF16),
            (line_shape, BF16),
            ((lines - late_lines, states, cols_z), BF16),
            (late_shape, BF16),
            ((bands * (rest + 1), states, cols_z), BF16),
        ],
        [pltpu.VMEM((states, lines, cols_z), BF16), copies((bands,)), copies((2 * bands + 3,))],
        (field,),
    )
    landed = lax.all_to_all(message, "band", split_axis=0, concat_axis=0, tiled=True)
    link_early = lax.ppermute(early_part, "domain", link_pairs)
    core_field = lax.ppermute(xt_far, "domain", core_pairs)

    group_shape = (groups, states, LANES)
    mine, late_part, to_core, to_link, *to_far = call(
        50,
        project_kernel,
        (),
        [SCALARS] * 3 + [NEAR, PINNED, UNREAD],
        [NEAR, UNREAD] + [WHOLE] * (2 + len(far_pairs)),
        [((3 * groups, states, LANES), F32), (late_shape, BF16)]
        + [((2 * groups, states, LANES), BF16)] * 2
        + [(group_shape, BF16)] * len(far_pairs),
        [
            pltpu.VMEM((3 * atoms_here + 1, proj_count, states), F32),
            pltpu.VMEM(projectors.shape, BF16),
            copies((4,)),
        ],
        (tile_atom, tile_line, tile_count, xt, projectors, late_part),
        aliases={5: 1},
        micros=10,
    )
    from_link = lax.ppermute(to_link, "domain", link_pairs)
    from_far = [lax.ppermute(value, "domain", pairs) for value, pairs in zip(to_far, far_pairs)]
    from_core = lax.ppermute(to_core, "domain", core_pairs)
    link_late = lax.ppermute(late_part, "domain", link_pairs)
    added, whole, summed_up, *messages = call(
        32,
        functools.partial(nonlocal_kernel, first, len(far_pairs)),
        (),
        [SCALARS] * 3 + [NEAR, PINNED, WHOLE, NEAR, WHOLE, WHOLE] + [WHOLE] * len(far_pairs) + [UNREAD] * 2,
        [PINNED, PINNED, WHOLE] + [WHOLE] * (bands - 1),
        [(line_shape, F32), (group_shape, BF16), ((8, LANES), F32)]
        + [((first + group_share, states, cols_z), BF16)] * (bands - 1),
        [
            pltpu.VMEM((lines + 1, states, cols_z), F32),
            pltpu.VMEM(group_shape, BF16),
            pltpu.VMEM((3 * groups, states, LANES), F32),
            pltpu.VMEM((3 * atoms_here, states, proj_count), BF16),
            pltpu.VMEM(projectors.shape, BF16),
            copies((3,)),
        ],
        (
            tile_atom, tile_line, tile_count, xt, projectors, energy, mine, from_core, from_link, *from_far,
            link_early[0, :ROWS], core_field[0, :ROWS],
        ),
        micros=30,
    )
    early = swapped(messages, "band")

    later_all, later_pass, later_token = call(
        32,
        functools.partial(later_kernel, bands),
        (),
        [FAR, UNREAD],
        [NEAR, FAR, WHOLE],
        [((rest + 1, total_states, cols_z), BF16), ((rest // 2, total_states, cols_z), BF16), ((8, LANES), F32)],
        [copies((bands,)), copies],
        (landed, summed_up),
    )
    later_link = lax.ppermute(later_pass, "domain", link_pairs)
    later_core = lax.ppermute(later_pass, "domain", core_pairs)

    span = 2 * ROWS
    steps, early_steps = lines // span, (lines - late_lines) // span
    block = pl.BlockSpec((span, states, cols_z), lambda i: (i, 0, 0))
    applied, done = call(
        32,
        functools.partial(stencil_kernel, early_steps),
        (steps,),
        [
            NEAR,
            block,
            pl.BlockSpec((span, states, cols_z), lambda i: (jnp.minimum(i, early_steps - 1), 0, 0)),
            pl.BlockSpec((span, states, cols_z), lambda i: (jnp.maximum(i - early_steps, 0), 0, 0)),
            block,
            pl.BlockSpec((span, cols_z), lambda i: (i, 0)),
            WHOLE,
            UNREAD,
        ],
        [pl.BlockSpec((states, span, cols_z), lambda i: (0, i, 0)), WHOLE],
        [((states, lines, cols_z), BF16), ((8, LANES), F32)],
        [],
        (
            xt, core_field, link_early, link_late, pltpu.with_memory_space_constraint(added, pltpu.HBM), pot, ring,
            later_token,
        ),
    )

    early_all, early_pass, projs, early_token = call(
        32,
        functools.partial(early_kernel, bands, share),
        (),
        [NEAR, PINNED, NEAR, WHOLE] + [FAR] * (bands - 1),
        [NEAR, FAR, NEAR, WHOLE],
        [
            ((first + 1, total_states, cols_z), BF16),
            ((first // 2, total_states, cols_z), BF16),
            ((group_share, total_states, LANES), BF16),
            ((8, LANES), F32),
        ],
        [copies((2 * bands + 1,)), copies],
        (xt, whole, later_all, done, *early),
        micros=30,
    )
    early_link = lax.ppermute(early_pass, "domain", link_pairs)
    early_core = lax.ppermute(early_pass, "domain", core_pairs)
    (begun,) = call(
        32,
        functools.partial(gram_kernel, first, share),
        (),
        [NEAR, WHOLE, WHOLE, WHOLE, UNREAD],
        [NEAR],
        [((2, total_states, total_states), F32)],
        [],
        (later_all, later_core, later_link, pot, early_token),
    )
    parts = domains * bands
    (blocks,) = call(
        32,
        functools.partial(final_kernel, bands, share),
        (),
        [NEAR, WHOLE, WHOLE, WHOLE, NEAR, NEAR, WHOLE],
        [WHOLE],
        [((parts, states, 2 * total_states // domains), BF16)],
        [pltpu.VMEM((2, total_states, total_states), F32)],
        (early_all, early_core, early_link, pot, begun, projs, energy),
    )
    summed = lax.all_to_all(blocks, ("domain", "band"), split_axis=0, concat_axis=0, tiled=True)
    (subspace,) = call(
        32,
        functools.partial(result_kernel, 1.0 / (lines * cols_z * domains)),
        (),
        [WHOLE],
        [WHOLE],
        [((2, states, total_states // domains), F32)],
        [],
        (summed,),
    )
    return applied.reshape(orbitals.shape), subspace


def solution(mesh):
    in_specs = (
        P("band", ("groups", "domain"), None, None),
        P(("groups", "domain"), None, None),
        P(("groups", "domain"), None, None),
        P(("groups", "domain")),
        P(("groups", "domain")),
        P(("groups", "domain")),
        P("groups", None),
    )
    out_specs = (P("band", ("groups", "domain"), None, None), P(None, ("groups", "band"), "domain"))
    return jax.shard_map(local, mesh=mesh, in_specs=in_specs, out_specs=out_specs, check_vma=False)
```

```python
import functools

import jax
import jax.numpy as jnp
import numpy as np
from jax import lax
from jax.experimental import pallas as pl
from jax.experimental.pallas import tpu as pltpu
from jax.sharding import PartitionSpec as P

F32 = jnp.float32
BF16 = jnp.bfloat16
LANES = 128
ROWS = 16
NT = (((1,), (1,)), ((), ()))
WHOLE = pl.BlockSpec(memory_space=pltpu.VMEM)
NEAR = pl.BlockSpec(memory_space=pltpu.VMEM)
SCALARS = pl.BlockSpec(memory_space=pltpu.SMEM)
FAR = pl.BlockSpec(memory_space=pltpu.HBM)
PINNED = pl.BlockSpec(memory_space=pltpu.HBM)
UNREAD = pl.BlockSpec(memory_space=pl.ANY)
copies = pltpu.SemaphoreType.DMA


def call(room, kernel, grid, in_specs, out_specs, outs, scratch, args, aliases=None, micros=0.001):
    def place(spec):
        return {id(NEAR): pltpu.VMEM, id(PINNED): pltpu.HBM}.get(id(spec))

    args = [
        pltpu.with_memory_space_constraint(arg, place(spec)) if place(spec) else arg
        for spec, arg in zip(in_specs, args)
    ]
    shapes = [(place(spec) or jax.ShapeDtypeStruct)(shape, kind) for spec, (shape, kind) in zip(out_specs, outs)]
    return pl.pallas_call(
        kernel,
        grid=grid,
        out_shape=shapes,
        in_specs=in_specs,
        out_specs=out_specs,
        scratch_shapes=scratch,
        input_output_aliases=aliases or {},
        compiler_params=pltpu.CompilerParams(vmem_limit_bytes=room << 20),
        cost_estimate=pl.CostEstimate(flops=int(micros * 1.1e9), bytes_accessed=1 << 10, transcendentals=0),
    )(*args)


def start(copy):
    copy.start()
    return copy


def start_all(pairs, sems):
    return [start(pltpu.make_async_copy(source, target, sems.at[i])) for i, (source, target) in enumerate(pairs)]


def wait_all(started):
    for copy in started:
        copy.wait()


def hand_on(*refs):
    pass


def pack_kernel(first, x_hbm, xt_hbm, early, late, message, x, xt, in_sems, out_sems):
    states, lines, _ = x.shape
    bands = in_sems.shape[0]
    share = lines // bands
    count = share - first
    loads, sends = [], []
    for c in range(bands):
        where = (slice(None), pl.ds(c * share, share), slice(None))
        loads.append(start(pltpu.make_async_copy(x_hbm.at[where], x.at[where], in_sems.at[c])))

    def send(line, number, target, at):
        copy = pltpu.make_async_copy(
            xt.at[pl.ds(line, number)], target.at[pl.ds(at, number)], out_sems.at[len(sends)]
        )
        sends.append(start(copy))

    for c in range(bands):
        loads[c].wait()
        for y0 in range(c * share, (c + 1) * share, ROWS):
            for s0 in range(0, states, ROWS):
                block = x[s0 : s0 + ROWS, y0 : y0 + ROWS, :].astype(F32)
                turned = jnp.swapaxes(block, 0, 1).astype(BF16)
                xt[y0 : y0 + ROWS, s0 : s0 + ROWS, :] = turned
        send(c * share + first, count, message, c * (count + 1))
        send(c * share, 1, message, (c + bands - 1) % bands * (count + 1) + count)
        if (c + 1) * share == early.shape[0]:
            send(0, early.shape[0], early, 0)
    send(early.shape[0], late.shape[0], late, 0)
    send(0, lines, xt_hbm, 0)
    for copy in sends:
        copy.wait()


def bases(groups):
    domain = lax.axis_index("domain")
    odd, upper = domain & 1, (domain >> 1) & 1
    return [2 * groups * side for side in (1 - odd, odd, 1 - upper, upper)]


def slot_reader(atom_ref, line_ref, count_ref, atoms_here):
    first = (lax.axis_index("domain") - 1) * atoms_here
    live = count_ref[0]

    def slot_at(t):
        return line_ref[t], jnp.clip(atom_ref[t] - first, 0, 3 * atoms_here - 1), t < live

    return slot_at


def project_kernel(atom_ref, line_ref, count_ref, xt_hbm, p_hbm, handed, mine_hbm, same, core_ref, link_ref, *refs):
    far_refs, (total, mine_ref, xt_ref, p_ref, sems, mine_sem) = refs[:-6], refs[-6:]
    slots, proj_count, _ = p_ref.shape
    groups, states = mine_ref.shape[0] // 3, mine_ref.shape[1]
    per_group = LANES // proj_count
    chunks = sems.shape[0] - 1
    size = slots // chunks
    unroll = 16
    pairs = [(p_hbm.at[pl.ds(c * size, size)], p_ref.at[pl.ds(c * size, size)]) for c in range(chunks)]
    xt_load, *loads = start_all([(xt_hbm, xt_ref), *pairs], sems)

    def clear(i, carry):
        for u in range(per_group):
            total[i * per_group + u] = jnp.zeros_like(total[0])
        return carry

    lax.fori_loop(0, 3 * groups, clear, 0)

    slot_at = slot_reader(atom_ref, line_ref, count_ref, groups * per_group)

    def body(i, carry):
        for u in range(unroll):
            t = i * unroll + u
            line, atom, live = slot_at(t)
            part = lax.dot_general(p_ref[t], xt_ref[line], NT, preferred_element_type=F32)
            total[jnp.where(live, atom, 3 * groups * per_group)] += part
        return carry

    xt_load.wait()
    for c in range(chunks):
        loads[c].wait()
        lax.fori_loop(c * size // unroll, (c + 1) * size // unroll, body, 0)

    for g in range(3 * groups):
        tiles = [total[g * per_group + u] for u in range(per_group)]
        mine_ref[g] = jnp.concatenate(tiles, axis=0).T
    send = start(pltpu.make_async_copy(mine_ref, mine_hbm, mine_sem))
    sides = bases(groups)
    for g in range(groups):
        own = mine_ref[groups + g].astype(BF16)
        for side, ref in zip(sides[:2], (core_ref, link_ref)):
            ref[g] = mine_ref[side + g].astype(BF16)
            ref[groups + g] = own
        for side, ref in zip(sides[2:], far_refs):
            ref[g] = mine_ref[side + g].astype(BF16)
    send.wait()


def nonlocal_kernel(
    first, fars, atom_ref, line_ref, count_ref, xt_hbm, p_hbm, energy_ref, mine_hbm, core_ref, link_ref, *refs
):
    far_refs, (_, _, out_hbm, whole_hbm, done_ref, *messages, lines_sum, whole_ref, total, atoms, xt_ref, p_ref, sems) = (
        refs[:fars],
        refs[fars:],
    )
    slots, proj_count, _ = p_ref.shape
    groups, states = total.shape[0] // 3, total.shape[1]
    per_group = LANES // proj_count
    lines = xt_ref.shape[0]
    unroll = 16
    mine_load, *loads = start_all([(mine_hbm, total), (xt_hbm, xt_ref), (p_hbm, p_ref)], sems)
    done_ref[...] = jnp.zeros_like(done_ref)

    def clear(i, carry):
        lines_sum[i] = jnp.zeros((states, LANES), F32)
        return carry

    lax.fori_loop(0, lines + 1, clear, 0)
    mine_load.wait()
    sides = bases(groups)
    for g in range(groups):
        total[groups + g] += core_ref[g].astype(F32) + link_ref[g].astype(F32)
        for side, ref in zip(sides[:2], (core_ref, link_ref)):
            total[side + g] += ref[groups + g].astype(F32)
        for side, ref in zip(sides[2:], far_refs):
            total[side + g] += ref[g].astype(F32)
    last = energy_ref.shape[0] - 1
    for g in range(3 * groups):
        row = jnp.clip((lax.axis_index("domain") - 1) * groups + g, 0, last)
        tile = (total[g] * energy_ref[pl.ds(row, 1), :]).astype(BF16)
        for u in range(per_group):
            atoms[g * per_group + u] = tile[:, u * proj_count : (u + 1) * proj_count]
    for g in range(groups):
        whole_ref[g] = total[groups + g].astype(BF16)
    send_whole = start(pltpu.make_async_copy(whole_ref, whole_hbm, sems.at[3]))
    wait_all(loads)
    share = xt_ref.shape[0] // (len(messages) + 1)
    held = groups // (len(messages) + 1)
    for k, message in enumerate(messages, 1):
        to = lax.axis_index("band") ^ k
        for i in range(first):
            message[i] = xt_ref[to * share + i]
        for i in range(held):
            message[first + i] = whole_ref[to * held + i]

    slot_at = slot_reader(atom_ref, line_ref, count_ref, groups * per_group)

    def body(i, carry):
        for u in range(unroll):
            t = i * unroll + u
            line, atom, live = slot_at(t)
            part = jnp.dot(atoms[atom], p_ref[t], preferred_element_type=F32)
            lines_sum[jnp.where(live, line, lines)] += part
        return carry

    lax.fori_loop(0, slots // unroll, body, 0)
    send = start(pltpu.make_async_copy(lines_sum.at[pl.ds(0, lines)], out_hbm, sems.at[4]))
    send_whole.wait()
    send.wait()


def stencil_kernel(
    early_steps, xt_ref, last_ref, next_ref, core_ref, early_link, late_link, added_ref, pot_ref, ring_ref,
    unread, out_ref, done_ref,
):
    states, here, _ = out_ref.shape
    done_ref[...] = jnp.zeros_like(done_ref)
    early = pl.program_id(0) < early_steps

    def line(i, rows):
        ref, at = (last_ref, 0) if i < 0 else (next_ref, 0) if i == here else (xt_ref, i)
        return ref[at, rows, :]

    for y0 in range(0, here, ROWS):
        for s0 in range(0, states, ROWS):
            rows = slice(s0, s0 + ROWS)
            results = []
            cells = jnp.concatenate([line(y0 + i, rows) for i in range(ROWS)], axis=0)
            along = jnp.dot(cells, ring_ref[...], preferred_element_type=F32)
            before, x = line(y0 - 1, rows).astype(F32), line(y0, rows).astype(F32)
            for i in range(ROWS):
                y = y0 + i
                after = line(y + 1, rows).astype(F32)
                core = core_ref[y, rows, :].astype(F32)
                link = jnp.where(early, early_link[y, rows, :], late_link[y, rows, :]).astype(F32)
                value = along[i * ROWS : (i + 1) * ROWS] + pot_ref[y : y + 1, :] * x + added_ref[y, rows, :]
                results.append(value - 0.5 * ((before + after) + (core + link)))
                before, x = x, after
            turned = jnp.swapaxes(jnp.stack(results, axis=0), 0, 1).astype(BF16)
            out_ref[rows, y0 : y0 + ROWS, :] = turned


def pass_half(all_ref, pass_hbm, sem):
    half = pass_hbm.shape[0]
    copy = start(pltpu.make_async_copy(all_ref.at[pl.ds((1 - (lax.axis_index("domain") & 1)) * half, half)], pass_hbm, sem))
    copy.wait()


def later_kernel(bands, landed, unread, all_ref, pass_hbm, done_ref, sems, pass_sem):
    done_ref[...] = jnp.zeros_like(done_ref)
    count, states = all_ref.shape[0], landed.shape[1]
    loads = [
        start(
            pltpu.make_async_copy(
                landed.at[pl.ds(b * count, count)], all_ref.at[:, pl.ds(b * states, states), :], sems.at[b]
            )
        )
        for b in range(bands)
    ]
    for copy in loads:
        copy.wait()
    pass_half(all_ref, pass_hbm, pass_sem)


def early_kernel(bands, share, xt_hbm, whole_ref, after_ref, unread, *refs):
    pieces, (all_ref, pass_hbm, projs_ref, done_ref, sems, pass_sem) = refs[: bands - 1], refs[bands - 1 :]
    done_ref[...] = jnp.zeros_like(done_ref)
    states = xt_hbm.shape[1]
    band = lax.axis_index("band")
    count, held = all_ref.shape[0] - 1, projs_ref.shape[0]
    loads = []

    def load(source, target):
        loads.append(start(pltpu.make_async_copy(source, target, sems.at[len(loads)])))

    for k in range(bands):
        at = pl.ds(pl.multiple_of((band ^ k) * states, states), states)
        if k == 0:
            load(xt_hbm.at[pl.ds(band * share, count)], all_ref.at[pl.ds(0, count), at, :])
            load(whole_ref.at[pl.ds(band * held, held)], projs_ref.at[:, at, :])
        else:
            load(pieces[k - 1].at[pl.ds(0, count)], all_ref.at[pl.ds(0, count), at, :])
            load(pieces[k - 1].at[pl.ds(count, held)], projs_ref.at[:, at, :])
    load(after_ref.at[pl.ds(0, 1)], all_ref.at[pl.ds(count, 1)])
    for copy in loads:
        copy.wait()
    pass_half(all_ref, pass_hbm, pass_sem)


def add_products(row, all_ref, core_ref, link_ref, pot_ref, acc):
    half = core_ref.shape[0]
    group = 4
    mine = (lax.axis_index("domain") & 1) * half
    for part, base in ((0, mine), (1, half - mine)):
        for i0 in range(0, half, group):
            xs, ys = [], []
            for i in range(i0, min(i0 + group, half)):
                cell = all_ref[base + i]
                x = cell.astype(F32)
                y = (3.0 + pot_ref[pl.ds(row + base + i, 1), :]) * x - pltpu.roll(x, x.shape[1] - 1, 1)
                y = y - all_ref[base + i + 1].astype(F32)
                if part == 0:
                    y = y - core_ref[i].astype(F32) - link_ref[i].astype(F32)
                xs.append(cell)
                ys.append(y.astype(BF16))
            flat_x = jnp.concatenate(xs, axis=1)
            flat_y = jnp.concatenate(ys, axis=1)
            acc[0] += lax.dot_general(flat_x, flat_x, NT, preferred_element_type=F32)
            acc[1] += lax.dot_general(flat_y, flat_x, NT, preferred_element_type=F32)


def gram_kernel(first, share, all_ref, core_ref, link_ref, pot_ref, unread, acc):
    acc[...] = jnp.zeros_like(acc)
    add_products(lax.axis_index("band") * share + first, all_ref, core_ref, link_ref, pot_ref, acc)


def final_kernel(
    bands, share, all_ref, core_ref, link_ref, pot_ref, begun_ref, proj_ref, energy_ref, out_ref, acc
):
    acc[...] = begun_ref[...]
    add_products(lax.axis_index("band") * share, all_ref, core_ref, link_ref, pot_ref, acc)
    groups = proj_ref.shape[0]
    first = (lax.axis_index("domain") * bands + lax.axis_index("band")) * groups
    for g in range(groups):
        here = proj_ref[g]
        scaled = (here.astype(F32) * energy_ref[pl.ds(first + g, 1), :]).astype(BF16)
        acc[1] += lax.dot_general(scaled, here, NT, preferred_element_type=F32)
    hamil = 0.5 * (acc[1] + acc[1].T)
    domains = out_ref.shape[0] // bands
    rows, cols = out_ref.shape[1], out_ref.shape[2] // 2
    for c in range(domains):
        for r in range(bands):
            r0, c0 = r * rows, c * cols
            out_ref[c * bands + r, :, :cols] = acc[0, r0 : r0 + rows, c0 : c0 + cols].astype(BF16)
            out_ref[c * bands + r, :, cols:] = hamil[r0 : r0 + rows, c0 : c0 + cols].astype(BF16)


def result_kernel(scale, parts_ref, out_ref):
    total = jnp.sum(parts_ref[...].astype(F32), axis=0) * scale
    cols = out_ref.shape[2]
    out_ref[0] = total[:, :cols]
    out_ref[1] = total[:, cols:]


def local(orbitals, potential, projectors, tile_atom, tile_line, tile_count, energies):
    states, _, lines, cols_z = orbitals.shape
    slots, proj_count, _ = projectors.shape
    atom_total = energies.shape[0]
    domains, bands = lax.axis_size("domain"), lax.axis_size("band")
    total_states = states * bands
    atoms_here = atom_total // domains
    per_group = LANES // proj_count
    groups = atoms_here // per_group
    group_share = groups // bands
    share = lines // bands
    first = share // 4
    rest = share - first

    core_pairs = [(i, i ^ 1) for i in range(domains) if i ^ 1 < domains]
    link_pairs = [(i, ((i + 1) ^ 1) - 1) for i in range(1, domains) if ((i + 1) ^ 1) - 1 < domains]
    near_far = [(i, i ^ 2) for i in range(domains) if i ^ 2 < domains]
    next_far = [(i, ((i + 2) ^ 2) - 2) for i in range(2, domains) if ((i + 2) ^ 2) - 2 < domains]
    far_pairs = [pairs for pairs in (near_far, next_far) if pairs]

    def swapped(values, axis):
        size = lax.axis_size(axis)
        got = {k: lax.ppermute(values[k - 1], axis, [(i, i ^ k) for i in range(size)]) for k in range(size - 1, 0, -1)}
        return [got[k] for k in range(1, size)]

    field = orbitals.reshape(states, lines, cols_z)
    pot = potential.reshape(lines, cols_z)
    energy = energies.reshape(atom_total // per_group, LANES)
    eye = np.eye(cols_z, dtype=np.float32)
    ring = jnp.asarray(3.0 * eye - 0.5 * (np.roll(eye, 1, axis=0) + np.roll(eye, -1, axis=0)), dtype=BF16)

    late_lines = lines // 2
    line_shape, late_shape = (lines, states, cols_z), (late_lines, states, cols_z)
    xt, early_part, late_part, message = call(
        63,
        functools.partial(pack_kernel, first),
        (),
        [FAR],
        [FAR] * 4,
        [
            (line_shape, BF16),
            ((lines - late_lines, states, cols_z), BF16),
            (late_shape, BF16),
            ((bands * (rest + 1), states, cols_z), BF16),
        ],
        [
            pltpu.VMEM((states, lines, cols_z), BF16),
            pltpu.VMEM(line_shape, BF16),
            copies((bands,)),
            copies((2 * bands + 3,)),
        ],
        (field,),
    )
    landed = lax.all_to_all(message, "band", split_axis=0, concat_axis=0, tiled=True)
    xt, early_part = call(
        63,
        hand_on,
        (),
        [UNREAD] * 2,
        [UNREAD] * 2,
        [(line_shape, BF16), (early_part.shape, BF16)],
        [],
        (xt, early_part),
        aliases={0: 0, 1: 1},
    )
    link_early = lax.ppermute(early_part, "domain", link_pairs)
    core_field = lax.ppermute(xt, "domain", core_pairs)

    group_shape = (groups, states, LANES)
    mine, late_part, to_core, to_link, *to_far = call(
        63,
        project_kernel,
        (),
        [SCALARS] * 3 + [FAR, PINNED, UNREAD],
        [PINNED, UNREAD] + [WHOLE] * (2 + len(far_pairs)),
        [((3 * groups, states, LANES), F32), (late_shape, BF16)]
        + [((2 * groups, states, LANES), BF16)] * 2
        + [(group_shape, BF16)] * len(far_pairs),
        [
            pltpu.VMEM((3 * atoms_here + 1, proj_count, states), F32),
            pltpu.VMEM((3 * groups, states, LANES), F32),
            pltpu.VMEM(line_shape, BF16),
            pltpu.VMEM(projectors.shape, BF16),
            copies((5,)),
            copies,
        ],
        (tile_atom, tile_line, tile_count, xt, projectors, late_part),
        aliases={5: 1},
        micros=10,
    )
    from_link = lax.ppermute(to_link, "domain", link_pairs)
    from_far = [lax.ppermute(value, "domain", pairs) for value, pairs in zip(to_far, far_pairs)]
    from_core = lax.ppermute(to_core, "domain", core_pairs)
    link_late = lax.ppermute(late_part, "domain", link_pairs)
    added, whole, summed_up, *messages = call(
        62,
        functools.partial(nonlocal_kernel, first, len(far_pairs)),
        (),
        [SCALARS] * 3 + [FAR, PINNED, WHOLE, PINNED, WHOLE, WHOLE] + [WHOLE] * len(far_pairs) + [UNREAD] * 2,
        [PINNED, PINNED, WHOLE] + [WHOLE] * (bands - 1),
        [(line_shape, F32), (group_shape, BF16), ((8, LANES), F32)]
        + [((first + group_share, states, cols_z), BF16)] * (bands - 1),
        [
            pltpu.VMEM((lines + 1, states, cols_z), F32),
            pltpu.VMEM(group_shape, BF16),
            pltpu.VMEM((3 * groups, states, LANES), F32),
            pltpu.VMEM((3 * atoms_here, states, proj_count), BF16),
            pltpu.VMEM(line_shape, BF16),
            pltpu.VMEM(projectors.shape, BF16),
            copies((5,)),
        ],
        (
            tile_atom, tile_line, tile_count, xt, projectors, energy, mine, from_core, from_link, *from_far,
            link_early[0, :ROWS], core_field[0, :ROWS],
        ),
        micros=30,
    )
    early = swapped(messages, "band")

    later_all, later_pass, later_token = call(
        32,
        functools.partial(later_kernel, bands),
        (),
        [FAR, UNREAD],
        [NEAR, FAR, WHOLE],
        [((rest + 1, total_states, cols_z), BF16), ((rest // 2, total_states, cols_z), BF16), ((8, LANES), F32)],
        [copies((bands,)), copies],
        (landed, summed_up),
    )
    later_link = lax.ppermute(later_pass, "domain", link_pairs)
    later_core = lax.ppermute(later_pass, "domain", core_pairs)

    span = 2 * ROWS
    steps, early_steps = lines // span, (lines - late_lines) // span
    block = pl.BlockSpec((span, states, cols_z), lambda i: (i, 0, 0))
    early_block = pl.BlockSpec((span, states, cols_z), lambda i: (jnp.minimum(i, early_steps - 1), 0, 0))
    late_block = pl.BlockSpec((span, states, cols_z), lambda i: (jnp.maximum(i - early_steps, 0), 0, 0))
    added_far = pltpu.with_memory_space_constraint(added, pltpu.HBM)
    applied, done = call(
        61,
        functools.partial(stencil_kernel, early_steps),
        (steps,),
        [
            block,
            pl.BlockSpec((1, states, cols_z), lambda i: (lax.rem(i * span + lines - 1, lines), 0, 0)),
            pl.BlockSpec((1, states, cols_z), lambda i: (lax.rem(i * span + span, lines), 0, 0)),
            block,
            early_block,
            late_block,
            block,
            pl.BlockSpec((span, cols_z), lambda i: (i, 0)),
            WHOLE,
            UNREAD,
        ],
        [pl.BlockSpec((states, span, cols_z), lambda i: (0, i, 0)), WHOLE],
        [((states, lines, cols_z), BF16), ((8, LANES), F32)],
        [],
        (
            xt, xt, xt, core_field, link_early, link_late, added_far, pot, ring, later_token,
        ),
    )

    early_all, early_pass, projs, early_token = call(
        60,
        functools.partial(early_kernel, bands, share),
        (),
        [FAR, PINNED, NEAR, WHOLE] + [FAR] * (bands - 1),
        [NEAR, FAR, NEAR, WHOLE],
        [
            ((first + 1, total_states, cols_z), BF16),
            ((first // 2, total_states, cols_z), BF16),
            ((group_share, total_states, LANES), BF16),
            ((8, LANES), F32),
        ],
        [copies((2 * bands + 1,)), copies],
        (xt, whole, later_all, done, *early),
        micros=30,
    )
    early_link = lax.ppermute(early_pass, "domain", link_pairs)
    early_core = lax.ppermute(early_pass, "domain", core_pairs)
    (begun,) = call(
        32,
        functools.partial(gram_kernel, first, share),
        (),
        [NEAR, WHOLE, WHOLE, WHOLE, UNREAD],
        [NEAR],
        [((2, total_states, total_states), F32)],
        [],
        (later_all, later_core, later_link, pot, early_token),
    )
    parts = domains * bands
    (blocks,) = call(
        32,
        functools.partial(final_kernel, bands, share),
        (),
        [NEAR, WHOLE, WHOLE, WHOLE, NEAR, NEAR, WHOLE],
        [WHOLE],
        [((parts, states, 2 * total_states // domains), BF16)],
        [pltpu.VMEM((2, total_states, total_states), F32)],
        (early_all, early_core, early_link, pot, begun, projs, energy),
    )
    summed = lax.all_to_all(blocks, ("domain", "band"), split_axis=0, concat_axis=0, tiled=True)
    (subspace,) = call(
        32,
        functools.partial(result_kernel, 1.0 / (lines * cols_z * domains)),
        (),
        [WHOLE],
        [WHOLE],
        [((2, states, total_states // domains), F32)],
        [],
        (summed,),
    )
    return applied.reshape(orbitals.shape), subspace


def solution(mesh):
    in_specs = (
        P("band", ("groups", "domain"), None, None),
        P(("groups", "domain"), None, None),
        P(("groups", "domain"), None, None),
        P(("groups", "domain")),
        P(("groups", "domain")),
        P(("groups", "domain")),
        P("groups", None),
    )
    out_specs = (P("band", ("groups", "domain"), None, None), P(None, ("groups", "band"), "domain"))
    return jax.shard_map(local, mesh=mesh, in_specs=in_specs, out_specs=out_specs, check_vma=False)
```

```python
import functools

import jax
import jax.numpy as jnp
import numpy as np
from jax import lax
from jax.experimental import pallas as pl
from jax.experimental.pallas import tpu as pltpu
from jax.sharding import PartitionSpec as P

F32 = jnp.float32
BF16 = jnp.bfloat16
LANES = 128
ROWS = 16
NT = (((1,), (1,)), ((), ()))
WHOLE = pl.BlockSpec(memory_space=pltpu.VMEM)
NEAR = pl.BlockSpec(memory_space=pltpu.VMEM)
SCALARS = pl.BlockSpec(memory_space=pltpu.SMEM)
FAR = pl.BlockSpec(memory_space=pltpu.HBM)
PINNED = pl.BlockSpec(memory_space=pltpu.HBM)
UNREAD = pl.BlockSpec(memory_space=pl.ANY)
copies = pltpu.SemaphoreType.DMA


def call(room, kernel, grid, in_specs, out_specs, outs, scratch, args, aliases=None, micros=0.001):
    def place(spec):
        return {id(NEAR): pltpu.VMEM, id(PINNED): pltpu.HBM}.get(id(spec))

    args = [
        pltpu.with_memory_space_constraint(arg, place(spec)) if place(spec) else arg
        for spec, arg in zip(in_specs, args)
    ]
    shapes = [(place(spec) or jax.ShapeDtypeStruct)(shape, kind) for spec, (shape, kind) in zip(out_specs, outs)]
    return pl.pallas_call(
        kernel,
        grid=grid,
        out_shape=shapes,
        in_specs=in_specs,
        out_specs=out_specs,
        scratch_shapes=scratch,
        input_output_aliases=aliases or {},
        compiler_params=pltpu.CompilerParams(vmem_limit_bytes=room << 20),
        cost_estimate=pl.CostEstimate(flops=int(micros * 1.1e9), bytes_accessed=1 << 10, transcendentals=0),
    )(*args)


def start(copy):
    copy.start()
    return copy


def pack_kernel(first, x_hbm, xt, xt_hbm, early, late, message, x, in_sems, out_sems):
    states, lines, _ = x.shape
    bands = in_sems.shape[0]
    share = lines // bands
    count = share - first
    loads, sends = [], []
    for c in range(bands):
        where = (slice(None), pl.ds(c * share, share), slice(None))
        loads.append(start(pltpu.make_async_copy(x_hbm.at[where], x.at[where], in_sems.at[c])))

    def send(line, number, target, at):
        copy = pltpu.make_async_copy(
            xt.at[pl.ds(line, number)], target.at[pl.ds(at, number)], out_sems.at[len(sends)]
        )
        sends.append(start(copy))

    for c in range(bands):
        loads[c].wait()
        for y0 in range(c * share, (c + 1) * share, ROWS):
            for s0 in range(0, states, ROWS):
                block = x[s0 : s0 + ROWS, y0 : y0 + ROWS, :].astype(F32)
                turned = jnp.swapaxes(block, 0, 1).astype(BF16)
                xt[y0 : y0 + ROWS, s0 : s0 + ROWS, :] = turned
        send(c * share + first, count, message, c * (count + 1))
        send(c * share, 1, message, (c + bands - 1) % bands * (count + 1) + count)
        if (c + 1) * share == early.shape[0]:
            send(0, early.shape[0], early, 0)
    send(early.shape[0], late.shape[0], late, 0)
    send(0, lines, xt_hbm, 0)
    for copy in sends:
        copy.wait()


def bases(groups):
    domain = lax.axis_index("domain")
    odd, upper = domain & 1, (domain >> 1) & 1
    return [2 * groups * side for side in (1 - odd, odd, 1 - upper, upper)]


def slot_reader(atom_ref, line_ref, count_ref, atoms_here):
    first = (lax.axis_index("domain") - 1) * atoms_here
    live = count_ref[0]

    def slot_at(t):
        return line_ref[t], jnp.clip(atom_ref[t] - first, 0, 3 * atoms_here - 1), t < live

    return slot_at


def project_kernel(atom_ref, line_ref, count_ref, xt_ref, p_hbm, handed, mine_ref, same, core_ref, link_ref, *refs):
    far_refs, (total, p_ref, sems) = refs[:-3], refs[-3:]
    slots, proj_count, _ = p_ref.shape
    groups, states = mine_ref.shape[0] // 3, mine_ref.shape[1]
    per_group = LANES // proj_count
    chunks = sems.shape[0]
    size = slots // chunks
    unroll = 16
    loads = []
    for c in range(chunks):
        where = pl.ds(c * size, size)
        loads.append(start(pltpu.make_async_copy(p_hbm.at[where], p_ref.at[where], sems.at[c])))

    def clear(i, carry):
        for u in range(per_group):
            total[i * per_group + u] = jnp.zeros_like(total[0])
        return carry

    lax.fori_loop(0, 3 * groups, clear, 0)

    slot_at = slot_reader(atom_ref, line_ref, count_ref, groups * per_group)

    def body(i, carry):
        for u in range(unroll):
            t = i * unroll + u
            line, atom, live = slot_at(t)
            part = lax.dot_general(p_ref[t], xt_ref[line], NT, preferred_element_type=F32)
            total[jnp.where(live, atom, 3 * groups * per_group)] += part
        return carry

    for c in range(chunks):
        loads[c].wait()
        lax.fori_loop(c * size // unroll, (c + 1) * size // unroll, body, 0)

    for g in range(3 * groups):
        tiles = [total[g * per_group + u] for u in range(per_group)]
        mine_ref[g] = jnp.concatenate(tiles, axis=0).T
    sides = bases(groups)
    for g in range(groups):
        own = mine_ref[groups + g].astype(BF16)
        for side, ref in zip(sides[:2], (core_ref, link_ref)):
            ref[g] = mine_ref[side + g].astype(BF16)
            ref[groups + g] = own
        for side, ref in zip(sides[2:], far_refs):
            ref[g] = mine_ref[side + g].astype(BF16)


def nonlocal_kernel(
    first, fars, atom_ref, line_ref, count_ref, xt_hbm, p_hbm, energy_ref, mine_ref, core_ref, link_ref, *refs
):
    far_refs, (_, _, out_hbm, whole_hbm, done_ref, *messages, lines_sum, whole_ref, total, atoms, p_ref, sems) = (
        refs[:fars],
        refs[fars:],
    )
    slots, proj_count, _ = p_ref.shape
    groups, states = mine_ref.shape[0] // 3, mine_ref.shape[1]
    per_group = LANES // proj_count
    lines = xt_hbm.shape[0]
    unroll = 16
    load = start(pltpu.make_async_copy(p_hbm, p_ref, sems.at[0]))
    done_ref[...] = jnp.zeros_like(done_ref)

    def clear(i, carry):
        lines_sum[i] = jnp.zeros((states, LANES), F32)
        return carry

    lax.fori_loop(0, lines + 1, clear, 0)
    total[...] = mine_ref[...]
    sides = bases(groups)
    for g in range(groups):
        total[groups + g] += core_ref[g].astype(F32) + link_ref[g].astype(F32)
        for side, ref in zip(sides[:2], (core_ref, link_ref)):
            total[side + g] += ref[groups + g].astype(F32)
        for side, ref in zip(sides[2:], far_refs):
            total[side + g] += ref[g].astype(F32)
    last = energy_ref.shape[0] - 1
    for g in range(3 * groups):
        row = jnp.clip((lax.axis_index("domain") - 1) * groups + g, 0, last)
        tile = (total[g] * energy_ref[pl.ds(row, 1), :]).astype(BF16)
        for u in range(per_group):
            atoms[g * per_group + u] = tile[:, u * proj_count : (u + 1) * proj_count]
    for g in range(groups):
        whole_ref[g] = total[groups + g].astype(BF16)
    send_whole = start(pltpu.make_async_copy(whole_ref, whole_hbm, sems.at[1]))
    share = lines // (len(messages) + 1)
    held = groups // (len(messages) + 1)
    brought = []
    for k, message in enumerate(messages, 1):
        to = lax.axis_index("band") ^ k
        target = message.at[pl.ds(0, first)]
        brought.append(start(pltpu.make_async_copy(xt_hbm.at[pl.ds(to * share, first)], target, sems.at[2 + k])))
        for i in range(held):
            message[first + i] = whole_ref[to * held + i]
    load.wait()

    slot_at = slot_reader(atom_ref, line_ref, count_ref, groups * per_group)

    def body(i, carry):
        for u in range(unroll):
            t = i * unroll + u
            line, atom, live = slot_at(t)
            part = jnp.dot(atoms[atom], p_ref[t], preferred_element_type=F32)
            lines_sum[jnp.where(live, line, lines)] += part
        return carry

    lax.fori_loop(0, slots // unroll, body, 0)
    send = start(pltpu.make_async_copy(lines_sum.at[pl.ds(0, lines)], out_hbm, sems.at[2]))
    for copy in (send_whole, send, *brought):
        copy.wait()


def stencil_kernel(
    early_steps, xt_ref, last_ref, next_ref, core_ref, early_ref, late_ref, added_ref, pot_ref, ring_ref, unread,
    out_ref, done_ref,
):
    states, here, _ = out_ref.shape
    done_ref[...] = jnp.zeros_like(done_ref)
    early = pl.program_id(0) < early_steps

    def line(i, rows):
        ref, at = (last_ref, 0) if i < 0 else (next_ref, 0) if i == here else (xt_ref, i)
        return ref[at, rows, :]

    for y0 in range(0, here, ROWS):
        for s0 in range(0, states, ROWS):
            rows = slice(s0, s0 + ROWS)
            results = []
            cells = jnp.concatenate([line(y0 + i, rows) for i in range(ROWS)], axis=0)
            along = jnp.dot(cells, ring_ref[...], preferred_element_type=F32)
            before, x = line(y0 - 1, rows).astype(F32), line(y0, rows).astype(F32)
            for i in range(ROWS):
                y = y0 + i
                after = line(y + 1, rows).astype(F32)
                link = jnp.where(early, early_ref[y, rows, :], late_ref[y, rows, :]).astype(F32)
                beside = (before + after) + (core_ref[y, rows, :].astype(F32) + link)
                value = along[i * ROWS : (i + 1) * ROWS] + pot_ref[y : y + 1, :] * x
                results.append(value + added_ref[y, rows, :] - 0.5 * beside)
                before, x = x, after
            turned = jnp.swapaxes(jnp.stack(results, axis=0), 0, 1).astype(BF16)
            out_ref[rows, y0 : y0 + ROWS, :] = turned


def pass_half(all_ref, pass_hbm, sem):
    half = pass_hbm.shape[0]
    copy = start(pltpu.make_async_copy(all_ref.at[pl.ds((1 - (lax.axis_index("domain") & 1)) * half, half)], pass_hbm, sem))
    copy.wait()


def later_kernel(bands, landed, unread, all_ref, pass_hbm, done_ref, sems, pass_sem):
    done_ref[...] = jnp.zeros_like(done_ref)
    count, states = all_ref.shape[0], landed.shape[1]
    loads = [
        start(
            pltpu.make_async_copy(
                landed.at[pl.ds(b * count, count)], all_ref.at[:, pl.ds(b * states, states), :], sems.at[b]
            )
        )
        for b in range(bands)
    ]
    for copy in loads:
        copy.wait()
    pass_half(all_ref, pass_hbm, pass_sem)


def early_kernel(bands, share, xt_hbm, whole_ref, after_ref, unread, *refs):
    pieces, (all_ref, pass_hbm, projs_ref, done_ref, sems, pass_sem) = refs[: bands - 1], refs[bands - 1 :]
    done_ref[...] = jnp.zeros_like(done_ref)
    states = xt_hbm.shape[1]
    band = lax.axis_index("band")
    count, held = all_ref.shape[0] - 1, projs_ref.shape[0]
    loads = []

    def load(source, target):
        loads.append(start(pltpu.make_async_copy(source, target, sems.at[len(loads)])))

    for k in range(bands):
        at = pl.ds(pl.multiple_of((band ^ k) * states, states), states)
        if k == 0:
            load(xt_hbm.at[pl.ds(band * share, count)], all_ref.at[pl.ds(0, count), at, :])
            load(whole_ref.at[pl.ds(band * held, held)], projs_ref.at[:, at, :])
        else:
            load(pieces[k - 1].at[pl.ds(0, count)], all_ref.at[pl.ds(0, count), at, :])
            load(pieces[k - 1].at[pl.ds(count, held)], projs_ref.at[:, at, :])
    load(after_ref.at[pl.ds(0, 1)], all_ref.at[pl.ds(count, 1)])
    for copy in loads:
        copy.wait()
    pass_half(all_ref, pass_hbm, pass_sem)


def add_products(row, all_ref, core_ref, link_ref, pot_ref, acc):
    half = core_ref.shape[0]
    group = 4
    mine = (lax.axis_index("domain") & 1) * half
    for part, base in ((0, mine), (1, half - mine)):
        for i0 in range(0, half, group):
            xs, ys = [], []
            for i in range(i0, min(i0 + group, half)):
                cell = all_ref[base + i]
                x = cell.astype(F32)
                y = (3.0 + pot_ref[pl.ds(row + base + i, 1), :]) * x - pltpu.roll(x, x.shape[1] - 1, 1)
                y = y - all_ref[base + i + 1].astype(F32)
                if part == 0:
                    y = y - core_ref[i].astype(F32) - link_ref[i].astype(F32)
                xs.append(cell)
                ys.append(y.astype(BF16))
            flat_x = jnp.concatenate(xs, axis=1)
            flat_y = jnp.concatenate(ys, axis=1)
            acc[0] += lax.dot_general(flat_x, flat_x, NT, preferred_element_type=F32)
            acc[1] += lax.dot_general(flat_y, flat_x, NT, preferred_element_type=F32)


def gram_kernel(first, share, all_ref, core_ref, link_ref, pot_ref, unread, acc):
    acc[...] = jnp.zeros_like(acc)
    add_products(lax.axis_index("band") * share + first, all_ref, core_ref, link_ref, pot_ref, acc)


def final_kernel(
    bands, share, all_ref, core_ref, link_ref, pot_ref, begun_ref, proj_ref, energy_ref, out_ref, acc
):
    acc[...] = begun_ref[...]
    add_products(lax.axis_index("band") * share, all_ref, core_ref, link_ref, pot_ref, acc)
    groups = proj_ref.shape[0]
    first = (lax.axis_index("domain") * bands + lax.axis_index("band")) * groups
    for g in range(groups):
        here = proj_ref[g]
        scaled = (here.astype(F32) * energy_ref[pl.ds(first + g, 1), :]).astype(BF16)
        acc[1] += lax.dot_general(scaled, here, NT, preferred_element_type=F32)
    hamil = 0.5 * (acc[1] + acc[1].T)
    domains = out_ref.shape[0] // bands
    rows, cols = out_ref.shape[1], out_ref.shape[2] // 2
    for c in range(domains):
        for r in range(bands):
            r0, c0 = r * rows, c * cols
            out_ref[c * bands + r, :, :cols] = acc[0, r0 : r0 + rows, c0 : c0 + cols].astype(BF16)
            out_ref[c * bands + r, :, cols:] = hamil[r0 : r0 + rows, c0 : c0 + cols].astype(BF16)


def result_kernel(scale, parts_ref, out_ref):
    total = jnp.sum(parts_ref[...].astype(F32), axis=0) * scale
    cols = out_ref.shape[2]
    out_ref[0] = total[:, :cols]
    out_ref[1] = total[:, cols:]


def local(orbitals, potential, projectors, tile_atom, tile_line, tile_count, energies):
    states, _, lines, cols_z = orbitals.shape
    slots, proj_count, _ = projectors.shape
    atom_total = energies.shape[0]
    domains, bands = lax.axis_size("domain"), lax.axis_size("band")
    total_states = states * bands
    atoms_here = atom_total // domains
    per_group = LANES // proj_count
    groups = atoms_here // per_group
    group_share = groups // bands
    share = lines // bands
    first = share // 4
    rest = share - first

    core_pairs = [(i, i ^ 1) for i in range(domains) if i ^ 1 < domains]
    link_pairs = [(i, ((i + 1) ^ 1) - 1) for i in range(1, domains) if ((i + 1) ^ 1) - 1 < domains]
    near_far = [(i, i ^ 2) for i in range(domains) if i ^ 2 < domains]
    next_far = [(i, ((i + 2) ^ 2) - 2) for i in range(2, domains) if ((i + 2) ^ 2) - 2 < domains]
    far_pairs = [pairs for pairs in (near_far, next_far) if pairs]

    def swapped(values, axis):
        size = lax.axis_size(axis)
        got = {k: lax.ppermute(values[k - 1], axis, [(i, i ^ k) for i in range(size)]) for k in range(size - 1, 0, -1)}
        return [got[k] for k in range(1, size)]

    field = orbitals.reshape(states, lines, cols_z)
    pot = potential.reshape(lines, cols_z)
    energy = energies.reshape(atom_total // per_group, LANES)
    eye = np.eye(cols_z, dtype=np.float32)
    ring = jnp.asarray(3.0 * eye - 0.5 * (np.roll(eye, 1, axis=0) + np.roll(eye, -1, axis=0)), dtype=BF16)

    late_lines = lines // 2
    line_shape, late_shape = (lines, states, cols_z), (late_lines, states, cols_z)
    xt, xt_far, early_part, late_part, message = call(
        58,
        functools.partial(pack_kernel, first),
        (),
        [FAR],
        [NEAR, FAR, FAR, FAR, FAR],
        [
            (line_shape, BF16),
            (line_shape, BF16),
            ((lines - late_lines, states, cols_z), BF16),
            (late_shape, BF16),
            ((bands * (rest + 1), states, cols_z), BF16),
        ],
        [pltpu.VMEM((states, lines, cols_z), BF16), copies((bands,)), copies((2 * bands + 3,))],
        (field,),
    )
    landed = lax.all_to_all(message, "band", split_axis=0, concat_axis=0, tiled=True)
    link_early = lax.ppermute(early_part, "domain", link_pairs)
    core_field = lax.ppermute(xt_far, "domain", core_pairs)

    group_shape = (groups, states, LANES)
    mine, late_part, to_core, to_link, *to_far = call(
        50,
        project_kernel,
        (),
        [SCALARS] * 3 + [NEAR, PINNED, UNREAD],
        [NEAR, UNREAD] + [WHOLE] * (2 + len(far_pairs)),
        [((3 * groups, states, LANES), F32), (late_shape, BF16)]
        + [((2 * groups, states, LANES), BF16)] * 2
        + [(group_shape, BF16)] * len(far_pairs),
        [
            pltpu.VMEM((3 * atoms_here + 1, proj_count, states), F32),
            pltpu.VMEM(projectors.shape, BF16),
            copies((4,)),
        ],
        (tile_atom, tile_line, tile_count, xt, projectors, late_part),
        aliases={5: 1},
    )
    from_link = lax.ppermute(to_link, "domain", link_pairs)
    from_far = [lax.ppermute(value, "domain", pairs) for value, pairs in zip(to_far, far_pairs)]
    from_core = lax.ppermute(to_core, "domain", core_pairs)
    link_late = lax.ppermute(late_part, "domain", link_pairs)
    added, whole, summed_up, *messages = call(
        61,
        functools.partial(nonlocal_kernel, first, len(far_pairs)),
        (),
        [SCALARS] * 3 + [FAR, PINNED, WHOLE, NEAR, WHOLE, WHOLE] + [WHOLE] * len(far_pairs) + [UNREAD] * 2,
        [PINNED, PINNED, WHOLE] + [WHOLE] * (bands - 1),
        [(line_shape, F32), (group_shape, BF16), ((8, LANES), F32)]
        + [((first + group_share, states, cols_z), BF16)] * (bands - 1),
        [
            pltpu.VMEM((lines + 1, states, cols_z), F32),
            pltpu.VMEM(group_shape, BF16),
            pltpu.VMEM((3 * groups, states, LANES), F32),
            pltpu.VMEM((3 * atoms_here, states, proj_count), BF16),
            pltpu.VMEM(projectors.shape, BF16),
            copies((2 + bands,)),
        ],
        (
            tile_atom, tile_line, tile_count, xt_far, projectors, energy, mine, from_core, from_link, *from_far,
            link_early[0, :ROWS], core_field[0, :ROWS],
        ),
    )
    early = swapped(messages, "band")

    later_all, later_pass, later_token = call(
        32,
        functools.partial(later_kernel, bands),
        (),
        [FAR, UNREAD],
        [NEAR, FAR, WHOLE],
        [((rest + 1, total_states, cols_z), BF16), ((rest // 2, total_states, cols_z), BF16), ((8, LANES), F32)],
        [copies((bands,)), copies],
        (landed, summed_up),
        micros=20,
    )
    later_link = lax.ppermute(later_pass, "domain", link_pairs)
    later_core = lax.ppermute(later_pass, "domain", core_pairs)

    span = 2 * ROWS
    steps, early_steps = lines // span, (lines - late_lines) // span
    block = pl.BlockSpec((span, states, cols_z), lambda i: (i, 0, 0))
    applied, done = call(
        32,
        functools.partial(stencil_kernel, early_steps),
        (steps,),
        [
            block,
            pl.BlockSpec((1, states, cols_z), lambda i: (lax.rem(i * span + lines - 1, lines), 0, 0)),
            pl.BlockSpec((1, states, cols_z), lambda i: (lax.rem(i * span + span, lines), 0, 0)),
            block,
            pl.BlockSpec((span, states, cols_z), lambda i: (jnp.minimum(i, early_steps - 1), 0, 0)),
            pl.BlockSpec((span, states, cols_z), lambda i: (jnp.maximum(i - early_steps, 0), 0, 0)),
            block,
            pl.BlockSpec((span, cols_z), lambda i: (i, 0)),
            WHOLE,
            UNREAD,
        ],
        [pl.BlockSpec((states, span, cols_z), lambda i: (0, i, 0)), WHOLE],
        [((states, lines, cols_z), BF16), ((8, LANES), F32)],
        [],
        (
            xt_far, xt_far, xt_far, core_field, link_early, link_late, pltpu.with_memory_space_constraint(added, pltpu.HBM), pot, ring,
            later_token,
        ),
    )

    early_all, early_pass, projs, early_token = call(
        32,
        functools.partial(early_kernel, bands, share),
        (),
        [FAR, PINNED, NEAR, WHOLE] + [FAR] * (bands - 1),
        [NEAR, FAR, NEAR, WHOLE],
        [
            ((first + 1, total_states, cols_z), BF16),
            ((first // 2, total_states, cols_z), BF16),
            ((group_share, total_states, LANES), BF16),
            ((8, LANES), F32),
        ],
        [copies((2 * bands + 1,)), copies],
        (xt_far, whole, later_all, done, *early),
        micros=30,
    )
    early_link = lax.ppermute(early_pass, "domain", link_pairs)
    early_core = lax.ppermute(early_pass, "domain", core_pairs)
    (begun,) = call(
        32,
        functools.partial(gram_kernel, first, share),
        (),
        [NEAR, WHOLE, WHOLE, WHOLE, UNREAD],
        [NEAR],
        [((2, total_states, total_states), F32)],
        [],
        (later_all, later_core, later_link, pot, early_token),
    )
    parts = domains * bands
    (blocks,) = call(
        32,
        functools.partial(final_kernel, bands, share),
        (),
        [NEAR, WHOLE, WHOLE, WHOLE, NEAR, NEAR, WHOLE],
        [WHOLE],
        [((parts, states, 2 * total_states // domains), BF16)],
        [pltpu.VMEM((2, total_states, total_states), F32)],
        (early_all, early_core, early_link, pot, begun, projs, energy),
    )
    summed = lax.all_to_all(blocks, ("domain", "band"), split_axis=0, concat_axis=0, tiled=True)
    (subspace,) = call(
        32,
        functools.partial(result_kernel, 1.0 / (lines * cols_z * domains)),
        (),
        [WHOLE],
        [WHOLE],
        [((2, states, total_states // domains), F32)],
        [],
        (summed,),
    )
    return applied.reshape(orbitals.shape), subspace


def solution(mesh):
    in_specs = (
        P("band", ("groups", "domain"), None, None),
        P(("groups", "domain"), None, None),
        P(("groups", "domain"), None, None),
        P(("groups", "domain")),
        P(("groups", "domain")),
        P(("groups", "domain")),
        P("groups", None),
    )
    out_specs = (P("band", ("groups", "domain"), None, None), P(None, ("groups", "band"), "domain"))
    return jax.shard_map(local, mesh=mesh, in_specs=in_specs, out_specs=out_specs, check_vma=False)
```

```python
import functools

import jax
import jax.numpy as jnp
import numpy as np
from jax import lax
from jax.experimental import pallas as pl
from jax.experimental.pallas import tpu as pltpu
from jax.sharding import PartitionSpec as P

F32 = jnp.float32
BF16 = jnp.bfloat16
LANES = 128
ROWS = 16
NT = (((1,), (1,)), ((), ()))
WHOLE = pl.BlockSpec(memory_space=pltpu.VMEM)
NEAR = pl.BlockSpec(memory_space=pltpu.VMEM)
SCALARS = pl.BlockSpec(memory_space=pltpu.SMEM)
FAR = pl.BlockSpec(memory_space=pltpu.HBM)
PINNED = pl.BlockSpec(memory_space=pltpu.HBM)
UNREAD = pl.BlockSpec(memory_space=pl.ANY)
copies = pltpu.SemaphoreType.DMA


def call(room, kernel, grid, in_specs, out_specs, outs, scratch, args, aliases=None, micros=0.001):
    def place(spec):
        return {id(NEAR): pltpu.VMEM, id(PINNED): pltpu.HBM}.get(id(spec))

    args = [
        pltpu.with_memory_space_constraint(arg, place(spec)) if place(spec) else arg
        for spec, arg in zip(in_specs, args)
    ]
    shapes = [(place(spec) or jax.ShapeDtypeStruct)(shape, kind) for spec, (shape, kind) in zip(out_specs, outs)]
    return pl.pallas_call(
        kernel,
        grid=grid,
        out_shape=shapes,
        in_specs=in_specs,
        out_specs=out_specs,
        scratch_shapes=scratch,
        input_output_aliases=aliases or {},
        compiler_params=pltpu.CompilerParams(vmem_limit_bytes=room << 20),
        cost_estimate=pl.CostEstimate(flops=int(micros * 1.1e9), bytes_accessed=1 << 10, transcendentals=0),
    )(*args)


def start(copy):
    copy.start()
    return copy


def start_all(pairs, sems):
    return [start(pltpu.make_async_copy(source, target, sems.at[i])) for i, (source, target) in enumerate(pairs)]


def wait_all(started):
    for copy in started:
        copy.wait()


def pack_kernel(first, x_hbm, xt_hbm, early, late, message, x, xt, in_sems, out_sems):
    states, lines, _ = x.shape
    bands = in_sems.shape[0]
    share = lines // bands
    count = share - first
    loads, sends = [], []
    for c in range(bands):
        where = (slice(None), pl.ds(c * share, share), slice(None))
        loads.append(start(pltpu.make_async_copy(x_hbm.at[where], x.at[where], in_sems.at[c])))

    def send(line, number, target, at):
        copy = pltpu.make_async_copy(
            xt.at[pl.ds(line, number)], target.at[pl.ds(at, number)], out_sems.at[len(sends)]
        )
        sends.append(start(copy))

    for c in range(bands):
        loads[c].wait()
        for y0 in range(c * share, (c + 1) * share, ROWS):
            for s0 in range(0, states, ROWS):
                block = x[s0 : s0 + ROWS, y0 : y0 + ROWS, :].astype(F32)
                turned = jnp.swapaxes(block, 0, 1).astype(BF16)
                xt[y0 : y0 + ROWS, s0 : s0 + ROWS, :] = turned
        send(c * share + first, count, message, c * (count + 1))
        send(c * share, 1, message, (c + bands - 1) % bands * (count + 1) + count)
        if (c + 1) * share == early.shape[0]:
            send(0, early.shape[0], early, 0)
    send(early.shape[0], late.shape[0], late, 0)
    send(0, lines, xt_hbm, 0)
    for copy in sends:
        copy.wait()


def bases(groups):
    domain = lax.axis_index("domain")
    odd, upper = domain & 1, (domain >> 1) & 1
    return [2 * groups * side for side in (1 - odd, odd, 1 - upper, upper)]


def slot_reader(atom_ref, line_ref, count_ref, atoms_here):
    first = (lax.axis_index("domain") - 1) * atoms_here
    live = count_ref[0]

    def slot_at(t):
        return line_ref[t], jnp.clip(atom_ref[t] - first, 0, 3 * atoms_here - 1), t < live

    return slot_at


def project_kernel(atom_ref, line_ref, count_ref, xt_hbm, p_hbm, handed, mine_hbm, same, core_ref, link_ref, *refs):
    far_refs, (total, mine_ref, xt_ref, p_ref, sems, out_sems) = refs[:-6], refs[-6:]
    slots, proj_count, _ = p_ref.shape
    groups, states = mine_ref.shape[0] // 3, mine_ref.shape[1]
    per_group = LANES // proj_count
    chunks = sems.shape[0] - 1
    size = slots // chunks
    unroll = 16
    pairs = [(p_hbm.at[pl.ds(c * size, size)], p_ref.at[pl.ds(c * size, size)]) for c in range(chunks)]
    xt_load, *loads = start_all([(xt_hbm, xt_ref), *pairs], sems)

    def clear(i, carry):
        for u in range(per_group):
            total[i * per_group + u] = jnp.zeros_like(total[0])
        return carry

    lax.fori_loop(0, 3 * groups, clear, 0)

    slot_at = slot_reader(atom_ref, line_ref, count_ref, groups * per_group)

    def body(i, carry):
        for u in range(unroll):
            t = i * unroll + u
            line, atom, live = slot_at(t)
            part = lax.dot_general(p_ref[t], xt_ref[line], NT, preferred_element_type=F32)
            total[jnp.where(live, atom, 3 * groups * per_group)] += part
        return carry

    xt_load.wait()
    for c in range(chunks):
        loads[c].wait()
        lax.fori_loop(c * size // unroll, (c + 1) * size // unroll, body, 0)

    sends = []
    for part in range(3):
        for g in range(part * groups, (part + 1) * groups):
            tiles = [total[g * per_group + u] for u in range(per_group)]
            mine_ref[g] = jnp.concatenate(tiles, axis=0).T.astype(BF16)
        where = pl.ds(part * groups, groups)
        sends.append(start(pltpu.make_async_copy(mine_ref.at[where], mine_hbm.at[where], out_sems.at[part])))
    sides = bases(groups)
    for g in range(groups):
        own = mine_ref[groups + g]
        for side, ref in zip(sides[:2], (core_ref, link_ref)):
            ref[g] = mine_ref[side + g]
            ref[groups + g] = own
        for side, ref in zip(sides[2:], far_refs):
            ref[g] = mine_ref[side + g]
    wait_all(sends)


def nonlocal_kernel(
    first, fars, atom_ref, line_ref, count_ref, xt_hbm, p_hbm, energy_ref, mine_hbm, core_ref, link_ref, *refs
):
    far_refs, (_, _, out_hbm, whole_hbm, *messages, lines_sum, whole_ref, mine_ref, total, atoms, p_ref, sems) = (
        refs[:fars],
        refs[fars:],
    )
    slots, proj_count, _ = p_ref.shape
    groups, states = total.shape[0] // 3, total.shape[1]
    per_group = LANES // proj_count
    lines = xt_hbm.shape[0]
    unroll = 16
    mine_load, load = start_all([(mine_hbm, mine_ref), (p_hbm, p_ref)], sems)
    share = lines // (len(messages) + 1)
    sends = []
    for k, message in enumerate(messages, 1):
        where = pl.ds((lax.axis_index("band") ^ k) * share, first)
        sends.append(start(pltpu.make_async_copy(xt_hbm.at[where], message, sems.at[3 + k])))

    def clear(i, carry):
        lines_sum[i] = jnp.zeros((states, LANES), F32)
        return carry

    lax.fori_loop(0, lines + 1, clear, 0)
    mine_load.wait()
    total[...] = mine_ref[...].astype(F32)
    sides = bases(groups)
    for g in range(groups):
        total[groups + g] += core_ref[g].astype(F32) + link_ref[g].astype(F32)
        for side, ref in zip(sides[:2], (core_ref, link_ref)):
            total[side + g] += ref[groups + g].astype(F32)
        for side, ref in zip(sides[2:], far_refs):
            total[side + g] += ref[g].astype(F32)
    last = energy_ref.shape[0] - 1
    for g in range(3 * groups):
        row = jnp.clip((lax.axis_index("domain") - 1) * groups + g, 0, last)
        tile = (total[g] * energy_ref[pl.ds(row, 1), :]).astype(BF16)
        for u in range(per_group):
            atoms[g * per_group + u] = tile[:, u * proj_count : (u + 1) * proj_count]
    for g in range(groups):
        whole_ref[g] = total[groups + g].astype(BF16)
    sends.append(start(pltpu.make_async_copy(whole_ref, whole_hbm, sems.at[2])))
    load.wait()

    slot_at = slot_reader(atom_ref, line_ref, count_ref, groups * per_group)

    def body(i, carry):
        for u in range(unroll):
            t = i * unroll + u
            line, atom, live = slot_at(t)
            part = jnp.dot(atoms[atom], p_ref[t], preferred_element_type=F32)
            lines_sum[jnp.where(live, line, lines)] += part
        return carry

    lax.fori_loop(0, slots // unroll, body, 0)
    sends.append(start(pltpu.make_async_copy(lines_sum.at[pl.ds(0, lines)], out_hbm, sems.at[3])))
    wait_all(sends)


def stencil_kernel(
    early_steps, xt_ref, last_ref, next_ref, core_ref, early_ref, late_ref, added_ref, pot_ref, ring_ref, unread,
    out_ref,
):
    states, here, _ = out_ref.shape
    early = pl.program_id(0) < early_steps

    def line(i, rows):
        ref, at = (last_ref, 0) if i < 0 else (next_ref, 0) if i == here else (xt_ref, i)
        return ref[at, rows, :]

    for y0 in range(0, here, ROWS):
        for s0 in range(0, states, ROWS):
            rows = slice(s0, s0 + ROWS)
            results = []
            cells = jnp.concatenate([line(y0 + i, rows) for i in range(ROWS)], axis=0)
            along = jnp.dot(cells, ring_ref[...], preferred_element_type=F32)
            before, x = line(y0 - 1, rows).astype(F32), line(y0, rows).astype(F32)
            for i in range(ROWS):
                y = y0 + i
                after = line(y + 1, rows).astype(F32)
                link = jnp.where(early, early_ref[y, rows, :], late_ref[y, rows, :]).astype(F32)
                beside = (before + after) + (core_ref[y, rows, :].astype(F32) + link)
                value = along[i * ROWS : (i + 1) * ROWS] + pot_ref[y : y + 1, :] * x
                results.append(value + added_ref[y, rows, :] - 0.5 * beside)
                before, x = x, after
            turned = jnp.swapaxes(jnp.stack(results, axis=0), 0, 1).astype(BF16)
            out_ref[rows, y0 : y0 + ROWS, :] = turned


def pass_half(all_ref, pass_hbm, sem):
    half = pass_hbm.shape[0]
    copy = start(pltpu.make_async_copy(all_ref.at[pl.ds((1 - (lax.axis_index("domain") & 1)) * half, half)], pass_hbm, sem))
    copy.wait()


def later_kernel(bands, landed, handed, unread, all_ref, pass_hbm, same, sems, pass_sem):
    count, states = all_ref.shape[0], landed.shape[1]
    loads = [
        start(
            pltpu.make_async_copy(
                landed.at[pl.ds(b * count, count)], all_ref.at[:, pl.ds(b * states, states), :], sems.at[b]
            )
        )
        for b in range(bands)
    ]
    for copy in loads:
        copy.wait()
    pass_half(all_ref, pass_hbm, pass_sem)


def early_kernel(share, xt_hbm, after_ref, *refs):
    pieces, (all_ref, pass_hbm, done_ref, sems, pass_sem) = refs[:-5], refs[-5:]
    done_ref[...] = jnp.zeros_like(done_ref)
    states = xt_hbm.shape[1]
    band = lax.axis_index("band")
    count = all_ref.shape[0] - 1
    pairs = []
    for k in range(len(pieces) + 1):
        at = pl.ds(pl.multiple_of((band ^ k) * states, states), states)
        source = pieces[k - 1] if k else xt_hbm.at[pl.ds(band * share, count)]
        pairs.append((source, all_ref.at[pl.ds(0, count), at, :]))
    loads = start_all(pairs, sems)
    all_ref[count] = after_ref[0]
    wait_all(loads)
    pass_half(all_ref, pass_hbm, pass_sem)


def add_products(row, all_ref, core_ref, link_ref, pot_ref, acc):
    half = core_ref.shape[0]
    group = 4
    mine = (lax.axis_index("domain") & 1) * half
    for part, base in ((0, mine), (1, half - mine)):
        for i0 in range(0, half, group):
            xs, ys = [], []
            for i in range(i0, min(i0 + group, half)):
                cell = all_ref[base + i]
                x = cell.astype(F32)
                y = (3.0 + pot_ref[pl.ds(row + base + i, 1), :]) * x - pltpu.roll(x, x.shape[1] - 1, 1)
                y = y - all_ref[base + i + 1].astype(F32)
                if part == 0:
                    y = y - core_ref[i].astype(F32) - link_ref[i].astype(F32)
                xs.append(cell)
                ys.append(y.astype(BF16))
            flat_x = jnp.concatenate(xs, axis=1)
            flat_y = jnp.concatenate(ys, axis=1)
            acc[0] += lax.dot_general(flat_x, flat_x, NT, preferred_element_type=F32)
            acc[1] += lax.dot_general(flat_y, flat_x, NT, preferred_element_type=F32)


def gram_kernel(first, share, all_ref, core_ref, link_ref, pot_ref, unread, acc):
    acc[...] = jnp.zeros_like(acc)
    add_products(lax.axis_index("band") * share + first, all_ref, core_ref, link_ref, pot_ref, acc)


def final_kernel(
    bands, share, all_ref, core_ref, link_ref, pot_ref, begun_ref, shares_ref, energy_ref, out_ref, done_ref, acc
):
    done_ref[...] = jnp.zeros_like(done_ref)
    acc[...] = begun_ref[...]
    add_products(lax.axis_index("band") * share, all_ref, core_ref, link_ref, pot_ref, acc)
    groups = shares_ref.shape[0] // bands
    first = (lax.axis_index("domain") * bands + lax.axis_index("band")) * groups
    for g in range(groups):
        here = jnp.concatenate([shares_ref[b * groups + g] for b in range(bands)], axis=0)
        scaled = (here.astype(F32) * energy_ref[pl.ds(first + g, 1), :]).astype(BF16)
        acc[1] += lax.dot_general(scaled, here, NT, preferred_element_type=F32)
    hamil = 0.5 * (acc[1] + acc[1].T)
    domains = out_ref.shape[0] // bands
    rows, cols = out_ref.shape[1], out_ref.shape[2] // 2
    for c in range(domains):
        for r in range(bands):
            r0, c0 = r * rows, c * cols
            out_ref[c * bands + r, :, :cols] = acc[0, r0 : r0 + rows, c0 : c0 + cols].astype(BF16)
            out_ref[c * bands + r, :, cols:] = hamil[r0 : r0 + rows, c0 : c0 + cols].astype(BF16)


def result_kernel(scale, parts_ref, out_ref):
    total = jnp.sum(parts_ref[...].astype(F32), axis=0) * scale
    cols = out_ref.shape[2]
    out_ref[0] = total[:, :cols]
    out_ref[1] = total[:, cols:]


def local(orbitals, potential, projectors, tile_atom, tile_line, tile_count, energies):
    states, _, lines, cols_z = orbitals.shape
    slots, proj_count, _ = projectors.shape
    atom_total = energies.shape[0]
    domains, bands = lax.axis_size("domain"), lax.axis_size("band")
    total_states = states * bands
    atoms_here = atom_total // domains
    per_group = LANES // proj_count
    groups = atoms_here // per_group
    share = lines // bands
    first = share // 4
    rest = share - first

    core_pairs = [(i, i ^ 1) for i in range(domains) if i ^ 1 < domains]
    link_pairs = [(i, ((i + 1) ^ 1) - 1) for i in range(1, domains) if ((i + 1) ^ 1) - 1 < domains]
    near_far = [(i, i ^ 2) for i in range(domains) if i ^ 2 < domains]
    next = [(i, ((i + 2) ^ 2) - 2) for i in range(2, domains) if ((i + 2) ^ 2) - 2 < domains]
    far_pairs = [pairs for pairs in (near_far, next) if pairs]

    def swapped(values, axis):
        size = lax.axis_size(axis)
        got = {k: lax.ppermute(values[k - 1], axis, [(i, i ^ k) for i in range(size)]) for k in range(size - 1, 0, -1)}
        return [got[k] for k in range(1, size)]

    field = orbitals.reshape(states, lines, cols_z)
    pot = potential.reshape(lines, cols_z)
    energy = energies.reshape(atom_total // per_group, LANES)
    eye = np.eye(cols_z, dtype=np.float32)
    ring = jnp.asarray(3.0 * eye - 0.5 * (np.roll(eye, 1, axis=0) + np.roll(eye, -1, axis=0)), dtype=BF16)

    late_lines = lines // 2
    line_shape, late_shape = (lines, states, cols_z), (late_lines, states, cols_z)
    xt, early_part, late_part, message = call(
        63,
        functools.partial(pack_kernel, first),
        (),
        [FAR],
        [FAR] * 4,
        [
            (line_shape, BF16),
            ((lines - late_lines, states, cols_z), BF16),
            (late_shape, BF16),
            ((bands * (rest + 1), states, cols_z), BF16),
        ],
        [
            pltpu.VMEM((states, lines, cols_z), BF16),
            pltpu.VMEM(line_shape, BF16),
            copies((bands,)),
            copies((2 * bands + 3,)),
        ],
        (field,),
    )
    landed = lax.all_to_all(message, "band", split_axis=0, concat_axis=0, tiled=True)
    link_early = lax.ppermute(early_part, "domain", link_pairs)
    core_field = lax.ppermute(xt, "domain", core_pairs)

    group_shape = (groups, states, LANES)
    mine, late_part, to_core, to_link, *to_far = call(
        63,
        project_kernel,
        (),
        [SCALARS] * 3 + [FAR, PINNED, UNREAD],
        [PINNED, UNREAD] + [WHOLE] * (2 + len(far_pairs)),
        [((3 * groups, states, LANES), BF16), (late_shape, BF16)]
        + [((2 * groups, states, LANES), BF16)] * 2
        + [(group_shape, BF16)] * len(far_pairs),
        [
            pltpu.VMEM((3 * atoms_here + 1, proj_count, states), F32),
            pltpu.VMEM((3 * groups, states, LANES), BF16),
            pltpu.VMEM(line_shape, BF16),
            pltpu.VMEM(projectors.shape, BF16),
            copies((5,)),
            copies((3,)),
        ],
        (tile_atom, tile_line, tile_count, xt, projectors, late_part),
        aliases={5: 1},
    )
    from_link = lax.ppermute(to_link, "domain", link_pairs)
    from_far = [lax.ppermute(value, "domain", pairs) for value, pairs in zip(to_far, far_pairs)]
    from_core = lax.ppermute(to_core, "domain", core_pairs)
    link_late = lax.ppermute(late_part, "domain", link_pairs)
    added, whole, *messages = call(
        62,
        functools.partial(nonlocal_kernel, first, len(far_pairs)),
        (),
        [SCALARS] * 3 + [FAR, PINNED, WHOLE, PINNED, WHOLE, WHOLE] + [WHOLE] * len(far_pairs) + [UNREAD] * 2,
        [PINNED, FAR] + [FAR] * (bands - 1),
        [(line_shape, F32), (group_shape, BF16)] + [((first, states, cols_z), BF16)] * (bands - 1),
        [
            pltpu.VMEM((lines + 1, states, cols_z), F32),
            pltpu.VMEM(group_shape, BF16),
            pltpu.VMEM((3 * groups, states, LANES), BF16),
            pltpu.VMEM((3 * groups, states, LANES), F32),
            pltpu.VMEM((3 * atoms_here, states, proj_count), BF16),
            pltpu.VMEM(projectors.shape, BF16),
            copies((3 + bands,)),
        ],
        (
            tile_atom, tile_line, tile_count, xt, projectors, energy, mine, from_core, from_link, *from_far,
            link_early, core_field,
        ),
    )
    early = swapped(messages, "band")

    later_all, later_pass, whole = call(
        62,
        functools.partial(later_kernel, bands),
        (),
        [FAR, UNREAD, UNREAD],
        [NEAR, FAR, UNREAD],
        [
            ((rest + 1, total_states, cols_z), BF16),
            ((rest // 2, total_states, cols_z), BF16),
            (group_shape, BF16),
        ],
        [copies((bands,)), copies],
        (landed, whole, link_late),
        aliases={1: 2},
        micros=20,
    )
    later_link = lax.ppermute(later_pass, "domain", link_pairs)
    later_core = lax.ppermute(later_pass, "domain", core_pairs)
    shares = lax.all_to_all(whole, "band", split_axis=0, concat_axis=0, tiled=True)

    early_all, early_pass, early_token = call(
        32,
        functools.partial(early_kernel, share),
        (),
        [FAR, NEAR] + [FAR] * (bands - 1),
        [NEAR, FAR, WHOLE],
        [
            ((first + 1, total_states, cols_z), BF16),
            ((first // 2, total_states, cols_z), BF16),
            ((8, LANES), F32),
        ],
        [copies((bands,)), copies],
        (xt, later_all, *early),
        micros=30,
    )
    early_link = lax.ppermute(early_pass, "domain", link_pairs)
    early_core = lax.ppermute(early_pass, "domain", core_pairs)
    (begun,) = call(
        32,
        functools.partial(gram_kernel, first, share),
        (),
        [NEAR, WHOLE, WHOLE, WHOLE, UNREAD],
        [NEAR],
        [((2, total_states, total_states), F32)],
        [],
        (later_all, later_core, later_link, pot, early_token),
    )
    parts = domains * bands
    blocks, final_token = call(
        32,
        functools.partial(final_kernel, bands, share),
        (),
        [NEAR, WHOLE, WHOLE, WHOLE, NEAR, WHOLE, WHOLE],
        [WHOLE, WHOLE],
        [((parts, states, 2 * total_states // domains), BF16), ((8, LANES), F32)],
        [pltpu.VMEM((2, total_states, total_states), F32)],
        (early_all, early_core, early_link, pot, begun, shares, energy),
    )
    summed = lax.all_to_all(blocks, ("domain", "band"), split_axis=0, concat_axis=0, tiled=True)
    span = 2 * ROWS
    steps, early_steps = lines // span, (lines - late_lines) // span
    block = pl.BlockSpec((span, states, cols_z), lambda i: (i, 0, 0))
    (applied,) = call(
        32,
        functools.partial(stencil_kernel, early_steps),
        (steps,),
        [
            block,
            pl.BlockSpec((1, states, cols_z), lambda i: (lax.rem(i * span + lines - 1, lines), 0, 0)),
            pl.BlockSpec((1, states, cols_z), lambda i: (lax.rem(i * span + span, lines), 0, 0)),
            block,
            pl.BlockSpec((span, states, cols_z), lambda i: (jnp.minimum(i, early_steps - 1), 0, 0)),
            pl.BlockSpec((span, states, cols_z), lambda i: (jnp.maximum(i - early_steps, 0), 0, 0)),
            block,
            pl.BlockSpec((span, cols_z), lambda i: (i, 0)),
            WHOLE,
            UNREAD,
        ],
        [pl.BlockSpec((states, span, cols_z), lambda i: (0, i, 0))],
        [((states, lines, cols_z), BF16)],
        [],
        (
            xt, xt, xt, core_field, link_early, link_late, pltpu.with_memory_space_constraint(added, pltpu.HBM), pot, ring,
            final_token,
        ),
    )

    (subspace,) = call(
        32,
        functools.partial(result_kernel, 1.0 / (lines * cols_z * domains)),
        (),
        [WHOLE],
        [WHOLE],
        [((2, states, total_states // domains), F32)],
        [],
        (summed,),
    )
    return applied.reshape(orbitals.shape), subspace


def solution(mesh):
    in_specs = (
        P("band", ("groups", "domain"), None, None),
        P(("groups", "domain"), None, None),
        P(("groups", "domain"), None, None),
        P(("groups", "domain")),
        P(("groups", "domain")),
        P(("groups", "domain")),
        P("groups", None),
    )
    out_specs = (P("band", ("groups", "domain"), None, None), P(None, ("groups", "band"), "domain"))
    return jax.shard_map(local, mesh=mesh, in_specs=in_specs, out_specs=out_specs, check_vma=False)
```

```python
import functools

import jax
import jax.numpy as jnp
import numpy as np
from jax import lax
from jax.experimental import pallas as pl
from jax.experimental.pallas import tpu as pltpu
from jax.sharding import PartitionSpec as P

F32 = jnp.float32
BF16 = jnp.bfloat16
LANES = 128
ROWS = 16
NT = (((1,), (1,)), ((), ()))
WHOLE = pl.BlockSpec(memory_space=pltpu.VMEM)
NEAR = pl.BlockSpec(memory_space=pltpu.VMEM)
SCALARS = pl.BlockSpec(memory_space=pltpu.SMEM)
FAR = pl.BlockSpec(memory_space=pltpu.HBM)
PINNED = pl.BlockSpec(memory_space=pltpu.HBM)
UNREAD = pl.BlockSpec(memory_space=pl.ANY)
copies = pltpu.SemaphoreType.DMA


def call(room, kernel, grid, in_specs, out_specs, outs, scratch, args, aliases=None, micros=0.001):
    def place(spec):
        return {id(NEAR): pltpu.VMEM, id(PINNED): pltpu.HBM}.get(id(spec))

    args = [
        pltpu.with_memory_space_constraint(arg, place(spec)) if place(spec) else arg
        for spec, arg in zip(in_specs, args)
    ]
    shapes = [(place(spec) or jax.ShapeDtypeStruct)(shape, kind) for spec, (shape, kind) in zip(out_specs, outs)]
    return pl.pallas_call(
        kernel,
        grid=grid,
        out_shape=shapes,
        in_specs=in_specs,
        out_specs=out_specs,
        scratch_shapes=scratch,
        input_output_aliases=aliases or {},
        compiler_params=pltpu.CompilerParams(vmem_limit_bytes=room << 20),
        cost_estimate=pl.CostEstimate(flops=int(micros * 1.1e9), bytes_accessed=1 << 10, transcendentals=0),
    )(*args)


def start(copy):
    copy.start()
    return copy


def start_all(pairs, sems):
    return [start(pltpu.make_async_copy(source, target, sems.at[i])) for i, (source, target) in enumerate(pairs)]


def wait_all(started):
    for copy in started:
        copy.wait()


def hand_on(*refs):
    pass


def pack_kernel(first, x_hbm, xt_hbm, early, late, message, x, xt, in_sems, out_sems):
    states, lines, _ = x.shape
    bands = in_sems.shape[0]
    share = lines // bands
    count = share - first
    loads, sends = [], []
    for c in range(bands):
        where = (slice(None), pl.ds(c * share, share), slice(None))
        loads.append(start(pltpu.make_async_copy(x_hbm.at[where], x.at[where], in_sems.at[c])))

    def send(line, number, target, at):
        copy = pltpu.make_async_copy(
            xt.at[pl.ds(line, number)], target.at[pl.ds(at, number)], out_sems.at[len(sends)]
        )
        sends.append(start(copy))

    for c in range(bands):
        loads[c].wait()
        for y0 in range(c * share, (c + 1) * share, ROWS):
            for s0 in range(0, states, ROWS):
                block = x[s0 : s0 + ROWS, y0 : y0 + ROWS, :].astype(F32)
                turned = jnp.swapaxes(block, 0, 1).astype(BF16)
                xt[y0 : y0 + ROWS, s0 : s0 + ROWS, :] = turned
        send(c * share + first, count, message, c * (count + 1))
        send(c * share, 1, message, (c + bands - 1) % bands * (count + 1) + count)
        if (c + 1) * share == early.shape[0]:
            send(0, early.shape[0], early, 0)
    send(early.shape[0], late.shape[0], late, 0)
    send(0, lines, xt_hbm, 0)
    for copy in sends:
        copy.wait()


def bases(groups):
    domain = lax.axis_index("domain")
    odd, upper = domain & 1, (domain >> 1) & 1
    return [2 * groups * side for side in (1 - odd, odd, 1 - upper, upper)]


def slot_reader(atom_ref, line_ref, count_ref, atoms_here):
    first = (lax.axis_index("domain") - 1) * atoms_here
    live = count_ref[0]

    def slot_at(t):
        return line_ref[t], jnp.clip(atom_ref[t] - first, 0, 3 * atoms_here - 1), t < live

    return slot_at


def project_kernel(atom_ref, line_ref, count_ref, xt_hbm, p_hbm, mine_hbm, core_ref, link_ref, *refs):
    far_refs, (total, mine_ref, xt_ref, p_ref, sems, out_sems) = refs[:-6], refs[-6:]
    slots, proj_count, _ = p_ref.shape
    groups, states = mine_ref.shape[0] // 3, mine_ref.shape[1]
    per_group = LANES // proj_count
    chunks = sems.shape[0] - 1
    size = slots // chunks
    unroll = 16
    pairs = [(p_hbm.at[pl.ds(c * size, size)], p_ref.at[pl.ds(c * size, size)]) for c in range(chunks)]
    xt_load, *loads = start_all([(xt_hbm, xt_ref), *pairs], sems)

    def clear(i, carry):
        for u in range(per_group):
            total[i * per_group + u] = jnp.zeros_like(total[0])
        return carry

    lax.fori_loop(0, 3 * groups, clear, 0)

    slot_at = slot_reader(atom_ref, line_ref, count_ref, groups * per_group)

    def body(i, carry):
        for u in range(unroll):
            t = i * unroll + u
            line, atom, live = slot_at(t)
            part = lax.dot_general(p_ref[t], xt_ref[line], NT, preferred_element_type=F32)
            total[jnp.where(live, atom, 3 * groups * per_group)] += part
        return carry

    xt_load.wait()
    for c in range(chunks):
        loads[c].wait()
        lax.fori_loop(c * size // unroll, (c + 1) * size // unroll, body, 0)

    sends = []
    for part in range(3):
        for g in range(part * groups, (part + 1) * groups):
            tiles = [total[g * per_group + u] for u in range(per_group)]
            mine_ref[g] = jnp.concatenate(tiles, axis=0).T.astype(BF16)
        where = pl.ds(part * groups, groups)
        sends.append(start(pltpu.make_async_copy(mine_ref.at[where], mine_hbm.at[where], out_sems.at[part])))
    sides = bases(groups)
    for g in range(groups):
        own = mine_ref[groups + g]
        for side, ref in zip(sides[:2], (core_ref, link_ref)):
            ref[g] = mine_ref[side + g]
            ref[groups + g] = own
        for side, ref in zip(sides[2:], far_refs):
            ref[g] = mine_ref[side + g]
    wait_all(sends)


def nonlocal_kernel(
    lines, fars, atom_ref, line_ref, count_ref, p_hbm, energy_ref, mine_hbm, core_ref, link_ref, *refs
):
    far_refs, (_, _, out_hbm, whole_hbm, lines_sum, whole_ref, mine_ref, total, atoms, p_ref, sems) = (
        refs[:fars],
        refs[fars:],
    )
    slots, proj_count, _ = p_ref.shape
    groups, states = total.shape[0] // 3, total.shape[1]
    per_group = LANES // proj_count
    unroll = 16
    mine_load, load = start_all([(mine_hbm, mine_ref), (p_hbm, p_ref)], sems)
    sends = []

    def clear(i, carry):
        lines_sum[i] = jnp.zeros((states, LANES), F32)
        return carry

    lax.fori_loop(0, lines + 1, clear, 0)
    mine_load.wait()
    total[...] = mine_ref[...].astype(F32)
    sides = bases(groups)
    for g in range(groups):
        total[groups + g] += core_ref[g].astype(F32) + link_ref[g].astype(F32)
        for side, ref in zip(sides[:2], (core_ref, link_ref)):
            total[side + g] += ref[groups + g].astype(F32)
        for side, ref in zip(sides[2:], far_refs):
            total[side + g] += ref[g].astype(F32)
    last = energy_ref.shape[0] - 1
    for g in range(3 * groups):
        row = jnp.clip((lax.axis_index("domain") - 1) * groups + g, 0, last)
        tile = (total[g] * energy_ref[pl.ds(row, 1), :]).astype(BF16)
        for u in range(per_group):
            atoms[g * per_group + u] = tile[:, u * proj_count : (u + 1) * proj_count]
    for g in range(groups):
        whole_ref[g] = total[groups + g].astype(BF16)
    sends.append(start(pltpu.make_async_copy(whole_ref, whole_hbm, sems.at[2])))
    load.wait()

    slot_at = slot_reader(atom_ref, line_ref, count_ref, groups * per_group)

    def body(i, carry):
        for u in range(unroll):
            t = i * unroll + u
            line, atom, live = slot_at(t)
            part = jnp.dot(atoms[atom], p_ref[t], preferred_element_type=F32)
            lines_sum[jnp.where(live, line, lines)] += part
        return carry

    lax.fori_loop(0, slots // unroll, body, 0)
    sends.append(start(pltpu.make_async_copy(lines_sum.at[pl.ds(0, lines)], out_hbm, sems.at[3])))
    wait_all(sends)


def second_kernel(share, xt_hbm, core_hbm, early_hbm, late_hbm, whole_hbm, *refs):
    messages, (built, cores, links, in_sems, out_sems) = refs[:-5], refs[-5:]
    bands = len(messages)
    half = cores.shape[1]
    first = 2 * half
    held = built.shape[1] - first - half
    early_lines = early_hbm.shape[0]
    mine = (lax.axis_index("domain") & 1) * half
    loads = []

    def load(source, target):
        loads.append(start(pltpu.make_async_copy(source, target, in_sems.at[len(loads)])))

    for k in range(bands):
        to = lax.axis_index("band") ^ k
        begin = to * share
        load(xt_hbm.at[pl.ds(begin, first)], built.at[k, pl.ds(0, first)])
        load(whole_hbm.at[pl.ds(to * held, held)], built.at[k, pl.ds(first + half, held)])
        load(core_hbm.at[pl.ds(begin + mine, half)], cores.at[k])
        sem = in_sems.at[len(loads)]

        @pl.when(begin < early_lines)
        def _():
            pltpu.make_async_copy(early_hbm.at[pl.ds(begin + mine, half)], links.at[k], sem).start()

        @pl.when(begin >= early_lines)
        def _():
            pltpu.make_async_copy(late_hbm.at[pl.ds(begin + mine - early_lines, half)], links.at[k], sem).start()

        loads.append(pltpu.make_async_copy(early_hbm.at[pl.ds(0, half)], links.at[k], sem))
    wait_all(loads)
    sends = []
    for k, message in enumerate(messages):
        for i in range(half):
            built[k, first + i] = (cores[k, i].astype(F32) + links[k, i].astype(F32)).astype(BF16)
        sends.append(start(pltpu.make_async_copy(built.at[k], message, out_sems.at[k])))
    wait_all(sends)


def stencil_kernel(
    early_steps, xt_ref, last_ref, next_ref, core_ref, early_ref, late_ref, added_ref, pot_ref, ring_ref, unread,
    out_ref, done_ref,
):
    states, here, _ = out_ref.shape
    done_ref[...] = jnp.zeros_like(done_ref)
    early = pl.program_id(0) < early_steps

    def line(i, rows):
        ref, at = (last_ref, 0) if i < 0 else (next_ref, 0) if i == here else (xt_ref, i)
        return ref[at, rows, :]

    for y0 in range(0, here, ROWS):
        for s0 in range(0, states, ROWS):
            rows = slice(s0, s0 + ROWS)
            results = []
            cells = jnp.concatenate([line(y0 + i, rows) for i in range(ROWS)], axis=0)
            along = jnp.dot(cells, ring_ref[...], preferred_element_type=F32)
            before, x = line(y0 - 1, rows).astype(F32), line(y0, rows).astype(F32)
            for i in range(ROWS):
                y = y0 + i
                after = line(y + 1, rows).astype(F32)
                link = jnp.where(early, early_ref[y, rows, :], late_ref[y, rows, :]).astype(F32)
                beside = (before + after) + (core_ref[y, rows, :].astype(F32) + link)
                value = along[i * ROWS : (i + 1) * ROWS] + pot_ref[y : y + 1, :] * x
                results.append(value + added_ref[y, rows, :] - 0.5 * beside)
                before, x = x, after
            turned = jnp.swapaxes(jnp.stack(results, axis=0), 0, 1).astype(BF16)
            out_ref[rows, y0 : y0 + ROWS, :] = turned


def pass_half(all_ref, pass_hbm, sem):
    half = pass_hbm.shape[0]
    copy = start(pltpu.make_async_copy(all_ref.at[pl.ds((1 - (lax.axis_index("domain") & 1)) * half, half)], pass_hbm, sem))
    copy.wait()


def later_kernel(bands, landed, unread, all_ref, pass_hbm, done_ref, sems, pass_sem):
    done_ref[...] = jnp.zeros_like(done_ref)
    count, states = all_ref.shape[0], landed.shape[1]
    loads = [
        start(
            pltpu.make_async_copy(
                landed.at[pl.ds(b * count, count)], all_ref.at[:, pl.ds(b * states, states), :], sems.at[b]
            )
        )
        for b in range(bands)
    ]
    for copy in loads:
        copy.wait()
    pass_half(all_ref, pass_hbm, pass_sem)


def early_kernel(after_ref, unread, *refs):
    pieces, (all_ref, beside_ref, projs_ref, done_ref, sems) = refs[:-5], refs[-5:]
    done_ref[...] = jnp.zeros_like(done_ref)
    states = pieces[0].shape[1]
    count, half, held = all_ref.shape[0] - 1, beside_ref.shape[0], projs_ref.shape[0]
    pairs = []
    for k, piece in enumerate(pieces):
        at = pl.ds(pl.multiple_of((lax.axis_index("band") ^ k) * states, states), states)
        pairs.append((piece.at[pl.ds(0, count)], all_ref.at[pl.ds(0, count), at, :]))
        pairs.append((piece.at[pl.ds(count, half)], beside_ref.at[:, at, :]))
        pairs.append((piece.at[pl.ds(count + half, held)], projs_ref.at[:, at, :]))
    loads = start_all(pairs, sems)
    all_ref[count] = after_ref[0]
    wait_all(loads)


def add_products(row, all_ref, beside_refs, pot_ref, acc):
    half = beside_refs[0].shape[0]
    group = 4
    mine = (lax.axis_index("domain") & 1) * half
    for part, base in ((0, mine), (1, half - mine)):
        for i0 in range(0, half, group):
            xs, ys = [], []
            for i in range(i0, min(i0 + group, half)):
                cell = all_ref[base + i]
                x = cell.astype(F32)
                y = (3.0 + pot_ref[pl.ds(row + base + i, 1), :]) * x - pltpu.roll(x, x.shape[1] - 1, 1)
                y = y - all_ref[base + i + 1].astype(F32)
                if part == 0:
                    for ref in beside_refs:
                        y = y - ref[i].astype(F32)
                xs.append(cell)
                ys.append(y.astype(BF16))
            flat_x = jnp.concatenate(xs, axis=1)
            flat_y = jnp.concatenate(ys, axis=1)
            acc[0] += lax.dot_general(flat_x, flat_x, NT, preferred_element_type=F32)
            acc[1] += lax.dot_general(flat_y, flat_x, NT, preferred_element_type=F32)


def gram_kernel(first, share, all_ref, core_ref, link_ref, pot_ref, unread, acc):
    acc[...] = jnp.zeros_like(acc)
    add_products(lax.axis_index("band") * share + first, all_ref, (core_ref, link_ref), pot_ref, acc)


def final_kernel(bands, share, all_ref, beside_ref, pot_ref, begun_ref, proj_ref, energy_ref, out_ref, acc):
    acc[...] = begun_ref[...]
    add_products(lax.axis_index("band") * share, all_ref, (beside_ref,), pot_ref, acc)
    groups = proj_ref.shape[0]
    first = (lax.axis_index("domain") * bands + lax.axis_index("band")) * groups
    for g in range(groups):
        here = proj_ref[g]
        scaled = (here.astype(F32) * energy_ref[pl.ds(first + g, 1), :]).astype(BF16)
        acc[1] += lax.dot_general(scaled, here, NT, preferred_element_type=F32)
    hamil = 0.5 * (acc[1] + acc[1].T)
    domains = out_ref.shape[0] // bands
    rows, cols = out_ref.shape[1], out_ref.shape[2] // 2
    for c in range(domains):
        for r in range(bands):
            r0, c0 = r * rows, c * cols
            out_ref[c * bands + r, :, :cols] = acc[0, r0 : r0 + rows, c0 : c0 + cols].astype(BF16)
            out_ref[c * bands + r, :, cols:] = hamil[r0 : r0 + rows, c0 : c0 + cols].astype(BF16)


def result_kernel(scale, parts_ref, out_ref):
    total = jnp.sum(parts_ref[...].astype(F32), axis=0) * scale
    cols = out_ref.shape[2]
    out_ref[0] = total[:, :cols]
    out_ref[1] = total[:, cols:]


def local(orbitals, potential, projectors, tile_atom, tile_line, tile_count, energies):
    states, _, lines, cols_z = orbitals.shape
    slots, proj_count, _ = projectors.shape
    atom_total = energies.shape[0]
    domains, bands = lax.axis_size("domain"), lax.axis_size("band")
    total_states = states * bands
    atoms_here = atom_total // domains
    per_group = LANES // proj_count
    groups = atoms_here // per_group
    share = lines // bands
    first = 2 * (share * 3 // 32)
    rest = share - first

    core_pairs = [(i, i ^ 1) for i in range(domains) if i ^ 1 < domains]
    link_pairs = [(i, ((i + 1) ^ 1) - 1) for i in range(1, domains) if ((i + 1) ^ 1) - 1 < domains]
    near_far = [(i, i ^ 2) for i in range(domains) if i ^ 2 < domains]
    next = [(i, ((i + 2) ^ 2) - 2) for i in range(2, domains) if ((i + 2) ^ 2) - 2 < domains]
    far_pairs = [pairs for pairs in (near_far, next) if pairs]

    def swapped(values, axis):
        size = lax.axis_size(axis)
        got = {k: lax.ppermute(values[k - 1], axis, [(i, i ^ k) for i in range(size)]) for k in range(size - 1, 0, -1)}
        return [got[k] for k in range(1, size)]

    field = orbitals.reshape(states, lines, cols_z)
    pot = potential.reshape(lines, cols_z)
    energy = energies.reshape(atom_total // per_group, LANES)
    eye = np.eye(cols_z, dtype=np.float32)
    ring = jnp.asarray(3.0 * eye - 0.5 * (np.roll(eye, 1, axis=0) + np.roll(eye, -1, axis=0)), dtype=BF16)

    late_lines = lines // 2
    line_shape, late_shape = (lines, states, cols_z), (late_lines, states, cols_z)
    xt, early_part, late_part, message = call(
        63,
        functools.partial(pack_kernel, first),
        (),
        [FAR],
        [FAR] * 4,
        [
            (line_shape, BF16),
            ((lines - late_lines, states, cols_z), BF16),
            (late_shape, BF16),
            ((bands * (rest + 1), states, cols_z), BF16),
        ],
        [
            pltpu.VMEM((states, lines, cols_z), BF16),
            pltpu.VMEM(line_shape, BF16),
            copies((bands,)),
            copies((2 * bands + 3,)),
        ],
        (field,),
    )
    landed = lax.all_to_all(message, "band", split_axis=0, concat_axis=0, tiled=True)
    link_early = lax.ppermute(early_part, "domain", link_pairs)
    core_field = lax.ppermute(xt, "domain", core_pairs)

    group_shape = (groups, states, LANES)
    mine, to_core, to_link, *to_far = call(
        63,
        project_kernel,
        (),
        [SCALARS] * 3 + [FAR, PINNED],
        [PINNED] + [WHOLE] * (2 + len(far_pairs)),
        [((3 * groups, states, LANES), BF16)]
        + [((2 * groups, states, LANES), BF16)] * 2
        + [(group_shape, BF16)] * len(far_pairs),
        [
            pltpu.VMEM((3 * atoms_here + 1, proj_count, states), F32),
            pltpu.VMEM((3 * groups, states, LANES), BF16),
            pltpu.VMEM(line_shape, BF16),
            pltpu.VMEM(projectors.shape, BF16),
            copies((5,)),
            copies((3,)),
        ],
        (tile_atom, tile_line, tile_count, xt, projectors),
    )
    from_link = lax.ppermute(to_link, "domain", link_pairs)
    from_far = [lax.ppermute(value, "domain", pairs) for value, pairs in zip(to_far, far_pairs)]
    from_core = lax.ppermute(to_core, "domain", core_pairs)
    (late_part,) = call(
        63,
        hand_on,
        (),
        [UNREAD] * (3 + len(far_pairs)),
        [UNREAD],
        [(late_shape, BF16)],
        [],
        (late_part, from_core, from_link, *from_far),
        aliases={0: 0},
    )
    link_late = lax.ppermute(late_part, "domain", link_pairs)
    added, whole = call(
        62,
        functools.partial(nonlocal_kernel, lines, len(far_pairs)),
        (),
        [SCALARS] * 3 + [PINNED, WHOLE, PINNED, WHOLE, WHOLE] + [WHOLE] * len(far_pairs) + [UNREAD] * 2,
        [PINNED, PINNED],
        [(line_shape, F32), (group_shape, BF16)],
        [
            pltpu.VMEM((lines + 1, states, cols_z), F32),
            pltpu.VMEM(group_shape, BF16),
            pltpu.VMEM((3 * groups, states, LANES), BF16),
            pltpu.VMEM((3 * groups, states, LANES), F32),
            pltpu.VMEM((3 * atoms_here, states, proj_count), BF16),
            pltpu.VMEM(projectors.shape, BF16),
            copies((4,)),
        ],
        (
            tile_atom, tile_line, tile_count, projectors, energy, mine, from_core, from_link, *from_far,
            link_early, core_field,
        ),
    )
    held = groups // bands
    built_shape = (first + first // 2 + held, states, cols_z)
    own_message, *messages = call(
        62,
        functools.partial(second_kernel, share),
        (),
        [FAR] * 4 + [PINNED],
        [PINNED] + [FAR] * (bands - 1),
        [(built_shape, BF16)] * bands,
        [
            pltpu.VMEM((bands, *built_shape), BF16),
            pltpu.VMEM((bands, first // 2, states, cols_z), BF16),
            pltpu.VMEM((bands, first // 2, states, cols_z), BF16),
            copies((4 * bands,)),
            copies((bands,)),
        ],
        (xt, core_field, link_early, link_late, whole),
    )
    early = swapped(messages, "band")

    later_all, later_pass, later_token = call(
        32,
        functools.partial(later_kernel, bands),
        (),
        [FAR, PINNED],
        [NEAR, FAR, WHOLE],
        [((rest + 1, total_states, cols_z), BF16), ((rest // 2, total_states, cols_z), BF16), ((8, LANES), F32)],
        [copies((bands,)), copies],
        (landed, own_message),
    )
    later_link = lax.ppermute(later_pass, "domain", link_pairs)
    later_core = lax.ppermute(later_pass, "domain", core_pairs)

    span = 2 * ROWS
    steps, early_steps = lines // span, (lines - late_lines) // span
    block = pl.BlockSpec((span, states, cols_z), lambda i: (i, 0, 0))
    applied, done = call(
        32,
        functools.partial(stencil_kernel, early_steps),
        (steps,),
        [
            block,
            pl.BlockSpec((1, states, cols_z), lambda i: (lax.rem(i * span + lines - 1, lines), 0, 0)),
            pl.BlockSpec((1, states, cols_z), lambda i: (lax.rem(i * span + span, lines), 0, 0)),
            block,
            pl.BlockSpec((span, states, cols_z), lambda i: (jnp.minimum(i, early_steps - 1), 0, 0)),
            pl.BlockSpec((span, states, cols_z), lambda i: (jnp.maximum(i - early_steps, 0), 0, 0)),
            block,
            pl.BlockSpec((span, cols_z), lambda i: (i, 0)),
            WHOLE,
            UNREAD,
        ],
        [pl.BlockSpec((states, span, cols_z), lambda i: (0, i, 0)), WHOLE],
        [((states, lines, cols_z), BF16), ((8, LANES), F32)],
        [],
        (
            xt, xt, xt, core_field, link_early, link_late, pltpu.with_memory_space_constraint(added, pltpu.HBM), pot, ring,
            later_token,
        ),
    )

    early_all, early_beside, projs, early_token = call(
        32,
        early_kernel,
        (),
        [NEAR, WHOLE, PINNED] + [FAR] * (bands - 1),
        [NEAR, NEAR, NEAR, WHOLE],
        [
            ((first + 1, total_states, cols_z), BF16),
            ((first // 2, total_states, cols_z), BF16),
            ((held, total_states, LANES), BF16),
            ((8, LANES), F32),
        ],
        [copies((3 * bands,))],
        (later_all, done, own_message, *early),
        micros=30,
    )
    (begun,) = call(
        32,
        functools.partial(gram_kernel, first, share),
        (),
        [NEAR, WHOLE, WHOLE, WHOLE, UNREAD],
        [NEAR],
        [((2, total_states, total_states), F32)],
        [],
        (later_all, later_core, later_link, pot, early_token),
    )
    parts = domains * bands
    (blocks,) = call(
        32,
        functools.partial(final_kernel, bands, share),
        (),
        [NEAR, NEAR, WHOLE, NEAR, NEAR, WHOLE],
        [WHOLE],
        [((parts, states, 2 * total_states // domains), BF16)],
        [pltpu.VMEM((2, total_states, total_states), F32)],
        (early_all, early_beside, pot, begun, projs, energy),
    )
    summed = lax.all_to_all(blocks, ("domain", "band"), split_axis=0, concat_axis=0, tiled=True)
    (subspace,) = call(
        32,
        functools.partial(result_kernel, 1.0 / (lines * cols_z * domains)),
        (),
        [WHOLE],
        [WHOLE],
        [((2, states, total_states // domains), F32)],
        [],
        (summed,),
    )
    return applied.reshape(orbitals.shape), subspace


def solution(mesh):
    in_specs = (
        P("band", ("groups", "domain"), None, None),
        P(("groups", "domain"), None, None),
        P(("groups", "domain"), None, None),
        P(("groups", "domain")),
        P(("groups", "domain")),
        P(("groups", "domain")),
        P("groups", None),
    )
    out_specs = (P("band", ("groups", "domain"), None, None), P(None, ("groups", "band"), "domain"))
    return jax.shard_map(local, mesh=mesh, in_specs=in_specs, out_specs=out_specs, check_vma=False)
```

```python
import functools

import jax
import jax.numpy as jnp
import numpy as np
from jax import lax
from jax.experimental import pallas as pl
from jax.experimental.pallas import tpu as pltpu
from jax.sharding import PartitionSpec as P

F32 = jnp.float32
BF16 = jnp.bfloat16
LANES = 128
ROWS = 16
NT = (((1,), (1,)), ((), ()))
WHOLE = pl.BlockSpec(memory_space=pltpu.VMEM)
NEAR = pl.BlockSpec(memory_space=pltpu.VMEM)
SCALARS = pl.BlockSpec(memory_space=pltpu.SMEM)
FAR = pl.BlockSpec(memory_space=pltpu.HBM)
PINNED = pl.BlockSpec(memory_space=pltpu.HBM)
UNREAD = pl.BlockSpec(memory_space=pl.ANY)
copies = pltpu.SemaphoreType.DMA


def call(room, kernel, grid, in_specs, out_specs, outs, scratch, args, aliases=None, micros=0.001):
    def place(spec):
        return {id(NEAR): pltpu.VMEM, id(PINNED): pltpu.HBM}.get(id(spec))

    args = [
        pltpu.with_memory_space_constraint(arg, place(spec)) if place(spec) else arg
        for spec, arg in zip(in_specs, args)
    ]
    shapes = [(place(spec) or jax.ShapeDtypeStruct)(shape, kind) for spec, (shape, kind) in zip(out_specs, outs)]
    return pl.pallas_call(
        kernel,
        grid=grid,
        out_shape=shapes,
        in_specs=in_specs,
        out_specs=out_specs,
        scratch_shapes=scratch,
        input_output_aliases=aliases or {},
        compiler_params=pltpu.CompilerParams(vmem_limit_bytes=room << 20),
        cost_estimate=pl.CostEstimate(flops=int(micros * 1.1e9), bytes_accessed=1 << 10, transcendentals=0),
    )(*args)


def start(copy):
    copy.start()
    return copy


def start_all(pairs, sems):
    return [start(pltpu.make_async_copy(source, target, sems.at[i])) for i, (source, target) in enumerate(pairs)]


def wait_all(started):
    for copy in started:
        copy.wait()


def hand_on(*refs):
    pass


def pack_kernel(first, x_hbm, xt_hbm, early, late, message, x, xt, in_sems, out_sems):
    states, lines, _ = x.shape
    bands = in_sems.shape[0]
    share = lines // bands
    count = share - first
    loads, sends = [], []
    for c in range(bands):
        where = (slice(None), pl.ds(c * share, share), slice(None))
        loads.append(start(pltpu.make_async_copy(x_hbm.at[where], x.at[where], in_sems.at[c])))

    def send(line, number, target, at):
        copy = pltpu.make_async_copy(
            xt.at[pl.ds(line, number)], target.at[pl.ds(at, number)], out_sems.at[len(sends)]
        )
        sends.append(start(copy))

    for c in range(bands):
        loads[c].wait()
        for y0 in range(c * share, (c + 1) * share, ROWS):
            for s0 in range(0, states, ROWS):
                block = x[s0 : s0 + ROWS, y0 : y0 + ROWS, :].astype(F32)
                turned = jnp.swapaxes(block, 0, 1).astype(BF16)
                xt[y0 : y0 + ROWS, s0 : s0 + ROWS, :] = turned
        send(c * share + first, count, message, c * (count + 1))
        send(c * share, 1, message, (c + bands - 1) % bands * (count + 1) + count)
        if (c + 1) * share == early.shape[0]:
            send(0, early.shape[0], early, 0)
    send(early.shape[0], late.shape[0], late, 0)
    send(0, lines, xt_hbm, 0)
    for copy in sends:
        copy.wait()


def bases(groups):
    domain = lax.axis_index("domain")
    odd, upper = domain & 1, (domain >> 1) & 1
    return [2 * groups * side for side in (1 - odd, odd, 1 - upper, upper)]


def slot_reader(atom_ref, line_ref, count_ref, atoms_here):
    first = (lax.axis_index("domain") - 1) * atoms_here
    live = count_ref[0]

    def slot_at(t):
        return line_ref[t], jnp.clip(atom_ref[t] - first, 0, 3 * atoms_here - 1), t < live

    return slot_at


def project_kernel(atom_ref, line_ref, count_ref, xt_hbm, p_hbm, mine_hbm, core_ref, link_ref, *refs):
    far_refs, (total, mine_ref, xt_ref, p_ref, sems, out_sems) = refs[:-6], refs[-6:]
    slots, proj_count, _ = p_ref.shape
    groups, states = mine_ref.shape[0] // 3, mine_ref.shape[1]
    per_group = LANES // proj_count
    chunks = sems.shape[0] - 1
    size = slots // chunks
    unroll = 16
    pairs = [(p_hbm.at[pl.ds(c * size, size)], p_ref.at[pl.ds(c * size, size)]) for c in range(chunks)]
    xt_load, *loads = start_all([(xt_hbm, xt_ref), *pairs], sems)

    def clear(i, carry):
        for u in range(per_group):
            total[i * per_group + u] = jnp.zeros_like(total[0])
        return carry

    lax.fori_loop(0, 3 * groups, clear, 0)

    slot_at = slot_reader(atom_ref, line_ref, count_ref, groups * per_group)

    def body(i, carry):
        for u in range(unroll):
            t = i * unroll + u
            line, atom, live = slot_at(t)
            part = lax.dot_general(p_ref[t], xt_ref[line], NT, preferred_element_type=F32)
            total[jnp.where(live, atom, 3 * groups * per_group)] += part
        return carry

    xt_load.wait()
    for c in range(chunks):
        loads[c].wait()
        lax.fori_loop(c * size // unroll, (c + 1) * size // unroll, body, 0)

    sends = []
    for part in range(3):
        for g in range(part * groups, (part + 1) * groups):
            tiles = [total[g * per_group + u] for u in range(per_group)]
            mine_ref[g] = jnp.concatenate(tiles, axis=0).T.astype(BF16)
        where = pl.ds(part * groups, groups)
        sends.append(start(pltpu.make_async_copy(mine_ref.at[where], mine_hbm.at[where], out_sems.at[part])))
    sides = bases(groups)
    for g in range(groups):
        own = mine_ref[groups + g]
        for side, ref in zip(sides[:2], (core_ref, link_ref)):
            ref[g] = mine_ref[side + g]
            ref[groups + g] = own
        for side, ref in zip(sides[2:], far_refs):
            ref[g] = mine_ref[side + g]
    wait_all(sends)


def nonlocal_kernel(
    lines, fars, atom_ref, line_ref, count_ref, p_hbm, energy_ref, mine_hbm, core_ref, link_ref, *refs
):
    far_refs, (out_hbm, whole_hbm, lines_sum, whole_ref, mine_ref, total, atoms, p_ref, sems) = (
        refs[:fars],
        refs[fars:],
    )
    slots, proj_count, _ = p_ref.shape
    groups, states = total.shape[0] // 3, total.shape[1]
    per_group = LANES // proj_count
    unroll = 16
    mine_load, load = start_all([(mine_hbm, mine_ref), (p_hbm, p_ref)], sems)
    sends = []

    def clear(i, carry):
        lines_sum[i] = jnp.zeros((states, LANES), F32)
        return carry

    lax.fori_loop(0, lines + 1, clear, 0)
    mine_load.wait()
    total[...] = mine_ref[...].astype(F32)
    sides = bases(groups)
    for g in range(groups):
        total[groups + g] += core_ref[g].astype(F32) + link_ref[g].astype(F32)
        for side, ref in zip(sides[:2], (core_ref, link_ref)):
            total[side + g] += ref[groups + g].astype(F32)
        for side, ref in zip(sides[2:], far_refs):
            total[side + g] += ref[g].astype(F32)
    last = energy_ref.shape[0] - 1
    for g in range(3 * groups):
        row = jnp.clip((lax.axis_index("domain") - 1) * groups + g, 0, last)
        tile = (total[g] * energy_ref[pl.ds(row, 1), :]).astype(BF16)
        for u in range(per_group):
            atoms[g * per_group + u] = tile[:, u * proj_count : (u + 1) * proj_count]
    for g in range(groups):
        whole_ref[g] = total[groups + g].astype(BF16)
    sends.append(start(pltpu.make_async_copy(whole_ref, whole_hbm, sems.at[2])))
    load.wait()

    slot_at = slot_reader(atom_ref, line_ref, count_ref, groups * per_group)

    def body(i, carry):
        for u in range(unroll):
            t = i * unroll + u
            line, atom, live = slot_at(t)
            part = jnp.dot(atoms[atom], p_ref[t], preferred_element_type=F32)
            lines_sum[jnp.where(live, line, lines)] += part
        return carry

    lax.fori_loop(0, slots // unroll, body, 0)
    sends.append(start(pltpu.make_async_copy(lines_sum.at[pl.ds(0, lines)], out_hbm, sems.at[3])))
    wait_all(sends)


def second_kernel(share, xt_hbm, core_hbm, early_hbm, late_hbm, whole_hbm, *refs):
    messages, (built, cores, links, in_sems, out_sems) = refs[:-5], refs[-5:]
    bands = len(messages)
    half = cores.shape[1]
    first = 2 * half
    held = built.shape[1] - first - half
    early_lines = early_hbm.shape[0]
    mine = (lax.axis_index("domain") & 1) * half
    loads = []

    def load(source, target):
        loads.append(start(pltpu.make_async_copy(source, target, in_sems.at[len(loads)])))

    for k in range(bands):
        to = lax.axis_index("band") ^ k
        begin = to * share
        load(xt_hbm.at[pl.ds(begin, first)], built.at[k, pl.ds(0, first)])
        load(whole_hbm.at[pl.ds(to * held, held)], built.at[k, pl.ds(first + half, held)])
        load(core_hbm.at[pl.ds(begin + mine, half)], cores.at[k])
        sem = in_sems.at[len(loads)]

        @pl.when(begin < early_lines)
        def _():
            pltpu.make_async_copy(early_hbm.at[pl.ds(begin + mine, half)], links.at[k], sem).start()

        @pl.when(begin >= early_lines)
        def _():
            pltpu.make_async_copy(late_hbm.at[pl.ds(begin + mine - early_lines, half)], links.at[k], sem).start()

        loads.append(pltpu.make_async_copy(early_hbm.at[pl.ds(0, half)], links.at[k], sem))
    wait_all(loads)
    sends = []
    for k, message in enumerate(messages):
        for i in range(half):
            built[k, first + i] = (cores[k, i].astype(F32) + links[k, i].astype(F32)).astype(BF16)
        sends.append(start(pltpu.make_async_copy(built.at[k], message, out_sems.at[k])))
    wait_all(sends)


def stencil_kernel(
    early_steps, xt_ref, last_ref, next_ref, core_ref, early_ref, late_ref, added_ref, pot_ref, ring_ref, unread,
    out_ref, done_ref,
):
    states, here, _ = out_ref.shape
    done_ref[...] = jnp.zeros_like(done_ref)
    early = pl.program_id(0) < early_steps

    def line(i, rows):
        ref, at = (last_ref, 0) if i < 0 else (next_ref, 0) if i == here else (xt_ref, i)
        return ref[at, rows, :]

    for y0 in range(0, here, ROWS):
        for s0 in range(0, states, ROWS):
            rows = slice(s0, s0 + ROWS)
            results = []
            cells = jnp.concatenate([line(y0 + i, rows) for i in range(ROWS)], axis=0)
            along = jnp.dot(cells, ring_ref[...], preferred_element_type=F32)
            before, x = line(y0 - 1, rows).astype(F32), line(y0, rows).astype(F32)
            for i in range(ROWS):
                y = y0 + i
                after = line(y + 1, rows).astype(F32)
                link = jnp.where(early, early_ref[y, rows, :], late_ref[y, rows, :]).astype(F32)
                beside = (before + after) + (core_ref[y, rows, :].astype(F32) + link)
                value = along[i * ROWS : (i + 1) * ROWS] + pot_ref[y : y + 1, :] * x
                results.append(value + added_ref[y, rows, :] - 0.5 * beside)
                before, x = x, after
            turned = jnp.swapaxes(jnp.stack(results, axis=0), 0, 1).astype(BF16)
            out_ref[rows, y0 : y0 + ROWS, :] = turned


def pass_half(all_ref, pass_hbm, sem):
    half = pass_hbm.shape[0]
    copy = start(pltpu.make_async_copy(all_ref.at[pl.ds((1 - (lax.axis_index("domain") & 1)) * half, half)], pass_hbm, sem))
    copy.wait()


def later_kernel(bands, landed, unread, all_ref, pass_hbm, done_ref, sems, pass_sem):
    done_ref[...] = jnp.zeros_like(done_ref)
    count, states = all_ref.shape[0], landed.shape[1]
    loads = [
        start(
            pltpu.make_async_copy(
                landed.at[pl.ds(b * count, count)], all_ref.at[:, pl.ds(b * states, states), :], sems.at[b]
            )
        )
        for b in range(bands)
    ]
    for copy in loads:
        copy.wait()
    pass_half(all_ref, pass_hbm, pass_sem)


def early_kernel(after_ref, unread, *refs):
    pieces, (all_ref, beside_ref, projs_ref, done_ref, sems) = refs[:-5], refs[-5:]
    done_ref[...] = jnp.zeros_like(done_ref)
    states = pieces[0].shape[1]
    count, half, held = all_ref.shape[0] - 1, beside_ref.shape[0], projs_ref.shape[0]
    pairs = []
    for k, piece in enumerate(pieces):
        at = pl.ds(pl.multiple_of((lax.axis_index("band") ^ k) * states, states), states)
        pairs.append((piece.at[pl.ds(0, count)], all_ref.at[pl.ds(0, count), at, :]))
        pairs.append((piece.at[pl.ds(count, half)], beside_ref.at[:, at, :]))
        pairs.append((piece.at[pl.ds(count + half, held)], projs_ref.at[:, at, :]))
    loads = start_all(pairs, sems)
    all_ref[count] = after_ref[0]
    wait_all(loads)


def add_products(row, all_ref, beside_refs, pot_ref, acc):
    half = beside_refs[0].shape[0]
    group = 4
    mine = (lax.axis_index("domain") & 1) * half
    for part, base in ((0, mine), (1, half - mine)):
        for i0 in range(0, half, group):
            xs, ys = [], []
            for i in range(i0, min(i0 + group, half)):
                cell = all_ref[base + i]
                x = cell.astype(F32)
                y = (3.0 + pot_ref[pl.ds(row + base + i, 1), :]) * x - pltpu.roll(x, x.shape[1] - 1, 1)
                y = y - all_ref[base + i + 1].astype(F32)
                if part == 0:
                    for ref in beside_refs:
                        y = y - ref[i].astype(F32)
                xs.append(cell)
                ys.append(y.astype(BF16))
            flat_x = jnp.concatenate(xs, axis=1)
            flat_y = jnp.concatenate(ys, axis=1)
            acc[0] += lax.dot_general(flat_x, flat_x, NT, preferred_element_type=F32)
            acc[1] += lax.dot_general(flat_y, flat_x, NT, preferred_element_type=F32)


def gram_kernel(first, share, all_ref, core_ref, link_ref, pot_ref, unread, acc):
    acc[...] = jnp.zeros_like(acc)
    add_products(lax.axis_index("band") * share + first, all_ref, (core_ref, link_ref), pot_ref, acc)


def final_kernel(bands, share, all_ref, beside_ref, pot_ref, begun_ref, proj_ref, energy_ref, out_ref, acc):
    acc[...] = begun_ref[...]
    add_products(lax.axis_index("band") * share, all_ref, (beside_ref,), pot_ref, acc)
    groups = proj_ref.shape[0]
    first = (lax.axis_index("domain") * bands + lax.axis_index("band")) * groups
    for g in range(groups):
        here = proj_ref[g]
        scaled = (here.astype(F32) * energy_ref[pl.ds(first + g, 1), :]).astype(BF16)
        acc[1] += lax.dot_general(scaled, here, NT, preferred_element_type=F32)
    hamil = 0.5 * (acc[1] + acc[1].T)
    domains = out_ref.shape[0] // bands
    rows, cols = out_ref.shape[1], out_ref.shape[2] // 2
    for c in range(domains):
        for r in range(bands):
            r0, c0 = r * rows, c * cols
            out_ref[c * bands + r, :, :cols] = acc[0, r0 : r0 + rows, c0 : c0 + cols].astype(BF16)
            out_ref[c * bands + r, :, cols:] = hamil[r0 : r0 + rows, c0 : c0 + cols].astype(BF16)


def result_kernel(scale, parts_ref, out_ref):
    total = jnp.sum(parts_ref[...].astype(F32), axis=0) * scale
    cols = out_ref.shape[2]
    out_ref[0] = total[:, :cols]
    out_ref[1] = total[:, cols:]


def local(orbitals, potential, projectors, tile_atom, tile_line, tile_count, energies):
    states, _, lines, cols_z = orbitals.shape
    slots, proj_count, _ = projectors.shape
    atom_total = energies.shape[0]
    domains, bands = lax.axis_size("domain"), lax.axis_size("band")
    total_states = states * bands
    atoms_here = atom_total // domains
    per_group = LANES // proj_count
    groups = atoms_here // per_group
    share = lines // bands
    first = 2 * (share * 3 // 32)
    rest = share - first

    core_pairs = [(i, i ^ 1) for i in range(domains) if i ^ 1 < domains]
    link_pairs = [(i, ((i + 1) ^ 1) - 1) for i in range(1, domains) if ((i + 1) ^ 1) - 1 < domains]
    near_far = [(i, i ^ 2) for i in range(domains) if i ^ 2 < domains]
    next = [(i, ((i + 2) ^ 2) - 2) for i in range(2, domains) if ((i + 2) ^ 2) - 2 < domains]
    far_pairs = [pairs for pairs in (near_far, next) if pairs]

    def swapped(values, axis):
        size = lax.axis_size(axis)
        got = {k: lax.ppermute(values[k - 1], axis, [(i, i ^ k) for i in range(size)]) for k in range(size - 1, 0, -1)}
        return [got[k] for k in range(1, size)]

    field = orbitals.reshape(states, lines, cols_z)
    pot = potential.reshape(lines, cols_z)
    energy = energies.reshape(atom_total // per_group, LANES)
    eye = np.eye(cols_z, dtype=np.float32)
    ring = jnp.asarray(3.0 * eye - 0.5 * (np.roll(eye, 1, axis=0) + np.roll(eye, -1, axis=0)), dtype=BF16)

    late_lines = lines // 2
    line_shape, late_shape = (lines, states, cols_z), (late_lines, states, cols_z)
    xt, early_part, late_part, message = call(
        63,
        functools.partial(pack_kernel, first),
        (),
        [FAR],
        [FAR] * 4,
        [
            (line_shape, BF16),
            ((lines - late_lines, states, cols_z), BF16),
            (late_shape, BF16),
            ((bands * (rest + 1), states, cols_z), BF16),
        ],
        [
            pltpu.VMEM((states, lines, cols_z), BF16),
            pltpu.VMEM(line_shape, BF16),
            copies((bands,)),
            copies((2 * bands + 3,)),
        ],
        (field,),
    )
    landed = lax.all_to_all(message, "band", split_axis=0, concat_axis=0, tiled=True)
    link_early = lax.ppermute(early_part, "domain", link_pairs)
    core_field = lax.ppermute(xt, "domain", core_pairs)

    group_shape = (groups, states, LANES)
    mine, to_core, to_link, *to_far = call(
        63,
        project_kernel,
        (),
        [SCALARS] * 3 + [FAR, PINNED],
        [PINNED] + [WHOLE] * (2 + len(far_pairs)),
        [((3 * groups, states, LANES), BF16)]
        + [((2 * groups, states, LANES), BF16)] * 2
        + [(group_shape, BF16)] * len(far_pairs),
        [
            pltpu.VMEM((3 * atoms_here + 1, proj_count, states), F32),
            pltpu.VMEM((3 * groups, states, LANES), BF16),
            pltpu.VMEM(line_shape, BF16),
            pltpu.VMEM(projectors.shape, BF16),
            copies((5,)),
            copies((3,)),
        ],
        (tile_atom, tile_line, tile_count, xt, projectors),
    )
    from_link = lax.ppermute(to_link, "domain", link_pairs)
    from_far = [lax.ppermute(value, "domain", pairs) for value, pairs in zip(to_far, far_pairs)]
    from_core = lax.ppermute(to_core, "domain", core_pairs)
    (late_part,) = call(
        63,
        hand_on,
        (),
        [UNREAD] * (5 + len(far_pairs)),
        [UNREAD],
        [(late_shape, BF16)],
        [],
        (late_part, from_core, from_link, *from_far, link_early, core_field),
        aliases={0: 0},
    )
    link_late = lax.ppermute(late_part, "domain", link_pairs)
    added, whole = call(
        62,
        functools.partial(nonlocal_kernel, lines, len(far_pairs)),
        (),
        [SCALARS] * 3 + [PINNED, WHOLE, PINNED, WHOLE, WHOLE] + [WHOLE] * len(far_pairs),
        [PINNED, PINNED],
        [(line_shape, F32), (group_shape, BF16)],
        [
            pltpu.VMEM((lines + 1, states, cols_z), F32),
            pltpu.VMEM(group_shape, BF16),
            pltpu.VMEM((3 * groups, states, LANES), BF16),
            pltpu.VMEM((3 * groups, states, LANES), F32),
            pltpu.VMEM((3 * atoms_here, states, proj_count), BF16),
            pltpu.VMEM(projectors.shape, BF16),
            copies((4,)),
        ],
        (tile_atom, tile_line, tile_count, projectors, energy, mine, from_core, from_link, *from_far),
    )
    held = groups // bands
    built_shape = (first + first // 2 + held, states, cols_z)
    own_message, *messages = call(
        62,
        functools.partial(second_kernel, share),
        (),
        [FAR] * 4 + [PINNED],
        [PINNED] + [FAR] * (bands - 1),
        [(built_shape, BF16)] * bands,
        [
            pltpu.VMEM((bands, *built_shape), BF16),
            pltpu.VMEM((bands, first // 2, states, cols_z), BF16),
            pltpu.VMEM((bands, first // 2, states, cols_z), BF16),
            copies((4 * bands,)),
            copies((bands,)),
        ],
        (xt, core_field, link_early, link_late, whole),
    )
    early = swapped(messages, "band")

    later_all, later_pass, later_token = call(
        32,
        functools.partial(later_kernel, bands),
        (),
        [FAR, PINNED],
        [NEAR, FAR, WHOLE],
        [((rest + 1, total_states, cols_z), BF16), ((rest // 2, total_states, cols_z), BF16), ((8, LANES), F32)],
        [copies((bands,)), copies],
        (landed, own_message),
    )
    later_link = lax.ppermute(later_pass, "domain", link_pairs)
    later_core = lax.ppermute(later_pass, "domain", core_pairs)

    span = 2 * ROWS
    steps, early_steps = lines // span, (lines - late_lines) // span
    block = pl.BlockSpec((span, states, cols_z), lambda i: (i, 0, 0))
    applied, done = call(
        32,
        functools.partial(stencil_kernel, early_steps),
        (steps,),
        [
            block,
            pl.BlockSpec((1, states, cols_z), lambda i: (lax.rem(i * span + lines - 1, lines), 0, 0)),
            pl.BlockSpec((1, states, cols_z), lambda i: (lax.rem(i * span + span, lines), 0, 0)),
            block,
            pl.BlockSpec((span, states, cols_z), lambda i: (jnp.minimum(i, early_steps - 1), 0, 0)),
            pl.BlockSpec((span, states, cols_z), lambda i: (jnp.maximum(i - early_steps, 0), 0, 0)),
            block,
            pl.BlockSpec((span, cols_z), lambda i: (i, 0)),
            WHOLE,
            UNREAD,
        ],
        [pl.BlockSpec((states, span, cols_z), lambda i: (0, i, 0)), WHOLE],
        [((states, lines, cols_z), BF16), ((8, LANES), F32)],
        [],
        (
            xt, xt, xt, core_field, link_early, link_late, pltpu.with_memory_space_constraint(added, pltpu.HBM), pot, ring,
            later_token,
        ),
    )

    early_all, early_beside, projs, early_token = call(
        32,
        early_kernel,
        (),
        [NEAR, WHOLE, PINNED] + [FAR] * (bands - 1),
        [NEAR, NEAR, NEAR, WHOLE],
        [
            ((first + 1, total_states, cols_z), BF16),
            ((first // 2, total_states, cols_z), BF16),
            ((held, total_states, LANES), BF16),
            ((8, LANES), F32),
        ],
        [copies((3 * bands,))],
        (later_all, done, own_message, *early),
        micros=30,
    )
    (begun,) = call(
        32,
        functools.partial(gram_kernel, first, share),
        (),
        [NEAR, WHOLE, WHOLE, WHOLE, UNREAD],
        [NEAR],
        [((2, total_states, total_states), F32)],
        [],
        (later_all, later_core, later_link, pot, early_token),
    )
    parts = domains * bands
    (blocks,) = call(
        32,
        functools.partial(final_kernel, bands, share),
        (),
        [NEAR, NEAR, WHOLE, NEAR, NEAR, WHOLE],
        [WHOLE],
        [((parts, states, 2 * total_states // domains), BF16)],
        [pltpu.VMEM((2, total_states, total_states), F32)],
        (early_all, early_beside, pot, begun, projs, energy),
    )
    summed = lax.all_to_all(blocks, ("domain", "band"), split_axis=0, concat_axis=0, tiled=True)
    (subspace,) = call(
        32,
        functools.partial(result_kernel, 1.0 / (lines * cols_z * domains)),
        (),
        [WHOLE],
        [WHOLE],
        [((2, states, total_states // domains), F32)],
        [],
        (summed,),
    )
    return applied.reshape(orbitals.shape), subspace


def solution(mesh):
    in_specs = (
        P("band", ("groups", "domain"), None, None),
        P(("groups", "domain"), None, None),
        P(("groups", "domain"), None, None),
        P(("groups", "domain")),
        P(("groups", "domain")),
        P(("groups", "domain")),
        P("groups", None),
    )
    out_specs = (P("band", ("groups", "domain"), None, None), P(None, ("groups", "band"), "domain"))
    return jax.shard_map(local, mesh=mesh, in_specs=in_specs, out_specs=out_specs, check_vma=False)
```

```python
import functools

import jax
import jax.numpy as jnp
import numpy as np
from jax import lax
from jax.experimental import pallas as pl
from jax.experimental.pallas import tpu as pltpu
from jax.sharding import PartitionSpec as P

F32 = jnp.float32
BF16 = jnp.bfloat16
LANES = 128
ROWS = 16
NT = (((1,), (1,)), ((), ()))
WHOLE = pl.BlockSpec(memory_space=pltpu.VMEM)
NEAR = pl.BlockSpec(memory_space=pltpu.VMEM)
SCALARS = pl.BlockSpec(memory_space=pltpu.SMEM)
FAR = pl.BlockSpec(memory_space=pltpu.HBM)
PINNED = pl.BlockSpec(memory_space=pltpu.HBM)
UNREAD = pl.BlockSpec(memory_space=pl.ANY)
copies = pltpu.SemaphoreType.DMA


def call(room, kernel, grid, in_specs, out_specs, outs, scratch, args, aliases=None, micros=0.001):
    def place(spec):
        return {id(NEAR): pltpu.VMEM, id(PINNED): pltpu.HBM}.get(id(spec))

    args = [
        pltpu.with_memory_space_constraint(arg, place(spec)) if place(spec) else arg
        for spec, arg in zip(in_specs, args)
    ]
    shapes = [(place(spec) or jax.ShapeDtypeStruct)(shape, kind) for spec, (shape, kind) in zip(out_specs, outs)]
    return pl.pallas_call(
        kernel,
        grid=grid,
        out_shape=shapes,
        in_specs=in_specs,
        out_specs=out_specs,
        scratch_shapes=scratch,
        input_output_aliases=aliases or {},
        compiler_params=pltpu.CompilerParams(vmem_limit_bytes=room << 20),
        cost_estimate=pl.CostEstimate(flops=int(micros * 1.1e9), bytes_accessed=1 << 10, transcendentals=0),
    )(*args)


def start(copy):
    copy.start()
    return copy


def start_all(pairs, sems):
    return [start(pltpu.make_async_copy(source, target, sems.at[i])) for i, (source, target) in enumerate(pairs)]


def wait_all(started):
    for copy in started:
        copy.wait()


def hand_on(*refs):
    pass


def pack_kernel(first, x_hbm, xt_hbm, early, late, message, x, xt, in_sems, out_sems):
    states, lines, _ = x.shape
    bands = in_sems.shape[0]
    share = lines // bands
    count = share - first
    loads, sends = [], []
    for c in range(bands):
        where = (slice(None), pl.ds(c * share, share), slice(None))
        loads.append(start(pltpu.make_async_copy(x_hbm.at[where], x.at[where], in_sems.at[c])))

    def send(line, number, target, at):
        copy = pltpu.make_async_copy(
            xt.at[pl.ds(line, number)], target.at[pl.ds(at, number)], out_sems.at[len(sends)]
        )
        sends.append(start(copy))

    for c in range(bands):
        loads[c].wait()
        for y0 in range(c * share, (c + 1) * share, ROWS):
            for s0 in range(0, states, ROWS):
                block = x[s0 : s0 + ROWS, y0 : y0 + ROWS, :].astype(F32)
                turned = jnp.swapaxes(block, 0, 1).astype(BF16)
                xt[y0 : y0 + ROWS, s0 : s0 + ROWS, :] = turned
        send(c * share + first, count, message, c * (count + 1))
        send(c * share, 1, message, (c + bands - 1) % bands * (count + 1) + count)
        if (c + 1) * share == early.shape[0]:
            send(0, early.shape[0], early, 0)
    send(early.shape[0], late.shape[0], late, 0)
    send(0, lines, xt_hbm, 0)
    for copy in sends:
        copy.wait()


def bases(groups):
    domain = lax.axis_index("domain")
    odd, upper = domain & 1, (domain >> 1) & 1
    return [2 * groups * side for side in (1 - odd, odd, 1 - upper, upper)]


def slot_reader(atom_ref, line_ref, count_ref, atoms_here):
    first = (lax.axis_index("domain") - 1) * atoms_here
    live = count_ref[0]

    def slot_at(t):
        return line_ref[t], jnp.clip(atom_ref[t] - first, 0, 3 * atoms_here - 1), t < live

    return slot_at


def energy_table(energy_ref):
    proj_count, atoms = energy_ref.shape
    per_group = LANES // proj_count
    lane = lax.broadcasted_iota(jnp.int32, (proj_count, LANES), 1)
    row = lax.broadcasted_iota(jnp.int32, (proj_count, LANES), 0)
    pick = jnp.where(lane % proj_count == row, 1.0, 0.0).astype(F32)
    spread = jnp.dot(energy_ref[...].T, pick, precision=lax.Precision.HIGHEST, preferred_element_type=F32)
    spread = spread.reshape(atoms // per_group, per_group, LANES)
    lane = lax.broadcasted_iota(jnp.int32, spread.shape, 2)
    atom = lax.broadcasted_iota(jnp.int32, spread.shape, 1)
    return jnp.sum(jnp.where(lane // proj_count == atom, spread, 0.0), axis=1)


def project_kernel(atom_ref, line_ref, count_ref, xt_hbm, p_hbm, mine_hbm, core_hbm, link_hbm, *refs):
    far_hbms, (total, mine_ref, xt_ref, p_ref, sems, out_sems) = refs[:-6], refs[-6:]
    slots, proj_count, _ = p_ref.shape
    groups, states = mine_ref.shape[0] // 3, mine_ref.shape[1]
    per_group = LANES // proj_count
    chunks = sems.shape[0] - 1
    size = slots // chunks
    unroll = 16
    pairs = [(p_hbm.at[pl.ds(c * size, size)], p_ref.at[pl.ds(c * size, size)]) for c in range(chunks)]
    xt_load, *loads = start_all([(xt_hbm, xt_ref), *pairs], sems)

    def clear(i, carry):
        for u in range(per_group):
            total[i * per_group + u] = jnp.zeros_like(total[0])
        return carry

    lax.fori_loop(0, 3 * groups, clear, 0)

    slot_at = slot_reader(atom_ref, line_ref, count_ref, groups * per_group)

    def body(i, carry):
        for u in range(unroll):
            t = i * unroll + u
            line, atom, live = slot_at(t)
            part = lax.dot_general(p_ref[t], xt_ref[line], NT, preferred_element_type=F32)
            total[jnp.where(live, atom, 3 * groups * per_group)] += part
        return carry

    xt_load.wait()
    for c in range(chunks):
        loads[c].wait()
        lax.fori_loop(c * size // unroll, (c + 1) * size // unroll, body, 0)

    for g in range(3 * groups):
        tiles = [total[g * per_group + u] for u in range(per_group)]
        mine_ref[g] = jnp.concatenate(tiles, axis=0).T.astype(BF16)
    sides = bases(groups)
    pairs = [(mine_ref, mine_hbm)]
    for side, far in zip(sides[:2], (core_hbm, link_hbm)):
        pairs.append((mine_ref.at[pl.ds(side, groups)], far.at[pl.ds(0, groups)]))
        pairs.append((mine_ref.at[pl.ds(groups, groups)], far.at[pl.ds(groups, groups)]))
    for side, far in zip(sides[2:], far_hbms):
        pairs.append((mine_ref.at[pl.ds(side, groups)], far))
    wait_all(start_all(pairs, out_sems))


def nonlocal_kernel(
    lines, fars, atom_ref, line_ref, count_ref, p_hbm, energy_ref, mine_hbm, core_ref, link_ref, *refs
):
    far_refs, (out_hbm, whole_hbm, lines_sum, whole_ref, mine_ref, total, table, atoms, p_ref, sems) = (
        refs[:fars],
        refs[fars:],
    )
    slots, proj_count, _ = p_ref.shape
    groups, states = total.shape[0] // 3, total.shape[1]
    per_group = LANES // proj_count
    unroll = 16
    mine_load, load = start_all([(mine_hbm, mine_ref), (p_hbm, p_ref)], sems)
    sends = []

    def clear(i, carry):
        lines_sum[i] = jnp.zeros((states, LANES), F32)
        return carry

    lax.fori_loop(0, lines + 1, clear, 0)
    mine_load.wait()
    total[...] = mine_ref[...].astype(F32)
    sides = bases(groups)
    for g in range(groups):
        total[groups + g] += core_ref[g].astype(F32) + link_ref[g].astype(F32)
        for side, ref in zip(sides[:2], (core_ref, link_ref)):
            total[side + g] += ref[groups + g].astype(F32)
        for side, ref in zip(sides[2:], far_refs):
            total[side + g] += ref[g].astype(F32)
    table[...] = energy_table(energy_ref)
    last = table.shape[0] - 1
    for g in range(3 * groups):
        row = jnp.clip((lax.axis_index("domain") - 1) * groups + g, 0, last)
        tile = (total[g] * table[pl.ds(row, 1), :]).astype(BF16)
        for u in range(per_group):
            atoms[g * per_group + u] = tile[:, u * proj_count : (u + 1) * proj_count]
    for g in range(groups):
        whole_ref[g] = total[groups + g].astype(BF16)
    sends.append(start(pltpu.make_async_copy(whole_ref, whole_hbm, sems.at[2])))
    load.wait()

    slot_at = slot_reader(atom_ref, line_ref, count_ref, groups * per_group)

    def body(i, carry):
        for u in range(unroll):
            t = i * unroll + u
            line, atom, live = slot_at(t)
            part = jnp.dot(atoms[atom], p_ref[t], preferred_element_type=F32)
            lines_sum[jnp.where(live, line, lines)] += part
        return carry

    lax.fori_loop(0, slots // unroll, body, 0)
    sends.append(start(pltpu.make_async_copy(lines_sum.at[pl.ds(0, lines)], out_hbm, sems.at[3])))
    wait_all(sends)


def second_kernel(share, xt_hbm, core_hbm, early_hbm, late_hbm, whole_hbm, *refs):
    messages, (built, cores, links, in_sems, out_sems) = refs[:-5], refs[-5:]
    bands = len(messages)
    half = cores.shape[1]
    first = 2 * half
    held = built.shape[1] - first - half
    early_lines = early_hbm.shape[0]
    mine = (lax.axis_index("domain") & 1) * half
    loads = []

    def load(source, target):
        loads.append(start(pltpu.make_async_copy(source, target, in_sems.at[len(loads)])))

    for k in range(bands):
        to = lax.axis_index("band") ^ k
        begin = to * share
        load(xt_hbm.at[pl.ds(begin, first)], built.at[k, pl.ds(0, first)])
        load(whole_hbm.at[pl.ds(to * held, held)], built.at[k, pl.ds(first + half, held)])
        load(core_hbm.at[pl.ds(begin + mine, half)], cores.at[k])
        sem = in_sems.at[len(loads)]

        @pl.when(begin < early_lines)
        def _():
            pltpu.make_async_copy(early_hbm.at[pl.ds(begin + mine, half)], links.at[k], sem).start()

        @pl.when(begin >= early_lines)
        def _():
            pltpu.make_async_copy(late_hbm.at[pl.ds(begin + mine - early_lines, half)], links.at[k], sem).start()

        loads.append(pltpu.make_async_copy(early_hbm.at[pl.ds(0, half)], links.at[k], sem))
    wait_all(loads)
    sends = []
    for k, message in enumerate(messages):
        for i in range(half):
            built[k, first + i] = (cores[k, i].astype(F32) + links[k, i].astype(F32)).astype(BF16)
        sends.append(start(pltpu.make_async_copy(built.at[k], message, out_sems.at[k])))
    wait_all(sends)


def stencil_kernel(
    early_steps, xt_ref, last_ref, next_ref, core_ref, early_ref, late_ref, added_ref, pot_ref, ring_ref, unread,
    out_ref, token,
):
    states, here, _ = out_ref.shape
    early = pl.program_id(0) < early_steps

    def line(i, rows):
        ref, at = (last_ref, 0) if i < 0 else (next_ref, 0) if i == here else (xt_ref, i)
        return ref[at, rows, :]

    for y0 in range(0, here, ROWS):
        for s0 in range(0, states, ROWS):
            rows = slice(s0, s0 + ROWS)
            results = []
            cells = jnp.concatenate([line(y0 + i, rows) for i in range(ROWS)], axis=0)
            along = jnp.dot(cells, ring_ref[...], preferred_element_type=F32)
            before, x = line(y0 - 1, rows).astype(F32), line(y0, rows).astype(F32)
            for i in range(ROWS):
                y = y0 + i
                after = line(y + 1, rows).astype(F32)
                link = jnp.where(early, early_ref[y, rows, :], late_ref[y, rows, :]).astype(F32)
                beside = (before + after) + (core_ref[y, rows, :].astype(F32) + link)
                value = along[i * ROWS : (i + 1) * ROWS] + pot_ref[y : y + 1, :] * x
                results.append(value + added_ref[y, rows, :] - 0.5 * beside)
                before, x = x, after
            turned = jnp.swapaxes(jnp.stack(results, axis=0), 0, 1).astype(BF16)
            out_ref[rows, y0 : y0 + ROWS, :] = turned


def pass_half(all_ref, pass_hbm, sem):
    half = pass_hbm.shape[0]
    copy = start(pltpu.make_async_copy(all_ref.at[pl.ds((1 - (lax.axis_index("domain") & 1)) * half, half)], pass_hbm, sem))
    copy.wait()


def later_kernel(bands, landed, unread, all_ref, pass_hbm, token, sems, pass_sem):
    count, states = all_ref.shape[0], landed.shape[1]
    loads = [
        start(
            pltpu.make_async_copy(
                landed.at[pl.ds(b * count, count)], all_ref.at[:, pl.ds(b * states, states), :], sems.at[b]
            )
        )
        for b in range(bands)
    ]
    for copy in loads:
        copy.wait()
    pass_half(all_ref, pass_hbm, pass_sem)


def early_kernel(after_ref, energy_ref, unread, *refs):
    pieces, (all_ref, beside_ref, projs_ref, table_ref, token, sems) = refs[:-6], refs[-6:]
    states = pieces[0].shape[1]
    count, half, held = all_ref.shape[0] - 1, beside_ref.shape[0], projs_ref.shape[0]
    pairs = []
    for k, piece in enumerate(pieces):
        at = pl.ds(pl.multiple_of((lax.axis_index("band") ^ k) * states, states), states)
        pairs.append((piece.at[pl.ds(0, count)], all_ref.at[pl.ds(0, count), at, :]))
        pairs.append((piece.at[pl.ds(count, half)], beside_ref.at[:, at, :]))
        pairs.append((piece.at[pl.ds(count + half, held)], projs_ref.at[:, at, :]))
    loads = start_all(pairs, sems)
    all_ref[count] = after_ref[0]
    table_ref[...] = energy_table(energy_ref)
    wait_all(loads)


def add_products(row, all_ref, beside_refs, pot_ref, acc):
    half = beside_refs[0].shape[0]
    group = 4
    mine = (lax.axis_index("domain") & 1) * half
    for part, base in ((0, mine), (1, half - mine)):
        for i0 in range(0, half, group):
            xs, ys = [], []
            for i in range(i0, min(i0 + group, half)):
                cell = all_ref[base + i]
                x = cell.astype(F32)
                y = (3.0 + pot_ref[pl.ds(row + base + i, 1), :]) * x - pltpu.roll(x, x.shape[1] - 1, 1)
                y = y - all_ref[base + i + 1].astype(F32)
                if part == 0:
                    for ref in beside_refs:
                        y = y - ref[i].astype(F32)
                xs.append(cell)
                ys.append(y.astype(BF16))
            flat_x = jnp.concatenate(xs, axis=1)
            flat_y = jnp.concatenate(ys, axis=1)
            acc[0] += lax.dot_general(flat_x, flat_x, NT, preferred_element_type=F32)
            acc[1] += lax.dot_general(flat_y, flat_x, NT, preferred_element_type=F32)


def gram_kernel(first, share, all_ref, core_ref, link_ref, pot_ref, unread, acc):
    acc[...] = jnp.zeros_like(acc)
    add_products(lax.axis_index("band") * share + first, all_ref, (core_ref, link_ref), pot_ref, acc)


def final_kernel(bands, share, all_ref, beside_ref, pot_ref, begun_ref, proj_ref, energy_ref, out_ref, acc):
    acc[...] = begun_ref[...]
    add_products(lax.axis_index("band") * share, all_ref, (beside_ref,), pot_ref, acc)
    groups = proj_ref.shape[0]
    first = (lax.axis_index("domain") * bands + lax.axis_index("band")) * groups
    for g in range(groups):
        here = proj_ref[g]
        scaled = (here.astype(F32) * energy_ref[pl.ds(first + g, 1), :]).astype(BF16)
        acc[1] += lax.dot_general(scaled, here, NT, preferred_element_type=F32)
    hamil = 0.5 * (acc[1] + acc[1].T)
    domains = out_ref.shape[0] // bands
    rows, cols = out_ref.shape[1], out_ref.shape[2] // 2
    for c in range(domains):
        for r in range(bands):
            r0, c0 = r * rows, c * cols
            out_ref[c * bands + r, :, :cols] = acc[0, r0 : r0 + rows, c0 : c0 + cols].astype(BF16)
            out_ref[c * bands + r, :, cols:] = hamil[r0 : r0 + rows, c0 : c0 + cols].astype(BF16)


def result_kernel(scale, parts_ref, out_ref):
    total = jnp.sum(parts_ref[...].astype(F32), axis=0) * scale
    cols = out_ref.shape[2]
    out_ref[0] = total[:, :cols]
    out_ref[1] = total[:, cols:]


def local(orbitals, potential, projectors, tile_atom, tile_line, tile_count, energies):
    states, _, lines, cols_z = orbitals.shape
    slots, proj_count, _ = projectors.shape
    atom_total = energies.shape[0]
    domains, bands = lax.axis_size("domain"), lax.axis_size("band")
    total_states = states * bands
    atoms_here = atom_total // domains
    per_group = LANES // proj_count
    groups = atoms_here // per_group
    share = lines // bands
    first = 2 * (share * 3 // 32)
    rest = share - first

    core_pairs = [(i, i ^ 1) for i in range(domains) if i ^ 1 < domains]
    link_pairs = [(i, ((i + 1) ^ 1) - 1) for i in range(1, domains) if ((i + 1) ^ 1) - 1 < domains]
    near_far = [(i, i ^ 2) for i in range(domains) if i ^ 2 < domains]
    next = [(i, ((i + 2) ^ 2) - 2) for i in range(2, domains) if ((i + 2) ^ 2) - 2 < domains]
    far_pairs = [pairs for pairs in (near_far, next) if pairs]

    def swapped(values, axis):
        size = lax.axis_size(axis)
        got = {k: lax.ppermute(values[k - 1], axis, [(i, i ^ k) for i in range(size)]) for k in range(size - 1, 0, -1)}
        return [got[k] for k in range(1, size)]

    field = orbitals.reshape(states, lines, cols_z)
    pot = potential.reshape(lines, cols_z)
    energy = energies.T
    energy_rows = (atom_total // per_group, LANES)
    token = ((8, LANES), F32)
    eye = np.eye(cols_z, dtype=np.float32)
    ring = jnp.asarray(3.0 * eye - 0.5 * (np.roll(eye, 1, axis=0) + np.roll(eye, -1, axis=0)), dtype=BF16)

    late_lines = lines // 2
    line_shape, late_shape = (lines, states, cols_z), (late_lines, states, cols_z)
    xt, early_part, late_part, message = call(
        63,
        functools.partial(pack_kernel, first),
        (),
        [FAR],
        [FAR] * 4,
        [
            (line_shape, BF16),
            ((lines - late_lines, states, cols_z), BF16),
            (late_shape, BF16),
            ((bands * (rest + 1), states, cols_z), BF16),
        ],
        [
            pltpu.VMEM((states, lines, cols_z), BF16),
            pltpu.VMEM(line_shape, BF16),
            copies((bands,)),
            copies((2 * bands + 3,)),
        ],
        (field,),
    )
    landed = lax.all_to_all(message, "band", split_axis=0, concat_axis=0, tiled=True)
    link_early = lax.ppermute(early_part, "domain", link_pairs)
    core_field = lax.ppermute(xt, "domain", core_pairs)

    group_shape = (groups, states, LANES)
    mine, to_core, to_link, *to_far = call(
        63,
        project_kernel,
        (),
        [SCALARS] * 3 + [FAR, PINNED],
        [PINNED] + [FAR] * (2 + len(far_pairs)),
        [((3 * groups, states, LANES), BF16)]
        + [((2 * groups, states, LANES), BF16)] * 2
        + [(group_shape, BF16)] * len(far_pairs),
        [
            pltpu.VMEM((3 * atoms_here + 1, proj_count, states), F32),
            pltpu.VMEM((3 * groups, states, LANES), BF16),
            pltpu.VMEM(line_shape, BF16),
            pltpu.VMEM(projectors.shape, BF16),
            copies((5,)),
            copies((5 + len(far_pairs),)),
        ],
        (tile_atom, tile_line, tile_count, xt, projectors),
    )
    from_link = lax.ppermute(to_link, "domain", link_pairs)
    from_far = [lax.ppermute(value, "domain", pairs) for value, pairs in zip(to_far, far_pairs)]
    from_core = lax.ppermute(to_core, "domain", core_pairs)
    (late_part,) = call(
        63,
        hand_on,
        (),
        [UNREAD] * (5 + len(far_pairs)),
        [UNREAD],
        [(late_shape, BF16)],
        [],
        (late_part, from_core, from_link, *from_far, link_early, core_field),
        aliases={0: 0},
    )
    link_late = lax.ppermute(late_part, "domain", link_pairs)
    added, whole = call(
        62,
        functools.partial(nonlocal_kernel, lines, len(far_pairs)),
        (),
        [SCALARS] * 3 + [PINNED, WHOLE, PINNED, WHOLE, WHOLE] + [WHOLE] * len(far_pairs),
        [PINNED, PINNED],
        [(line_shape, F32), (group_shape, BF16)],
        [
            pltpu.VMEM((lines + 1, states, cols_z), F32),
            pltpu.VMEM(group_shape, BF16),
            pltpu.VMEM((3 * groups, states, LANES), BF16),
            pltpu.VMEM((3 * groups, states, LANES), F32),
            pltpu.VMEM(energy_rows, F32),
            pltpu.VMEM((3 * atoms_here, states, proj_count), BF16),
            pltpu.VMEM(projectors.shape, BF16),
            copies((4,)),
        ],
        (tile_atom, tile_line, tile_count, projectors, energy, mine, from_core, from_link, *from_far),
    )
    held = groups // bands
    built_shape = (first + first // 2 + held, states, cols_z)
    own_message, *messages = call(
        63,
        functools.partial(second_kernel, share),
        (),
        [FAR] * 4 + [PINNED],
        [PINNED] + [FAR] * (bands - 1),
        [(built_shape, BF16)] * bands,
        [
            pltpu.VMEM((bands, *built_shape), BF16),
            pltpu.VMEM((bands, first // 2, states, cols_z), BF16),
            pltpu.VMEM((bands, first // 2, states, cols_z), BF16),
            copies((4 * bands,)),
            copies((bands,)),
        ],
        (xt, core_field, link_early, link_late, whole),
    )
    early = swapped(messages, "band")

    later_all, later_pass, later_token = call(
        32,
        functools.partial(later_kernel, bands),
        (),
        [FAR, PINNED],
        [NEAR, FAR, PINNED],
        [((rest + 1, total_states, cols_z), BF16), ((rest // 2, total_states, cols_z), BF16), token],
        [copies((bands,)), copies],
        (landed, own_message),
    )
    later_link = lax.ppermute(later_pass, "domain", link_pairs)
    later_core = lax.ppermute(later_pass, "domain", core_pairs)

    span = 2 * ROWS
    steps, early_steps = lines // span, (lines - late_lines) // span
    block = pl.BlockSpec((span, states, cols_z), lambda i: (i, 0, 0))
    applied, done = call(
        62,
        functools.partial(stencil_kernel, early_steps),
        (steps,),
        [
            block,
            pl.BlockSpec((1, states, cols_z), lambda i: (lax.rem(i * span + lines - 1, lines), 0, 0)),
            pl.BlockSpec((1, states, cols_z), lambda i: (lax.rem(i * span + span, lines), 0, 0)),
            block,
            pl.BlockSpec((span, states, cols_z), lambda i: (jnp.minimum(i, early_steps - 1), 0, 0)),
            pl.BlockSpec((span, states, cols_z), lambda i: (jnp.maximum(i - early_steps, 0), 0, 0)),
            block,
            pl.BlockSpec((span, cols_z), lambda i: (i, 0)),
            WHOLE,
            PINNED,
        ],
        [pl.BlockSpec((states, span, cols_z), lambda i: (0, i, 0)), PINNED],
        [((states, lines, cols_z), BF16), token],
        [],
        (
            xt, xt, xt, core_field, link_early, link_late, pltpu.with_memory_space_constraint(added, pltpu.HBM), pot, ring,
            later_token,
        ),
    )

    early_all, early_beside, projs, energy_table_here, early_token = call(
        32,
        early_kernel,
        (),
        [NEAR, WHOLE, PINNED, PINNED] + [FAR] * (bands - 1),
        [NEAR, NEAR, NEAR, NEAR, PINNED],
        [
            ((first + 1, total_states, cols_z), BF16),
            ((first // 2, total_states, cols_z), BF16),
            ((held, total_states, LANES), BF16),
            (energy_rows, F32),
            token,
        ],
        [copies((3 * bands,))],
        (later_all, energy, done, own_message, *early),
        micros=30,
    )
    (begun,) = call(
        32,
        functools.partial(gram_kernel, first, share),
        (),
        [NEAR, WHOLE, WHOLE, WHOLE, PINNED],
        [NEAR],
        [((2, total_states, total_states), F32)],
        [],
        (later_all, later_core, later_link, pot, early_token),
    )
    parts = domains * bands
    (blocks,) = call(
        32,
        functools.partial(final_kernel, bands, share),
        (),
        [NEAR, NEAR, WHOLE, NEAR, NEAR, NEAR],
        [WHOLE],
        [((parts, states, 2 * total_states // domains), BF16)],
        [pltpu.VMEM((2, total_states, total_states), F32)],
        (early_all, early_beside, pot, begun, projs, energy_table_here),
    )
    summed = lax.all_to_all(blocks, ("domain", "band"), split_axis=0, concat_axis=0, tiled=True)
    (subspace,) = call(
        32,
        functools.partial(result_kernel, 1.0 / (lines * cols_z * domains)),
        (),
        [WHOLE],
        [WHOLE],
        [((2, states, total_states // domains), F32)],
        [],
        (summed,),
    )
    return applied.reshape(orbitals.shape), subspace


def solution(mesh):
    in_specs = (
        P("band", ("groups", "domain"), None, None),
        P(("groups", "domain"), None, None),
        P(("groups", "domain"), None, None),
        P(("groups", "domain")),
        P(("groups", "domain")),
        P(("groups", "domain")),
        P("groups", None),
    )
    out_specs = (P("band", ("groups", "domain"), None, None), P(None, ("groups", "band"), "domain"))
    return jax.shard_map(local, mesh=mesh, in_specs=in_specs, out_specs=out_specs, check_vma=False)
```

```python
import functools

import jax
import jax.numpy as jnp
import numpy as np
from jax import lax
from jax.experimental import pallas as pl
from jax.experimental.pallas import tpu as pltpu
from jax.sharding import PartitionSpec as P

F32 = jnp.float32
BF16 = jnp.bfloat16
LANES = 128
ROWS = 16
NT = (((1,), (1,)), ((), ()))
WHOLE = pl.BlockSpec(memory_space=pltpu.VMEM)
NEAR = pl.BlockSpec(memory_space=pltpu.VMEM)
SCALARS = pl.BlockSpec(memory_space=pltpu.SMEM)
FAR = pl.BlockSpec(memory_space=pltpu.HBM)
PINNED = pl.BlockSpec(memory_space=pltpu.HBM)
UNREAD = pl.BlockSpec(memory_space=pl.ANY)
copies = pltpu.SemaphoreType.DMA


def call(room, kernel, grid, in_specs, out_specs, outs, scratch, args, aliases=None, micros=0.001):
    def place(spec):
        return {id(NEAR): pltpu.VMEM, id(PINNED): pltpu.HBM}.get(id(spec))

    args = [
        pltpu.with_memory_space_constraint(arg, place(spec)) if place(spec) else arg
        for spec, arg in zip(in_specs, args)
    ]
    shapes = [(place(spec) or jax.ShapeDtypeStruct)(shape, kind) for spec, (shape, kind) in zip(out_specs, outs)]
    return pl.pallas_call(
        kernel,
        grid=grid,
        out_shape=shapes,
        in_specs=in_specs,
        out_specs=out_specs,
        scratch_shapes=scratch,
        input_output_aliases=aliases or {},
        compiler_params=pltpu.CompilerParams(vmem_limit_bytes=room << 20),
        cost_estimate=pl.CostEstimate(flops=int(micros * 1.1e9), bytes_accessed=1 << 10, transcendentals=0),
    )(*args)


def start(copy):
    copy.start()
    return copy


def start_all(pairs, sems):
    return [start(pltpu.make_async_copy(source, target, sems.at[i])) for i, (source, target) in enumerate(pairs)]


def wait_all(started):
    for copy in started:
        copy.wait()


def hand_on(*refs):
    pass


def pack_kernel(first, x_hbm, xt_hbm, early, late, message, x, xt, in_sems, out_sems):
    states, lines, _ = x.shape
    bands = in_sems.shape[0]
    share = lines // bands
    count = share - first
    loads, sends = [], []
    for c in range(bands):
        where = (slice(None), pl.ds(c * share, share), slice(None))
        loads.append(start(pltpu.make_async_copy(x_hbm.at[where], x.at[where], in_sems.at[c])))

    def send(line, number, target, at):
        copy = pltpu.make_async_copy(
            xt.at[pl.ds(line, number)], target.at[pl.ds(at, number)], out_sems.at[len(sends)]
        )
        sends.append(start(copy))

    for c in range(bands):
        loads[c].wait()
        for y0 in range(c * share, (c + 1) * share, ROWS):
            for s0 in range(0, states, ROWS):
                block = x[s0 : s0 + ROWS, y0 : y0 + ROWS, :].astype(F32)
                turned = jnp.swapaxes(block, 0, 1).astype(BF16)
                xt[y0 : y0 + ROWS, s0 : s0 + ROWS, :] = turned
        send(c * share, share, early if c < bands // 2 else late, c % (bands // 2) * share)
        send(c * share + first, count, message, c * (count + 1))
        send(c * share, 1, message, (c + bands - 1) % bands * (count + 1) + count)
        send(c * share, share, xt_hbm, c * share)
    for copy in sends:
        copy.wait()


def bases(groups):
    domain = lax.axis_index("domain")
    odd, upper = domain & 1, (domain >> 1) & 1
    return [2 * groups * side for side in (1 - odd, odd, 1 - upper, upper)]


def slot_reader(atom_ref, line_ref, count_ref, atoms_here):
    first = (lax.axis_index("domain") - 1) * atoms_here
    live = count_ref[0]

    def slot_at(t):
        return line_ref[t], jnp.clip(atom_ref[t] - first, 0, 3 * atoms_here - 1), t < live

    return slot_at


def energy_table(energy_ref):
    proj_count, atoms = energy_ref.shape
    per_group = LANES // proj_count
    lane = lax.broadcasted_iota(jnp.int32, (proj_count, LANES), 1)
    row = lax.broadcasted_iota(jnp.int32, (proj_count, LANES), 0)
    pick = jnp.where(lane % proj_count == row, 1.0, 0.0).astype(F32)
    spread = jnp.dot(energy_ref[...].T, pick, precision=lax.Precision.HIGHEST, preferred_element_type=F32)
    spread = spread.reshape(atoms // per_group, per_group, LANES)
    lane = lax.broadcasted_iota(jnp.int32, spread.shape, 2)
    atom = lax.broadcasted_iota(jnp.int32, spread.shape, 1)
    return jnp.sum(jnp.where(lane // proj_count == atom, spread, 0.0), axis=1)


def project_kernel(atom_ref, line_ref, count_ref, xt_hbm, p_hbm, mine_hbm, core_hbm, link_hbm, *refs):
    far_hbms, (total, mine_ref, xt_ref, p_ref, sems, out_sems) = refs[:-6], refs[-6:]
    slots, proj_count, _ = p_ref.shape
    groups, states = mine_ref.shape[0] // 3, mine_ref.shape[1]
    per_group = LANES // proj_count
    chunks = sems.shape[0] - 1
    size = slots // chunks
    unroll = 16
    pairs = [(p_hbm.at[pl.ds(c * size, size)], p_ref.at[pl.ds(c * size, size)]) for c in range(chunks)]
    xt_load, *loads = start_all([(xt_hbm, xt_ref), *pairs], sems)

    def clear(i, carry):
        for u in range(per_group):
            total[i * per_group + u] = jnp.zeros_like(total[0])
        return carry

    lax.fori_loop(0, 3 * groups, clear, 0)

    slot_at = slot_reader(atom_ref, line_ref, count_ref, groups * per_group)

    def body(i, carry):
        for u in range(unroll):
            t = i * unroll + u
            line, atom, live = slot_at(t)
            part = lax.dot_general(p_ref[t], xt_ref[line], NT, preferred_element_type=F32)
            total[jnp.where(live, atom, 3 * groups * per_group)] += part
        return carry

    xt_load.wait()
    for c in range(chunks):
        loads[c].wait()
        lax.fori_loop(c * size // unroll, (c + 1) * size // unroll, body, 0)

    for g in range(3 * groups):
        tiles = [total[g * per_group + u] for u in range(per_group)]
        mine_ref[g] = jnp.concatenate(tiles, axis=0).T.astype(BF16)
    sides = bases(groups)
    pairs = [(mine_ref, mine_hbm)]
    for side, far in zip(sides[:2], (core_hbm, link_hbm)):
        pairs.append((mine_ref.at[pl.ds(side, groups)], far.at[pl.ds(0, groups)]))
        pairs.append((mine_ref.at[pl.ds(groups, groups)], far.at[pl.ds(groups, groups)]))
    for side, far in zip(sides[2:], far_hbms):
        pairs.append((mine_ref.at[pl.ds(side, groups)], far))
    wait_all(start_all(pairs, out_sems))


def nonlocal_kernel(
    lines, fars, atom_ref, line_ref, count_ref, p_hbm, energy_ref, mine_hbm, core_ref, link_ref, *refs
):
    far_refs, (out_hbm, whole_hbm, lines_sum, whole_ref, mine_ref, total, table, atoms, p_ref, sems) = (
        refs[:fars],
        refs[fars:],
    )
    slots, proj_count, _ = p_ref.shape
    groups, states = total.shape[0] // 3, total.shape[1]
    per_group = LANES // proj_count
    unroll = 16
    mine_load, load = start_all([(mine_hbm, mine_ref), (p_hbm, p_ref)], sems)
    sends = []

    def clear(i, carry):
        lines_sum[i] = jnp.zeros((states, LANES), F32)
        return carry

    lax.fori_loop(0, lines + 1, clear, 0)
    mine_load.wait()
    total[...] = mine_ref[...].astype(F32)
    sides = bases(groups)
    for g in range(groups):
        total[groups + g] += core_ref[g].astype(F32) + link_ref[g].astype(F32)
        for side, ref in zip(sides[:2], (core_ref, link_ref)):
            total[side + g] += ref[groups + g].astype(F32)
        for side, ref in zip(sides[2:], far_refs):
            total[side + g] += ref[g].astype(F32)
    table[...] = energy_table(energy_ref)
    last = table.shape[0] - 1
    for g in range(3 * groups):
        row = jnp.clip((lax.axis_index("domain") - 1) * groups + g, 0, last)
        tile = (total[g] * table[pl.ds(row, 1), :]).astype(BF16)
        for u in range(per_group):
            atoms[g * per_group + u] = tile[:, u * proj_count : (u + 1) * proj_count]
    for g in range(groups):
        whole_ref[g] = total[groups + g].astype(BF16)
    sends.append(start(pltpu.make_async_copy(whole_ref, whole_hbm, sems.at[2])))
    load.wait()

    slot_at = slot_reader(atom_ref, line_ref, count_ref, groups * per_group)

    def body(i, carry):
        for u in range(unroll):
            t = i * unroll + u
            line, atom, live = slot_at(t)
            part = jnp.dot(atoms[atom], p_ref[t], preferred_element_type=F32)
            lines_sum[jnp.where(live, line, lines)] += part
        return carry

    lax.fori_loop(0, slots // unroll, body, 0)
    sends.append(start(pltpu.make_async_copy(lines_sum.at[pl.ds(0, lines)], out_hbm, sems.at[3])))
    wait_all(sends)


def second_kernel(share, xt_hbm, core_hbm, early_hbm, late_hbm, whole_hbm, *refs):
    messages, (built, cores, links, in_sems, out_sems) = refs[:-5], refs[-5:]
    bands = len(messages)
    half = cores.shape[1]
    first = 2 * half
    held = built.shape[1] - first - half
    early_lines = early_hbm.shape[0]
    mine = (lax.axis_index("domain") & 1) * half
    loads = []

    def load(source, target):
        loads.append(start(pltpu.make_async_copy(source, target, in_sems.at[len(loads)])))

    for k in range(bands):
        to = lax.axis_index("band") ^ k
        begin = to * share
        load(xt_hbm.at[pl.ds(begin, first)], built.at[k, pl.ds(0, first)])
        load(whole_hbm.at[pl.ds(to * held, held)], built.at[k, pl.ds(first + half, held)])
        load(core_hbm.at[pl.ds(begin + mine, half)], cores.at[k])
        sem = in_sems.at[len(loads)]

        @pl.when(begin < early_lines)
        def _():
            pltpu.make_async_copy(early_hbm.at[pl.ds(begin + mine, half)], links.at[k], sem).start()

        @pl.when(begin >= early_lines)
        def _():
            pltpu.make_async_copy(late_hbm.at[pl.ds(begin + mine - early_lines, half)], links.at[k], sem).start()

        loads.append(pltpu.make_async_copy(early_hbm.at[pl.ds(0, half)], links.at[k], sem))
    wait_all(loads)
    sends = []
    for k, message in enumerate(messages):
        for i in range(half):
            built[k, first + i] = (cores[k, i].astype(F32) + links[k, i].astype(F32)).astype(BF16)
        sends.append(start(pltpu.make_async_copy(built.at[k], message, out_sems.at[k])))
    wait_all(sends)


def stencil_kernel(
    early_steps, xt_ref, last_ref, next_ref, core_ref, early_ref, late_ref, added_ref, pot_ref, ring_ref, unread,
    out_ref,
):
    states, here, _ = out_ref.shape
    early = pl.program_id(0) < early_steps

    def line(i, rows):
        ref, at = (last_ref, 0) if i < 0 else (next_ref, 0) if i == here else (xt_ref, i)
        return ref[at, rows, :]

    for y0 in range(0, here, ROWS):
        for s0 in range(0, states, ROWS):
            rows = slice(s0, s0 + ROWS)
            results = []
            cells = jnp.concatenate([line(y0 + i, rows) for i in range(ROWS)], axis=0)
            along = jnp.dot(cells, ring_ref[...], preferred_element_type=F32)
            before, x = line(y0 - 1, rows).astype(F32), line(y0, rows).astype(F32)
            for i in range(ROWS):
                y = y0 + i
                after = line(y + 1, rows).astype(F32)
                link = jnp.where(early, early_ref[y, rows, :], late_ref[y, rows, :]).astype(F32)
                beside = (before + after) + (core_ref[y, rows, :].astype(F32) + link)
                value = along[i * ROWS : (i + 1) * ROWS] + pot_ref[y : y + 1, :] * x
                results.append(value + added_ref[y, rows, :] - 0.5 * beside)
                before, x = x, after
            turned = jnp.swapaxes(jnp.stack(results, axis=0), 0, 1).astype(BF16)
            out_ref[rows, y0 : y0 + ROWS, :] = turned


def pass_half(all_ref, pass_hbm, sem):
    half = pass_hbm.shape[0]
    copy = start(pltpu.make_async_copy(all_ref.at[pl.ds((1 - (lax.axis_index("domain") & 1)) * half, half)], pass_hbm, sem))
    copy.wait()


def later_kernel(bands, landed, unread, all_ref, pass_hbm, sems, pass_sem):
    count, states = all_ref.shape[0], landed.shape[1]
    loads = [
        start(
            pltpu.make_async_copy(
                landed.at[pl.ds(b * count, count)], all_ref.at[:, pl.ds(b * states, states), :], sems.at[b]
            )
        )
        for b in range(bands)
    ]
    for copy in loads:
        copy.wait()
    pass_half(all_ref, pass_hbm, pass_sem)


def early_kernel(after_ref, energy_ref, *refs):
    pieces, (all_ref, beside_ref, projs_ref, table_ref, token, sems) = refs[:-6], refs[-6:]
    states = pieces[0].shape[1]
    count, half, held = all_ref.shape[0] - 1, beside_ref.shape[0], projs_ref.shape[0]
    pairs = []
    for k, piece in enumerate(pieces):
        at = pl.ds(pl.multiple_of((lax.axis_index("band") ^ k) * states, states), states)
        pairs.append((piece.at[pl.ds(0, count)], all_ref.at[pl.ds(0, count), at, :]))
        pairs.append((piece.at[pl.ds(count, half)], beside_ref.at[:, at, :]))
        pairs.append((piece.at[pl.ds(count + half, held)], projs_ref.at[:, at, :]))
    loads = start_all(pairs, sems)
    all_ref[count] = after_ref[0]
    table_ref[...] = energy_table(energy_ref)
    wait_all(loads)


def add_products(row, all_ref, beside_refs, pot_ref, acc):
    half = beside_refs[0].shape[0]
    group = 4
    mine = (lax.axis_index("domain") & 1) * half
    for part, base in ((0, mine), (1, half - mine)):
        for i0 in range(0, half, group):
            xs, ys = [], []
            for i in range(i0, min(i0 + group, half)):
                cell = all_ref[base + i]
                x = cell.astype(F32)
                y = (3.0 + pot_ref[pl.ds(row + base + i, 1), :]) * x - pltpu.roll(x, x.shape[1] - 1, 1)
                y = y - all_ref[base + i + 1].astype(F32)
                if part == 0:
                    for ref in beside_refs:
                        y = y - ref[i].astype(F32)
                xs.append(cell)
                ys.append(y.astype(BF16))
            flat_x = jnp.concatenate(xs, axis=1)
            flat_y = jnp.concatenate(ys, axis=1)
            acc[0] += lax.dot_general(flat_x, flat_x, NT, preferred_element_type=F32)
            acc[1] += lax.dot_general(flat_y, flat_x, NT, preferred_element_type=F32)


def gram_kernel(first, share, all_ref, core_ref, link_ref, pot_ref, unread, acc):
    acc[...] = jnp.zeros_like(acc)
    add_products(lax.axis_index("band") * share + first, all_ref, (core_ref, link_ref), pot_ref, acc)


def final_kernel(bands, share, all_ref, beside_ref, pot_ref, begun_ref, proj_ref, energy_ref, out_ref, token, acc):
    acc[...] = begun_ref[...]
    add_products(lax.axis_index("band") * share, all_ref, (beside_ref,), pot_ref, acc)
    groups = proj_ref.shape[0]
    first = (lax.axis_index("domain") * bands + lax.axis_index("band")) * groups
    for g in range(groups):
        here = proj_ref[g]
        scaled = (here.astype(F32) * energy_ref[pl.ds(first + g, 1), :]).astype(BF16)
        acc[1] += lax.dot_general(scaled, here, NT, preferred_element_type=F32)
    hamil = 0.5 * (acc[1] + acc[1].T)
    domains = out_ref.shape[0] // bands
    rows, cols = out_ref.shape[1], out_ref.shape[2] // 2
    for c in range(domains):
        for r in range(bands):
            r0, c0 = r * rows, c * cols
            out_ref[c * bands + r, :, :cols] = acc[0, r0 : r0 + rows, c0 : c0 + cols].astype(BF16)
            out_ref[c * bands + r, :, cols:] = hamil[r0 : r0 + rows, c0 : c0 + cols].astype(BF16)


def result_kernel(scale, parts_ref, out_ref):
    total = jnp.sum(parts_ref[...].astype(F32), axis=0) * scale
    cols = out_ref.shape[2]
    out_ref[0] = total[:, :cols]
    out_ref[1] = total[:, cols:]


def local(orbitals, potential, projectors, tile_atom, tile_line, tile_count, energies):
    states, _, lines, cols_z = orbitals.shape
    slots, proj_count, _ = projectors.shape
    atom_total = energies.shape[0]
    domains, bands = lax.axis_size("domain"), lax.axis_size("band")
    total_states = states * bands
    atoms_here = atom_total // domains
    per_group = LANES // proj_count
    groups = atoms_here // per_group
    share = lines // bands
    first = 2 * (share * 3 // 32)
    rest = share - first

    core_pairs = [(i, i ^ 1) for i in range(domains) if i ^ 1 < domains]
    link_pairs = [(i, ((i + 1) ^ 1) - 1) for i in range(1, domains) if ((i + 1) ^ 1) - 1 < domains]
    near_far = [(i, i ^ 2) for i in range(domains) if i ^ 2 < domains]
    next = [(i, ((i + 2) ^ 2) - 2) for i in range(2, domains) if ((i + 2) ^ 2) - 2 < domains]
    far_pairs = [pairs for pairs in (near_far, next) if pairs]

    def swapped(values, axis):
        size = lax.axis_size(axis)
        got = {k: lax.ppermute(values[k - 1], axis, [(i, i ^ k) for i in range(size)]) for k in range(size - 1, 0, -1)}
        return [got[k] for k in range(1, size)]

    field = orbitals.reshape(states, lines, cols_z)
    pot = potential.reshape(lines, cols_z)
    energy = energies.T
    energy_rows = (atom_total // per_group, LANES)
    token = ((8, LANES), F32)
    eye = np.eye(cols_z, dtype=np.float32)
    ring = jnp.asarray(3.0 * eye - 0.5 * (np.roll(eye, 1, axis=0) + np.roll(eye, -1, axis=0)), dtype=BF16)

    late_lines = lines // 2
    line_shape, late_shape = (lines, states, cols_z), (late_lines, states, cols_z)
    xt, early_part, late_part, message = call(
        63,
        functools.partial(pack_kernel, first),
        (),
        [FAR],
        [FAR] * 4,
        [
            (line_shape, BF16),
            ((lines - late_lines, states, cols_z), BF16),
            (late_shape, BF16),
            ((bands * (rest + 1), states, cols_z), BF16),
        ],
        [
            pltpu.VMEM((states, lines, cols_z), BF16),
            pltpu.VMEM(line_shape, BF16),
            copies((bands,)),
            copies((4 * bands,)),
        ],
        (field,),
    )
    landed = lax.all_to_all(message, "band", split_axis=0, concat_axis=0, tiled=True)
    link_early = lax.ppermute(early_part, "domain", link_pairs)
    core_field = lax.ppermute(xt, "domain", core_pairs)

    group_shape = (groups, states, LANES)
    mine, to_core, to_link, *to_far = call(
        63,
        project_kernel,
        (),
        [SCALARS] * 3 + [FAR, PINNED],
        [PINNED] + [FAR] * (2 + len(far_pairs)),
        [((3 * groups, states, LANES), BF16)]
        + [((2 * groups, states, LANES), BF16)] * 2
        + [(group_shape, BF16)] * len(far_pairs),
        [
            pltpu.VMEM((3 * atoms_here + 1, proj_count, states), F32),
            pltpu.VMEM((3 * groups, states, LANES), BF16),
            pltpu.VMEM(line_shape, BF16),
            pltpu.VMEM(projectors.shape, BF16),
            copies((5,)),
            copies((5 + len(far_pairs),)),
        ],
        (tile_atom, tile_line, tile_count, xt, projectors),
    )
    from_link = lax.ppermute(to_link, "domain", link_pairs)
    from_far = [lax.ppermute(value, "domain", pairs) for value, pairs in zip(to_far, far_pairs)]
    from_core = lax.ppermute(to_core, "domain", core_pairs)
    (late_part,) = call(
        63,
        hand_on,
        (),
        [UNREAD] * (5 + len(far_pairs)),
        [UNREAD],
        [(late_shape, BF16)],
        [],
        (late_part, from_core, from_link, *from_far, link_early, core_field),
        aliases={0: 0},
    )
    link_late = lax.ppermute(late_part, "domain", link_pairs)
    added, whole = call(
        62,
        functools.partial(nonlocal_kernel, lines, len(far_pairs)),
        (),
        [SCALARS] * 3 + [PINNED, WHOLE, PINNED, WHOLE, WHOLE] + [WHOLE] * len(far_pairs),
        [PINNED, PINNED],
        [(line_shape, F32), (group_shape, BF16)],
        [
            pltpu.VMEM((lines + 1, states, cols_z), F32),
            pltpu.VMEM(group_shape, BF16),
            pltpu.VMEM((3 * groups, states, LANES), BF16),
            pltpu.VMEM((3 * groups, states, LANES), F32),
            pltpu.VMEM(energy_rows, F32),
            pltpu.VMEM((3 * atoms_here, states, proj_count), BF16),
            pltpu.VMEM(projectors.shape, BF16),
            copies((4,)),
        ],
        (tile_atom, tile_line, tile_count, projectors, energy, mine, from_core, from_link, *from_far),
        micros=30,
    )
    held = groups // bands
    built_shape = (first + first // 2 + held, states, cols_z)
    own_message, *messages = call(
        63,
        functools.partial(second_kernel, share),
        (),
        [FAR] * 4 + [PINNED],
        [PINNED] + [FAR] * (bands - 1),
        [(built_shape, BF16)] * bands,
        [
            pltpu.VMEM((bands, *built_shape), BF16),
            pltpu.VMEM((bands, first // 2, states, cols_z), BF16),
            pltpu.VMEM((bands, first // 2, states, cols_z), BF16),
            copies((4 * bands,)),
            copies((bands,)),
        ],
        (xt, core_field, link_early, link_late, whole),
    )
    early = swapped(messages, "band")

    later_all, later_pass = call(
        32,
        functools.partial(later_kernel, bands),
        (),
        [FAR, PINNED],
        [NEAR, FAR],
        [((rest + 1, total_states, cols_z), BF16), ((rest // 2, total_states, cols_z), BF16)],
        [copies((bands,)), copies],
        (landed, own_message),
    )
    later_link = lax.ppermute(later_pass, "domain", link_pairs)
    later_core = lax.ppermute(later_pass, "domain", core_pairs)

    early_all, early_beside, projs, energy_table_here, early_token = call(
        32,
        early_kernel,
        (),
        [NEAR, WHOLE, PINNED] + [FAR] * (bands - 1),
        [NEAR, NEAR, NEAR, NEAR, PINNED],
        [
            ((first + 1, total_states, cols_z), BF16),
            ((first // 2, total_states, cols_z), BF16),
            ((held, total_states, LANES), BF16),
            (energy_rows, F32),
            token,
        ],
        [copies((3 * bands,))],
        (later_all, energy, own_message, *early),
        micros=30,
    )
    (begun,) = call(
        32,
        functools.partial(gram_kernel, first, share),
        (),
        [NEAR, WHOLE, WHOLE, WHOLE, PINNED],
        [NEAR],
        [((2, total_states, total_states), F32)],
        [],
        (later_all, later_core, later_link, pot, early_token),
    )
    parts = domains * bands
    blocks, final_token = call(
        32,
        functools.partial(final_kernel, bands, share),
        (),
        [NEAR, NEAR, WHOLE, NEAR, NEAR, NEAR],
        [WHOLE, PINNED],
        [((parts, states, 2 * total_states // domains), BF16), token],
        [pltpu.VMEM((2, total_states, total_states), F32)],
        (early_all, early_beside, pot, begun, projs, energy_table_here),
    )
    summed = lax.all_to_all(blocks, ("domain", "band"), split_axis=0, concat_axis=0, tiled=True)
    span = 2 * ROWS
    steps, early_steps = lines // span, (lines - late_lines) // span
    block = pl.BlockSpec((span, states, cols_z), lambda i: (i, 0, 0))
    (applied,) = call(
        60,
        functools.partial(stencil_kernel, early_steps),
        (steps,),
        [
            block,
            pl.BlockSpec((1, states, cols_z), lambda i: (lax.rem(i * span + lines - 1, lines), 0, 0)),
            pl.BlockSpec((1, states, cols_z), lambda i: (lax.rem(i * span + span, lines), 0, 0)),
            block,
            pl.BlockSpec((span, states, cols_z), lambda i: (jnp.minimum(i, early_steps - 1), 0, 0)),
            pl.BlockSpec((span, states, cols_z), lambda i: (jnp.maximum(i - early_steps, 0), 0, 0)),
            block,
            pl.BlockSpec((span, cols_z), lambda i: (i, 0)),
            WHOLE,
            PINNED,
        ],
        [pl.BlockSpec((states, span, cols_z), lambda i: (0, i, 0))],
        [((states, lines, cols_z), BF16)],
        [],
        (
            xt, xt, xt, core_field, link_early, link_late, pltpu.with_memory_space_constraint(added, pltpu.HBM), pot, ring,
            final_token,
        ),
    )

    (subspace,) = call(
        32,
        functools.partial(result_kernel, 1.0 / (lines * cols_z * domains)),
        (),
        [WHOLE],
        [WHOLE],
        [((2, states, total_states // domains), F32)],
        [],
        (summed,),
    )
    return applied.reshape(orbitals.shape), subspace


def solution(mesh):
    in_specs = (
        P("band", ("groups", "domain"), None, None),
        P(("groups", "domain"), None, None),
        P(("groups", "domain"), None, None),
        P(("groups", "domain")),
        P(("groups", "domain")),
        P(("groups", "domain")),
        P("groups", None),
    )
    out_specs = (P("band", ("groups", "domain"), None, None), P(None, ("groups", "band"), "domain"))
    return jax.shard_map(local, mesh=mesh, in_specs=in_specs, out_specs=out_specs, check_vma=False)
```

```python
import functools

import jax
import jax.numpy as jnp
import numpy as np
from jax import lax
from jax.experimental import pallas as pl
from jax.experimental.pallas import tpu as pltpu
from jax.sharding import PartitionSpec as P

F32 = jnp.float32
BF16 = jnp.bfloat16
LANES = 128
ROWS = 16
NT = (((1,), (1,)), ((), ()))
WHOLE = pl.BlockSpec(memory_space=pltpu.VMEM)
NEAR = pl.BlockSpec(memory_space=pltpu.VMEM)
SCALARS = pl.BlockSpec(memory_space=pltpu.SMEM)
FAR = pl.BlockSpec(memory_space=pltpu.HBM)
PINNED = pl.BlockSpec(memory_space=pltpu.HBM)
UNREAD = pl.BlockSpec(memory_space=pl.ANY)
copies = pltpu.SemaphoreType.DMA


def call(room, kernel, grid, in_specs, out_specs, outs, scratch, args, aliases=None, micros=0.001):
    def place(spec):
        return {id(NEAR): pltpu.VMEM, id(PINNED): pltpu.HBM}.get(id(spec))

    args = [
        pltpu.with_memory_space_constraint(arg, place(spec)) if place(spec) else arg
        for spec, arg in zip(in_specs, args)
    ]
    shapes = [(place(spec) or jax.ShapeDtypeStruct)(shape, kind) for spec, (shape, kind) in zip(out_specs, outs)]
    return pl.pallas_call(
        kernel,
        grid=grid,
        out_shape=shapes,
        in_specs=in_specs,
        out_specs=out_specs,
        scratch_shapes=scratch,
        input_output_aliases=aliases or {},
        compiler_params=pltpu.CompilerParams(vmem_limit_bytes=room << 20),
        cost_estimate=pl.CostEstimate(flops=int(micros * 1.1e9), bytes_accessed=1 << 10, transcendentals=0),
    )(*args)


def start(copy):
    copy.start()
    return copy


def start_all(pairs, sems):
    return [start(pltpu.make_async_copy(source, target, sems.at[i])) for i, (source, target) in enumerate(pairs)]


def wait_all(started):
    for copy in started:
        copy.wait()


def hand_on(*refs):
    pass


def pack_kernel(first, x_hbm, xt_hbm, early, late, message, x, xt, in_sems, out_sems):
    states, lines, _ = x.shape
    bands = in_sems.shape[0]
    share = lines // bands
    count = share - first
    loads, sends = [], []
    for c in range(bands):
        where = (slice(None), pl.ds(c * share, share), slice(None))
        loads.append(start(pltpu.make_async_copy(x_hbm.at[where], x.at[where], in_sems.at[c])))

    def send(line, number, target, at):
        copy = pltpu.make_async_copy(
            xt.at[pl.ds(line, number)], target.at[pl.ds(at, number)], out_sems.at[len(sends)]
        )
        sends.append(start(copy))

    for c in range(bands):
        loads[c].wait()
        for y0 in range(c * share, (c + 1) * share, ROWS):
            for s0 in range(0, states, ROWS):
                block = x[s0 : s0 + ROWS, y0 : y0 + ROWS, :].astype(F32)
                turned = jnp.swapaxes(block, 0, 1).astype(BF16)
                xt[y0 : y0 + ROWS, s0 : s0 + ROWS, :] = turned
        send(c * share, share, early if c < bands // 2 else late, c % (bands // 2) * share)
        send(c * share + first, count, message, c * (count + 1))
        send(c * share, 1, message, (c + bands - 1) % bands * (count + 1) + count)
        send(c * share, share, xt_hbm, c * share)
    for copy in sends:
        copy.wait()


def bases(groups):
    domain = lax.axis_index("domain")
    odd, upper = domain & 1, (domain >> 1) & 1
    return [2 * groups * side for side in (1 - odd, odd, 1 - upper, upper)]


def slot_reader(atom_ref, line_ref, count_ref, atoms_here):
    first = (lax.axis_index("domain") - 1) * atoms_here
    live = count_ref[0]

    def slot_at(t):
        return line_ref[t], jnp.clip(atom_ref[t] - first, 0, 3 * atoms_here - 1), t < live

    return slot_at


def energy_table(energy_ref):
    proj_count, atoms = energy_ref.shape
    per_group = LANES // proj_count
    lane = lax.broadcasted_iota(jnp.int32, (proj_count, LANES), 1)
    row = lax.broadcasted_iota(jnp.int32, (proj_count, LANES), 0)
    pick = jnp.where(lane % proj_count == row, 1.0, 0.0).astype(F32)
    spread = jnp.dot(energy_ref[...].T, pick, precision=lax.Precision.HIGHEST, preferred_element_type=F32)
    spread = spread.reshape(atoms // per_group, per_group, LANES)
    lane = lax.broadcasted_iota(jnp.int32, spread.shape, 2)
    atom = lax.broadcasted_iota(jnp.int32, spread.shape, 1)
    return jnp.sum(jnp.where(lane // proj_count == atom, spread, 0.0), axis=1)


def project_kernel(atom_ref, line_ref, count_ref, xt_hbm, p_hbm, mine_hbm, core_hbm, link_hbm, *refs):
    far_hbms, (total, mine_ref, xt_ref, p_ref, sems, out_sems) = refs[:-6], refs[-6:]
    slots, proj_count, _ = p_ref.shape
    groups, states = mine_ref.shape[0] // 3, mine_ref.shape[1]
    per_group = LANES // proj_count
    chunks = sems.shape[0] - 1
    size = slots // chunks
    unroll = 16
    pairs = [(p_hbm.at[pl.ds(c * size, size)], p_ref.at[pl.ds(c * size, size)]) for c in range(chunks)]
    xt_load, *loads = start_all([(xt_hbm, xt_ref), *pairs], sems)

    def clear(i, carry):
        for u in range(per_group):
            total[i * per_group + u] = jnp.zeros_like(total[0])
        return carry

    lax.fori_loop(0, 3 * groups, clear, 0)

    slot_at = slot_reader(atom_ref, line_ref, count_ref, groups * per_group)

    def body(i, carry):
        for u in range(unroll):
            t = i * unroll + u
            line, atom, live = slot_at(t)
            part = lax.dot_general(p_ref[t], xt_ref[line], NT, preferred_element_type=F32)
            total[jnp.where(live, atom, 3 * groups * per_group)] += part
        return carry

    xt_load.wait()
    for c in range(chunks):
        loads[c].wait()
        lax.fori_loop(c * size // unroll, (c + 1) * size // unroll, body, 0)

    for g in range(3 * groups):
        tiles = [total[g * per_group + u] for u in range(per_group)]
        mine_ref[g] = jnp.concatenate(tiles, axis=0).T.astype(BF16)
    sides = bases(groups)
    pairs = [(mine_ref, mine_hbm)]
    for side, far in zip(sides[:2], (core_hbm, link_hbm)):
        pairs.append((mine_ref.at[pl.ds(side, groups)], far.at[pl.ds(0, groups)]))
        pairs.append((mine_ref.at[pl.ds(groups, groups)], far.at[pl.ds(groups, groups)]))
    for side, far in zip(sides[2:], far_hbms):
        pairs.append((mine_ref.at[pl.ds(side, groups)], far))
    wait_all(start_all(pairs, out_sems))


def nonlocal_kernel(
    lines, fars, atom_ref, line_ref, count_ref, p_hbm, energy_ref, mine_hbm, core_ref, link_ref, *refs
):
    far_refs, (out_hbm, whole_hbm, lines_sum, whole_ref, mine_ref, total, table, atoms, p_ref, sems) = (
        refs[:fars],
        refs[fars:],
    )
    slots, proj_count, _ = p_ref.shape
    groups, states = total.shape[0] // 3, total.shape[1]
    per_group = LANES // proj_count
    unroll = 16
    mine_load, load = start_all([(mine_hbm, mine_ref), (p_hbm, p_ref)], sems)
    sends = []

    def clear(i, carry):
        lines_sum[i] = jnp.zeros((states, LANES), F32)
        return carry

    lax.fori_loop(0, lines + 1, clear, 0)
    mine_load.wait()
    total[...] = mine_ref[...].astype(F32)
    sides = bases(groups)
    for g in range(groups):
        total[groups + g] += core_ref[g].astype(F32) + link_ref[g].astype(F32)
        for side, ref in zip(sides[:2], (core_ref, link_ref)):
            total[side + g] += ref[groups + g].astype(F32)
        for side, ref in zip(sides[2:], far_refs):
            total[side + g] += ref[g].astype(F32)
    table[...] = energy_table(energy_ref)
    last = table.shape[0] - 1
    for g in range(3 * groups):
        row = jnp.clip((lax.axis_index("domain") - 1) * groups + g, 0, last)
        tile = (total[g] * table[pl.ds(row, 1), :]).astype(BF16)
        for u in range(per_group):
            atoms[g * per_group + u] = tile[:, u * proj_count : (u + 1) * proj_count]
    for g in range(groups):
        whole_ref[g] = total[groups + g].astype(BF16)
    sends.append(start(pltpu.make_async_copy(whole_ref, whole_hbm, sems.at[2])))
    load.wait()

    slot_at = slot_reader(atom_ref, line_ref, count_ref, groups * per_group)

    def body(i, carry):
        for u in range(unroll):
            t = i * unroll + u
            line, atom, live = slot_at(t)
            part = jnp.dot(atoms[atom], p_ref[t], preferred_element_type=F32)
            lines_sum[jnp.where(live, line, lines)] += part
        return carry

    lax.fori_loop(0, slots // unroll, body, 0)
    sends.append(start(pltpu.make_async_copy(lines_sum.at[pl.ds(0, lines)], out_hbm, sems.at[3])))
    wait_all(sends)


def second_kernel(share, xt_hbm, core_hbm, early_hbm, late_hbm, whole_hbm, *refs):
    messages, (built, cores, links, in_sems, out_sems) = refs[:-5], refs[-5:]
    bands = len(messages)
    half = cores.shape[1]
    first = 2 * half
    held = built.shape[1] - first - half
    early_lines = early_hbm.shape[0]
    mine = (lax.axis_index("domain") & 1) * half
    loads = []

    def load(source, target):
        loads.append(start(pltpu.make_async_copy(source, target, in_sems.at[len(loads)])))

    for k in range(bands):
        to = lax.axis_index("band") ^ k
        begin = to * share
        load(xt_hbm.at[pl.ds(begin, first)], built.at[k, pl.ds(0, first)])
        load(whole_hbm.at[pl.ds(to * held, held)], built.at[k, pl.ds(first + half, held)])
        load(core_hbm.at[pl.ds(begin + mine, half)], cores.at[k])
        sem = in_sems.at[len(loads)]

        @pl.when(begin < early_lines)
        def _():
            pltpu.make_async_copy(early_hbm.at[pl.ds(begin + mine, half)], links.at[k], sem).start()

        @pl.when(begin >= early_lines)
        def _():
            pltpu.make_async_copy(late_hbm.at[pl.ds(begin + mine - early_lines, half)], links.at[k], sem).start()

        loads.append(pltpu.make_async_copy(early_hbm.at[pl.ds(0, half)], links.at[k], sem))
    wait_all(loads)
    sends = []
    for k, message in enumerate(messages):
        for i in range(half):
            built[k, first + i] = (cores[k, i].astype(F32) + links[k, i].astype(F32)).astype(BF16)
        sends.append(start(pltpu.make_async_copy(built.at[k], message, out_sems.at[k])))
    wait_all(sends)


def stencil_kernel(
    early_steps, xt_ref, last_ref, next_ref, core_ref, early_ref, late_ref, added_ref, pot_ref, ring_ref, unread,
    out_ref,
):
    states, here, _ = out_ref.shape
    early = pl.program_id(0) < early_steps

    def line(i, rows):
        ref, at = (last_ref, 0) if i < 0 else (next_ref, 0) if i == here else (xt_ref, i)
        return ref[at, rows, :]

    for y0 in range(0, here, ROWS):
        for s0 in range(0, states, ROWS):
            rows = slice(s0, s0 + ROWS)
            results = []
            cells = jnp.concatenate([line(y0 + i, rows) for i in range(ROWS)], axis=0)
            along = jnp.dot(cells, ring_ref[...], preferred_element_type=F32)
            before, x = line(y0 - 1, rows).astype(F32), line(y0, rows).astype(F32)
            for i in range(ROWS):
                y = y0 + i
                after = line(y + 1, rows).astype(F32)
                link = jnp.where(early, early_ref[y, rows, :], late_ref[y, rows, :]).astype(F32)
                beside = (before + after) + (core_ref[y, rows, :].astype(F32) + link)
                value = along[i * ROWS : (i + 1) * ROWS] + pot_ref[y : y + 1, :] * x
                results.append(value + added_ref[y, rows, :] - 0.5 * beside)
                before, x = x, after
            turned = jnp.swapaxes(jnp.stack(results, axis=0), 0, 1).astype(BF16)
            out_ref[rows, y0 : y0 + ROWS, :] = turned


def pass_half(all_ref, pass_hbm, sem):
    half = pass_hbm.shape[0]
    copy = start(pltpu.make_async_copy(all_ref.at[pl.ds((1 - (lax.axis_index("domain") & 1)) * half, half)], pass_hbm, sem))
    copy.wait()


def later_kernel(bands, landed, unread, all_ref, pass_hbm, sems, pass_sem):
    count, states = all_ref.shape[0], landed.shape[1]
    loads = [
        start(
            pltpu.make_async_copy(
                landed.at[pl.ds(b * count, count)], all_ref.at[:, pl.ds(b * states, states), :], sems.at[b]
            )
        )
        for b in range(bands)
    ]
    for copy in loads:
        copy.wait()
    pass_half(all_ref, pass_hbm, pass_sem)


def early_kernel(after_ref, energy_ref, *refs):
    pieces, (all_ref, beside_ref, projs_ref, table_ref, token, sems) = refs[:-6], refs[-6:]
    states = pieces[0].shape[1]
    count, half, held = all_ref.shape[0] - 1, beside_ref.shape[0], projs_ref.shape[0]
    pairs = []
    for k, piece in enumerate(pieces):
        at = pl.ds(pl.multiple_of((lax.axis_index("band") ^ k) * states, states), states)
        pairs.append((piece.at[pl.ds(0, count)], all_ref.at[pl.ds(0, count), at, :]))
        pairs.append((piece.at[pl.ds(count, half)], beside_ref.at[:, at, :]))
        pairs.append((piece.at[pl.ds(count + half, held)], projs_ref.at[:, at, :]))
    loads = start_all(pairs, sems)
    all_ref[count] = after_ref[0]
    table_ref[...] = energy_table(energy_ref)
    wait_all(loads)


def add_products(row, all_ref, beside_refs, pot_ref, acc):
    half = beside_refs[0].shape[0]
    group = 4
    mine = (lax.axis_index("domain") & 1) * half
    for part, base in ((0, mine), (1, half - mine)):
        for i0 in range(0, half, group):
            xs, ys = [], []
            for i in range(i0, min(i0 + group, half)):
                cell = all_ref[base + i]
                x = cell.astype(F32)
                y = (3.0 + pot_ref[pl.ds(row + base + i, 1), :]) * x - pltpu.roll(x, x.shape[1] - 1, 1)
                y = y - all_ref[base + i + 1].astype(F32)
                if part == 0:
                    for ref in beside_refs:
                        y = y - ref[i].astype(F32)
                xs.append(cell)
                ys.append(y.astype(BF16))
            flat_x = jnp.concatenate(xs, axis=1)
            flat_y = jnp.concatenate(ys, axis=1)
            acc[0] += lax.dot_general(flat_x, flat_x, NT, preferred_element_type=F32)
            acc[1] += lax.dot_general(flat_y, flat_x, NT, preferred_element_type=F32)


def gram_kernel(first, share, all_ref, core_ref, link_ref, pot_ref, unread, acc):
    acc[...] = jnp.zeros_like(acc)
    add_products(lax.axis_index("band") * share + first, all_ref, (core_ref, link_ref), pot_ref, acc)


def final_kernel(bands, share, all_ref, beside_ref, pot_ref, begun_ref, proj_ref, energy_ref, out_ref, token, acc):
    acc[...] = begun_ref[...]
    add_products(lax.axis_index("band") * share, all_ref, (beside_ref,), pot_ref, acc)
    groups = proj_ref.shape[0]
    first = (lax.axis_index("domain") * bands + lax.axis_index("band")) * groups
    for g in range(groups):
        here = proj_ref[g]
        scaled = (here.astype(F32) * energy_ref[pl.ds(first + g, 1), :]).astype(BF16)
        acc[1] += lax.dot_general(scaled, here, NT, preferred_element_type=F32)
    hamil = 0.5 * (acc[1] + acc[1].T)
    domains = out_ref.shape[0] // bands
    rows, cols = out_ref.shape[1], out_ref.shape[2] // 2
    for c in range(domains):
        for r in range(bands):
            r0, c0 = r * rows, c * cols
            out_ref[c * bands + r, :, :cols] = acc[0, r0 : r0 + rows, c0 : c0 + cols].astype(BF16)
            out_ref[c * bands + r, :, cols:] = hamil[r0 : r0 + rows, c0 : c0 + cols].astype(BF16)


def result_kernel(scale, parts_ref, out_ref):
    total = jnp.sum(parts_ref[...].astype(F32), axis=0) * scale
    cols = out_ref.shape[2]
    out_ref[0] = total[:, :cols]
    out_ref[1] = total[:, cols:]


def local(orbitals, potential, projectors, tile_atom, tile_line, tile_count, energies):
    states, _, lines, cols_z = orbitals.shape
    slots, proj_count, _ = projectors.shape
    atom_total = energies.shape[0]
    domains, bands = lax.axis_size("domain"), lax.axis_size("band")
    total_states = states * bands
    atoms_here = atom_total // domains
    per_group = LANES // proj_count
    groups = atoms_here // per_group
    share = lines // bands
    first = 2 * (share * 3 // 32)
    rest = share - first

    core_pairs = [(i, i ^ 1) for i in range(domains) if i ^ 1 < domains]
    link_pairs = [(i, ((i + 1) ^ 1) - 1) for i in range(1, domains) if ((i + 1) ^ 1) - 1 < domains]
    near_far = [(i, i ^ 2) for i in range(domains) if i ^ 2 < domains]
    next = [(i, ((i + 2) ^ 2) - 2) for i in range(2, domains) if ((i + 2) ^ 2) - 2 < domains]
    far_pairs = [pairs for pairs in (near_far, next) if pairs]

    def swapped(values, axis):
        size = lax.axis_size(axis)
        got = {k: lax.ppermute(values[k - 1], axis, [(i, i ^ k) for i in range(size)]) for k in range(size - 1, 0, -1)}
        return [got[k] for k in range(1, size)]

    field = orbitals.reshape(states, lines, cols_z)
    pot = potential.reshape(lines, cols_z)
    energy = energies.T
    energy_rows = (atom_total // per_group, LANES)
    token = ((8, LANES), F32)
    eye = np.eye(cols_z, dtype=np.float32)
    ring = jnp.asarray(3.0 * eye - 0.5 * (np.roll(eye, 1, axis=0) + np.roll(eye, -1, axis=0)), dtype=BF16)

    late_lines = lines // 2
    line_shape, late_shape = (lines, states, cols_z), (late_lines, states, cols_z)
    xt, early_part, late_part, message = call(
        63,
        functools.partial(pack_kernel, first),
        (),
        [FAR],
        [FAR] * 4,
        [
            (line_shape, BF16),
            ((lines - late_lines, states, cols_z), BF16),
            (late_shape, BF16),
            ((bands * (rest + 1), states, cols_z), BF16),
        ],
        [
            pltpu.VMEM((states, lines, cols_z), BF16),
            pltpu.VMEM(line_shape, BF16),
            copies((bands,)),
            copies((4 * bands,)),
        ],
        (field,),
    )
    landed = lax.all_to_all(message, "band", split_axis=0, concat_axis=0, tiled=True)
    link_early = lax.ppermute(early_part, "domain", link_pairs)
    core_field = lax.ppermute(xt, "domain", core_pairs)

    group_shape = (groups, states, LANES)
    mine, to_core, to_link, *to_far = call(
        63,
        project_kernel,
        (),
        [SCALARS] * 3 + [FAR, PINNED],
        [PINNED] + [FAR] * (2 + len(far_pairs)),
        [((3 * groups, states, LANES), BF16)]
        + [((2 * groups, states, LANES), BF16)] * 2
        + [(group_shape, BF16)] * len(far_pairs),
        [
            pltpu.VMEM((3 * atoms_here + 1, proj_count, states), F32),
            pltpu.VMEM((3 * groups, states, LANES), BF16),
            pltpu.VMEM(line_shape, BF16),
            pltpu.VMEM(projectors.shape, BF16),
            copies((5,)),
            copies((5 + len(far_pairs),)),
        ],
        (tile_atom, tile_line, tile_count, xt, projectors),
    )
    from_link = lax.ppermute(to_link, "domain", link_pairs)
    from_far = [lax.ppermute(value, "domain", pairs) for value, pairs in zip(to_far, far_pairs)]
    from_core = lax.ppermute(to_core, "domain", core_pairs)
    (late_part,) = call(
        63,
        hand_on,
        (),
        [UNREAD] * (5 + len(far_pairs)),
        [UNREAD],
        [(late_shape, BF16)],
        [],
        (late_part, from_core, from_link, *from_far, link_early, core_field),
        aliases={0: 0},
    )
    link_late = lax.ppermute(late_part, "domain", link_pairs)
    added, whole = call(
        62,
        functools.partial(nonlocal_kernel, lines, len(far_pairs)),
        (),
        [SCALARS] * 3 + [PINNED, WHOLE, PINNED, WHOLE, WHOLE] + [WHOLE] * len(far_pairs),
        [PINNED, PINNED],
        [(line_shape, F32), (group_shape, BF16)],
        [
            pltpu.VMEM((lines + 1, states, cols_z), F32),
            pltpu.VMEM(group_shape, BF16),
            pltpu.VMEM((3 * groups, states, LANES), BF16),
            pltpu.VMEM((3 * groups, states, LANES), F32),
            pltpu.VMEM(energy_rows, F32),
            pltpu.VMEM((3 * atoms_here, states, proj_count), BF16),
            pltpu.VMEM(projectors.shape, BF16),
            copies((4,)),
        ],
        (tile_atom, tile_line, tile_count, projectors, energy, mine, from_core, from_link, *from_far),
        micros=8,
    )
    held = groups // bands
    built_shape = (first + first // 2 + held, states, cols_z)
    own_message, *messages = call(
        63,
        functools.partial(second_kernel, share),
        (),
        [FAR] * 4 + [PINNED],
        [PINNED] + [FAR] * (bands - 1),
        [(built_shape, BF16)] * bands,
        [
            pltpu.VMEM((bands, *built_shape), BF16),
            pltpu.VMEM((bands, first // 2, states, cols_z), BF16),
            pltpu.VMEM((bands, first // 2, states, cols_z), BF16),
            copies((4 * bands,)),
            copies((bands,)),
        ],
        (xt, core_field, link_early, link_late, whole),
    )
    early = swapped(messages, "band")

    later_all, later_pass = call(
        32,
        functools.partial(later_kernel, bands),
        (),
        [FAR, PINNED],
        [NEAR, FAR],
        [((rest + 1, total_states, cols_z), BF16), ((rest // 2, total_states, cols_z), BF16)],
        [copies((bands,)), copies],
        (landed, own_message),
    )
    later_link = lax.ppermute(later_pass, "domain", link_pairs)
    later_core = lax.ppermute(later_pass, "domain", core_pairs)

    early_all, early_beside, projs, energy_table_here, early_token = call(
        32,
        early_kernel,
        (),
        [NEAR, WHOLE, PINNED] + [FAR] * (bands - 1),
        [NEAR, NEAR, NEAR, NEAR, PINNED],
        [
            ((first + 1, total_states, cols_z), BF16),
            ((first // 2, total_states, cols_z), BF16),
            ((held, total_states, LANES), BF16),
            (energy_rows, F32),
            token,
        ],
        [copies((3 * bands,))],
        (later_all, energy, own_message, *early),
        micros=30,
    )
    (begun,) = call(
        32,
        functools.partial(gram_kernel, first, share),
        (),
        [NEAR, WHOLE, WHOLE, WHOLE, PINNED],
        [NEAR],
        [((2, total_states, total_states), F32)],
        [],
        (later_all, later_core, later_link, pot, early_token),
    )
    parts = domains * bands
    blocks, final_token = call(
        32,
        functools.partial(final_kernel, bands, share),
        (),
        [NEAR, NEAR, WHOLE, NEAR, NEAR, NEAR],
        [WHOLE, PINNED],
        [((parts, states, 2 * total_states // domains), BF16), token],
        [pltpu.VMEM((2, total_states, total_states), F32)],
        (early_all, early_beside, pot, begun, projs, energy_table_here),
    )
    summed = lax.all_to_all(blocks, ("domain", "band"), split_axis=0, concat_axis=0, tiled=True)
    span = 2 * ROWS
    steps, early_steps = lines // span, (lines - late_lines) // span
    block = pl.BlockSpec((span, states, cols_z), lambda i: (i, 0, 0))
    (applied,) = call(
        60,
        functools.partial(stencil_kernel, early_steps),
        (steps,),
        [
            block,
            pl.BlockSpec((1, states, cols_z), lambda i: (lax.rem(i * span + lines - 1, lines), 0, 0)),
            pl.BlockSpec((1, states, cols_z), lambda i: (lax.rem(i * span + span, lines), 0, 0)),
            block,
            pl.BlockSpec((span, states, cols_z), lambda i: (jnp.minimum(i, early_steps - 1), 0, 0)),
            pl.BlockSpec((span, states, cols_z), lambda i: (jnp.maximum(i - early_steps, 0), 0, 0)),
            block,
            pl.BlockSpec((span, cols_z), lambda i: (i, 0)),
            WHOLE,
            PINNED,
        ],
        [pl.BlockSpec((states, span, cols_z), lambda i: (0, i, 0))],
        [((states, lines, cols_z), BF16)],
        [],
        (
            xt, xt, xt, core_field, link_early, link_late, pltpu.with_memory_space_constraint(added, pltpu.HBM), pot, ring,
            final_token,
        ),
    )

    (subspace,) = call(
        32,
        functools.partial(result_kernel, 1.0 / (lines * cols_z * domains)),
        (),
        [WHOLE],
        [WHOLE],
        [((2, states, total_states // domains), F32)],
        [],
        (summed,),
    )
    return applied.reshape(orbitals.shape), subspace


def solution(mesh):
    in_specs = (
        P("band", ("groups", "domain"), None, None),
        P(("groups", "domain"), None, None),
        P(("groups", "domain"), None, None),
        P(("groups", "domain")),
        P(("groups", "domain")),
        P(("groups", "domain")),
        P("groups", None),
    )
    out_specs = (P("band", ("groups", "domain"), None, None), P(None, ("groups", "band"), "domain"))
    return jax.shard_map(local, mesh=mesh, in_specs=in_specs, out_specs=out_specs, check_vma=False)
```

```python
import functools

import jax
import jax.numpy as jnp
import numpy as np
from jax import lax
from jax.experimental import pallas as pl
from jax.experimental.pallas import tpu as pltpu
from jax.sharding import PartitionSpec as P

F32 = jnp.float32
BF16 = jnp.bfloat16
LANES = 128
ROWS = 16
NT = (((1,), (1,)), ((), ()))
WHOLE = pl.BlockSpec(memory_space=pltpu.VMEM)
NEAR = pl.BlockSpec(memory_space=pltpu.VMEM)
SCALARS = pl.BlockSpec(memory_space=pltpu.SMEM)
FAR = pl.BlockSpec(memory_space=pltpu.HBM)
PINNED = pl.BlockSpec(memory_space=pltpu.HBM)
UNREAD = pl.BlockSpec(memory_space=pl.ANY)
copies = pltpu.SemaphoreType.DMA


def call(room, kernel, grid, in_specs, out_specs, outs, scratch, args, aliases=None, micros=0.001):
    def place(spec):
        return {id(NEAR): pltpu.VMEM, id(PINNED): pltpu.HBM}.get(id(spec))

    args = [
        pltpu.with_memory_space_constraint(arg, place(spec)) if place(spec) else arg
        for spec, arg in zip(in_specs, args)
    ]
    shapes = [(place(spec) or jax.ShapeDtypeStruct)(shape, kind) for spec, (shape, kind) in zip(out_specs, outs)]
    return pl.pallas_call(
        kernel,
        grid=grid,
        out_shape=shapes,
        in_specs=in_specs,
        out_specs=out_specs,
        scratch_shapes=scratch,
        input_output_aliases=aliases or {},
        compiler_params=pltpu.CompilerParams(vmem_limit_bytes=room << 20),
        cost_estimate=pl.CostEstimate(flops=int(micros * 1.1e9), bytes_accessed=1 << 10, transcendentals=0),
    )(*args)


def start(copy):
    copy.start()
    return copy


def start_all(pairs, sems):
    return [start(pltpu.make_async_copy(source, target, sems.at[i])) for i, (source, target) in enumerate(pairs)]


def wait_all(started):
    for copy in started:
        copy.wait()


def hand_on(*refs):
    pass


def pack_kernel(first, x_hbm, xt_hbm, early, late, message, x, xt, in_sems, out_sems):
    states, lines, _ = x.shape
    bands = in_sems.shape[0]
    share = lines // bands
    count = share - first
    loads, sends = [], []
    for c in range(bands):
        where = (slice(None), pl.ds(c * share, share), slice(None))
        loads.append(start(pltpu.make_async_copy(x_hbm.at[where], x.at[where], in_sems.at[c])))

    def send(line, number, target, at):
        copy = pltpu.make_async_copy(
            xt.at[pl.ds(line, number)], target.at[pl.ds(at, number)], out_sems.at[len(sends)]
        )
        sends.append(start(copy))

    for c in range(bands):
        loads[c].wait()
        for y0 in range(c * share, (c + 1) * share, ROWS):
            for s0 in range(0, states, ROWS):
                block = x[s0 : s0 + ROWS, y0 : y0 + ROWS, :].astype(F32)
                turned = jnp.swapaxes(block, 0, 1).astype(BF16)
                xt[y0 : y0 + ROWS, s0 : s0 + ROWS, :] = turned
        send(c * share, share, early if c < bands // 2 else late, c % (bands // 2) * share)
        send(c * share + first, count, message, c * (count + 1))
        send(c * share, 1, message, (c + bands - 1) % bands * (count + 1) + count)
        send(c * share, share, xt_hbm, c * share)
    for copy in sends:
        copy.wait()


def bases(groups):
    domain = lax.axis_index("domain")
    odd, upper = domain & 1, (domain >> 1) & 1
    return [2 * groups * side for side in (1 - odd, odd, 1 - upper, upper)]


def slot_reader(atom_ref, line_ref, count_ref, atoms_here):
    first = (lax.axis_index("domain") - 1) * atoms_here
    live = count_ref[0]

    def slot_at(t):
        return line_ref[t], jnp.clip(atom_ref[t] - first, 0, 3 * atoms_here - 1), t < live

    return slot_at


def energy_table(energy_ref):
    proj_count, atoms = energy_ref.shape
    per_group = LANES // proj_count
    lane = lax.broadcasted_iota(jnp.int32, (proj_count, LANES), 1)
    row = lax.broadcasted_iota(jnp.int32, (proj_count, LANES), 0)
    pick = jnp.where(lane % proj_count == row, 1.0, 0.0).astype(F32)
    spread = jnp.dot(energy_ref[...].T, pick, precision=lax.Precision.HIGHEST, preferred_element_type=F32)
    spread = spread.reshape(atoms // per_group, per_group, LANES)
    lane = lax.broadcasted_iota(jnp.int32, spread.shape, 2)
    atom = lax.broadcasted_iota(jnp.int32, spread.shape, 1)
    return jnp.sum(jnp.where(lane // proj_count == atom, spread, 0.0), axis=1)


def project_kernel(atom_ref, line_ref, count_ref, xt_hbm, p_hbm, mine_hbm, core_hbm, link_hbm, *refs):
    far_hbms, (total, mine_ref, xt_ref, p_ref, sems, out_sems) = refs[:-6], refs[-6:]
    slots, proj_count, _ = p_ref.shape
    groups, states = mine_ref.shape[0] // 3, mine_ref.shape[1]
    per_group = LANES // proj_count
    chunks = sems.shape[0] - 1
    size = slots // chunks
    unroll = 16
    pairs = [(p_hbm.at[pl.ds(c * size, size)], p_ref.at[pl.ds(c * size, size)]) for c in range(chunks)]
    xt_load, *loads = start_all([(xt_hbm, xt_ref), *pairs], sems)

    def clear(i, carry):
        for u in range(per_group):
            total[i * per_group + u] = jnp.zeros_like(total[0])
        return carry

    lax.fori_loop(0, 3 * groups, clear, 0)

    slot_at = slot_reader(atom_ref, line_ref, count_ref, groups * per_group)

    def body(i, carry):
        for u in range(unroll):
            t = i * unroll + u
            line, atom, live = slot_at(t)
            part = lax.dot_general(p_ref[t], xt_ref[line], NT, preferred_element_type=F32)
            total[jnp.where(live, atom, 3 * groups * per_group)] += part
        return carry

    xt_load.wait()
    for c in range(chunks):
        loads[c].wait()
        lax.fori_loop(c * size // unroll, (c + 1) * size // unroll, body, 0)

    for g in range(3 * groups):
        tiles = [total[g * per_group + u] for u in range(per_group)]
        mine_ref[g] = jnp.concatenate(tiles, axis=0).T.astype(BF16)
    sides = bases(groups)
    pairs = [(mine_ref, mine_hbm)]
    for side, far in zip(sides[:2], (core_hbm, link_hbm)):
        pairs.append((mine_ref.at[pl.ds(side, groups)], far.at[pl.ds(0, groups)]))
        pairs.append((mine_ref.at[pl.ds(groups, groups)], far.at[pl.ds(groups, groups)]))
    for side, far in zip(sides[2:], far_hbms):
        pairs.append((mine_ref.at[pl.ds(side, groups)], far))
    wait_all(start_all(pairs, out_sems))


def nonlocal_kernel(
    lines, fars, atom_ref, line_ref, count_ref, p_hbm, energy_ref, mine_hbm, core_ref, link_ref, *refs
):
    far_refs, (out_hbm, whole_hbm, lines_sum, whole_ref, mine_ref, total, table, atoms, p_ref, sems) = (
        refs[:fars],
        refs[fars:],
    )
    slots, proj_count, _ = p_ref.shape
    groups, states = total.shape[0] // 3, total.shape[1]
    per_group = LANES // proj_count
    unroll = 16
    mine_load, load = start_all([(mine_hbm, mine_ref), (p_hbm, p_ref)], sems)
    sends = []

    def clear(i, carry):
        lines_sum[i] = jnp.zeros((states, LANES), F32)
        return carry

    lax.fori_loop(0, lines + 1, clear, 0)
    mine_load.wait()
    total[...] = mine_ref[...].astype(F32)
    sides = bases(groups)
    for g in range(groups):
        total[groups + g] += core_ref[g].astype(F32) + link_ref[g].astype(F32)
        for side, ref in zip(sides[:2], (core_ref, link_ref)):
            total[side + g] += ref[groups + g].astype(F32)
        for side, ref in zip(sides[2:], far_refs):
            total[side + g] += ref[g].astype(F32)
    table[...] = energy_table(energy_ref)
    last = table.shape[0] - 1
    for g in range(3 * groups):
        row = jnp.clip((lax.axis_index("domain") - 1) * groups + g, 0, last)
        tile = (total[g] * table[pl.ds(row, 1), :]).astype(BF16)
        for u in range(per_group):
            atoms[g * per_group + u] = tile[:, u * proj_count : (u + 1) * proj_count]
    for g in range(groups):
        whole_ref[g] = total[groups + g].astype(BF16)
    sends.append(start(pltpu.make_async_copy(whole_ref, whole_hbm, sems.at[2])))
    load.wait()

    slot_at = slot_reader(atom_ref, line_ref, count_ref, groups * per_group)

    def body(i, carry):
        for u in range(unroll):
            t = i * unroll + u
            line, atom, live = slot_at(t)
            part = jnp.dot(atoms[atom], p_ref[t], preferred_element_type=F32)
            lines_sum[jnp.where(live, line, lines)] += part
        return carry

    lax.fori_loop(0, slots // unroll, body, 0)
    sends.append(start(pltpu.make_async_copy(lines_sum.at[pl.ds(0, lines)], out_hbm, sems.at[3])))
    wait_all(sends)


def second_kernel(share, xt_hbm, core_hbm, early_hbm, late_hbm, whole_hbm, *refs):
    messages, (built, cores, links, in_sems, out_sems) = refs[:-5], refs[-5:]
    bands = len(messages)
    half = cores.shape[1]
    first = 2 * half
    held = built.shape[1] - first - half
    early_lines = early_hbm.shape[0]
    mine = (lax.axis_index("domain") & 1) * half
    loads = []

    def load(source, target):
        loads.append(start(pltpu.make_async_copy(source, target, in_sems.at[len(loads)])))

    for k in range(bands):
        to = lax.axis_index("band") ^ k
        begin = to * share
        load(xt_hbm.at[pl.ds(begin, first)], built.at[k, pl.ds(0, first)])
        load(whole_hbm.at[pl.ds(to * held, held)], built.at[k, pl.ds(first + half, held)])
        load(core_hbm.at[pl.ds(begin + mine, half)], cores.at[k])
        sem = in_sems.at[len(loads)]

        @pl.when(begin < early_lines)
        def _():
            pltpu.make_async_copy(early_hbm.at[pl.ds(begin + mine, half)], links.at[k], sem).start()

        @pl.when(begin >= early_lines)
        def _():
            pltpu.make_async_copy(late_hbm.at[pl.ds(begin + mine - early_lines, half)], links.at[k], sem).start()

        loads.append(pltpu.make_async_copy(early_hbm.at[pl.ds(0, half)], links.at[k], sem))
    wait_all(loads)
    sends = []
    for k, message in enumerate(messages):
        for i in range(half):
            built[k, first + i] = (cores[k, i].astype(F32) + links[k, i].astype(F32)).astype(BF16)
        sends.append(start(pltpu.make_async_copy(built.at[k], message, out_sems.at[k])))
    wait_all(sends)


def stencil_kernel(xt_ref, last_ref, next_ref, core_ref, link_ref, added_ref, pot_ref, ring_ref, *refs):
    out_ref = refs[-2]
    states, here, _ = out_ref.shape

    def line(i, rows):
        ref, at = (last_ref, 0) if i < 0 else (next_ref, 0) if i == here else (xt_ref, i)
        return ref[at, rows, :]

    for y0 in range(0, here, ROWS):
        for s0 in range(0, states, ROWS):
            rows = slice(s0, s0 + ROWS)
            results = []
            cells = jnp.concatenate([line(y0 + i, rows) for i in range(ROWS)], axis=0)
            along = jnp.dot(cells, ring_ref[...], preferred_element_type=F32)
            before, x = line(y0 - 1, rows).astype(F32), line(y0, rows).astype(F32)
            for i in range(ROWS):
                y = y0 + i
                after = line(y + 1, rows).astype(F32)
                beside = (before + after) + (core_ref[y, rows, :].astype(F32) + link_ref[y, rows, :].astype(F32))
                value = along[i * ROWS : (i + 1) * ROWS] + pot_ref[y : y + 1, :] * x
                results.append(value + added_ref[y, rows, :] - 0.5 * beside)
                before, x = x, after
            turned = jnp.swapaxes(jnp.stack(results, axis=0), 0, 1).astype(BF16)
            out_ref[rows, y0 : y0 + ROWS, :] = turned


def pass_half(all_ref, pass_hbm, sem):
    half = pass_hbm.shape[0]
    copy = start(pltpu.make_async_copy(all_ref.at[pl.ds((1 - (lax.axis_index("domain") & 1)) * half, half)], pass_hbm, sem))
    copy.wait()


def later_kernel(bands, landed, unread, all_ref, pass_hbm, token, sems, pass_sem):
    count, states = all_ref.shape[0], landed.shape[1]
    loads = [
        start(
            pltpu.make_async_copy(
                landed.at[pl.ds(b * count, count)], all_ref.at[:, pl.ds(b * states, states), :], sems.at[b]
            )
        )
        for b in range(bands)
    ]
    for copy in loads:
        copy.wait()
    pass_half(all_ref, pass_hbm, pass_sem)


def early_kernel(after_ref, energy_ref, unread, *refs):
    pieces, (all_ref, beside_ref, projs_ref, table_ref, token, sems) = refs[:-6], refs[-6:]
    states = pieces[0].shape[1]
    count, half, held = all_ref.shape[0] - 1, beside_ref.shape[0], projs_ref.shape[0]
    pairs = []
    for k, piece in enumerate(pieces):
        at = pl.ds(pl.multiple_of((lax.axis_index("band") ^ k) * states, states), states)
        pairs.append((piece.at[pl.ds(0, count)], all_ref.at[pl.ds(0, count), at, :]))
        pairs.append((piece.at[pl.ds(count, half)], beside_ref.at[:, at, :]))
        pairs.append((piece.at[pl.ds(count + half, held)], projs_ref.at[:, at, :]))
    loads = start_all(pairs, sems)
    all_ref[count] = after_ref[0]
    table_ref[...] = energy_table(energy_ref)
    wait_all(loads)


def add_products(row, all_ref, beside_refs, pot_ref, acc):
    half = beside_refs[0].shape[0]
    group = 4
    mine = (lax.axis_index("domain") & 1) * half
    for part, base in ((0, mine), (1, half - mine)):
        for i0 in range(0, half, group):
            xs, ys = [], []
            for i in range(i0, min(i0 + group, half)):
                cell = all_ref[base + i]
                x = cell.astype(F32)
                y = (3.0 + pot_ref[pl.ds(row + base + i, 1), :]) * x - pltpu.roll(x, x.shape[1] - 1, 1)
                y = y - all_ref[base + i + 1].astype(F32)
                if part == 0:
                    for ref in beside_refs:
                        y = y - ref[i].astype(F32)
                xs.append(cell)
                ys.append(y.astype(BF16))
            flat_x = jnp.concatenate(xs, axis=1)
            flat_y = jnp.concatenate(ys, axis=1)
            acc[0] += lax.dot_general(flat_x, flat_x, NT, preferred_element_type=F32)
            acc[1] += lax.dot_general(flat_y, flat_x, NT, preferred_element_type=F32)


def gram_kernel(first, share, all_ref, core_ref, link_ref, pot_ref, unread, acc):
    acc[...] = jnp.zeros_like(acc)
    add_products(lax.axis_index("band") * share + first, all_ref, (core_ref, link_ref), pot_ref, acc)


def final_kernel(bands, share, all_ref, beside_ref, pot_ref, begun_ref, proj_ref, energy_ref, out_ref, token, acc):
    acc[...] = begun_ref[...]
    add_products(lax.axis_index("band") * share, all_ref, (beside_ref,), pot_ref, acc)
    groups = proj_ref.shape[0]
    first = (lax.axis_index("domain") * bands + lax.axis_index("band")) * groups
    for g in range(groups):
        here = proj_ref[g]
        scaled = (here.astype(F32) * energy_ref[pl.ds(first + g, 1), :]).astype(BF16)
        acc[1] += lax.dot_general(scaled, here, NT, preferred_element_type=F32)
    hamil = 0.5 * (acc[1] + acc[1].T)
    domains = out_ref.shape[0] // bands
    rows, cols = out_ref.shape[1], out_ref.shape[2] // 2
    for c in range(domains):
        for r in range(bands):
            r0, c0 = r * rows, c * cols
            out_ref[c * bands + r, :, :cols] = acc[0, r0 : r0 + rows, c0 : c0 + cols].astype(BF16)
            out_ref[c * bands + r, :, cols:] = hamil[r0 : r0 + rows, c0 : c0 + cols].astype(BF16)


def result_kernel(scale, parts_ref, out_ref):
    total = jnp.sum(parts_ref[...].astype(F32), axis=0) * scale
    cols = out_ref.shape[2]
    out_ref[0] = total[:, :cols]
    out_ref[1] = total[:, cols:]


def local(orbitals, potential, projectors, tile_atom, tile_line, tile_count, energies):
    states, _, lines, cols_z = orbitals.shape
    slots, proj_count, _ = projectors.shape
    atom_total = energies.shape[0]
    domains, bands = lax.axis_size("domain"), lax.axis_size("band")
    total_states = states * bands
    atoms_here = atom_total // domains
    per_group = LANES // proj_count
    groups = atoms_here // per_group
    share = lines // bands
    first = 2 * (share * 3 // 32)
    rest = share - first

    core_pairs = [(i, i ^ 1) for i in range(domains) if i ^ 1 < domains]
    link_pairs = [(i, ((i + 1) ^ 1) - 1) for i in range(1, domains) if ((i + 1) ^ 1) - 1 < domains]
    near_far = [(i, i ^ 2) for i in range(domains) if i ^ 2 < domains]
    next = [(i, ((i + 2) ^ 2) - 2) for i in range(2, domains) if ((i + 2) ^ 2) - 2 < domains]
    far_pairs = [pairs for pairs in (near_far, next) if pairs]

    def swapped(values, axis):
        size = lax.axis_size(axis)
        got = {k: lax.ppermute(values[k - 1], axis, [(i, i ^ k) for i in range(size)]) for k in range(size - 1, 0, -1)}
        return [got[k] for k in range(1, size)]

    field = orbitals.reshape(states, lines, cols_z)
    pot = potential.reshape(lines, cols_z)
    energy = energies.T
    energy_rows = (atom_total // per_group, LANES)
    token = ((8, LANES), F32)
    eye = np.eye(cols_z, dtype=np.float32)
    ring = jnp.asarray(3.0 * eye - 0.5 * (np.roll(eye, 1, axis=0) + np.roll(eye, -1, axis=0)), dtype=BF16)

    late_lines = lines // 2
    line_shape, late_shape = (lines, states, cols_z), (late_lines, states, cols_z)
    xt, early_part, late_part, message = call(
        63,
        functools.partial(pack_kernel, first),
        (),
        [FAR],
        [FAR] * 4,
        [
            (line_shape, BF16),
            ((lines - late_lines, states, cols_z), BF16),
            (late_shape, BF16),
            ((bands * (rest + 1), states, cols_z), BF16),
        ],
        [
            pltpu.VMEM((states, lines, cols_z), BF16),
            pltpu.VMEM(line_shape, BF16),
            copies((bands,)),
            copies((4 * bands,)),
        ],
        (field,),
    )
    landed = lax.all_to_all(message, "band", split_axis=0, concat_axis=0, tiled=True)
    link_early = lax.ppermute(early_part, "domain", link_pairs)
    core_field = lax.ppermute(xt, "domain", core_pairs)

    group_shape = (groups, states, LANES)
    mine, to_core, to_link, *to_far = call(
        63,
        project_kernel,
        (),
        [SCALARS] * 3 + [FAR, PINNED],
        [PINNED] + [FAR] * (2 + len(far_pairs)),
        [((3 * groups, states, LANES), BF16)]
        + [((2 * groups, states, LANES), BF16)] * 2
        + [(group_shape, BF16)] * len(far_pairs),
        [
            pltpu.VMEM((3 * atoms_here + 1, proj_count, states), F32),
            pltpu.VMEM((3 * groups, states, LANES), BF16),
            pltpu.VMEM(line_shape, BF16),
            pltpu.VMEM(projectors.shape, BF16),
            copies((5,)),
            copies((5 + len(far_pairs),)),
        ],
        (tile_atom, tile_line, tile_count, xt, projectors),
    )
    from_link = lax.ppermute(to_link, "domain", link_pairs)
    from_far = [lax.ppermute(value, "domain", pairs) for value, pairs in zip(to_far, far_pairs)]
    from_core = lax.ppermute(to_core, "domain", core_pairs)
    (late_part,) = call(
        63,
        hand_on,
        (),
        [UNREAD] * (5 + len(far_pairs)),
        [UNREAD],
        [(late_shape, BF16)],
        [],
        (late_part, from_core, from_link, *from_far, link_early, core_field),
        aliases={0: 0},
    )
    link_late = lax.ppermute(late_part, "domain", link_pairs)
    added, whole = call(
        62,
        functools.partial(nonlocal_kernel, lines, len(far_pairs)),
        (),
        [SCALARS] * 3 + [PINNED, WHOLE, PINNED, WHOLE, WHOLE] + [WHOLE] * len(far_pairs),
        [PINNED, PINNED],
        [(line_shape, F32), (group_shape, BF16)],
        [
            pltpu.VMEM((lines + 1, states, cols_z), F32),
            pltpu.VMEM(group_shape, BF16),
            pltpu.VMEM((3 * groups, states, LANES), BF16),
            pltpu.VMEM((3 * groups, states, LANES), F32),
            pltpu.VMEM(energy_rows, F32),
            pltpu.VMEM((3 * atoms_here, states, proj_count), BF16),
            pltpu.VMEM(projectors.shape, BF16),
            copies((4,)),
        ],
        (tile_atom, tile_line, tile_count, projectors, energy, mine, from_core, from_link, *from_far),
        micros=18,
    )
    held = groups // bands
    built_shape = (first + first // 2 + held, states, cols_z)
    own_message, *messages = call(
        63,
        functools.partial(second_kernel, share),
        (),
        [FAR] * 4 + [PINNED],
        [PINNED] + [FAR] * (bands - 1),
        [(built_shape, BF16)] * bands,
        [
            pltpu.VMEM((bands, *built_shape), BF16),
            pltpu.VMEM((bands, first // 2, states, cols_z), BF16),
            pltpu.VMEM((bands, first // 2, states, cols_z), BF16),
            copies((4 * bands,)),
            copies((bands,)),
        ],
        (xt, core_field, link_early, link_late, whole),
    )
    early = swapped(messages, "band")

    later_all, later_pass, later_token = call(
        32,
        functools.partial(later_kernel, bands),
        (),
        [FAR, PINNED],
        [NEAR, FAR, PINNED],
        [((rest + 1, total_states, cols_z), BF16), ((rest // 2, total_states, cols_z), BF16), token],
        [copies((bands,)), copies],
        (landed, own_message),
    )
    later_link = lax.ppermute(later_pass, "domain", link_pairs)
    later_core = lax.ppermute(later_pass, "domain", core_pairs)

    span = 2 * ROWS
    added_far = pltpu.with_memory_space_constraint(added, pltpu.HBM)

    def stencil(link_half, begin, extra):
        steps, skip = link_half.shape[0] // span, begin // span
        block = pl.BlockSpec((span, states, cols_z), lambda i: (i + skip, 0, 0))
        return call(
            62,
            stencil_kernel,
            (steps,),
            [
                block,
                pl.BlockSpec((1, states, cols_z), lambda i: (lax.rem((i + skip) * span + lines - 1, lines), 0, 0)),
                pl.BlockSpec((1, states, cols_z), lambda i: (lax.rem((i + skip) * span + span, lines), 0, 0)),
                block,
                pl.BlockSpec((span, states, cols_z), lambda i: (i, 0, 0)),
                block,
                pl.BlockSpec((span, cols_z), lambda i: (i + skip, 0)),
                WHOLE,
                PINNED,
            ]
            + [UNREAD] * (len(extra) - 1),
            [pl.BlockSpec((states, span, cols_z), lambda i: (0, i + skip, 0)), PINNED],
            [((states, lines, cols_z), BF16), token],
            [],
            (xt, xt, xt, core_field, link_half, added_far, pot, ring, *extra),
            aliases={9: 0} if len(extra) > 1 else None,
        )

    applied, applied_token = stencil(link_early, 0, (later_token,))
    early_all, early_beside, projs, energy_table_here, early_token = call(
        32,
        early_kernel,
        (),
        [NEAR, WHOLE, PINNED, PINNED] + [FAR] * (bands - 1),
        [NEAR, NEAR, NEAR, NEAR, PINNED],
        [
            ((first + 1, total_states, cols_z), BF16),
            ((first // 2, total_states, cols_z), BF16),
            ((held, total_states, LANES), BF16),
            (energy_rows, F32),
            token,
        ],
        [copies((3 * bands,))],
        (later_all, energy, applied_token, own_message, *early),
        micros=30,
    )
    (begun,) = call(
        32,
        functools.partial(gram_kernel, first, share),
        (),
        [NEAR, WHOLE, WHOLE, WHOLE, PINNED],
        [NEAR],
        [((2, total_states, total_states), F32)],
        [],
        (later_all, later_core, later_link, pot, early_token),
    )
    parts = domains * bands
    blocks, final_token = call(
        32,
        functools.partial(final_kernel, bands, share),
        (),
        [NEAR, NEAR, WHOLE, NEAR, NEAR, NEAR],
        [WHOLE, PINNED],
        [((parts, states, 2 * total_states // domains), BF16), token],
        [pltpu.VMEM((2, total_states, total_states), F32)],
        (early_all, early_beside, pot, begun, projs, energy_table_here),
    )
    summed = lax.all_to_all(blocks, ("domain", "band"), split_axis=0, concat_axis=0, tiled=True)
    applied, _ = stencil(link_late, lines - late_lines, (final_token, applied))
    (subspace,) = call(
        32,
        functools.partial(result_kernel, 1.0 / (lines * cols_z * domains)),
        (),
        [WHOLE],
        [WHOLE],
        [((2, states, total_states // domains), F32)],
        [],
        (summed,),
    )
    return applied.reshape(orbitals.shape), subspace


def solution(mesh):
    in_specs = (
        P("band", ("groups", "domain"), None, None),
        P(("groups", "domain"), None, None),
        P(("groups", "domain"), None, None),
        P(("groups", "domain")),
        P(("groups", "domain")),
        P(("groups", "domain")),
        P("groups", None),
    )
    out_specs = (P("band", ("groups", "domain"), None, None), P(None, ("groups", "band"), "domain"))
    return jax.shard_map(local, mesh=mesh, in_specs=in_specs, out_specs=out_specs, check_vma=False)
```

```python
import functools

import jax
import jax.numpy as jnp
import numpy as np
from jax import lax
from jax.experimental import pallas as pl
from jax.experimental.pallas import tpu as pltpu
from jax.sharding import PartitionSpec as P

F32 = jnp.float32
BF16 = jnp.bfloat16
LANES = 128
ROWS = 16
NT = (((1,), (1,)), ((), ()))
WHOLE = pl.BlockSpec(memory_space=pltpu.VMEM)
NEAR = pl.BlockSpec(memory_space=pltpu.VMEM)
SCALARS = pl.BlockSpec(memory_space=pltpu.SMEM)
FAR = pl.BlockSpec(memory_space=pltpu.HBM)
PINNED = pl.BlockSpec(memory_space=pltpu.HBM)
UNREAD = pl.BlockSpec(memory_space=pl.ANY)
copies = pltpu.SemaphoreType.DMA


def call(room, kernel, grid, in_specs, out_specs, outs, scratch, args, aliases=None, micros=0.001):
    def place(spec):
        return {id(NEAR): pltpu.VMEM, id(PINNED): pltpu.HBM}.get(id(spec))

    args = [
        pltpu.with_memory_space_constraint(arg, place(spec)) if place(spec) else arg
        for spec, arg in zip(in_specs, args)
    ]
    shapes = [(place(spec) or jax.ShapeDtypeStruct)(shape, kind) for spec, (shape, kind) in zip(out_specs, outs)]
    return pl.pallas_call(
        kernel,
        grid=grid,
        out_shape=shapes,
        in_specs=in_specs,
        out_specs=out_specs,
        scratch_shapes=scratch,
        input_output_aliases=aliases or {},
        compiler_params=pltpu.CompilerParams(vmem_limit_bytes=room << 20),
        cost_estimate=pl.CostEstimate(flops=int(micros * 1.1e9), bytes_accessed=1 << 10, transcendentals=0),
    )(*args)


def start(copy):
    copy.start()
    return copy


def start_all(pairs, sems):
    return [start(pltpu.make_async_copy(source, target, sems.at[i])) for i, (source, target) in enumerate(pairs)]


def wait_all(started):
    for copy in started:
        copy.wait()


def hand_on(*refs):
    pass


def pack_kernel(first, x_hbm, xt_hbm, early, late, message, x, xt, in_sems, out_sems):
    states, lines, _ = x.shape
    bands = in_sems.shape[0]
    share = lines // bands
    count = share - first
    loads, sends = [], []
    for c in range(bands):
        where = (slice(None), pl.ds(c * share, share), slice(None))
        loads.append(start(pltpu.make_async_copy(x_hbm.at[where], x.at[where], in_sems.at[c])))

    def send(line, number, target, at):
        copy = pltpu.make_async_copy(
            xt.at[pl.ds(line, number)], target.at[pl.ds(at, number)], out_sems.at[len(sends)]
        )
        sends.append(start(copy))

    for c in range(bands):
        loads[c].wait()
        for y0 in range(c * share, (c + 1) * share, ROWS):
            for s0 in range(0, states, ROWS):
                block = x[s0 : s0 + ROWS, y0 : y0 + ROWS, :].astype(F32)
                turned = jnp.swapaxes(block, 0, 1).astype(BF16)
                xt[y0 : y0 + ROWS, s0 : s0 + ROWS, :] = turned
        send(c * share, share // 2, early, c * (share // 2))
        send(c * share + share // 2, share // 2, late, c * (share // 2))
        send(c * share + first, count, message, c * (count + 1))
        send(c * share, 1, message, (c + bands - 1) % bands * (count + 1) + count)
        send(c * share, share, xt_hbm, c * share)
    for copy in sends:
        copy.wait()


def bases(groups):
    domain = lax.axis_index("domain")
    odd, upper = domain & 1, (domain >> 1) & 1
    return [2 * groups * side for side in (1 - odd, odd, 1 - upper, upper)]


def slot_reader(atom_ref, line_ref, count_ref, atoms_here):
    first = (lax.axis_index("domain") - 1) * atoms_here
    live = count_ref[0]

    def slot_at(t):
        return line_ref[t], jnp.clip(atom_ref[t] - first, 0, 3 * atoms_here - 1), t < live

    return slot_at


def energy_table(energy_ref):
    proj_count, atoms = energy_ref.shape
    per_group = LANES // proj_count
    lane = lax.broadcasted_iota(jnp.int32, (proj_count, LANES), 1)
    row = lax.broadcasted_iota(jnp.int32, (proj_count, LANES), 0)
    pick = jnp.where(lane % proj_count == row, 1.0, 0.0).astype(F32)
    spread = jnp.dot(energy_ref[...].T, pick, precision=lax.Precision.HIGHEST, preferred_element_type=F32)
    spread = spread.reshape(atoms // per_group, per_group, LANES)
    lane = lax.broadcasted_iota(jnp.int32, spread.shape, 2)
    atom = lax.broadcasted_iota(jnp.int32, spread.shape, 1)
    return jnp.sum(jnp.where(lane // proj_count == atom, spread, 0.0), axis=1)


def project_kernel(atom_ref, line_ref, count_ref, xt_hbm, p_hbm, mine_hbm, core_hbm, link_hbm, *refs):
    far_hbms, (total, mine_ref, xt_ref, p_ref, sems, out_sems) = refs[:-6], refs[-6:]
    slots, proj_count, _ = p_ref.shape
    groups, states = mine_ref.shape[0] // 3, mine_ref.shape[1]
    per_group = LANES // proj_count
    chunks = sems.shape[0] - 1
    size = slots // chunks
    unroll = 16
    pairs = [(p_hbm.at[pl.ds(c * size, size)], p_ref.at[pl.ds(c * size, size)]) for c in range(chunks)]
    xt_load, *loads = start_all([(xt_hbm, xt_ref), *pairs], sems)

    def clear(i, carry):
        for u in range(per_group):
            total[i * per_group + u] = jnp.zeros_like(total[0])
        return carry

    lax.fori_loop(0, 3 * groups, clear, 0)

    slot_at = slot_reader(atom_ref, line_ref, count_ref, groups * per_group)

    def body(i, carry):
        for u in range(unroll):
            t = i * unroll + u
            line, atom, live = slot_at(t)
            part = lax.dot_general(p_ref[t], xt_ref[line], NT, preferred_element_type=F32)
            total[jnp.where(live, atom, 3 * groups * per_group)] += part
        return carry

    xt_load.wait()
    for c in range(chunks):
        loads[c].wait()
        lax.fori_loop(c * size // unroll, (c + 1) * size // unroll, body, 0)

    for g in range(3 * groups):
        tiles = [total[g * per_group + u] for u in range(per_group)]
        mine_ref[g] = jnp.concatenate(tiles, axis=0).T.astype(BF16)
    sides = bases(groups)
    pairs = [(mine_ref, mine_hbm)]
    for side, far in zip(sides[:2], (core_hbm, link_hbm)):
        pairs.append((mine_ref.at[pl.ds(side, groups)], far.at[pl.ds(0, groups)]))
        pairs.append((mine_ref.at[pl.ds(groups, groups)], far.at[pl.ds(groups, groups)]))
    for side, far in zip(sides[2:], far_hbms):
        pairs.append((mine_ref.at[pl.ds(side, groups)], far))
    wait_all(start_all(pairs, out_sems))


def nonlocal_kernel(
    fars, atom_ref, line_ref, count_ref, xt_hbm, beside_hbm, early_hbm, p_hbm, energy_ref, mine_hbm, core_ref, link_ref, *refs
):
    far_refs, out_hbm, messages, scratch = refs[:fars], refs[fars], refs[fars + 1 : -13], refs[-13:]
    lines_sum, whole_ref, mine_ref, total, table, atoms, p_ref, built, cores, links, sems, in_sems, out_sems = scratch
    lines = xt_hbm.shape[0]
    bands, half = cores.shape[:2]
    share, first = lines // bands, 2 * half
    held = built.shape[1] - first - half
    mine = (lax.axis_index("domain") & 1) * half
    pairs = []
    for k in range(bands):
        to = lax.axis_index("band") ^ k
        pairs.append((xt_hbm.at[pl.ds(to * share, first)], built.at[k, pl.ds(0, first)]))
        pairs.append((beside_hbm.at[pl.ds(to * share + mine, half)], cores.at[k]))
        pairs.append((early_hbm.at[pl.ds(to * (share // 2) + mine, half)], links.at[k]))
    brought = start_all(pairs, in_sems)
    slots, proj_count, _ = p_ref.shape
    groups, states = total.shape[0] // 3, total.shape[1]
    per_group = LANES // proj_count
    unroll = 16
    mine_load, load = start_all([(mine_hbm, mine_ref), (p_hbm, p_ref)], sems)
    sends = []

    def clear(i, carry):
        lines_sum[i] = jnp.zeros((states, LANES), F32)
        return carry

    lax.fori_loop(0, lines + 1, clear, 0)
    mine_load.wait()
    total[...] = mine_ref[...].astype(F32)
    sides = bases(groups)
    for g in range(groups):
        total[groups + g] += core_ref[g].astype(F32) + link_ref[g].astype(F32)
        for side, ref in zip(sides[:2], (core_ref, link_ref)):
            total[side + g] += ref[groups + g].astype(F32)
        for side, ref in zip(sides[2:], far_refs):
            total[side + g] += ref[g].astype(F32)
    table[...] = energy_table(energy_ref)
    last = table.shape[0] - 1
    for g in range(3 * groups):
        row = jnp.clip((lax.axis_index("domain") - 1) * groups + g, 0, last)
        tile = (total[g] * table[pl.ds(row, 1), :]).astype(BF16)
        for u in range(per_group):
            atoms[g * per_group + u] = tile[:, u * proj_count : (u + 1) * proj_count]
    for g in range(groups):
        whole_ref[g] = total[groups + g].astype(BF16)
    wait_all(brought)
    for k, message in enumerate(messages):
        to = lax.axis_index("band") ^ k
        for i in range(half):
            built[k, first + i] = (cores[k, i].astype(F32) + links[k, i].astype(F32)).astype(BF16)
        for i in range(held):
            built[k, first + half + i] = whole_ref[to * held + i]
        sends.append(start(pltpu.make_async_copy(built.at[k], message, out_sems.at[k])))
    load.wait()

    slot_at = slot_reader(atom_ref, line_ref, count_ref, groups * per_group)

    def body(i, carry):
        for u in range(unroll):
            t = i * unroll + u
            line, atom, live = slot_at(t)
            part = jnp.dot(atoms[atom], p_ref[t], preferred_element_type=F32)
            lines_sum[jnp.where(live, line, lines)] += part
        return carry

    lax.fori_loop(0, slots // unroll, body, 0)
    sends.append(start(pltpu.make_async_copy(lines_sum.at[pl.ds(0, lines)], out_hbm, sems.at[3])))
    wait_all(sends)


def stencil_kernel(
    share, xt_ref, last_ref, next_ref, core_ref, early_ref, late_ref, added_ref, pot_ref, ring_ref, unread,
    out_ref,
):
    states, here, _ = out_ref.shape

    def link(i, rows):
        chunk, at = divmod(i, share)
        ref = early_ref if at < share // 2 else late_ref
        return ref[chunk * (share // 2) + at % (share // 2), rows, :]

    def line(i, rows):
        ref, at = (last_ref, 0) if i < 0 else (next_ref, 0) if i == here else (xt_ref, i)
        return ref[at, rows, :]

    for y0 in range(0, here, ROWS):
        for s0 in range(0, states, ROWS):
            rows = slice(s0, s0 + ROWS)
            results = []
            cells = jnp.concatenate([line(y0 + i, rows) for i in range(ROWS)], axis=0)
            along = jnp.dot(cells, ring_ref[...], preferred_element_type=F32)
            before, x = line(y0 - 1, rows).astype(F32), line(y0, rows).astype(F32)
            for i in range(ROWS):
                y = y0 + i
                after = line(y + 1, rows).astype(F32)
                beside = (before + after) + (core_ref[y, rows, :].astype(F32) + link(y, rows).astype(F32))
                value = along[i * ROWS : (i + 1) * ROWS] + pot_ref[y : y + 1, :] * x
                results.append(value + added_ref[y, rows, :] - 0.5 * beside)
                before, x = x, after
            turned = jnp.swapaxes(jnp.stack(results, axis=0), 0, 1).astype(BF16)
            out_ref[rows, y0 : y0 + ROWS, :] = turned


def pass_half(all_ref, pass_hbm, sem):
    half = pass_hbm.shape[0]
    copy = start(pltpu.make_async_copy(all_ref.at[pl.ds((1 - (lax.axis_index("domain") & 1)) * half, half)], pass_hbm, sem))
    copy.wait()


def later_kernel(bands, landed, unread, all_ref, pass_hbm, sems, pass_sem):
    count, states = all_ref.shape[0], landed.shape[1]
    loads = [
        start(
            pltpu.make_async_copy(
                landed.at[pl.ds(b * count, count)], all_ref.at[:, pl.ds(b * states, states), :], sems.at[b]
            )
        )
        for b in range(bands)
    ]
    for copy in loads:
        copy.wait()
    pass_half(all_ref, pass_hbm, pass_sem)


def early_kernel(after_ref, energy_ref, *refs):
    pieces, (all_ref, beside_ref, projs_ref, table_ref, token, sems) = refs[:-6], refs[-6:]
    states = pieces[0].shape[1]
    count, half, held = all_ref.shape[0] - 1, beside_ref.shape[0], projs_ref.shape[0]
    pairs = []
    for k, piece in enumerate(pieces):
        at = pl.ds(pl.multiple_of((lax.axis_index("band") ^ k) * states, states), states)
        pairs.append((piece.at[pl.ds(0, count)], all_ref.at[pl.ds(0, count), at, :]))
        pairs.append((piece.at[pl.ds(count, half)], beside_ref.at[:, at, :]))
        pairs.append((piece.at[pl.ds(count + half, held)], projs_ref.at[:, at, :]))
    loads = start_all(pairs, sems)
    all_ref[count] = after_ref[0]
    table_ref[...] = energy_table(energy_ref)
    wait_all(loads)


def add_products(row, all_ref, beside_refs, pot_ref, acc):
    half = beside_refs[0].shape[0]
    group = 4
    mine = (lax.axis_index("domain") & 1) * half
    for part, base in ((0, mine), (1, half - mine)):
        for i0 in range(0, half, group):
            xs, ys = [], []
            for i in range(i0, min(i0 + group, half)):
                cell = all_ref[base + i]
                x = cell.astype(F32)
                y = (3.0 + pot_ref[pl.ds(row + base + i, 1), :]) * x - pltpu.roll(x, x.shape[1] - 1, 1)
                y = y - all_ref[base + i + 1].astype(F32)
                if part == 0:
                    for ref in beside_refs:
                        y = y - ref[i].astype(F32)
                xs.append(cell)
                ys.append(y.astype(BF16))
            flat_x = jnp.concatenate(xs, axis=1)
            flat_y = jnp.concatenate(ys, axis=1)
            acc[0] += lax.dot_general(flat_x, flat_x, NT, preferred_element_type=F32)
            acc[1] += lax.dot_general(flat_y, flat_x, NT, preferred_element_type=F32)


def gram_kernel(first, share, all_ref, core_ref, link_ref, pot_ref, unread, acc):
    acc[...] = jnp.zeros_like(acc)
    add_products(lax.axis_index("band") * share + first, all_ref, (core_ref, link_ref), pot_ref, acc)


def final_kernel(bands, share, all_ref, beside_ref, pot_ref, begun_ref, proj_ref, energy_ref, out_ref, token, acc):
    acc[...] = begun_ref[...]
    add_products(lax.axis_index("band") * share, all_ref, (beside_ref,), pot_ref, acc)
    groups = proj_ref.shape[0]
    first = (lax.axis_index("domain") * bands + lax.axis_index("band")) * groups
    for g in range(groups):
        here = proj_ref[g]
        scaled = (here.astype(F32) * energy_ref[pl.ds(first + g, 1), :]).astype(BF16)
        acc[1] += lax.dot_general(scaled, here, NT, preferred_element_type=F32)
    hamil = 0.5 * (acc[1] + acc[1].T)
    domains = out_ref.shape[0] // bands
    rows, cols = out_ref.shape[1], out_ref.shape[2] // 2
    for c in range(domains):
        for r in range(bands):
            r0, c0 = r * rows, c * cols
            out_ref[c * bands + r, :, :cols] = acc[0, r0 : r0 + rows, c0 : c0 + cols].astype(BF16)
            out_ref[c * bands + r, :, cols:] = hamil[r0 : r0 + rows, c0 : c0 + cols].astype(BF16)


def result_kernel(scale, parts_ref, out_ref):
    total = jnp.sum(parts_ref[...].astype(F32), axis=0) * scale
    cols = out_ref.shape[2]
    out_ref[0] = total[:, :cols]
    out_ref[1] = total[:, cols:]


def local(orbitals, potential, projectors, tile_atom, tile_line, tile_count, energies):
    states, _, lines, cols_z = orbitals.shape
    slots, proj_count, _ = projectors.shape
    atom_total = energies.shape[0]
    domains, bands = lax.axis_size("domain"), lax.axis_size("band")
    total_states = states * bands
    atoms_here = atom_total // domains
    per_group = LANES // proj_count
    groups = atoms_here // per_group
    share = lines // bands
    first = 2 * (share * 3 // 32)
    rest = share - first

    core_pairs = [(i, i ^ 1) for i in range(domains) if i ^ 1 < domains]
    link_pairs = [(i, ((i + 1) ^ 1) - 1) for i in range(1, domains) if ((i + 1) ^ 1) - 1 < domains]
    near_far = [(i, i ^ 2) for i in range(domains) if i ^ 2 < domains]
    next = [(i, ((i + 2) ^ 2) - 2) for i in range(2, domains) if ((i + 2) ^ 2) - 2 < domains]
    far_pairs = [pairs for pairs in (near_far, next) if pairs]

    def swapped(values, axis):
        size = lax.axis_size(axis)
        got = {k: lax.ppermute(values[k - 1], axis, [(i, i ^ k) for i in range(size)]) for k in range(size - 1, 0, -1)}
        return [got[k] for k in range(1, size)]

    field = orbitals.reshape(states, lines, cols_z)
    pot = potential.reshape(lines, cols_z)
    energy = energies.T
    energy_rows = (atom_total // per_group, LANES)
    token = ((8, LANES), F32)
    eye = np.eye(cols_z, dtype=np.float32)
    ring = jnp.asarray(3.0 * eye - 0.5 * (np.roll(eye, 1, axis=0) + np.roll(eye, -1, axis=0)), dtype=BF16)

    late_lines = lines // 2
    line_shape, late_shape = (lines, states, cols_z), (late_lines, states, cols_z)
    xt, early_part, late_part, message = call(
        63,
        functools.partial(pack_kernel, first),
        (),
        [FAR],
        [FAR] * 4,
        [
            (line_shape, BF16),
            ((lines - late_lines, states, cols_z), BF16),
            (late_shape, BF16),
            ((bands * (rest + 1), states, cols_z), BF16),
        ],
        [
            pltpu.VMEM((states, lines, cols_z), BF16),
            pltpu.VMEM(line_shape, BF16),
            copies((bands,)),
            copies((5 * bands,)),
        ],
        (field,),
    )
    landed = lax.all_to_all(message, "band", split_axis=0, concat_axis=0, tiled=True)
    link_early = lax.ppermute(early_part, "domain", link_pairs)
    core_field = lax.ppermute(xt, "domain", core_pairs)

    group_shape = (groups, states, LANES)
    mine, to_core, to_link, *to_far = call(
        63,
        project_kernel,
        (),
        [SCALARS] * 3 + [FAR, PINNED],
        [PINNED] + [FAR] * (2 + len(far_pairs)),
        [((3 * groups, states, LANES), BF16)]
        + [((2 * groups, states, LANES), BF16)] * 2
        + [(group_shape, BF16)] * len(far_pairs),
        [
            pltpu.VMEM((3 * atoms_here + 1, proj_count, states), F32),
            pltpu.VMEM((3 * groups, states, LANES), BF16),
            pltpu.VMEM(line_shape, BF16),
            pltpu.VMEM(projectors.shape, BF16),
            copies((5,)),
            copies((5 + len(far_pairs),)),
        ],
        (tile_atom, tile_line, tile_count, xt, projectors),
    )
    from_link = lax.ppermute(to_link, "domain", link_pairs)
    from_far = [lax.ppermute(value, "domain", pairs) for value, pairs in zip(to_far, far_pairs)]
    from_core = lax.ppermute(to_core, "domain", core_pairs)
    (late_part,) = call(
        56,
        hand_on,
        (),
        [UNREAD] * (5 + len(far_pairs)),
        [UNREAD],
        [(late_shape, BF16)],
        [],
        (late_part, from_core, from_link, *from_far, link_early, core_field),
        aliases={0: 0},
    )
    link_late = lax.ppermute(late_part, "domain", link_pairs)
    held = groups // bands
    built_shape = (first + first // 2 + held, states, cols_z)
    beside_shape = (bands, first // 2, states, cols_z)
    added, own_message, *messages = call(
        62,
        functools.partial(nonlocal_kernel, len(far_pairs)),
        (),
        [SCALARS] * 3 + [FAR] * 3 + [PINNED, WHOLE, PINNED, WHOLE, WHOLE] + [WHOLE] * len(far_pairs),
        [PINNED, PINNED] + [FAR] * (bands - 1),
        [(line_shape, F32)] + [(built_shape, BF16)] * bands,
        [
            pltpu.VMEM((lines + 1, states, cols_z), F32),
            pltpu.VMEM(group_shape, BF16),
            pltpu.VMEM((3 * groups, states, LANES), BF16),
            pltpu.VMEM((3 * groups, states, LANES), F32),
            pltpu.VMEM(energy_rows, F32),
            pltpu.VMEM((3 * atoms_here, states, proj_count), BF16),
            pltpu.VMEM(projectors.shape, BF16),
            pltpu.VMEM((bands, *built_shape), BF16),
            pltpu.VMEM(beside_shape, BF16),
            pltpu.VMEM(beside_shape, BF16),
            copies((4,)),
            copies((3 * bands,)),
            copies((bands,)),
        ],
        (
            tile_atom, tile_line, tile_count, xt, core_field, link_early, projectors, energy, mine, from_core,
            from_link, *from_far,
        ),
        micros=8,
    )
    early = swapped(messages, "band")

    later_all, later_pass = call(
        32,
        functools.partial(later_kernel, bands),
        (),
        [FAR, PINNED],
        [NEAR, FAR],
        [((rest + 1, total_states, cols_z), BF16), ((rest // 2, total_states, cols_z), BF16)],
        [copies((bands,)), copies],
        (landed, own_message),
    )
    later_link = lax.ppermute(later_pass, "domain", link_pairs)
    later_core = lax.ppermute(later_pass, "domain", core_pairs)

    early_all, early_beside, projs, energy_table_here, early_token = call(
        32,
        early_kernel,
        (),
        [NEAR, WHOLE, PINNED] + [FAR] * (bands - 1),
        [NEAR, NEAR, NEAR, NEAR, PINNED],
        [
            ((first + 1, total_states, cols_z), BF16),
            ((first // 2, total_states, cols_z), BF16),
            ((held, total_states, LANES), BF16),
            (energy_rows, F32),
            token,
        ],
        [copies((3 * bands,))],
        (later_all, energy, own_message, *early),
        micros=30,
    )
    (begun,) = call(
        32,
        functools.partial(gram_kernel, first, share),
        (),
        [NEAR, WHOLE, WHOLE, WHOLE, PINNED],
        [NEAR],
        [((2, total_states, total_states), F32)],
        [],
        (later_all, later_core, later_link, pot, early_token),
    )
    parts = domains * bands
    blocks, final_token = call(
        32,
        functools.partial(final_kernel, bands, share),
        (),
        [NEAR, NEAR, WHOLE, NEAR, NEAR, NEAR],
        [WHOLE, PINNED],
        [((parts, states, 2 * total_states // domains), BF16), token],
        [pltpu.VMEM((2, total_states, total_states), F32)],
        (early_all, early_beside, pot, begun, projs, energy_table_here),
    )
    summed = lax.all_to_all(blocks, ("domain", "band"), split_axis=0, concat_axis=0, tiled=True)
    span = 2 * ROWS
    steps = lines // span
    block = pl.BlockSpec((span, states, cols_z), lambda i: (i, 0, 0))
    (applied,) = call(
        60,
        functools.partial(stencil_kernel, share),
        (steps,),
        [
            block,
            pl.BlockSpec((1, states, cols_z), lambda i: (lax.rem(i * span + lines - 1, lines), 0, 0)),
            pl.BlockSpec((1, states, cols_z), lambda i: (lax.rem(i * span + span, lines), 0, 0)),
            block,
            pl.BlockSpec((span // 2, states, cols_z), lambda i: (i, 0, 0)),
            pl.BlockSpec((span // 2, states, cols_z), lambda i: (i, 0, 0)),
            block,
            pl.BlockSpec((span, cols_z), lambda i: (i, 0)),
            WHOLE,
            PINNED,
        ],
        [pl.BlockSpec((states, span, cols_z), lambda i: (0, i, 0))],
        [((states, lines, cols_z), BF16)],
        [],
        (
            xt, xt, xt, core_field, link_early, link_late, pltpu.with_memory_space_constraint(added, pltpu.HBM), pot, ring,
            final_token,
        ),
    )

    (subspace,) = call(
        32,
        functools.partial(result_kernel, 1.0 / (lines * cols_z * domains)),
        (),
        [WHOLE],
        [WHOLE],
        [((2, states, total_states // domains), F32)],
        [],
        (summed,),
    )
    return applied.reshape(orbitals.shape), subspace


def solution(mesh):
    in_specs = (
        P("band", ("groups", "domain"), None, None),
        P(("groups", "domain"), None, None),
        P(("groups", "domain"), None, None),
        P(("groups", "domain")),
        P(("groups", "domain")),
        P(("groups", "domain")),
        P("groups", None),
    )
    out_specs = (P("band", ("groups", "domain"), None, None), P(None, ("groups", "band"), "domain"))
    return jax.shard_map(local, mesh=mesh, in_specs=in_specs, out_specs=out_specs, check_vma=False)
```

```python
import functools

import jax
import jax.numpy as jnp
import numpy as np
from jax import lax
from jax.experimental import pallas as pl
from jax.experimental.pallas import tpu as pltpu
from jax.sharding import PartitionSpec as P

F32 = jnp.float32
BF16 = jnp.bfloat16
LANES = 128
ROWS = 16
NT = (((1,), (1,)), ((), ()))
WHOLE = pl.BlockSpec(memory_space=pltpu.VMEM)
NEAR = pl.BlockSpec(memory_space=pltpu.VMEM)
SCALARS = pl.BlockSpec(memory_space=pltpu.SMEM)
FAR = pl.BlockSpec(memory_space=pltpu.HBM)
PINNED = pl.BlockSpec(memory_space=pltpu.HBM)
UNREAD = pl.BlockSpec(memory_space=pl.ANY)
copies = pltpu.SemaphoreType.DMA


def call(room, kernel, grid, in_specs, out_specs, outs, scratch, args, aliases=None, micros=0.001):
    def place(spec):
        return {id(NEAR): pltpu.VMEM, id(PINNED): pltpu.HBM}.get(id(spec))

    args = [
        pltpu.with_memory_space_constraint(arg, place(spec)) if place(spec) else arg
        for spec, arg in zip(in_specs, args)
    ]
    shapes = [(place(spec) or jax.ShapeDtypeStruct)(shape, kind) for spec, (shape, kind) in zip(out_specs, outs)]
    return pl.pallas_call(
        kernel,
        grid=grid,
        out_shape=shapes,
        in_specs=in_specs,
        out_specs=out_specs,
        scratch_shapes=scratch,
        input_output_aliases=aliases or {},
        compiler_params=pltpu.CompilerParams(vmem_limit_bytes=room << 20),
        cost_estimate=pl.CostEstimate(flops=int(micros * 1.1e9), bytes_accessed=1 << 10, transcendentals=0),
    )(*args)


def start(copy):
    copy.start()
    return copy


def start_all(pairs, sems):
    return [start(pltpu.make_async_copy(source, target, sems.at[i])) for i, (source, target) in enumerate(pairs)]


def wait_all(started):
    for copy in started:
        copy.wait()


def wait_for(*refs):
    pass


def pack_kernel(first, x_hbm, xt_hbm, early, late, message, x, xt, in_sems, out_sems):
    states, lines, _ = x.shape
    bands = in_sems.shape[0]
    share = lines // bands
    count = share - first
    loads, sends = [], []
    for c in range(bands):
        where = (slice(None), pl.ds(c * share, share), slice(None))
        loads.append(start(pltpu.make_async_copy(x_hbm.at[where], x.at[where], in_sems.at[c])))

    def send(line, number, target, at):
        copy = pltpu.make_async_copy(
            xt.at[pl.ds(line, number)], target.at[pl.ds(at, number)], out_sems.at[len(sends)]
        )
        sends.append(start(copy))

    for c in range(bands):
        loads[c].wait()
        for y0 in range(c * share, (c + 1) * share, ROWS):
            for s0 in range(0, states, ROWS):
                block = x[s0 : s0 + ROWS, y0 : y0 + ROWS, :].astype(F32)
                turned = jnp.swapaxes(block, 0, 1).astype(BF16)
                xt[y0 : y0 + ROWS, s0 : s0 + ROWS, :] = turned
        send(c * share, share // 2, early, c * (share // 2))
        send(c * share + share // 2, share // 2, late, c * (share // 2))
        send(c * share + first, count, message, c * (count + 1))
        send(c * share, 1, message, (c + bands - 1) % bands * (count + 1) + count)
        send(c * share, share, xt_hbm, c * share)
    for copy in sends:
        copy.wait()


def bases(groups):
    domain = lax.axis_index("domain")
    odd, upper = domain & 1, (domain >> 1) & 1
    return [2 * groups * side for side in (1 - odd, odd, 1 - upper, upper)]


def slot_reader(atom_ref, line_ref, count_ref, atoms_here):
    first = (lax.axis_index("domain") - 1) * atoms_here
    live = count_ref[0]

    def slot_at(t):
        return line_ref[t], jnp.clip(atom_ref[t] - first, 0, 3 * atoms_here - 1), t < live

    return slot_at


def energy_table(energy_ref):
    proj_count, atoms = energy_ref.shape
    per_group = LANES // proj_count
    lane = lax.broadcasted_iota(jnp.int32, (proj_count, LANES), 1)
    row = lax.broadcasted_iota(jnp.int32, (proj_count, LANES), 0)
    pick = jnp.where(lane % proj_count == row, 1.0, 0.0).astype(F32)
    spread = jnp.dot(energy_ref[...].T, pick, precision=lax.Precision.HIGHEST, preferred_element_type=F32)
    spread = spread.reshape(atoms // per_group, per_group, LANES)
    lane = lax.broadcasted_iota(jnp.int32, spread.shape, 2)
    atom = lax.broadcasted_iota(jnp.int32, spread.shape, 1)
    return jnp.sum(jnp.where(lane // proj_count == atom, spread, 0.0), axis=1)


def project_kernel(atom_ref, line_ref, count_ref, xt_hbm, p_hbm, mine_hbm, core_hbm, link_hbm, *refs):
    far_hbms, (total, mine_ref, xt_ref, p_ref, sems, out_sems) = refs[:-6], refs[-6:]
    slots, proj_count, _ = p_ref.shape
    groups, states = mine_ref.shape[0] // 3, mine_ref.shape[1]
    per_group = LANES // proj_count
    chunks = sems.shape[0] - 1
    size = slots // chunks
    unroll = 16
    pairs = [(p_hbm.at[pl.ds(c * size, size)], p_ref.at[pl.ds(c * size, size)]) for c in range(chunks)]
    xt_load, *loads = start_all([(xt_hbm, xt_ref), *pairs], sems)

    def clear(i, carry):
        for u in range(per_group):
            total[i * per_group + u] = jnp.zeros_like(total[0])
        return carry

    lax.fori_loop(0, 3 * groups, clear, 0)

    slot_at = slot_reader(atom_ref, line_ref, count_ref, groups * per_group)

    def body(i, carry):
        for u in range(unroll):
            t = i * unroll + u
            line, atom, live = slot_at(t)
            part = lax.dot_general(p_ref[t], xt_ref[line], NT, preferred_element_type=F32)
            total[jnp.where(live, atom, 3 * groups * per_group)] += part
        return carry

    xt_load.wait()
    for c in range(chunks):
        loads[c].wait()
        lax.fori_loop(c * size // unroll, (c + 1) * size // unroll, body, 0)

    for g in range(3 * groups):
        tiles = [total[g * per_group + u] for u in range(per_group)]
        mine_ref[g] = jnp.concatenate(tiles, axis=0).T.astype(BF16)
    sides = bases(groups)
    pairs = [(mine_ref, mine_hbm)]
    for side, far in zip(sides[:2], (core_hbm, link_hbm)):
        pairs.append((mine_ref.at[pl.ds(side, groups)], far.at[pl.ds(0, groups)]))
        pairs.append((mine_ref.at[pl.ds(groups, groups)], far.at[pl.ds(groups, groups)]))
    for side, far in zip(sides[2:], far_hbms):
        pairs.append((mine_ref.at[pl.ds(side, groups)], far))
    wait_all(start_all(pairs, out_sems))


def nonlocal_kernel(
    fars, atom_ref, line_ref, count_ref, xt_hbm, beside_hbm, early_hbm, p_hbm, energy_ref, mine_hbm, core_ref, link_ref, *refs
):
    far_refs, out_hbm, messages, scratch = refs[:fars], refs[fars + 1], refs[fars + 2 : -13], refs[-13:]
    lines_sum, whole_ref, mine_ref, total, table, atoms, p_ref, built, cores, links, sems, in_sems, out_sems = scratch
    lines = xt_hbm.shape[0]
    bands, half = cores.shape[:2]
    share, first = lines // bands, 2 * half
    held = built.shape[1] - first - half
    mine = (lax.axis_index("domain") & 1) * half
    pairs = []
    for k in range(bands):
        to = lax.axis_index("band") ^ k
        pairs.append((xt_hbm.at[pl.ds(to * share, first)], built.at[k, pl.ds(0, first)]))
        pairs.append((beside_hbm.at[pl.ds(to * share + mine, half)], cores.at[k]))
        pairs.append((early_hbm.at[pl.ds(to * (share // 2) + mine, half)], links.at[k]))
    brought = start_all(pairs, in_sems)
    slots, proj_count, _ = p_ref.shape
    groups, states = total.shape[0] // 3, total.shape[1]
    per_group = LANES // proj_count
    unroll = 16
    mine_load, load = start_all([(mine_hbm, mine_ref), (p_hbm, p_ref)], sems)
    sends = []

    def clear(i, carry):
        lines_sum[i] = jnp.zeros((states, LANES), F32)
        return carry

    lax.fori_loop(0, lines + 1, clear, 0)
    mine_load.wait()
    total[...] = mine_ref[...].astype(F32)
    sides = bases(groups)
    for g in range(groups):
        total[groups + g] += core_ref[g].astype(F32) + link_ref[g].astype(F32)
        for side, ref in zip(sides[:2], (core_ref, link_ref)):
            total[side + g] += ref[groups + g].astype(F32)
        for side, ref in zip(sides[2:], far_refs):
            total[side + g] += ref[g].astype(F32)
    table[...] = energy_table(energy_ref)
    last = table.shape[0] - 1
    for g in range(3 * groups):
        row = jnp.clip((lax.axis_index("domain") - 1) * groups + g, 0, last)
        tile = (total[g] * table[pl.ds(row, 1), :]).astype(BF16)
        for u in range(per_group):
            atoms[g * per_group + u] = tile[:, u * proj_count : (u + 1) * proj_count]
    for g in range(groups):
        whole_ref[g] = total[groups + g].astype(BF16)
    wait_all(brought)
    for k, message in enumerate(messages):
        to = lax.axis_index("band") ^ k
        for i in range(half):
            built[k, first + i] = (cores[k, i].astype(F32) + links[k, i].astype(F32)).astype(BF16)
        for i in range(held):
            built[k, first + half + i] = whole_ref[to * held + i]
        sends.append(start(pltpu.make_async_copy(built.at[k], message, out_sems.at[k])))
    load.wait()

    slot_at = slot_reader(atom_ref, line_ref, count_ref, groups * per_group)

    def body(i, carry):
        for u in range(unroll):
            t = i * unroll + u
            line, atom, live = slot_at(t)
            part = jnp.dot(atoms[atom], p_ref[t], preferred_element_type=F32)
            lines_sum[jnp.where(live, line, lines)] += part
        return carry

    lax.fori_loop(0, slots // unroll, body, 0)
    sends.append(start(pltpu.make_async_copy(lines_sum.at[pl.ds(0, lines)], out_hbm, sems.at[3])))
    wait_all(sends)


def stencil_kernel(
    share, xt_ref, last_ref, next_ref, core_ref, early_ref, late_ref, added_ref, pot_ref, ring_ref, unread,
    out_ref,
):
    states, here, _ = out_ref.shape

    def link(i, rows):
        chunk, at = divmod(i, share)
        ref = early_ref if at < share // 2 else late_ref
        return ref[chunk * (share // 2) + at % (share // 2), rows, :]

    def line(i, rows):
        ref, at = (last_ref, 0) if i < 0 else (next_ref, 0) if i == here else (xt_ref, i)
        return ref[at, rows, :]

    for y0 in range(0, here, ROWS):
        for s0 in range(0, states, ROWS):
            rows = slice(s0, s0 + ROWS)
            results = []
            cells = jnp.concatenate([line(y0 + i, rows) for i in range(ROWS)], axis=0)
            along = jnp.dot(cells, ring_ref[...], preferred_element_type=F32)
            before, x = line(y0 - 1, rows).astype(F32), line(y0, rows).astype(F32)
            for i in range(ROWS):
                y = y0 + i
                after = line(y + 1, rows).astype(F32)
                beside = (before + after) + (core_ref[y, rows, :].astype(F32) + link(y, rows).astype(F32))
                value = along[i * ROWS : (i + 1) * ROWS] + pot_ref[y : y + 1, :] * x
                results.append(value + added_ref[y, rows, :] - 0.5 * beside)
                before, x = x, after
            turned = jnp.swapaxes(jnp.stack(results, axis=0), 0, 1).astype(BF16)
            out_ref[rows, y0 : y0 + ROWS, :] = turned


def pass_half(all_ref, pass_hbm, sem):
    half = pass_hbm.shape[0]
    copy = start(pltpu.make_async_copy(all_ref.at[pl.ds((1 - (lax.axis_index("domain") & 1)) * half, half)], pass_hbm, sem))
    copy.wait()


def later_kernel(bands, landed, unread, handed, all_ref, pass_hbm, same, sems, pass_sem):
    count, states = all_ref.shape[0], landed.shape[1]
    loads = [
        start(
            pltpu.make_async_copy(
                landed.at[pl.ds(b * count, count)], all_ref.at[:, pl.ds(b * states, states), :], sems.at[b]
            )
        )
        for b in range(bands)
    ]
    for copy in loads:
        copy.wait()
    pass_half(all_ref, pass_hbm, pass_sem)


def early_kernel(after_ref, energy_ref, *refs):
    pieces, (all_ref, beside_ref, projs_ref, table_ref, token, sems) = refs[:-6], refs[-6:]
    states = pieces[0].shape[1]
    count, half, held = all_ref.shape[0] - 1, beside_ref.shape[0], projs_ref.shape[0]
    pairs = []
    for k, piece in enumerate(pieces):
        at = pl.ds(pl.multiple_of((lax.axis_index("band") ^ k) * states, states), states)
        pairs.append((piece.at[pl.ds(0, count)], all_ref.at[pl.ds(0, count), at, :]))
        pairs.append((piece.at[pl.ds(count, half)], beside_ref.at[:, at, :]))
        pairs.append((piece.at[pl.ds(count + half, held)], projs_ref.at[:, at, :]))
    loads = start_all(pairs, sems)
    all_ref[count] = after_ref[0]
    table_ref[...] = energy_table(energy_ref)
    wait_all(loads)


def add_products(row, all_ref, beside_refs, pot_ref, acc):
    half = beside_refs[0].shape[0]
    group = 4
    mine = (lax.axis_index("domain") & 1) * half
    for part, base in ((0, mine), (1, half - mine)):
        for i0 in range(0, half, group):
            xs, ys = [], []
            for i in range(i0, min(i0 + group, half)):
                cell = all_ref[base + i]
                x = cell.astype(F32)
                y = (3.0 + pot_ref[pl.ds(row + base + i, 1), :]) * x - pltpu.roll(x, x.shape[1] - 1, 1)
                y = y - all_ref[base + i + 1].astype(F32)
                if part == 0:
                    for ref in beside_refs:
                        y = y - ref[i].astype(F32)
                xs.append(cell)
                ys.append(y.astype(BF16))
            flat_x = jnp.concatenate(xs, axis=1)
            flat_y = jnp.concatenate(ys, axis=1)
            acc[0] += lax.dot_general(flat_x, flat_x, NT, preferred_element_type=F32)
            acc[1] += lax.dot_general(flat_y, flat_x, NT, preferred_element_type=F32)


def gram_kernel(first, share, all_ref, core_ref, link_ref, pot_ref, unread, acc):
    acc[...] = jnp.zeros_like(acc)
    add_products(lax.axis_index("band") * share + first, all_ref, (core_ref, link_ref), pot_ref, acc)


def final_kernel(bands, share, all_ref, beside_ref, pot_ref, begun_ref, proj_ref, energy_ref, out_ref, token, acc):
    acc[...] = begun_ref[...]
    add_products(lax.axis_index("band") * share, all_ref, (beside_ref,), pot_ref, acc)
    groups = proj_ref.shape[0]
    first = (lax.axis_index("domain") * bands + lax.axis_index("band")) * groups
    for g in range(groups):
        here = proj_ref[g]
        scaled = (here.astype(F32) * energy_ref[pl.ds(first + g, 1), :]).astype(BF16)
        acc[1] += lax.dot_general(scaled, here, NT, preferred_element_type=F32)
    hamil = 0.5 * (acc[1] + acc[1].T)
    domains = out_ref.shape[0] // bands
    rows, cols = out_ref.shape[1], out_ref.shape[2] // 2
    for c in range(domains):
        for r in range(bands):
            r0, c0 = r * rows, c * cols
            out_ref[c * bands + r, :, :cols] = acc[0, r0 : r0 + rows, c0 : c0 + cols].astype(BF16)
            out_ref[c * bands + r, :, cols:] = hamil[r0 : r0 + rows, c0 : c0 + cols].astype(BF16)


def result_kernel(scale, parts_ref, out_ref):
    total = jnp.sum(parts_ref[...].astype(F32), axis=0) * scale
    cols = out_ref.shape[2]
    out_ref[0] = total[:, :cols]
    out_ref[1] = total[:, cols:]


def local(orbitals, potential, projectors, tile_atom, tile_line, tile_count, energies):
    states, _, lines, cols_z = orbitals.shape
    slots, proj_count, _ = projectors.shape
    atom_total = energies.shape[0]
    domains, bands = lax.axis_size("domain"), lax.axis_size("band")
    total_states = states * bands
    atoms_here = atom_total // domains
    per_group = LANES // proj_count
    groups = atoms_here // per_group
    share = lines // bands
    first = 2 * (share * 3 // 32)
    rest = share - first

    core_pairs = [(i, i ^ 1) for i in range(domains) if i ^ 1 < domains]
    link_pairs = [(i, ((i + 1) ^ 1) - 1) for i in range(1, domains) if ((i + 1) ^ 1) - 1 < domains]
    near_far = [(i, i ^ 2) for i in range(domains) if i ^ 2 < domains]
    next = [(i, ((i + 2) ^ 2) - 2) for i in range(2, domains) if ((i + 2) ^ 2) - 2 < domains]
    far_pairs = [pairs for pairs in (near_far, next) if pairs]

    def swapped(values, axis):
        size = lax.axis_size(axis)
        got = {k: lax.ppermute(values[k - 1], axis, [(i, i ^ k) for i in range(size)]) for k in range(size - 1, 0, -1)}
        return [got[k] for k in range(1, size)]

    field = orbitals.reshape(states, lines, cols_z)
    pot = potential.reshape(lines, cols_z)
    energy = energies.T
    energy_rows = (atom_total // per_group, LANES)
    token = ((8, LANES), F32)
    eye = np.eye(cols_z, dtype=np.float32)
    ring = jnp.asarray(3.0 * eye - 0.5 * (np.roll(eye, 1, axis=0) + np.roll(eye, -1, axis=0)), dtype=BF16)

    late_lines = lines // 2
    line_shape, late_shape = (lines, states, cols_z), (late_lines, states, cols_z)
    xt, early_part, late_part, message = call(
        63,
        functools.partial(pack_kernel, first),
        (),
        [FAR],
        [FAR] * 4,
        [
            (line_shape, BF16),
            ((lines - late_lines, states, cols_z), BF16),
            (late_shape, BF16),
            ((bands * (rest + 1), states, cols_z), BF16),
        ],
        [
            pltpu.VMEM((states, lines, cols_z), BF16),
            pltpu.VMEM(line_shape, BF16),
            copies((bands,)),
            copies((5 * bands,)),
        ],
        (field,),
    )
    landed = lax.all_to_all(message, "band", split_axis=0, concat_axis=0, tiled=True)
    link_early = lax.ppermute(early_part, "domain", link_pairs)
    core_field = lax.ppermute(xt, "domain", core_pairs)

    group_shape = (groups, states, LANES)
    mine, to_core, to_link, *to_far = call(
        63,
        project_kernel,
        (),
        [SCALARS] * 3 + [FAR, PINNED],
        [PINNED] + [FAR] * (2 + len(far_pairs)),
        [((3 * groups, states, LANES), BF16)]
        + [((2 * groups, states, LANES), BF16)] * 2
        + [(group_shape, BF16)] * len(far_pairs),
        [
            pltpu.VMEM((3 * atoms_here + 1, proj_count, states), F32),
            pltpu.VMEM((3 * groups, states, LANES), BF16),
            pltpu.VMEM(line_shape, BF16),
            pltpu.VMEM(projectors.shape, BF16),
            copies((5,)),
            copies((5 + len(far_pairs),)),
        ],
        (tile_atom, tile_line, tile_count, xt, projectors),
    )
    from_link = lax.ppermute(to_link, "domain", link_pairs)
    from_far = [lax.ppermute(value, "domain", pairs) for value, pairs in zip(to_far, far_pairs)]
    from_core = lax.ppermute(to_core, "domain", core_pairs)
    (gate,) = call(
        63,
        wait_for,
        (),
        [UNREAD] * (4 + len(far_pairs)),
        [PINNED],
        [token],
        [],
        (from_core, from_link, *from_far, link_early, core_field),
    )
    held = groups // bands
    built_shape = (first + first // 2 + held, states, cols_z)
    beside_shape = (bands, first // 2, states, cols_z)
    added, own_message, *messages = call(
        62,
        functools.partial(nonlocal_kernel, len(far_pairs)),
        (),
        [SCALARS] * 3 + [FAR] * 3 + [PINNED, WHOLE, PINNED, WHOLE, WHOLE] + [WHOLE] * len(far_pairs) + [PINNED],
        [PINNED, PINNED] + [FAR] * (bands - 1),
        [(line_shape, F32)] + [(built_shape, BF16)] * bands,
        [
            pltpu.VMEM((lines + 1, states, cols_z), F32),
            pltpu.VMEM(group_shape, BF16),
            pltpu.VMEM((3 * groups, states, LANES), BF16),
            pltpu.VMEM((3 * groups, states, LANES), F32),
            pltpu.VMEM(energy_rows, F32),
            pltpu.VMEM((3 * atoms_here, states, proj_count), BF16),
            pltpu.VMEM(projectors.shape, BF16),
            pltpu.VMEM((bands, *built_shape), BF16),
            pltpu.VMEM(beside_shape, BF16),
            pltpu.VMEM(beside_shape, BF16),
            copies((4,)),
            copies((3 * bands,)),
            copies((bands,)),
        ],
        (
            tile_atom, tile_line, tile_count, xt, core_field, link_early, projectors, energy, mine, from_core,
            from_link, *from_far, gate,
        ),
        micros=8,
    )
    early = swapped(messages, "band")

    later_all, later_pass, late_part = call(
        32,
        functools.partial(later_kernel, bands),
        (),
        [FAR, PINNED, UNREAD],
        [NEAR, FAR, UNREAD],
        [
            ((rest + 1, total_states, cols_z), BF16),
            ((rest // 2, total_states, cols_z), BF16),
            (late_shape, BF16),
        ],
        [copies((bands,)), copies],
        (landed, own_message, late_part),
        aliases={2: 2},
    )
    later_link = lax.ppermute(later_pass, "domain", link_pairs)
    later_core = lax.ppermute(later_pass, "domain", core_pairs)
    link_late = lax.ppermute(late_part, "domain", link_pairs)

    early_all, early_beside, projs, energy_table_here, early_token = call(
        32,
        early_kernel,
        (),
        [NEAR, WHOLE, PINNED] + [FAR] * (bands - 1),
        [NEAR, NEAR, NEAR, NEAR, PINNED],
        [
            ((first + 1, total_states, cols_z), BF16),
            ((first // 2, total_states, cols_z), BF16),
            ((held, total_states, LANES), BF16),
            (energy_rows, F32),
            token,
        ],
        [copies((3 * bands,))],
        (later_all, energy, own_message, *early),
        micros=30,
    )
    (begun,) = call(
        32,
        functools.partial(gram_kernel, first, share),
        (),
        [NEAR, WHOLE, WHOLE, WHOLE, PINNED],
        [NEAR],
        [((2, total_states, total_states), F32)],
        [],
        (later_all, later_core, later_link, pot, early_token),
    )
    parts = domains * bands
    blocks, final_token = call(
        32,
        functools.partial(final_kernel, bands, share),
        (),
        [NEAR, NEAR, WHOLE, NEAR, NEAR, NEAR],
        [WHOLE, PINNED],
        [((parts, states, 2 * total_states // domains), BF16), token],
        [pltpu.VMEM((2, total_states, total_states), F32)],
        (early_all, early_beside, pot, begun, projs, energy_table_here),
    )
    summed = lax.all_to_all(blocks, ("domain", "band"), split_axis=0, concat_axis=0, tiled=True)
    span = 2 * ROWS
    steps = lines // span
    block = pl.BlockSpec((span, states, cols_z), lambda i: (i, 0, 0))
    (applied,) = call(
        60,
        functools.partial(stencil_kernel, share),
        (steps,),
        [
            block,
            pl.BlockSpec((1, states, cols_z), lambda i: (lax.rem(i * span + lines - 1, lines), 0, 0)),
            pl.BlockSpec((1, states, cols_z), lambda i: (lax.rem(i * span + span, lines), 0, 0)),
            block,
            pl.BlockSpec((span // 2, states, cols_z), lambda i: (i, 0, 0)),
            pl.BlockSpec((span // 2, states, cols_z), lambda i: (i, 0, 0)),
            block,
            pl.BlockSpec((span, cols_z), lambda i: (i, 0)),
            WHOLE,
            PINNED,
        ],
        [pl.BlockSpec((states, span, cols_z), lambda i: (0, i, 0))],
        [((states, lines, cols_z), BF16)],
        [],
        (
            xt, xt, xt, core_field, link_early, link_late, pltpu.with_memory_space_constraint(added, pltpu.HBM), pot, ring,
            final_token,
        ),
    )

    (subspace,) = call(
        32,
        functools.partial(result_kernel, 1.0 / (lines * cols_z * domains)),
        (),
        [WHOLE],
        [WHOLE],
        [((2, states, total_states // domains), F32)],
        [],
        (summed,),
    )
    return applied.reshape(orbitals.shape), subspace


def solution(mesh):
    in_specs = (
        P("band", ("groups", "domain"), None, None),
        P(("groups", "domain"), None, None),
        P(("groups", "domain"), None, None),
        P(("groups", "domain")),
        P(("groups", "domain")),
        P(("groups", "domain")),
        P("groups", None),
    )
    out_specs = (P("band", ("groups", "domain"), None, None), P(None, ("groups", "band"), "domain"))
    return jax.shard_map(local, mesh=mesh, in_specs=in_specs, out_specs=out_specs, check_vma=False)
```

```python
import functools

import jax
import jax.numpy as jnp
import numpy as np
from jax import lax
from jax.experimental import pallas as pl
from jax.experimental.pallas import tpu as pltpu
from jax.sharding import PartitionSpec as P

F32 = jnp.float32
BF16 = jnp.bfloat16
LANES = 128
ROWS = 16
NT = (((1,), (1,)), ((), ()))
WHOLE = pl.BlockSpec(memory_space=pltpu.VMEM)
NEAR = pl.BlockSpec(memory_space=pltpu.VMEM)
SCALARS = pl.BlockSpec(memory_space=pltpu.SMEM)
FAR = pl.BlockSpec(memory_space=pltpu.HBM)
PINNED = pl.BlockSpec(memory_space=pltpu.HBM)
UNREAD = pl.BlockSpec(memory_space=pl.ANY)
copies = pltpu.SemaphoreType.DMA


def call(room, kernel, grid, in_specs, out_specs, outs, scratch, args, aliases=None, micros=0.001):
    def place(spec):
        return {id(NEAR): pltpu.VMEM, id(PINNED): pltpu.HBM}.get(id(spec))

    args = [
        pltpu.with_memory_space_constraint(arg, place(spec)) if place(spec) else arg
        for spec, arg in zip(in_specs, args)
    ]
    shapes = [(place(spec) or jax.ShapeDtypeStruct)(shape, kind) for spec, (shape, kind) in zip(out_specs, outs)]
    return pl.pallas_call(
        kernel,
        grid=grid,
        out_shape=shapes,
        in_specs=in_specs,
        out_specs=out_specs,
        scratch_shapes=scratch,
        input_output_aliases=aliases or {},
        compiler_params=pltpu.CompilerParams(vmem_limit_bytes=room << 20),
        cost_estimate=pl.CostEstimate(flops=int(micros * 1.1e9), bytes_accessed=1 << 10, transcendentals=0),
    )(*args)


def start(copy):
    copy.start()
    return copy


def start_all(pairs, sems):
    return [start(pltpu.make_async_copy(source, target, sems.at[i])) for i, (source, target) in enumerate(pairs)]


def wait_all(started):
    for copy in started:
        copy.wait()


def wait_for(*refs):
    pass


def pack_kernel(first, x_hbm, xt_hbm, early, late, message, x, xt, in_sems, out_sems):
    states, lines, _ = x.shape
    bands = in_sems.shape[0]
    share = lines // bands
    count = share - first
    loads, sends = [], []
    for c in range(bands):
        where = (slice(None), pl.ds(c * share, share), slice(None))
        loads.append(start(pltpu.make_async_copy(x_hbm.at[where], x.at[where], in_sems.at[c])))

    def send(line, number, target, at):
        copy = pltpu.make_async_copy(
            xt.at[pl.ds(line, number)], target.at[pl.ds(at, number)], out_sems.at[len(sends)]
        )
        sends.append(start(copy))

    for c in range(bands):
        loads[c].wait()
        for y0 in range(c * share, (c + 1) * share, ROWS):
            for s0 in range(0, states, ROWS):
                block = x[s0 : s0 + ROWS, y0 : y0 + ROWS, :].astype(F32)
                turned = jnp.swapaxes(block, 0, 1).astype(BF16)
                xt[y0 : y0 + ROWS, s0 : s0 + ROWS, :] = turned
        send(c * share, share // 2, early, c * (share // 2))
        send(c * share + share // 2, share // 2, late, c * (share // 2))
        send(c * share + first, count, message, c * (count + 1))
        send(c * share, 1, message, (c + bands - 1) % bands * (count + 1) + count)
        send(c * share, share, xt_hbm, c * share)
    for copy in sends:
        copy.wait()


def bases(groups):
    domain = lax.axis_index("domain")
    odd, upper = domain & 1, (domain >> 1) & 1
    return [2 * groups * side for side in (1 - odd, odd, 1 - upper, upper)]


def slot_reader(atom_ref, line_ref, count_ref, atoms_here):
    first = (lax.axis_index("domain") - 1) * atoms_here
    live = count_ref[0]

    def slot_at(t):
        return line_ref[t], jnp.clip(atom_ref[t] - first, 0, 3 * atoms_here - 1), t < live

    return slot_at


def energy_table(energy_ref):
    proj_count, atoms = energy_ref.shape
    per_group = LANES // proj_count
    lane = lax.broadcasted_iota(jnp.int32, (proj_count, LANES), 1)
    row = lax.broadcasted_iota(jnp.int32, (proj_count, LANES), 0)
    pick = jnp.where(lane % proj_count == row, 1.0, 0.0).astype(F32)
    spread = jnp.dot(energy_ref[...].T, pick, precision=lax.Precision.HIGHEST, preferred_element_type=F32)
    spread = spread.reshape(atoms // per_group, per_group, LANES)
    lane = lax.broadcasted_iota(jnp.int32, spread.shape, 2)
    atom = lax.broadcasted_iota(jnp.int32, spread.shape, 1)
    return jnp.sum(jnp.where(lane // proj_count == atom, spread, 0.0), axis=1)


def project_kernel(atom_ref, line_ref, count_ref, xt_hbm, p_hbm, mine_hbm, core_hbm, link_hbm, *refs):
    far_hbms, (total, mine_ref, xt_ref, p_ref, sems, out_sems) = refs[:-6], refs[-6:]
    slots, proj_count, _ = p_ref.shape
    groups, states = mine_ref.shape[0] // 3, mine_ref.shape[1]
    per_group = LANES // proj_count
    chunks = sems.shape[0] - 1
    size = slots // chunks
    unroll = 16
    pairs = [(p_hbm.at[pl.ds(c * size, size)], p_ref.at[pl.ds(c * size, size)]) for c in range(chunks)]
    xt_load, *loads = start_all([(xt_hbm, xt_ref), *pairs], sems)

    def clear(i, carry):
        for u in range(per_group):
            total[i * per_group + u] = jnp.zeros_like(total[0])
        return carry

    lax.fori_loop(0, 3 * groups, clear, 0)

    slot_at = slot_reader(atom_ref, line_ref, count_ref, groups * per_group)

    def body(i, carry):
        for u in range(unroll):
            t = i * unroll + u
            line, atom, live = slot_at(t)
            part = lax.dot_general(p_ref[t], xt_ref[line], NT, preferred_element_type=F32)
            total[jnp.where(live, atom, 3 * groups * per_group)] += part
        return carry

    xt_load.wait()
    for c in range(chunks):
        loads[c].wait()
        lax.fori_loop(c * size // unroll, (c + 1) * size // unroll, body, 0)

    for g in range(3 * groups):
        tiles = [total[g * per_group + u] for u in range(per_group)]
        mine_ref[g] = jnp.concatenate(tiles, axis=0).T.astype(BF16)
    sides = bases(groups)
    pairs = [(mine_ref, mine_hbm)]
    for side, far in zip(sides[:2], (core_hbm, link_hbm)):
        pairs.append((mine_ref.at[pl.ds(side, groups)], far.at[pl.ds(0, groups)]))
        pairs.append((mine_ref.at[pl.ds(groups, groups)], far.at[pl.ds(groups, groups)]))
    for side, far in zip(sides[2:], far_hbms):
        pairs.append((mine_ref.at[pl.ds(side, groups)], far))
    wait_all(start_all(pairs, out_sems))


def nonlocal_kernel(
    fars, atom_ref, line_ref, count_ref, xt_hbm, beside_hbm, early_hbm, p_hbm, energy_ref, mine_hbm, core_ref, link_ref, *refs
):
    far_refs, out_hbm, messages, scratch = refs[:fars], refs[fars + 1], refs[fars + 2 : -13], refs[-13:]
    lines_sum, whole_ref, mine_ref, total, table, atoms, p_ref, built, cores, links, sems, in_sems, out_sems = scratch
    lines = xt_hbm.shape[0]
    bands, half = cores.shape[:2]
    share, first = lines // bands, 2 * half
    held = built.shape[1] - first - half
    mine = (lax.axis_index("domain") & 1) * half
    pairs = []
    for k in range(bands):
        to = lax.axis_index("band") ^ k
        pairs.append((xt_hbm.at[pl.ds(to * share, first)], built.at[k, pl.ds(0, first)]))
        pairs.append((beside_hbm.at[pl.ds(to * share + mine, half)], cores.at[k]))
        pairs.append((early_hbm.at[pl.ds(to * (share // 2) + mine, half)], links.at[k]))
    brought = start_all(pairs, in_sems)
    slots, proj_count, _ = p_ref.shape
    groups, states = total.shape[0] // 3, total.shape[1]
    per_group = LANES // proj_count
    unroll = 16
    mine_load, load = start_all([(mine_hbm, mine_ref), (p_hbm, p_ref)], sems)
    sends = []

    def clear(i, carry):
        lines_sum[i] = jnp.zeros((states, LANES), F32)
        return carry

    lax.fori_loop(0, lines + 1, clear, 0)
    mine_load.wait()
    total[...] = mine_ref[...].astype(F32)
    sides = bases(groups)
    for g in range(groups):
        total[groups + g] += core_ref[g].astype(F32) + link_ref[g].astype(F32)
        for side, ref in zip(sides[:2], (core_ref, link_ref)):
            total[side + g] += ref[groups + g].astype(F32)
        for side, ref in zip(sides[2:], far_refs):
            total[side + g] += ref[g].astype(F32)
    table[...] = energy_table(energy_ref)
    last = table.shape[0] - 1
    for g in range(3 * groups):
        row = jnp.clip((lax.axis_index("domain") - 1) * groups + g, 0, last)
        tile = (total[g] * table[pl.ds(row, 1), :]).astype(BF16)
        for u in range(per_group):
            atoms[g * per_group + u] = tile[:, u * proj_count : (u + 1) * proj_count]
    for g in range(groups):
        whole_ref[g] = total[groups + g].astype(BF16)
    wait_all(brought)
    for k, message in enumerate(messages):
        to = lax.axis_index("band") ^ k
        for i in range(half):
            built[k, first + i] = (cores[k, i].astype(F32) + links[k, i].astype(F32)).astype(BF16)
        for i in range(held):
            built[k, first + half + i] = whole_ref[to * held + i]
        sends.append(start(pltpu.make_async_copy(built.at[k], message, out_sems.at[k])))
    load.wait()

    slot_at = slot_reader(atom_ref, line_ref, count_ref, groups * per_group)

    def body(i, carry):
        for u in range(unroll):
            t = i * unroll + u
            line, atom, live = slot_at(t)
            part = jnp.dot(atoms[atom], p_ref[t], preferred_element_type=F32)
            lines_sum[jnp.where(live, line, lines)] += part
        return carry

    lax.fori_loop(0, slots // unroll, body, 0)
    sends.append(start(pltpu.make_async_copy(lines_sum.at[pl.ds(0, lines)], out_hbm, sems.at[3])))
    wait_all(sends)


def stencil_kernel(
    share, xt_ref, last_ref, next_ref, core_ref, early_ref, late_ref, added_ref, pot_ref, ring_ref, *refs
):
    out_ref = refs[-2]
    states, here, _ = out_ref.shape

    def link(i, rows):
        chunk, at = divmod(i, share)
        ref = early_ref if at < share // 2 else late_ref
        return ref[chunk * (share // 2) + at % (share // 2), rows, :]

    def line(i, rows):
        ref, at = (last_ref, 0) if i < 0 else (next_ref, 0) if i == here else (xt_ref, i)
        return ref[at, rows, :]

    for y0 in range(0, here, ROWS):
        for s0 in range(0, states, ROWS):
            rows = slice(s0, s0 + ROWS)
            results = []
            cells = jnp.concatenate([line(y0 + i, rows) for i in range(ROWS)], axis=0)
            along = jnp.dot(cells, ring_ref[...], preferred_element_type=F32)
            before, x = line(y0 - 1, rows).astype(F32), line(y0, rows).astype(F32)
            for i in range(ROWS):
                y = y0 + i
                after = line(y + 1, rows).astype(F32)
                beside = (before + after) + (core_ref[y, rows, :].astype(F32) + link(y, rows).astype(F32))
                value = along[i * ROWS : (i + 1) * ROWS] + pot_ref[y : y + 1, :] * x
                results.append(value + added_ref[y, rows, :] - 0.5 * beside)
                before, x = x, after
            turned = jnp.swapaxes(jnp.stack(results, axis=0), 0, 1).astype(BF16)
            out_ref[rows, y0 : y0 + ROWS, :] = turned


def pass_half(all_ref, pass_hbm, sem):
    half = pass_hbm.shape[0]
    copy = start(pltpu.make_async_copy(all_ref.at[pl.ds((1 - (lax.axis_index("domain") & 1)) * half, half)], pass_hbm, sem))
    copy.wait()


def later_kernel(bands, landed, unread, handed, all_ref, pass_hbm, same, token, sems, pass_sem):
    count, states = all_ref.shape[0], landed.shape[1]
    loads = [
        start(
            pltpu.make_async_copy(
                landed.at[pl.ds(b * count, count)], all_ref.at[:, pl.ds(b * states, states), :], sems.at[b]
            )
        )
        for b in range(bands)
    ]
    for copy in loads:
        copy.wait()
    pass_half(all_ref, pass_hbm, pass_sem)


def early_kernel(after_ref, energy_ref, unread, *refs):
    pieces, (all_ref, beside_ref, projs_ref, table_ref, token, sems) = refs[:-6], refs[-6:]
    states = pieces[0].shape[1]
    count, half, held = all_ref.shape[0] - 1, beside_ref.shape[0], projs_ref.shape[0]
    pairs = []
    for k, piece in enumerate(pieces):
        at = pl.ds(pl.multiple_of((lax.axis_index("band") ^ k) * states, states), states)
        pairs.append((piece.at[pl.ds(0, count)], all_ref.at[pl.ds(0, count), at, :]))
        pairs.append((piece.at[pl.ds(count, half)], beside_ref.at[:, at, :]))
        pairs.append((piece.at[pl.ds(count + half, held)], projs_ref.at[:, at, :]))
    loads = start_all(pairs, sems)
    all_ref[count] = after_ref[0]
    table_ref[...] = energy_table(energy_ref)
    wait_all(loads)


def add_products(row, all_ref, beside_refs, pot_ref, acc):
    half = beside_refs[0].shape[0]
    group = 4
    mine = (lax.axis_index("domain") & 1) * half
    for part, base in ((0, mine), (1, half - mine)):
        for i0 in range(0, half, group):
            xs, ys = [], []
            for i in range(i0, min(i0 + group, half)):
                cell = all_ref[base + i]
                x = cell.astype(F32)
                y = (3.0 + pot_ref[pl.ds(row + base + i, 1), :]) * x - pltpu.roll(x, x.shape[1] - 1, 1)
                y = y - all_ref[base + i + 1].astype(F32)
                if part == 0:
                    for ref in beside_refs:
                        y = y - ref[i].astype(F32)
                xs.append(cell)
                ys.append(y.astype(BF16))
            flat_x = jnp.concatenate(xs, axis=1)
            flat_y = jnp.concatenate(ys, axis=1)
            acc[0] += lax.dot_general(flat_x, flat_x, NT, preferred_element_type=F32)
            acc[1] += lax.dot_general(flat_y, flat_x, NT, preferred_element_type=F32)


def gram_kernel(first, share, all_ref, core_ref, link_ref, pot_ref, unread, acc):
    acc[...] = jnp.zeros_like(acc)
    add_products(lax.axis_index("band") * share + first, all_ref, (core_ref, link_ref), pot_ref, acc)


def final_kernel(bands, share, all_ref, beside_ref, pot_ref, begun_ref, proj_ref, energy_ref, out_ref, token, acc):
    acc[...] = begun_ref[...]
    add_products(lax.axis_index("band") * share, all_ref, (beside_ref,), pot_ref, acc)
    groups = proj_ref.shape[0]
    first = (lax.axis_index("domain") * bands + lax.axis_index("band")) * groups
    for g in range(groups):
        here = proj_ref[g]
        scaled = (here.astype(F32) * energy_ref[pl.ds(first + g, 1), :]).astype(BF16)
        acc[1] += lax.dot_general(scaled, here, NT, preferred_element_type=F32)
    hamil = 0.5 * (acc[1] + acc[1].T)
    domains = out_ref.shape[0] // bands
    rows, cols = out_ref.shape[1], out_ref.shape[2] // 2
    for c in range(domains):
        for r in range(bands):
            r0, c0 = r * rows, c * cols
            out_ref[c * bands + r, :, :cols] = acc[0, r0 : r0 + rows, c0 : c0 + cols].astype(BF16)
            out_ref[c * bands + r, :, cols:] = hamil[r0 : r0 + rows, c0 : c0 + cols].astype(BF16)


def result_kernel(scale, parts_ref, out_ref):
    total = jnp.sum(parts_ref[...].astype(F32), axis=0) * scale
    cols = out_ref.shape[2]
    out_ref[0] = total[:, :cols]
    out_ref[1] = total[:, cols:]


def local(orbitals, potential, projectors, tile_atom, tile_line, tile_count, energies):
    states, _, lines, cols_z = orbitals.shape
    slots, proj_count, _ = projectors.shape
    atom_total = energies.shape[0]
    domains, bands = lax.axis_size("domain"), lax.axis_size("band")
    total_states = states * bands
    atoms_here = atom_total // domains
    per_group = LANES // proj_count
    groups = atoms_here // per_group
    share = lines // bands
    first = 2 * (share * 3 // 32)
    rest = share - first

    core_pairs = [(i, i ^ 1) for i in range(domains) if i ^ 1 < domains]
    link_pairs = [(i, ((i + 1) ^ 1) - 1) for i in range(1, domains) if ((i + 1) ^ 1) - 1 < domains]
    near_far = [(i, i ^ 2) for i in range(domains) if i ^ 2 < domains]
    next = [(i, ((i + 2) ^ 2) - 2) for i in range(2, domains) if ((i + 2) ^ 2) - 2 < domains]
    far_pairs = [pairs for pairs in (near_far, next) if pairs]

    def swapped(values, axis):
        size = lax.axis_size(axis)
        got = {k: lax.ppermute(values[k - 1], axis, [(i, i ^ k) for i in range(size)]) for k in range(size - 1, 0, -1)}
        return [got[k] for k in range(1, size)]

    field = orbitals.reshape(states, lines, cols_z)
    pot = potential.reshape(lines, cols_z)
    energy = energies.T
    energy_rows = (atom_total // per_group, LANES)
    token = ((8, LANES), F32)
    eye = np.eye(cols_z, dtype=np.float32)
    ring = jnp.asarray(3.0 * eye - 0.5 * (np.roll(eye, 1, axis=0) + np.roll(eye, -1, axis=0)), dtype=BF16)

    late_lines = lines // 2
    line_shape, late_shape = (lines, states, cols_z), (late_lines, states, cols_z)
    xt, early_part, late_part, message = call(
        63,
        functools.partial(pack_kernel, first),
        (),
        [FAR],
        [FAR] * 4,
        [
            (line_shape, BF16),
            ((lines - late_lines, states, cols_z), BF16),
            (late_shape, BF16),
            ((bands * (rest + 1), states, cols_z), BF16),
        ],
        [
            pltpu.VMEM((states, lines, cols_z), BF16),
            pltpu.VMEM(line_shape, BF16),
            copies((bands,)),
            copies((5 * bands,)),
        ],
        (field,),
    )
    landed = lax.all_to_all(message, "band", split_axis=0, concat_axis=0, tiled=True)
    link_early = lax.ppermute(early_part, "domain", link_pairs)
    core_field = lax.ppermute(xt, "domain", core_pairs)

    group_shape = (groups, states, LANES)
    mine, to_core, to_link, *to_far = call(
        63,
        project_kernel,
        (),
        [SCALARS] * 3 + [FAR, PINNED],
        [PINNED] + [FAR] * (2 + len(far_pairs)),
        [((3 * groups, states, LANES), BF16)]
        + [((2 * groups, states, LANES), BF16)] * 2
        + [(group_shape, BF16)] * len(far_pairs),
        [
            pltpu.VMEM((3 * atoms_here + 1, proj_count, states), F32),
            pltpu.VMEM((3 * groups, states, LANES), BF16),
            pltpu.VMEM(line_shape, BF16),
            pltpu.VMEM(projectors.shape, BF16),
            copies((5,)),
            copies((5 + len(far_pairs),)),
        ],
        (tile_atom, tile_line, tile_count, xt, projectors),
    )
    from_link = lax.ppermute(to_link, "domain", link_pairs)
    from_far = [lax.ppermute(value, "domain", pairs) for value, pairs in zip(to_far, far_pairs)]
    from_core = lax.ppermute(to_core, "domain", core_pairs)
    (gate,) = call(
        63,
        wait_for,
        (),
        [UNREAD] * (4 + len(far_pairs)),
        [PINNED],
        [token],
        [],
        (from_core, from_link, *from_far, link_early, core_field),
    )
    held = groups // bands
    built_shape = (first + first // 2 + held, states, cols_z)
    beside_shape = (bands, first // 2, states, cols_z)
    added, own_message, *messages = call(
        62,
        functools.partial(nonlocal_kernel, len(far_pairs)),
        (),
        [SCALARS] * 3 + [FAR] * 3 + [PINNED, WHOLE, PINNED, WHOLE, WHOLE] + [WHOLE] * len(far_pairs) + [PINNED],
        [PINNED, PINNED] + [FAR] * (bands - 1),
        [(line_shape, F32)] + [(built_shape, BF16)] * bands,
        [
            pltpu.VMEM((lines + 1, states, cols_z), F32),
            pltpu.VMEM(group_shape, BF16),
            pltpu.VMEM((3 * groups, states, LANES), BF16),
            pltpu.VMEM((3 * groups, states, LANES), F32),
            pltpu.VMEM(energy_rows, F32),
            pltpu.VMEM((3 * atoms_here, states, proj_count), BF16),
            pltpu.VMEM(projectors.shape, BF16),
            pltpu.VMEM((bands, *built_shape), BF16),
            pltpu.VMEM(beside_shape, BF16),
            pltpu.VMEM(beside_shape, BF16),
            copies((4,)),
            copies((3 * bands,)),
            copies((bands,)),
        ],
        (
            tile_atom, tile_line, tile_count, xt, core_field, link_early, projectors, energy, mine, from_core,
            from_link, *from_far, gate,
        ),
        micros=8,
    )
    early = swapped(messages, "band")

    later_all, later_pass, late_part, later_token = call(
        32,
        functools.partial(later_kernel, bands),
        (),
        [FAR, PINNED, UNREAD],
        [NEAR, FAR, UNREAD, PINNED],
        [
            ((rest + 1, total_states, cols_z), BF16),
            ((rest // 2, total_states, cols_z), BF16),
            (late_shape, BF16),
            token,
        ],
        [copies((bands,)), copies],
        (landed, own_message, late_part),
        aliases={2: 2},
    )
    later_link = lax.ppermute(later_pass, "domain", link_pairs)
    later_core = lax.ppermute(later_pass, "domain", core_pairs)
    link_late = lax.ppermute(late_part, "domain", link_pairs)

    added_far = pltpu.with_memory_space_constraint(added, pltpu.HBM)

    def stencil(room, part, extra):
        span, every, skip, links = part
        steps = lines // (span * every)

        def place(i):
            return i * every + skip

        def line_of(offset):
            return pl.BlockSpec(
                (1, states, cols_z), lambda i: (lax.rem(place(i) * span + offset + lines, lines), 0, 0)
            )

        block = pl.BlockSpec((span, states, cols_z), lambda i: (place(i), 0, 0))
        link_block = pl.BlockSpec((span * every // 2, states, cols_z), lambda i: (i, 0, 0))
        return call(
            room,
            functools.partial(stencil_kernel, share if every == 1 else 2 * span),
            (steps,),
            [block, line_of(-1), line_of(span), block, link_block, link_block, block]
            + [pl.BlockSpec((span, cols_z), lambda i: (place(i), 0)), WHOLE, PINNED]
            + [UNREAD] * (len(extra) - 1),
            [pl.BlockSpec((states, span, cols_z), lambda i: (0, place(i), 0)), PINNED],
            [((states, lines, cols_z), BF16), token],
            [],
            (xt, xt, xt, core_field, *links, added_far, pot, ring, *extra),
            aliases={10: 0} if len(extra) > 1 else None,
        )

    applied, applied_token = [], later_token
    late_parts = (2 * ROWS, 1, 0, (link_early, link_late))
    if share // 2 % ROWS == 0:
        early_parts = (share // 2, 2, 0, (link_early, link_early))
        late_parts = (share // 2, 2, 1, (link_late, link_late))
        *applied, applied_token = stencil(32, early_parts, (later_token,))

    early_all, early_beside, projs, energy_table_here, early_token = call(
        32,
        early_kernel,
        (),
        [NEAR, WHOLE, PINNED, PINNED] + [FAR] * (bands - 1),
        [NEAR, NEAR, NEAR, NEAR, PINNED],
        [
            ((first + 1, total_states, cols_z), BF16),
            ((first // 2, total_states, cols_z), BF16),
            ((held, total_states, LANES), BF16),
            (energy_rows, F32),
            token,
        ],
        [copies((3 * bands,))],
        (later_all, energy, applied_token, own_message, *early),
        micros=30,
    )
    (begun,) = call(
        32,
        functools.partial(gram_kernel, first, share),
        (),
        [NEAR, WHOLE, WHOLE, WHOLE, PINNED],
        [NEAR],
        [((2, total_states, total_states), F32)],
        [],
        (later_all, later_core, later_link, pot, early_token),
    )
    parts = domains * bands
    blocks, final_token = call(
        32,
        functools.partial(final_kernel, bands, share),
        (),
        [NEAR, NEAR, WHOLE, NEAR, NEAR, NEAR],
        [WHOLE, PINNED],
        [((parts, states, 2 * total_states // domains), BF16), token],
        [pltpu.VMEM((2, total_states, total_states), F32)],
        (early_all, early_beside, pot, begun, projs, energy_table_here),
    )
    summed = lax.all_to_all(blocks, ("domain", "band"), split_axis=0, concat_axis=0, tiled=True)
    applied, _ = stencil(60, late_parts, (final_token, *applied))
    (subspace,) = call(
        32,
        functools.partial(result_kernel, 1.0 / (lines * cols_z * domains)),
        (),
        [WHOLE],
        [WHOLE],
        [((2, states, total_states // domains), F32)],
        [],
        (summed,),
    )
    return applied.reshape(orbitals.shape), subspace


def solution(mesh):
    in_specs = (
        P("band", ("groups", "domain"), None, None),
        P(("groups", "domain"), None, None),
        P(("groups", "domain"), None, None),
        P(("groups", "domain")),
        P(("groups", "domain")),
        P(("groups", "domain")),
        P("groups", None),
    )
    out_specs = (P("band", ("groups", "domain"), None, None), P(None, ("groups", "band"), "domain"))
    return jax.shard_map(local, mesh=mesh, in_specs=in_specs, out_specs=out_specs, check_vma=False)
```

```python
import functools

import jax
import jax.numpy as jnp
import numpy as np
from jax import lax
from jax.experimental import pallas as pl
from jax.experimental.pallas import tpu as pltpu
from jax.sharding import PartitionSpec as P

F32 = jnp.float32
BF16 = jnp.bfloat16
LANES = 128
ROWS = 16
NT = (((1,), (1,)), ((), ()))
WHOLE = pl.BlockSpec(memory_space=pltpu.VMEM)
NEAR = pl.BlockSpec(memory_space=pltpu.VMEM)
SCALARS = pl.BlockSpec(memory_space=pltpu.SMEM)
FAR = pl.BlockSpec(memory_space=pltpu.HBM)
PINNED = pl.BlockSpec(memory_space=pltpu.HBM)
UNREAD = pl.BlockSpec(memory_space=pl.ANY)
copies = pltpu.SemaphoreType.DMA


def call(room, kernel, grid, in_specs, out_specs, outs, scratch, args, aliases=None, micros=0.001):
    def place(spec):
        return {id(NEAR): pltpu.VMEM, id(PINNED): pltpu.HBM}.get(id(spec))

    args = [
        pltpu.with_memory_space_constraint(arg, place(spec)) if place(spec) else arg
        for spec, arg in zip(in_specs, args)
    ]
    shapes = [(place(spec) or jax.ShapeDtypeStruct)(shape, kind) for spec, (shape, kind) in zip(out_specs, outs)]
    return pl.pallas_call(
        kernel,
        grid=grid,
        out_shape=shapes,
        in_specs=in_specs,
        out_specs=out_specs,
        scratch_shapes=scratch,
        input_output_aliases=aliases or {},
        compiler_params=pltpu.CompilerParams(vmem_limit_bytes=room << 20),
        cost_estimate=pl.CostEstimate(flops=int(micros * 1.1e9), bytes_accessed=1 << 10, transcendentals=0),
    )(*args)


def start(copy):
    copy.start()
    return copy


def start_all(pairs, sems):
    return [start(pltpu.make_async_copy(source, target, sems.at[i])) for i, (source, target) in enumerate(pairs)]


def wait_all(started):
    for copy in started:
        copy.wait()


def wait_for(*refs):
    pass


def pack_kernel(first, x_hbm, xt_hbm, early, late, message, x, xt, in_sems, out_sems):
    states, lines, _ = x.shape
    bands = in_sems.shape[0]
    share = lines // bands
    count = share - first
    ahead = early.shape[0] // bands
    loads, sends = [], []
    for c in range(bands):
        where = (slice(None), pl.ds(c * share, share), slice(None))
        loads.append(start(pltpu.make_async_copy(x_hbm.at[where], x.at[where], in_sems.at[c])))

    def send(line, number, target, at):
        copy = pltpu.make_async_copy(
            xt.at[pl.ds(line, number)], target.at[pl.ds(at, number)], out_sems.at[len(sends)]
        )
        sends.append(start(copy))

    for c in range(bands):
        loads[c].wait()
        for y0 in range(c * share, (c + 1) * share, ROWS):
            for s0 in range(0, states, ROWS):
                block = x[s0 : s0 + ROWS, y0 : y0 + ROWS, :].astype(F32)
                turned = jnp.swapaxes(block, 0, 1).astype(BF16)
                xt[y0 : y0 + ROWS, s0 : s0 + ROWS, :] = turned
        send(c * share, ahead, early, c * ahead)
        send(c * share + ahead, share - ahead, late, c * (share - ahead))
        send(c * share + first, count, message, c * (count + 1))
        send(c * share, 1, message, (c + bands - 1) % bands * (count + 1) + count)
        send(c * share, share, xt_hbm, c * share)
    for copy in sends:
        copy.wait()


def bases(groups):
    domain = lax.axis_index("domain")
    odd, upper = domain & 1, (domain >> 1) & 1
    return [2 * groups * side for side in (1 - odd, odd, 1 - upper, upper)]


def slot_reader(atom_ref, line_ref, count_ref, atoms_here):
    first = (lax.axis_index("domain") - 1) * atoms_here
    live = count_ref[0]

    def slot_at(t):
        return line_ref[t], jnp.clip(atom_ref[t] - first, 0, 3 * atoms_here - 1), t < live

    return slot_at


def energy_table(energy_ref):
    proj_count, atoms = energy_ref.shape
    per_group = LANES // proj_count
    lane = lax.broadcasted_iota(jnp.int32, (proj_count, LANES), 1)
    row = lax.broadcasted_iota(jnp.int32, (proj_count, LANES), 0)
    pick = jnp.where(lane % proj_count == row, 1.0, 0.0).astype(F32)
    spread = jnp.dot(energy_ref[...].T, pick, precision=lax.Precision.HIGHEST, preferred_element_type=F32)
    spread = spread.reshape(atoms // per_group, per_group, LANES)
    lane = lax.broadcasted_iota(jnp.int32, spread.shape, 2)
    atom = lax.broadcasted_iota(jnp.int32, spread.shape, 1)
    return jnp.sum(jnp.where(lane // proj_count == atom, spread, 0.0), axis=1)


def project_kernel(atom_ref, line_ref, count_ref, xt_hbm, p_hbm, mine_hbm, core_hbm, link_hbm, *refs):
    far_hbms, (total, mine_ref, xt_ref, p_ref, sems, out_sems) = refs[:-6], refs[-6:]
    slots, proj_count, _ = p_ref.shape
    groups, states = mine_ref.shape[0] // 3, mine_ref.shape[1]
    per_group = LANES // proj_count
    chunks = sems.shape[0] - 1
    size = slots // chunks
    unroll = 16
    pairs = [(p_hbm.at[pl.ds(c * size, size)], p_ref.at[pl.ds(c * size, size)]) for c in range(chunks)]
    xt_load, *loads = start_all([(xt_hbm, xt_ref), *pairs], sems)

    def clear(i, carry):
        for u in range(per_group):
            total[i * per_group + u] = jnp.zeros_like(total[0])
        return carry

    lax.fori_loop(0, 3 * groups, clear, 0)

    slot_at = slot_reader(atom_ref, line_ref, count_ref, groups * per_group)

    def body(i, carry):
        for u in range(unroll):
            t = i * unroll + u
            line, atom, live = slot_at(t)
            part = lax.dot_general(p_ref[t], xt_ref[line], NT, preferred_element_type=F32)
            total[jnp.where(live, atom, 3 * groups * per_group)] += part
        return carry

    xt_load.wait()
    for c in range(chunks):
        loads[c].wait()
        lax.fori_loop(c * size // unroll, (c + 1) * size // unroll, body, 0)

    for g in range(3 * groups):
        tiles = [total[g * per_group + u] for u in range(per_group)]
        mine_ref[g] = jnp.concatenate(tiles, axis=0).T.astype(BF16)
    sides = bases(groups)
    pairs = [(mine_ref, mine_hbm)]
    for side, far in zip(sides[:2], (core_hbm, link_hbm)):
        pairs.append((mine_ref.at[pl.ds(side, groups)], far.at[pl.ds(0, groups)]))
        pairs.append((mine_ref.at[pl.ds(groups, groups)], far.at[pl.ds(groups, groups)]))
    for side, far in zip(sides[2:], far_hbms):
        pairs.append((mine_ref.at[pl.ds(side, groups)], far))
    wait_all(start_all(pairs, out_sems))


def nonlocal_kernel(
    fars, atom_ref, line_ref, count_ref, xt_hbm, beside_hbm, early_hbm, p_hbm, energy_ref, mine_hbm, core_ref, link_ref, *refs
):
    far_refs, out_hbm, messages, scratch = refs[:fars], refs[fars + 1], refs[fars + 2 : -13], refs[-13:]
    lines_sum, whole_ref, mine_ref, total, table, atoms, p_ref, built, cores, links, sems, in_sems, out_sems = scratch
    lines = xt_hbm.shape[0]
    bands, half = cores.shape[:2]
    share, first = lines // bands, 2 * half
    held = built.shape[1] - first - half
    ahead = early_hbm.shape[0] // bands
    mine = (lax.axis_index("domain") & 1) * half
    pairs = []
    for k in range(bands):
        to = lax.axis_index("band") ^ k
        pairs.append((xt_hbm.at[pl.ds(to * share, first)], built.at[k, pl.ds(0, first)]))
        pairs.append((beside_hbm.at[pl.ds(to * share + mine, half)], cores.at[k]))
        pairs.append((early_hbm.at[pl.ds(to * ahead + mine, half)], links.at[k]))
    brought = start_all(pairs, in_sems)
    slots, proj_count, _ = p_ref.shape
    groups, states = total.shape[0] // 3, total.shape[1]
    per_group = LANES // proj_count
    unroll = 16
    mine_load, load = start_all([(mine_hbm, mine_ref), (p_hbm, p_ref)], sems)
    sends = []

    def clear(i, carry):
        lines_sum[i] = jnp.zeros((states, LANES), F32)
        return carry

    lax.fori_loop(0, lines + 1, clear, 0)
    mine_load.wait()
    total[...] = mine_ref[...].astype(F32)
    sides = bases(groups)
    for g in range(groups):
        total[groups + g] += core_ref[g].astype(F32) + link_ref[g].astype(F32)
        for side, ref in zip(sides[:2], (core_ref, link_ref)):
            total[side + g] += ref[groups + g].astype(F32)
        for side, ref in zip(sides[2:], far_refs):
            total[side + g] += ref[g].astype(F32)
    table[...] = energy_table(energy_ref)
    last = table.shape[0] - 1
    for g in range(3 * groups):
        row = jnp.clip((lax.axis_index("domain") - 1) * groups + g, 0, last)
        tile = (total[g] * table[pl.ds(row, 1), :]).astype(BF16)
        for u in range(per_group):
            atoms[g * per_group + u] = tile[:, u * proj_count : (u + 1) * proj_count]
    for g in range(groups):
        whole_ref[g] = total[groups + g].astype(BF16)
    wait_all(brought)
    for k, message in enumerate(messages):
        to = lax.axis_index("band") ^ k
        for i in range(half):
            built[k, first + i] = (cores[k, i].astype(F32) + links[k, i].astype(F32)).astype(BF16)
        for i in range(held):
            built[k, first + half + i] = whole_ref[to * held + i]
        sends.append(start(pltpu.make_async_copy(built.at[k], message, out_sems.at[k])))
    load.wait()

    slot_at = slot_reader(atom_ref, line_ref, count_ref, groups * per_group)

    def body(i, carry):
        for u in range(unroll):
            t = i * unroll + u
            line, atom, live = slot_at(t)
            part = jnp.dot(atoms[atom], p_ref[t], preferred_element_type=F32)
            lines_sum[jnp.where(live, line, lines)] += part
        return carry

    lax.fori_loop(0, slots // unroll, body, 0)
    sends.append(start(pltpu.make_async_copy(lines_sum.at[pl.ds(0, lines)], out_hbm, sems.at[3])))
    wait_all(sends)


def stencil_kernel(
    share, xt_ref, last_ref, next_ref, core_ref, early_ref, late_ref, added_ref, pot_ref, ring_ref, unread,
    out_ref,
):
    states, here, _ = out_ref.shape

    ahead = early_ref.shape[0] * share // here

    def link(i, rows):
        chunk, at = divmod(i, share)
        if at < ahead:
            return early_ref[chunk * ahead + at, rows, :]
        return late_ref[chunk * (share - ahead) + at - ahead, rows, :]

    def line(i, rows):
        ref, at = (last_ref, 0) if i < 0 else (next_ref, 0) if i == here else (xt_ref, i)
        return ref[at, rows, :]

    for y0 in range(0, here, ROWS):
        for s0 in range(0, states, ROWS):
            rows = slice(s0, s0 + ROWS)
            results = []
            cells = jnp.concatenate([line(y0 + i, rows) for i in range(ROWS)], axis=0)
            along = jnp.dot(cells, ring_ref[...], preferred_element_type=F32)
            before, x = line(y0 - 1, rows).astype(F32), line(y0, rows).astype(F32)
            for i in range(ROWS):
                y = y0 + i
                after = line(y + 1, rows).astype(F32)
                beside = (before + after) + (core_ref[y, rows, :].astype(F32) + link(y, rows).astype(F32))
                value = along[i * ROWS : (i + 1) * ROWS] + pot_ref[y : y + 1, :] * x
                results.append(value + added_ref[y, rows, :] - 0.5 * beside)
                before, x = x, after
            turned = jnp.swapaxes(jnp.stack(results, axis=0), 0, 1).astype(BF16)
            out_ref[rows, y0 : y0 + ROWS, :] = turned


def pass_half(all_ref, pass_hbm, sem):
    half = pass_hbm.shape[0]
    copy = start(pltpu.make_async_copy(all_ref.at[pl.ds((1 - (lax.axis_index("domain") & 1)) * half, half)], pass_hbm, sem))
    copy.wait()


def later_kernel(bands, landed, unread, handed, all_ref, pass_hbm, same, sems, pass_sem):
    count, states = all_ref.shape[0], landed.shape[1]
    loads = [
        start(
            pltpu.make_async_copy(
                landed.at[pl.ds(b * count, count)], all_ref.at[:, pl.ds(b * states, states), :], sems.at[b]
            )
        )
        for b in range(bands)
    ]
    for copy in loads:
        copy.wait()
    pass_half(all_ref, pass_hbm, pass_sem)


def early_kernel(after_ref, energy_ref, *refs):
    pieces, (all_ref, beside_ref, projs_ref, table_ref, token, sems) = refs[:-6], refs[-6:]
    states = pieces[0].shape[1]
    count, half, held = all_ref.shape[0] - 1, beside_ref.shape[0], projs_ref.shape[0]
    pairs = []
    for k, piece in enumerate(pieces):
        at = pl.ds(pl.multiple_of((lax.axis_index("band") ^ k) * states, states), states)
        pairs.append((piece.at[pl.ds(0, count)], all_ref.at[pl.ds(0, count), at, :]))
        pairs.append((piece.at[pl.ds(count, half)], beside_ref.at[:, at, :]))
        pairs.append((piece.at[pl.ds(count + half, held)], projs_ref.at[:, at, :]))
    loads = start_all(pairs, sems)
    all_ref[count] = after_ref[0]
    table_ref[...] = energy_table(energy_ref)
    wait_all(loads)


def add_products(row, all_ref, beside_refs, pot_ref, acc):
    half = beside_refs[0].shape[0]
    group = 4
    mine = (lax.axis_index("domain") & 1) * half
    for part, base in ((0, mine), (1, half - mine)):
        for i0 in range(0, half, group):
            xs, ys = [], []
            for i in range(i0, min(i0 + group, half)):
                cell = all_ref[base + i]
                x = cell.astype(F32)
                y = (3.0 + pot_ref[pl.ds(row + base + i, 1), :]) * x - pltpu.roll(x, x.shape[1] - 1, 1)
                y = y - all_ref[base + i + 1].astype(F32)
                if part == 0:
                    for ref in beside_refs:
                        y = y - ref[i].astype(F32)
                xs.append(cell)
                ys.append(y.astype(BF16))
            flat_x = jnp.concatenate(xs, axis=1)
            flat_y = jnp.concatenate(ys, axis=1)
            acc[0] += lax.dot_general(flat_x, flat_x, NT, preferred_element_type=F32)
            acc[1] += lax.dot_general(flat_y, flat_x, NT, preferred_element_type=F32)


def gram_kernel(first, share, all_ref, core_ref, link_ref, pot_ref, unread, acc):
    acc[...] = jnp.zeros_like(acc)
    add_products(lax.axis_index("band") * share + first, all_ref, (core_ref, link_ref), pot_ref, acc)


def final_kernel(bands, share, all_ref, beside_ref, pot_ref, begun_ref, proj_ref, energy_ref, out_ref, token, acc):
    acc[...] = begun_ref[...]
    add_products(lax.axis_index("band") * share, all_ref, (beside_ref,), pot_ref, acc)
    groups = proj_ref.shape[0]
    first = (lax.axis_index("domain") * bands + lax.axis_index("band")) * groups
    for g in range(groups):
        here = proj_ref[g]
        scaled = (here.astype(F32) * energy_ref[pl.ds(first + g, 1), :]).astype(BF16)
        acc[1] += lax.dot_general(scaled, here, NT, preferred_element_type=F32)
    hamil = 0.5 * (acc[1] + acc[1].T)
    domains = out_ref.shape[0] // bands
    rows, cols = out_ref.shape[1], out_ref.shape[2] // 2
    for c in range(domains):
        for r in range(bands):
            r0, c0 = r * rows, c * cols
            out_ref[c * bands + r, :, :cols] = acc[0, r0 : r0 + rows, c0 : c0 + cols].astype(BF16)
            out_ref[c * bands + r, :, cols:] = hamil[r0 : r0 + rows, c0 : c0 + cols].astype(BF16)


def result_kernel(scale, parts_ref, out_ref):
    total = jnp.sum(parts_ref[...].astype(F32), axis=0) * scale
    cols = out_ref.shape[2]
    out_ref[0] = total[:, :cols]
    out_ref[1] = total[:, cols:]


def local(orbitals, potential, projectors, tile_atom, tile_line, tile_count, energies):
    states, _, lines, cols_z = orbitals.shape
    slots, proj_count, _ = projectors.shape
    atom_total = energies.shape[0]
    domains, bands = lax.axis_size("domain"), lax.axis_size("band")
    total_states = states * bands
    atoms_here = atom_total // domains
    per_group = LANES // proj_count
    groups = atoms_here // per_group
    share = lines // bands
    first = 2 * (share * 3 // 32)
    rest = share - first

    core_pairs = [(i, i ^ 1) for i in range(domains) if i ^ 1 < domains]
    link_pairs = [(i, ((i + 1) ^ 1) - 1) for i in range(1, domains) if ((i + 1) ^ 1) - 1 < domains]
    near_far = [(i, i ^ 2) for i in range(domains) if i ^ 2 < domains]
    next = [(i, ((i + 2) ^ 2) - 2) for i in range(2, domains) if ((i + 2) ^ 2) - 2 < domains]
    far_pairs = [pairs for pairs in (near_far, next) if pairs]

    def swapped(values, axis):
        size = lax.axis_size(axis)
        got = {k: lax.ppermute(values[k - 1], axis, [(i, i ^ k) for i in range(size)]) for k in range(size - 1, 0, -1)}
        return [got[k] for k in range(1, size)]

    field = orbitals.reshape(states, lines, cols_z)
    pot = potential.reshape(lines, cols_z)
    energy = energies.T
    energy_rows = (atom_total // per_group, LANES)
    token = ((8, LANES), F32)
    eye = np.eye(cols_z, dtype=np.float32)
    ring = jnp.asarray(3.0 * eye - 0.5 * (np.roll(eye, 1, axis=0) + np.roll(eye, -1, axis=0)), dtype=BF16)

    ahead = share * 5 // 8
    late_lines = lines - ahead * bands
    line_shape, late_shape = (lines, states, cols_z), (late_lines, states, cols_z)
    xt, early_part, late_part, message = call(
        63,
        functools.partial(pack_kernel, first),
        (),
        [FAR],
        [FAR] * 4,
        [
            (line_shape, BF16),
            ((lines - late_lines, states, cols_z), BF16),
            (late_shape, BF16),
            ((bands * (rest + 1), states, cols_z), BF16),
        ],
        [
            pltpu.VMEM((states, lines, cols_z), BF16),
            pltpu.VMEM(line_shape, BF16),
            copies((bands,)),
            copies((5 * bands,)),
        ],
        (field,),
    )
    landed = lax.all_to_all(message, "band", split_axis=0, concat_axis=0, tiled=True)
    link_early = lax.ppermute(early_part, "domain", link_pairs)
    core_field = lax.ppermute(xt, "domain", core_pairs)

    group_shape = (groups, states, LANES)
    mine, to_core, to_link, *to_far = call(
        63,
        project_kernel,
        (),
        [SCALARS] * 3 + [FAR, PINNED],
        [PINNED] + [FAR] * (2 + len(far_pairs)),
        [((3 * groups, states, LANES), BF16)]
        + [((2 * groups, states, LANES), BF16)] * 2
        + [(group_shape, BF16)] * len(far_pairs),
        [
            pltpu.VMEM((3 * atoms_here + 1, proj_count, states), F32),
            pltpu.VMEM((3 * groups, states, LANES), BF16),
            pltpu.VMEM(line_shape, BF16),
            pltpu.VMEM(projectors.shape, BF16),
            copies((5,)),
            copies((5 + len(far_pairs),)),
        ],
        (tile_atom, tile_line, tile_count, xt, projectors),
    )
    from_link = lax.ppermute(to_link, "domain", link_pairs)
    from_far = [lax.ppermute(value, "domain", pairs) for value, pairs in zip(to_far, far_pairs)]
    from_core = lax.ppermute(to_core, "domain", core_pairs)
    (gate,) = call(
        63,
        wait_for,
        (),
        [UNREAD] * (4 + len(far_pairs)),
        [PINNED],
        [token],
        [],
        (from_core, from_link, *from_far, link_early, core_field),
    )
    held = groups // bands
    built_shape = (first + first // 2 + held, states, cols_z)
    beside_shape = (bands, first // 2, states, cols_z)
    added, own_message, *messages = call(
        62,
        functools.partial(nonlocal_kernel, len(far_pairs)),
        (),
        [SCALARS] * 3 + [FAR] * 3 + [PINNED, WHOLE, PINNED, WHOLE, WHOLE] + [WHOLE] * len(far_pairs) + [PINNED],
        [PINNED, PINNED] + [FAR] * (bands - 1),
        [(line_shape, F32)] + [(built_shape, BF16)] * bands,
        [
            pltpu.VMEM((lines + 1, states, cols_z), F32),
            pltpu.VMEM(group_shape, BF16),
            pltpu.VMEM((3 * groups, states, LANES), BF16),
            pltpu.VMEM((3 * groups, states, LANES), F32),
            pltpu.VMEM(energy_rows, F32),
            pltpu.VMEM((3 * atoms_here, states, proj_count), BF16),
            pltpu.VMEM(projectors.shape, BF16),
            pltpu.VMEM((bands, *built_shape), BF16),
            pltpu.VMEM(beside_shape, BF16),
            pltpu.VMEM(beside_shape, BF16),
            copies((4,)),
            copies((3 * bands,)),
            copies((bands,)),
        ],
        (
            tile_atom, tile_line, tile_count, xt, core_field, link_early, projectors, energy, mine, from_core,
            from_link, *from_far, gate,
        ),
        micros=8,
    )
    early = swapped(messages, "band")

    later_all, later_pass, late_part = call(
        32,
        functools.partial(later_kernel, bands),
        (),
        [FAR, PINNED, UNREAD],
        [NEAR, FAR, UNREAD],
        [
            ((rest + 1, total_states, cols_z), BF16),
            ((rest // 2, total_states, cols_z), BF16),
            (late_shape, BF16),
        ],
        [copies((bands,)), copies],
        (landed, own_message, late_part),
        aliases={2: 2},
    )
    later_link = lax.ppermute(later_pass, "domain", link_pairs)
    later_core = lax.ppermute(later_pass, "domain", core_pairs)
    link_late = lax.ppermute(late_part, "domain", link_pairs)

    early_all, early_beside, projs, energy_table_here, early_token = call(
        32,
        early_kernel,
        (),
        [NEAR, WHOLE, PINNED] + [FAR] * (bands - 1),
        [NEAR, NEAR, NEAR, NEAR, PINNED],
        [
            ((first + 1, total_states, cols_z), BF16),
            ((first // 2, total_states, cols_z), BF16),
            ((held, total_states, LANES), BF16),
            (energy_rows, F32),
            token,
        ],
        [copies((3 * bands,))],
        (later_all, energy, own_message, *early),
        micros=30,
    )
    (begun,) = call(
        32,
        functools.partial(gram_kernel, first, share),
        (),
        [NEAR, WHOLE, WHOLE, WHOLE, PINNED],
        [NEAR],
        [((2, total_states, total_states), F32)],
        [],
        (later_all, later_core, later_link, pot, early_token),
    )
    parts = domains * bands
    blocks, final_token = call(
        32,
        functools.partial(final_kernel, bands, share),
        (),
        [NEAR, NEAR, WHOLE, NEAR, NEAR, NEAR],
        [WHOLE, PINNED],
        [((parts, states, 2 * total_states // domains), BF16), token],
        [pltpu.VMEM((2, total_states, total_states), F32)],
        (early_all, early_beside, pot, begun, projs, energy_table_here),
    )
    summed = lax.all_to_all(blocks, ("domain", "band"), split_axis=0, concat_axis=0, tiled=True)
    span = 2 * ROWS
    steps = lines // span
    block = pl.BlockSpec((span, states, cols_z), lambda i: (i, 0, 0))
    (applied,) = call(
        60,
        functools.partial(stencil_kernel, share),
        (steps,),
        [
            block,
            pl.BlockSpec((1, states, cols_z), lambda i: (lax.rem(i * span + lines - 1, lines), 0, 0)),
            pl.BlockSpec((1, states, cols_z), lambda i: (lax.rem(i * span + span, lines), 0, 0)),
            block,
            pl.BlockSpec((ahead * bands // steps, states, cols_z), lambda i: (i, 0, 0)),
            pl.BlockSpec((late_lines // steps, states, cols_z), lambda i: (i, 0, 0)),
            block,
            pl.BlockSpec((span, cols_z), lambda i: (i, 0)),
            WHOLE,
            PINNED,
        ],
        [pl.BlockSpec((states, span, cols_z), lambda i: (0, i, 0))],
        [((states, lines, cols_z), BF16)],
        [],
        (
            xt, xt, xt, core_field, link_early, link_late, pltpu.with_memory_space_constraint(added, pltpu.HBM), pot, ring,
            final_token,
        ),
    )

    (subspace,) = call(
        32,
        functools.partial(result_kernel, 1.0 / (lines * cols_z * domains)),
        (),
        [WHOLE],
        [WHOLE],
        [((2, states, total_states // domains), F32)],
        [],
        (summed,),
    )
    return applied.reshape(orbitals.shape), subspace


def solution(mesh):
    in_specs = (
        P("band", ("groups", "domain"), None, None),
        P(("groups", "domain"), None, None),
        P(("groups", "domain"), None, None),
        P(("groups", "domain")),
        P(("groups", "domain")),
        P(("groups", "domain")),
        P("groups", None),
    )
    out_specs = (P("band", ("groups", "domain"), None, None), P(None, ("groups", "band"), "domain"))
    return jax.shard_map(local, mesh=mesh, in_specs=in_specs, out_specs=out_specs, check_vma=False)
```

```python
import functools

import jax
import jax.numpy as jnp
import numpy as np
from jax import lax
from jax.experimental import pallas as pl
from jax.experimental.pallas import tpu as pltpu
from jax.sharding import PartitionSpec as P

F32 = jnp.float32
BF16 = jnp.bfloat16
LANES = 128
ROWS = 16
NT = (((1,), (1,)), ((), ()))
WHOLE = pl.BlockSpec(memory_space=pltpu.VMEM)
NEAR = pl.BlockSpec(memory_space=pltpu.VMEM)
SCALARS = pl.BlockSpec(memory_space=pltpu.SMEM)
FAR = pl.BlockSpec(memory_space=pltpu.HBM)
PINNED = pl.BlockSpec(memory_space=pltpu.HBM)
UNREAD = pl.BlockSpec(memory_space=pl.ANY)
copies = pltpu.SemaphoreType.DMA


def call(room, kernel, grid, in_specs, out_specs, outs, scratch, args, aliases=None, micros=0.001):
    def place(spec):
        return {id(NEAR): pltpu.VMEM, id(PINNED): pltpu.HBM}.get(id(spec))

    args = [
        pltpu.with_memory_space_constraint(arg, place(spec)) if place(spec) else arg
        for spec, arg in zip(in_specs, args)
    ]
    shapes = [(place(spec) or jax.ShapeDtypeStruct)(shape, kind) for spec, (shape, kind) in zip(out_specs, outs)]
    return pl.pallas_call(
        kernel,
        grid=grid,
        out_shape=shapes,
        in_specs=in_specs,
        out_specs=out_specs,
        scratch_shapes=scratch,
        input_output_aliases=aliases or {},
        compiler_params=pltpu.CompilerParams(vmem_limit_bytes=room << 20),
        cost_estimate=pl.CostEstimate(flops=int(micros * 1.1e9), bytes_accessed=1 << 10, transcendentals=0),
    )(*args)


def start(copy):
    copy.start()
    return copy


def start_all(pairs, sems):
    return [start(pltpu.make_async_copy(source, target, sems.at[i])) for i, (source, target) in enumerate(pairs)]


def wait_all(started):
    for copy in started:
        copy.wait()


def wait_for(*refs):
    pass


def pack_kernel(first, x_hbm, xt_hbm, early, late, message, x, xt, in_sems, out_sems):
    states, lines, _ = x.shape
    bands = in_sems.shape[0]
    share = lines // bands
    count = share - first
    ahead = early.shape[0] // bands
    loads, sends = [], []
    for c in range(bands):
        where = (slice(None), pl.ds(c * share, share), slice(None))
        loads.append(start(pltpu.make_async_copy(x_hbm.at[where], x.at[where], in_sems.at[c])))

    def send(line, number, target, at):
        copy = pltpu.make_async_copy(
            xt.at[pl.ds(line, number)], target.at[pl.ds(at, number)], out_sems.at[len(sends)]
        )
        sends.append(start(copy))

    for c in range(bands):
        loads[c].wait()
        for y0 in range(c * share, (c + 1) * share, ROWS):
            for s0 in range(0, states, ROWS):
                block = x[s0 : s0 + ROWS, y0 : y0 + ROWS, :]
                xt[y0 : y0 + ROWS, s0 : s0 + ROWS, :] = jnp.swapaxes(block, 0, 1)
        send(c * share, ahead, early, c * ahead)
        send(c * share + ahead, share - ahead, late, c * (share - ahead))
        send(c * share + first, count, message, c * (count + 1))
        send(c * share, 1, message, (c + bands - 1) % bands * (count + 1) + count)
        send(c * share, share, xt_hbm, c * share)
    for copy in sends:
        copy.wait()


def bases(groups):
    domain = lax.axis_index("domain")
    odd, upper = domain & 1, (domain >> 1) & 1
    return [2 * groups * side for side in (1 - odd, odd, 1 - upper, upper)]


def slot_reader(atom_ref, line_ref, count_ref, atoms_here):
    first = (lax.axis_index("domain") - 1) * atoms_here
    live = count_ref[0]

    def slot_at(t):
        return line_ref[t], jnp.clip(atom_ref[t] - first, 0, 3 * atoms_here - 1), t < live

    return slot_at


def energy_table(energy_ref):
    proj_count, atoms = energy_ref.shape
    per_group = LANES // proj_count
    lane = lax.broadcasted_iota(jnp.int32, (proj_count, LANES), 1)
    row = lax.broadcasted_iota(jnp.int32, (proj_count, LANES), 0)
    pick = jnp.where(lane % proj_count == row, 1.0, 0.0).astype(F32)
    spread = jnp.dot(energy_ref[...].T, pick, precision=lax.Precision.HIGHEST, preferred_element_type=F32)
    spread = spread.reshape(atoms // per_group, per_group, LANES)
    lane = lax.broadcasted_iota(jnp.int32, spread.shape, 2)
    atom = lax.broadcasted_iota(jnp.int32, spread.shape, 1)
    return jnp.sum(jnp.where(lane // proj_count == atom, spread, 0.0), axis=1)


def project_kernel(atom_ref, line_ref, count_ref, xt_hbm, p_hbm, mine_hbm, core_hbm, link_hbm, *refs):
    far_hbms, (total, mine_ref, xt_ref, p_ref, sems, out_sems) = refs[:-6], refs[-6:]
    slots, proj_count, _ = p_ref.shape
    groups, states = mine_ref.shape[0] // 3, mine_ref.shape[1]
    per_group = LANES // proj_count
    chunks = sems.shape[0] - 1
    size = slots // chunks
    unroll = 32
    pairs = [(p_hbm.at[pl.ds(c * size, size)], p_ref.at[pl.ds(c * size, size)]) for c in range(chunks)]
    xt_load, *loads = start_all([(xt_hbm, xt_ref), *pairs], sems)

    def clear(i, carry):
        for u in range(per_group):
            total[i * per_group + u] = jnp.zeros_like(total[0])
        return carry

    lax.fori_loop(0, 3 * groups, clear, 0)

    slot_at = slot_reader(atom_ref, line_ref, count_ref, groups * per_group)

    def body(i, carry):
        for u in range(unroll):
            t = i * unroll + u
            line, atom, live = slot_at(t)
            part = lax.dot_general(p_ref[t], xt_ref[line], NT, preferred_element_type=F32)
            total[jnp.where(live, atom, 3 * groups * per_group)] += part
        return carry

    xt_load.wait()
    for c in range(chunks):
        loads[c].wait()
        lax.fori_loop(c * size // unroll, (c + 1) * size // unroll, body, 0)

    for g in range(3 * groups):
        tiles = [total[g * per_group + u] for u in range(per_group)]
        mine_ref[g] = jnp.concatenate(tiles, axis=0).T.astype(BF16)
    sides = bases(groups)
    pairs = [(mine_ref, mine_hbm)]
    for side, far in zip(sides[:2], (core_hbm, link_hbm)):
        pairs.append((mine_ref.at[pl.ds(side, groups)], far.at[pl.ds(0, groups)]))
        pairs.append((mine_ref.at[pl.ds(groups, groups)], far.at[pl.ds(groups, groups)]))
    for side, far in zip(sides[2:], far_hbms):
        pairs.append((mine_ref.at[pl.ds(side, groups)], far))
    wait_all(start_all(pairs, out_sems))


def nonlocal_kernel(
    fars, atom_ref, line_ref, count_ref, xt_hbm, beside_hbm, early_hbm, p_hbm, energy_ref, mine_hbm, core_ref, link_ref, *refs
):
    far_refs, out_hbm, messages, scratch = refs[:fars], refs[fars + 1], refs[fars + 2 : -13], refs[-13:]
    lines_sum, whole_ref, mine_ref, total, table, atoms, p_ref, built, cores, links, sems, in_sems, out_sems = scratch
    lines = xt_hbm.shape[0]
    bands, half = cores.shape[:2]
    share, first = lines // bands, 2 * half
    held = built.shape[1] - first - half
    ahead = early_hbm.shape[0] // bands
    mine = (lax.axis_index("domain") & 1) * half
    pairs = []
    for k in range(bands):
        to = lax.axis_index("band") ^ k
        pairs.append((xt_hbm.at[pl.ds(to * share, first)], built.at[k, pl.ds(0, first)]))
        pairs.append((beside_hbm.at[pl.ds(to * share + mine, half)], cores.at[k]))
        pairs.append((early_hbm.at[pl.ds(to * ahead + mine, half)], links.at[k]))
    brought = start_all(pairs, in_sems)
    slots, proj_count, _ = p_ref.shape
    groups, states = total.shape[0] // 3, total.shape[1]
    per_group = LANES // proj_count
    unroll = 32
    mine_load, load = start_all([(mine_hbm, mine_ref), (p_hbm, p_ref)], sems)
    sends = []

    def clear(i, carry):
        lines_sum[i] = jnp.zeros((states, LANES), F32)
        return carry

    lax.fori_loop(0, lines + 1, clear, 0)
    mine_load.wait()
    total[...] = mine_ref[...].astype(F32)
    sides = bases(groups)
    for g in range(groups):
        total[groups + g] += core_ref[g].astype(F32) + link_ref[g].astype(F32)
        for side, ref in zip(sides[:2], (core_ref, link_ref)):
            total[side + g] += ref[groups + g].astype(F32)
        for side, ref in zip(sides[2:], far_refs):
            total[side + g] += ref[g].astype(F32)
    table[...] = energy_table(energy_ref)
    last = table.shape[0] - 1
    for g in range(3 * groups):
        row = jnp.clip((lax.axis_index("domain") - 1) * groups + g, 0, last)
        tile = (total[g] * table[pl.ds(row, 1), :]).astype(BF16)
        for u in range(per_group):
            atoms[g * per_group + u] = tile[:, u * proj_count : (u + 1) * proj_count]
    for g in range(groups):
        whole_ref[g] = total[groups + g].astype(BF16)
    wait_all(brought)
    for k, message in enumerate(messages):
        to = lax.axis_index("band") ^ k
        for i in range(half):
            built[k, first + i] = (cores[k, i].astype(F32) + links[k, i].astype(F32)).astype(BF16)
        for i in range(held):
            built[k, first + half + i] = whole_ref[to * held + i]
        sends.append(start(pltpu.make_async_copy(built.at[k], message, out_sems.at[k])))
    load.wait()

    slot_at = slot_reader(atom_ref, line_ref, count_ref, groups * per_group)

    def body(i, carry):
        for u in range(unroll):
            t = i * unroll + u
            line, atom, live = slot_at(t)
            part = jnp.dot(atoms[atom], p_ref[t], preferred_element_type=F32)
            lines_sum[jnp.where(live, line, lines)] += part
        return carry

    lax.fori_loop(0, slots // unroll, body, 0)
    sends.append(start(pltpu.make_async_copy(lines_sum.at[pl.ds(0, lines)], out_hbm, sems.at[3])))
    wait_all(sends)


def stencil_kernel(
    share, xt_ref, last_ref, next_ref, core_ref, early_ref, late_ref, added_ref, pot_ref, ring_ref, unread,
    out_ref,
):
    states, here, _ = out_ref.shape

    ahead = early_ref.shape[0] * share // here

    def link(i, rows):
        chunk, at = divmod(i, share)
        if at < ahead:
            return early_ref[chunk * ahead + at, rows, :]
        return late_ref[chunk * (share - ahead) + at - ahead, rows, :]

    def line(i, rows):
        ref, at = (last_ref, 0) if i < 0 else (next_ref, 0) if i == here else (xt_ref, i)
        return ref[at, rows, :]

    for y0 in range(0, here, ROWS):
        for s0 in range(0, states, ROWS):
            rows = slice(s0, s0 + ROWS)
            results = []
            cells = jnp.concatenate([line(y0 + i, rows) for i in range(ROWS)], axis=0)
            along = jnp.dot(cells, ring_ref[...], preferred_element_type=F32)
            before, x = line(y0 - 1, rows).astype(F32), line(y0, rows).astype(F32)
            for i in range(ROWS):
                y = y0 + i
                after = line(y + 1, rows).astype(F32)
                beside = (before + after) + (core_ref[y, rows, :].astype(F32) + link(y, rows).astype(F32))
                value = along[i * ROWS : (i + 1) * ROWS] + pot_ref[y : y + 1, :] * x
                results.append((value + added_ref[y, rows, :] - 0.5 * beside).astype(BF16))
                before, x = x, after
            out_ref[rows, y0 : y0 + ROWS, :] = jnp.swapaxes(jnp.stack(results, axis=0), 0, 1)


def pass_half(all_ref, pass_hbm, sem):
    half = pass_hbm.shape[0]
    copy = start(pltpu.make_async_copy(all_ref.at[pl.ds((1 - (lax.axis_index("domain") & 1)) * half, half)], pass_hbm, sem))
    copy.wait()


def later_kernel(bands, landed, unread, handed, all_ref, pass_hbm, same, sems, pass_sem):
    count, states = all_ref.shape[0], landed.shape[1]
    loads = [
        start(
            pltpu.make_async_copy(
                landed.at[pl.ds(b * count, count)], all_ref.at[:, pl.ds(b * states, states), :], sems.at[b]
            )
        )
        for b in range(bands)
    ]
    for copy in loads:
        copy.wait()
    pass_half(all_ref, pass_hbm, pass_sem)


def early_kernel(after_ref, energy_ref, *refs):
    pieces, (all_ref, beside_ref, projs_ref, table_ref, token, sems) = refs[:-6], refs[-6:]
    states = pieces[0].shape[1]
    count, half, held = all_ref.shape[0] - 1, beside_ref.shape[0], projs_ref.shape[0]
    pairs = []
    for k, piece in enumerate(pieces):
        at = pl.ds(pl.multiple_of((lax.axis_index("band") ^ k) * states, states), states)
        pairs.append((piece.at[pl.ds(0, count)], all_ref.at[pl.ds(0, count), at, :]))
        pairs.append((piece.at[pl.ds(count, half)], beside_ref.at[:, at, :]))
        pairs.append((piece.at[pl.ds(count + half, held)], projs_ref.at[:, at, :]))
    loads = start_all(pairs, sems)
    all_ref[count] = after_ref[0]
    table_ref[...] = energy_table(energy_ref)
    wait_all(loads)


def add_products(row, all_ref, beside_refs, pot_ref, acc):
    half = beside_refs[0].shape[0]
    group = 4
    mine = (lax.axis_index("domain") & 1) * half
    for part, base in ((0, mine), (1, half - mine)):
        for i0 in range(0, half, group):
            xs, ys = [], []
            for i in range(i0, min(i0 + group, half)):
                cell = all_ref[base + i]
                x = cell.astype(F32)
                y = (3.0 + pot_ref[pl.ds(row + base + i, 1), :]) * x - pltpu.roll(x, x.shape[1] - 1, 1)
                y = y - all_ref[base + i + 1].astype(F32)
                if part == 0:
                    for ref in beside_refs:
                        y = y - ref[i].astype(F32)
                xs.append(cell)
                ys.append(y.astype(BF16))
            flat_x = jnp.concatenate(xs, axis=1)
            flat_y = jnp.concatenate(ys, axis=1)
            acc[0] += lax.dot_general(flat_x, flat_x, NT, preferred_element_type=F32)
            acc[1] += lax.dot_general(flat_y, flat_x, NT, preferred_element_type=F32)


def gram_kernel(first, share, all_ref, core_ref, link_ref, pot_ref, unread, acc):
    acc[...] = jnp.zeros_like(acc)
    add_products(lax.axis_index("band") * share + first, all_ref, (core_ref, link_ref), pot_ref, acc)


def final_kernel(bands, share, all_ref, beside_ref, pot_ref, begun_ref, proj_ref, energy_ref, out_ref, token, acc):
    acc[...] = begun_ref[...]
    add_products(lax.axis_index("band") * share, all_ref, (beside_ref,), pot_ref, acc)
    groups = proj_ref.shape[0]
    first = (lax.axis_index("domain") * bands + lax.axis_index("band")) * groups
    for g in range(groups):
        here = proj_ref[g]
        scaled = (here.astype(F32) * energy_ref[pl.ds(first + g, 1), :]).astype(BF16)
        acc[1] += lax.dot_general(scaled, here, NT, preferred_element_type=F32)
    hamil = 0.5 * (acc[1] + acc[1].T)
    domains = out_ref.shape[0] // bands
    rows, cols = out_ref.shape[1], out_ref.shape[2] // 2
    for c in range(domains):
        for r in range(bands):
            r0, c0 = r * rows, c * cols
            out_ref[c * bands + r, :, :cols] = acc[0, r0 : r0 + rows, c0 : c0 + cols].astype(BF16)
            out_ref[c * bands + r, :, cols:] = hamil[r0 : r0 + rows, c0 : c0 + cols].astype(BF16)


def result_kernel(scale, parts_ref, out_ref):
    total = jnp.sum(parts_ref[...].astype(F32), axis=0) * scale
    cols = out_ref.shape[2]
    out_ref[0] = total[:, :cols]
    out_ref[1] = total[:, cols:]


def local(orbitals, potential, projectors, tile_atom, tile_line, tile_count, energies):
    states, _, lines, cols_z = orbitals.shape
    slots, proj_count, _ = projectors.shape
    atom_total = energies.shape[0]
    domains, bands = lax.axis_size("domain"), lax.axis_size("band")
    total_states = states * bands
    atoms_here = atom_total // domains
    per_group = LANES // proj_count
    groups = atoms_here // per_group
    share = lines // bands
    first = 2 * (share * 3 // 32)
    rest = share - first

    core_pairs = [(i, i ^ 1) for i in range(domains) if i ^ 1 < domains]
    link_pairs = [(i, ((i + 1) ^ 1) - 1) for i in range(1, domains) if ((i + 1) ^ 1) - 1 < domains]
    near_far = [(i, i ^ 2) for i in range(domains) if i ^ 2 < domains]
    next = [(i, ((i + 2) ^ 2) - 2) for i in range(2, domains) if ((i + 2) ^ 2) - 2 < domains]
    far_pairs = [pairs for pairs in (near_far, next) if pairs]

    def swapped(values, axis):
        size = lax.axis_size(axis)
        got = {k: lax.ppermute(values[k - 1], axis, [(i, i ^ k) for i in range(size)]) for k in range(size - 1, 0, -1)}
        return [got[k] for k in range(1, size)]

    field = orbitals.reshape(states, lines, cols_z)
    pot = potential.reshape(lines, cols_z)
    energy = energies.T
    energy_rows = (atom_total // per_group, LANES)
    token = ((8, LANES), F32)
    eye = np.eye(cols_z, dtype=np.float32)
    ring = jnp.asarray(3.0 * eye - 0.5 * (np.roll(eye, 1, axis=0) + np.roll(eye, -1, axis=0)), dtype=BF16)

    ahead = share * 9 // 16
    late_lines = lines - ahead * bands
    line_shape, late_shape = (lines, states, cols_z), (late_lines, states, cols_z)
    xt, early_part, late_part, message = call(
        63,
        functools.partial(pack_kernel, first),
        (),
        [FAR],
        [FAR] * 4,
        [
            (line_shape, BF16),
            ((lines - late_lines, states, cols_z), BF16),
            (late_shape, BF16),
            ((bands * (rest + 1), states, cols_z), BF16),
        ],
        [
            pltpu.VMEM((states, lines, cols_z), BF16),
            pltpu.VMEM(line_shape, BF16),
            copies((bands,)),
            copies((5 * bands,)),
        ],
        (field,),
    )
    landed = lax.all_to_all(message, "band", split_axis=0, concat_axis=0, tiled=True)
    link_early = lax.ppermute(early_part, "domain", link_pairs)
    core_field = lax.ppermute(xt, "domain", core_pairs)

    group_shape = (groups, states, LANES)
    mine, to_core, to_link, *to_far = call(
        63,
        project_kernel,
        (),
        [SCALARS] * 3 + [FAR, PINNED],
        [PINNED] + [FAR] * (2 + len(far_pairs)),
        [((3 * groups, states, LANES), BF16)]
        + [((2 * groups, states, LANES), BF16)] * 2
        + [(group_shape, BF16)] * len(far_pairs),
        [
            pltpu.VMEM((3 * atoms_here + 1, proj_count, states), F32),
            pltpu.VMEM((3 * groups, states, LANES), BF16),
            pltpu.VMEM(line_shape, BF16),
            pltpu.VMEM(projectors.shape, BF16),
            copies((5,)),
            copies((5 + len(far_pairs),)),
        ],
        (tile_atom, tile_line, tile_count, xt, projectors),
    )
    from_link = lax.ppermute(to_link, "domain", link_pairs)
    from_far = [lax.ppermute(value, "domain", pairs) for value, pairs in zip(to_far, far_pairs)]
    from_core = lax.ppermute(to_core, "domain", core_pairs)
    (gate,) = call(
        63,
        wait_for,
        (),
        [UNREAD] * (4 + len(far_pairs)),
        [PINNED],
        [token],
        [],
        (from_core, from_link, *from_far, link_early, core_field),
    )
    held = groups // bands
    built_shape = (first + first // 2 + held, states, cols_z)
    beside_shape = (bands, first // 2, states, cols_z)
    added, own_message, *messages = call(
        62,
        functools.partial(nonlocal_kernel, len(far_pairs)),
        (),
        [SCALARS] * 3 + [FAR] * 3 + [PINNED, WHOLE, PINNED, WHOLE, WHOLE] + [WHOLE] * len(far_pairs) + [PINNED],
        [PINNED, PINNED] + [FAR] * (bands - 1),
        [(line_shape, F32)] + [(built_shape, BF16)] * bands,
        [
            pltpu.VMEM((lines + 1, states, cols_z), F32),
            pltpu.VMEM(group_shape, BF16),
            pltpu.VMEM((3 * groups, states, LANES), BF16),
            pltpu.VMEM((3 * groups, states, LANES), F32),
            pltpu.VMEM(energy_rows, F32),
            pltpu.VMEM((3 * atoms_here, states, proj_count), BF16),
            pltpu.VMEM(projectors.shape, BF16),
            pltpu.VMEM((bands, *built_shape), BF16),
            pltpu.VMEM(beside_shape, BF16),
            pltpu.VMEM(beside_shape, BF16),
            copies((4,)),
            copies((3 * bands,)),
            copies((bands,)),
        ],
        (
            tile_atom, tile_line, tile_count, xt, core_field, link_early, projectors, energy, mine, from_core,
            from_link, *from_far, gate,
        ),
        micros=8,
    )
    early = swapped(messages, "band")

    later_all, later_pass, late_part = call(
        32,
        functools.partial(later_kernel, bands),
        (),
        [FAR, PINNED, UNREAD],
        [NEAR, FAR, UNREAD],
        [
            ((rest + 1, total_states, cols_z), BF16),
            ((rest // 2, total_states, cols_z), BF16),
            (late_shape, BF16),
        ],
        [copies((bands,)), copies],
        (landed, own_message, late_part),
        aliases={2: 2},
    )
    later_link = lax.ppermute(later_pass, "domain", link_pairs)
    later_core = lax.ppermute(later_pass, "domain", core_pairs)
    link_late = lax.ppermute(late_part, "domain", link_pairs)

    early_all, early_beside, projs, energy_table_here, early_token = call(
        32,
        early_kernel,
        (),
        [NEAR, WHOLE, PINNED] + [FAR] * (bands - 1),
        [NEAR, NEAR, NEAR, NEAR, PINNED],
        [
            ((first + 1, total_states, cols_z), BF16),
            ((first // 2, total_states, cols_z), BF16),
            ((held, total_states, LANES), BF16),
            (energy_rows, F32),
            token,
        ],
        [copies((3 * bands,))],
        (later_all, energy, own_message, *early),
        micros=30,
    )
    (begun,) = call(
        32,
        functools.partial(gram_kernel, first, share),
        (),
        [NEAR, WHOLE, WHOLE, WHOLE, PINNED],
        [NEAR],
        [((2, total_states, total_states), F32)],
        [],
        (later_all, later_core, later_link, pot, early_token),
    )
    parts = domains * bands
    blocks, final_token = call(
        32,
        functools.partial(final_kernel, bands, share),
        (),
        [NEAR, NEAR, WHOLE, NEAR, NEAR, NEAR],
        [WHOLE, PINNED],
        [((parts, states, 2 * total_states // domains), BF16), token],
        [pltpu.VMEM((2, total_states, total_states), F32)],
        (early_all, early_beside, pot, begun, projs, energy_table_here),
    )
    summed = lax.all_to_all(blocks, ("domain", "band"), split_axis=0, concat_axis=0, tiled=True)
    span = 2 * ROWS
    steps = lines // span
    block = pl.BlockSpec((span, states, cols_z), lambda i: (i, 0, 0))
    (applied,) = call(
        62,
        functools.partial(stencil_kernel, share),
        (steps,),
        [
            block,
            pl.BlockSpec((1, states, cols_z), lambda i: (lax.rem(i * span + lines - 1, lines), 0, 0)),
            pl.BlockSpec((1, states, cols_z), lambda i: (lax.rem(i * span + span, lines), 0, 0)),
            block,
            pl.BlockSpec((ahead * bands // steps, states, cols_z), lambda i: (i, 0, 0)),
            pl.BlockSpec((late_lines // steps, states, cols_z), lambda i: (i, 0, 0)),
            block,
            pl.BlockSpec((span, cols_z), lambda i: (i, 0)),
            WHOLE,
            PINNED,
        ],
        [pl.BlockSpec((states, span, cols_z), lambda i: (0, i, 0))],
        [((states, lines, cols_z), BF16)],
        [],
        (
            xt, xt, xt, core_field, link_early, link_late, pltpu.with_memory_space_constraint(added, pltpu.HBM), pot, ring,
            final_token,
        ),
    )

    (subspace,) = call(
        32,
        functools.partial(result_kernel, 1.0 / (lines * cols_z * domains)),
        (),
        [WHOLE],
        [WHOLE],
        [((2, states, total_states // domains), F32)],
        [],
        (summed,),
    )
    return applied.reshape(orbitals.shape), subspace


def solution(mesh):
    in_specs = (
        P("band", ("groups", "domain"), None, None),
        P(("groups", "domain"), None, None),
        P(("groups", "domain"), None, None),
        P(("groups", "domain")),
        P(("groups", "domain")),
        P(("groups", "domain")),
        P("groups", None),
    )
    out_specs = (P("band", ("groups", "domain"), None, None), P(None, ("groups", "band"), "domain"))
    return jax.shard_map(local, mesh=mesh, in_specs=in_specs, out_specs=out_specs, check_vma=False)
```

```python
import functools

import jax
import jax.numpy as jnp
import numpy as np
from jax import lax
from jax.experimental import pallas as pl
from jax.experimental.pallas import tpu as pltpu
from jax.sharding import PartitionSpec as P

F32 = jnp.float32
BF16 = jnp.bfloat16
LANES = 128
ROWS = 16
NT = (((1,), (1,)), ((), ()))
WHOLE = pl.BlockSpec(memory_space=pltpu.VMEM)
NEAR = pl.BlockSpec(memory_space=pltpu.VMEM)
SCALARS = pl.BlockSpec(memory_space=pltpu.SMEM)
FAR = pl.BlockSpec(memory_space=pltpu.HBM)
PINNED = pl.BlockSpec(memory_space=pltpu.HBM)
UNREAD = pl.BlockSpec(memory_space=pl.ANY)
copies = pltpu.SemaphoreType.DMA


def call(room, kernel, grid, in_specs, out_specs, outs, scratch, args, aliases=None, micros=0.001):
    def place(spec):
        return {id(NEAR): pltpu.VMEM, id(PINNED): pltpu.HBM}.get(id(spec))

    args = [
        pltpu.with_memory_space_constraint(arg, place(spec)) if place(spec) else arg
        for spec, arg in zip(in_specs, args)
    ]
    shapes = [(place(spec) or jax.ShapeDtypeStruct)(shape, kind) for spec, (shape, kind) in zip(out_specs, outs)]
    return pl.pallas_call(
        kernel,
        grid=grid,
        out_shape=shapes,
        in_specs=in_specs,
        out_specs=out_specs,
        scratch_shapes=scratch,
        input_output_aliases=aliases or {},
        compiler_params=pltpu.CompilerParams(vmem_limit_bytes=room << 20),
        cost_estimate=pl.CostEstimate(flops=int(micros * 1.1e9), bytes_accessed=1 << 10, transcendentals=0),
    )(*args)


def start(copy):
    copy.start()
    return copy


def start_all(pairs, sems):
    return [start(pltpu.make_async_copy(source, target, sems.at[i])) for i, (source, target) in enumerate(pairs)]


def wait_all(started):
    for copy in started:
        copy.wait()


def wait_for(*refs):
    pass


def pack_kernel(first, x_hbm, xt_hbm, early, late, message, x, xt, in_sems, out_sems):
    states, lines, _ = x.shape
    bands = in_sems.shape[0]
    share = lines // bands
    count = share - first
    ahead = early.shape[0] // bands
    loads, sends = [], []
    for c in range(bands):
        where = (slice(None), pl.ds(c * share, share), slice(None))
        loads.append(start(pltpu.make_async_copy(x_hbm.at[where], x.at[where], in_sems.at[c])))

    def send(line, number, target, at):
        copy = pltpu.make_async_copy(
            xt.at[pl.ds(line, number)], target.at[pl.ds(at, number)], out_sems.at[len(sends)]
        )
        sends.append(start(copy))

    for c in range(bands):
        loads[c].wait()
        for y0 in range(c * share, (c + 1) * share, ROWS):
            for s0 in range(0, states, ROWS):
                block = x[s0 : s0 + ROWS, y0 : y0 + ROWS, :]
                xt[y0 : y0 + ROWS, s0 : s0 + ROWS, :] = jnp.swapaxes(block, 0, 1)
        send(c * share, ahead, early, c * ahead)
        send(c * share + ahead, share - ahead, late, c * (share - ahead))
        send(c * share + first, count, message, c * (count + 1))
        send(c * share, 1, message, (c + bands - 1) % bands * (count + 1) + count)
        send(c * share, share, xt_hbm, c * share)
    for copy in sends:
        copy.wait()


def bases(groups):
    domain = lax.axis_index("domain")
    odd, upper = domain & 1, (domain >> 1) & 1
    return [2 * groups * side for side in (1 - odd, odd, 1 - upper, upper)]


def slot_reader(atom_ref, line_ref, count_ref, atoms_here):
    first = (lax.axis_index("domain") - 1) * atoms_here
    live = count_ref[0]

    def slot_at(t):
        return line_ref[t], jnp.clip(atom_ref[t] - first, 0, 3 * atoms_here - 1), t < live

    return slot_at


def energy_table(energy_ref):
    proj_count, atoms = energy_ref.shape
    per_group = LANES // proj_count
    lane = lax.broadcasted_iota(jnp.int32, (proj_count, LANES), 1)
    row = lax.broadcasted_iota(jnp.int32, (proj_count, LANES), 0)
    pick = jnp.where(lane % proj_count == row, 1.0, 0.0).astype(F32)
    spread = jnp.dot(energy_ref[...].T, pick, precision=lax.Precision.HIGHEST, preferred_element_type=F32)
    spread = spread.reshape(atoms // per_group, per_group, LANES)
    lane = lax.broadcasted_iota(jnp.int32, spread.shape, 2)
    atom = lax.broadcasted_iota(jnp.int32, spread.shape, 1)
    return jnp.sum(jnp.where(lane // proj_count == atom, spread, 0.0), axis=1)


def project_kernel(atom_ref, line_ref, count_ref, xt_hbm, p_hbm, mine_hbm, core_hbm, link_hbm, *refs):
    far_hbms, (total, mine_ref, xt_ref, p_ref, sems, out_sems) = refs[:-6], refs[-6:]
    slots, proj_count, _ = p_ref.shape
    groups, states = mine_ref.shape[0] // 3, mine_ref.shape[1]
    per_group = LANES // proj_count
    chunks = sems.shape[0] - 1
    size = slots // chunks
    unroll = 48
    pairs = [(p_hbm.at[pl.ds(c * size, size)], p_ref.at[pl.ds(c * size, size)]) for c in range(chunks)]
    xt_load, *loads = start_all([(xt_hbm, xt_ref), *pairs], sems)

    def clear(i, carry):
        for u in range(per_group):
            total[i * per_group + u] = jnp.zeros_like(total[0])
        return carry

    lax.fori_loop(0, 3 * groups, clear, 0)

    slot_at = slot_reader(atom_ref, line_ref, count_ref, groups * per_group)

    def body(i, carry):
        for u in range(unroll):
            t = i * unroll + u
            line, atom, live = slot_at(t)
            part = lax.dot_general(p_ref[t], xt_ref[line], NT, preferred_element_type=F32)
            total[jnp.where(live, atom, 3 * groups * per_group)] += part
        return carry

    xt_load.wait()
    for c in range(chunks):
        loads[c].wait()
        lax.fori_loop(c * size // unroll, (c + 1) * size // unroll, body, 0)

    for g in range(3 * groups):
        tiles = [total[g * per_group + u] for u in range(per_group)]
        mine_ref[g] = jnp.concatenate(tiles, axis=0).T.astype(BF16)
    sides = bases(groups)
    pairs = [(mine_ref, mine_hbm)]
    for side, far in zip(sides[:2], (core_hbm, link_hbm)):
        pairs.append((mine_ref.at[pl.ds(side, groups)], far.at[pl.ds(0, groups)]))
        pairs.append((mine_ref.at[pl.ds(groups, groups)], far.at[pl.ds(groups, groups)]))
    for side, far in zip(sides[2:], far_hbms):
        pairs.append((mine_ref.at[pl.ds(side, groups)], far))
    wait_all(start_all(pairs, out_sems))


def nonlocal_kernel(
    fars, atom_ref, line_ref, count_ref, xt_hbm, beside_hbm, early_hbm, p_hbm, energy_ref, mine_hbm, core_ref, link_ref, *refs
):
    far_refs, out_hbm, messages, scratch = refs[:fars], refs[fars + 1], refs[fars + 2 : -13], refs[-13:]
    lines_sum, whole_ref, mine_ref, total, table, atoms, p_ref, built, cores, links, sems, in_sems, out_sems = scratch
    lines = xt_hbm.shape[0]
    bands, half = cores.shape[:2]
    share, first = lines // bands, 2 * half
    held = built.shape[1] - first - half
    ahead = early_hbm.shape[0] // bands
    mine = (lax.axis_index("domain") & 1) * half
    pairs = []
    for k in range(bands):
        to = lax.axis_index("band") ^ k
        pairs.append((xt_hbm.at[pl.ds(to * share, first)], built.at[k, pl.ds(0, first)]))
        pairs.append((beside_hbm.at[pl.ds(to * share + mine, half)], cores.at[k]))
        pairs.append((early_hbm.at[pl.ds(to * ahead + mine, half)], links.at[k]))
    brought = start_all(pairs, in_sems)
    slots, proj_count, _ = p_ref.shape
    groups, states = total.shape[0] // 3, total.shape[1]
    per_group = LANES // proj_count
    unroll = 48
    mine_load, load = start_all([(mine_hbm, mine_ref), (p_hbm, p_ref)], sems)
    sends = []

    def clear(i, carry):
        lines_sum[i] = jnp.zeros((states, LANES), F32)
        return carry

    lax.fori_loop(0, lines + 1, clear, 0)
    mine_load.wait()
    total[...] = mine_ref[...].astype(F32)
    sides = bases(groups)
    for g in range(groups):
        total[groups + g] += core_ref[g].astype(F32) + link_ref[g].astype(F32)
        for side, ref in zip(sides[:2], (core_ref, link_ref)):
            total[side + g] += ref[groups + g].astype(F32)
        for side, ref in zip(sides[2:], far_refs):
            total[side + g] += ref[g].astype(F32)
    table[...] = energy_table(energy_ref)
    last = table.shape[0] - 1
    for g in range(3 * groups):
        row = jnp.clip((lax.axis_index("domain") - 1) * groups + g, 0, last)
        tile = (total[g] * table[pl.ds(row, 1), :]).astype(BF16)
        for u in range(per_group):
            atoms[g * per_group + u] = tile[:, u * proj_count : (u + 1) * proj_count]
    for g in range(groups):
        whole_ref[g] = total[groups + g].astype(BF16)
    wait_all(brought)
    for k, message in enumerate(messages):
        to = lax.axis_index("band") ^ k
        for i in range(half):
            built[k, first + i] = (cores[k, i].astype(F32) + links[k, i].astype(F32)).astype(BF16)
        for i in range(held):
            built[k, first + half + i] = whole_ref[to * held + i]
        sends.append(start(pltpu.make_async_copy(built.at[k], message, out_sems.at[k])))
    load.wait()

    slot_at = slot_reader(atom_ref, line_ref, count_ref, groups * per_group)

    def body(i, carry):
        for u in range(unroll):
            t = i * unroll + u
            line, atom, live = slot_at(t)
            part = jnp.dot(atoms[atom], p_ref[t], preferred_element_type=F32)
            lines_sum[jnp.where(live, line, lines)] += part
        return carry

    lax.fori_loop(0, slots // unroll, body, 0)
    sends.append(start(pltpu.make_async_copy(lines_sum.at[pl.ds(0, lines)], out_hbm, sems.at[3])))
    wait_all(sends)


def stencil_kernel(
    share, xt_ref, last_ref, next_ref, core_ref, early_ref, late_ref, added_ref, pot_ref, ring_ref, unread,
    out_ref,
):
    states, here, _ = out_ref.shape

    ahead = early_ref.shape[0] * share // here

    def link(i, rows):
        chunk, at = divmod(i, share)
        if at < ahead:
            return early_ref[chunk * ahead + at, rows, :]
        return late_ref[chunk * (share - ahead) + at - ahead, rows, :]

    def line(i, rows):
        ref, at = (last_ref, 0) if i < 0 else (next_ref, 0) if i == here else (xt_ref, i)
        return ref[at, rows, :]

    for y0 in range(0, here, ROWS):
        for s0 in range(0, states, ROWS):
            rows = slice(s0, s0 + ROWS)
            results = []
            cells = jnp.concatenate([line(y0 + i, rows) for i in range(ROWS)], axis=0)
            along = jnp.dot(cells, ring_ref[...], preferred_element_type=F32)
            before, x = line(y0 - 1, rows).astype(F32), line(y0, rows).astype(F32)
            for i in range(ROWS):
                y = y0 + i
                after = line(y + 1, rows).astype(F32)
                beside = (before + after) + (core_ref[y, rows, :].astype(F32) + link(y, rows).astype(F32))
                value = along[i * ROWS : (i + 1) * ROWS] + pot_ref[y : y + 1, :] * x
                results.append((value + added_ref[y, rows, :] - 0.5 * beside).astype(BF16))
                before, x = x, after
            out_ref[rows, y0 : y0 + ROWS, :] = jnp.swapaxes(jnp.stack(results, axis=0), 0, 1)


def pass_half(all_ref, pass_hbm, sem):
    half = pass_hbm.shape[0]
    copy = start(pltpu.make_async_copy(all_ref.at[pl.ds((1 - (lax.axis_index("domain") & 1)) * half, half)], pass_hbm, sem))
    copy.wait()


def later_kernel(bands, landed, unread, handed, all_ref, pass_hbm, same, sems, pass_sem):
    count, states = all_ref.shape[0], landed.shape[1]
    loads = [
        start(
            pltpu.make_async_copy(
                landed.at[pl.ds(b * count, count)], all_ref.at[:, pl.ds(b * states, states), :], sems.at[b]
            )
        )
        for b in range(bands)
    ]
    for copy in loads:
        copy.wait()
    pass_half(all_ref, pass_hbm, pass_sem)


def early_kernel(after_ref, energy_ref, *refs):
    pieces, (all_ref, beside_ref, projs_ref, table_ref, token, sems) = refs[:-6], refs[-6:]
    states = pieces[0].shape[1]
    count, half, held = all_ref.shape[0] - 1, beside_ref.shape[0], projs_ref.shape[0]
    pairs = []
    for k, piece in enumerate(pieces):
        at = pl.ds(pl.multiple_of((lax.axis_index("band") ^ k) * states, states), states)
        pairs.append((piece.at[pl.ds(0, count)], all_ref.at[pl.ds(0, count), at, :]))
        pairs.append((piece.at[pl.ds(count, half)], beside_ref.at[:, at, :]))
        pairs.append((piece.at[pl.ds(count + half, held)], projs_ref.at[:, at, :]))
    loads = start_all(pairs, sems)
    all_ref[count] = after_ref[0]
    table_ref[...] = energy_table(energy_ref)
    wait_all(loads)


def add_products(row, all_ref, beside_refs, pot_ref, acc):
    half = beside_refs[0].shape[0]
    group = 4
    mine = (lax.axis_index("domain") & 1) * half
    for part, base in ((0, mine), (1, half - mine)):
        for i0 in range(0, half, group):
            xs, ys = [], []
            for i in range(i0, min(i0 + group, half)):
                cell = all_ref[base + i]
                x = cell.astype(F32)
                y = (3.0 + pot_ref[pl.ds(row + base + i, 1), :]) * x - pltpu.roll(x, x.shape[1] - 1, 1)
                y = y - all_ref[base + i + 1].astype(F32)
                if part == 0:
                    for ref in beside_refs:
                        y = y - ref[i].astype(F32)
                xs.append(cell)
                ys.append(y.astype(BF16))
            flat_x = jnp.concatenate(xs, axis=1)
            flat_y = jnp.concatenate(ys, axis=1)
            acc[0] += lax.dot_general(flat_x, flat_x, NT, preferred_element_type=F32)
            acc[1] += lax.dot_general(flat_y, flat_x, NT, preferred_element_type=F32)


def gram_kernel(first, share, all_ref, core_ref, link_ref, pot_ref, unread, acc):
    acc[...] = jnp.zeros_like(acc)
    add_products(lax.axis_index("band") * share + first, all_ref, (core_ref, link_ref), pot_ref, acc)


def final_kernel(bands, share, all_ref, beside_ref, pot_ref, begun_ref, proj_ref, energy_ref, out_ref, token, acc):
    acc[...] = begun_ref[...]
    add_products(lax.axis_index("band") * share, all_ref, (beside_ref,), pot_ref, acc)
    groups = proj_ref.shape[0]
    first = (lax.axis_index("domain") * bands + lax.axis_index("band")) * groups
    for g in range(groups):
        here = proj_ref[g]
        scaled = (here.astype(F32) * energy_ref[pl.ds(first + g, 1), :]).astype(BF16)
        acc[1] += lax.dot_general(scaled, here, NT, preferred_element_type=F32)
    hamil = 0.5 * (acc[1] + acc[1].T)
    domains = out_ref.shape[0] // bands
    rows, cols = out_ref.shape[1], out_ref.shape[2] // 2
    for c in range(domains):
        for r in range(bands):
            r0, c0 = r * rows, c * cols
            out_ref[c * bands + r, :, :cols] = acc[0, r0 : r0 + rows, c0 : c0 + cols].astype(BF16)
            out_ref[c * bands + r, :, cols:] = hamil[r0 : r0 + rows, c0 : c0 + cols].astype(BF16)


def result_kernel(scale, parts_ref, out_ref):
    total = jnp.sum(parts_ref[...].astype(F32), axis=0) * scale
    cols = out_ref.shape[2]
    out_ref[0] = total[:, :cols]
    out_ref[1] = total[:, cols:]


def local(orbitals, potential, projectors, tile_atom, tile_line, tile_count, energies):
    states, _, lines, cols_z = orbitals.shape
    slots, proj_count, _ = projectors.shape
    atom_total = energies.shape[0]
    domains, bands = lax.axis_size("domain"), lax.axis_size("band")
    total_states = states * bands
    atoms_here = atom_total // domains
    per_group = LANES // proj_count
    groups = atoms_here // per_group
    share = lines // bands
    first = 2 * (share * 3 // 32)
    rest = share - first

    core_pairs = [(i, i ^ 1) for i in range(domains) if i ^ 1 < domains]
    link_pairs = [(i, ((i + 1) ^ 1) - 1) for i in range(1, domains) if ((i + 1) ^ 1) - 1 < domains]
    near_far = [(i, i ^ 2) for i in range(domains) if i ^ 2 < domains]
    next = [(i, ((i + 2) ^ 2) - 2) for i in range(2, domains) if ((i + 2) ^ 2) - 2 < domains]
    far_pairs = [pairs for pairs in (near_far, next) if pairs]

    def swapped(values, axis):
        size = lax.axis_size(axis)
        got = {k: lax.ppermute(values[k - 1], axis, [(i, i ^ k) for i in range(size)]) for k in range(size - 1, 0, -1)}
        return [got[k] for k in range(1, size)]

    field = orbitals.reshape(states, lines, cols_z)
    pot = potential.reshape(lines, cols_z)
    energy = energies.T
    energy_rows = (atom_total // per_group, LANES)
    token = ((8, LANES), F32)
    eye = np.eye(cols_z, dtype=np.float32)
    ring = jnp.asarray(3.0 * eye - 0.5 * (np.roll(eye, 1, axis=0) + np.roll(eye, -1, axis=0)), dtype=BF16)

    ahead = share * 3 // 4
    late_lines = lines - ahead * bands
    line_shape, late_shape = (lines, states, cols_z), (late_lines, states, cols_z)
    xt, early_part, late_part, message = call(
        63,
        functools.partial(pack_kernel, first),
        (),
        [FAR],
        [FAR] * 4,
        [
            (line_shape, BF16),
            ((lines - late_lines, states, cols_z), BF16),
            (late_shape, BF16),
            ((bands * (rest + 1), states, cols_z), BF16),
        ],
        [
            pltpu.VMEM((states, lines, cols_z), BF16),
            pltpu.VMEM(line_shape, BF16),
            copies((bands,)),
            copies((5 * bands,)),
        ],
        (field,),
    )
    landed = lax.all_to_all(message, "band", split_axis=0, concat_axis=0, tiled=True)
    link_early = lax.ppermute(early_part, "domain", link_pairs)
    core_field = lax.ppermute(xt, "domain", core_pairs)

    group_shape = (groups, states, LANES)
    mine, to_core, to_link, *to_far = call(
        63,
        project_kernel,
        (),
        [SCALARS] * 3 + [FAR, PINNED],
        [PINNED] + [FAR] * (2 + len(far_pairs)),
        [((3 * groups, states, LANES), BF16)]
        + [((2 * groups, states, LANES), BF16)] * 2
        + [(group_shape, BF16)] * len(far_pairs),
        [
            pltpu.VMEM((3 * atoms_here + 1, proj_count, states), F32),
            pltpu.VMEM((3 * groups, states, LANES), BF16),
            pltpu.VMEM(line_shape, BF16),
            pltpu.VMEM(projectors.shape, BF16),
            copies((5,)),
            copies((5 + len(far_pairs),)),
        ],
        (tile_atom, tile_line, tile_count, xt, projectors),
    )
    from_link = lax.ppermute(to_link, "domain", link_pairs)
    from_far = [lax.ppermute(value, "domain", pairs) for value, pairs in zip(to_far, far_pairs)]
    from_core = lax.ppermute(to_core, "domain", core_pairs)
    (gate,) = call(
        63,
        wait_for,
        (),
        [UNREAD] * (4 + len(far_pairs)),
        [PINNED],
        [token],
        [],
        (from_core, from_link, *from_far, link_early, core_field),
    )
    held = groups // bands
    built_shape = (first + first // 2 + held, states, cols_z)
    beside_shape = (bands, first // 2, states, cols_z)
    added, own_message, *messages = call(
        62,
        functools.partial(nonlocal_kernel, len(far_pairs)),
        (),
        [SCALARS] * 3 + [FAR] * 3 + [PINNED, WHOLE, PINNED, WHOLE, WHOLE] + [WHOLE] * len(far_pairs) + [PINNED],
        [PINNED, PINNED] + [FAR] * (bands - 1),
        [(line_shape, F32)] + [(built_shape, BF16)] * bands,
        [
            pltpu.VMEM((lines + 1, states, cols_z), F32),
            pltpu.VMEM(group_shape, BF16),
            pltpu.VMEM((3 * groups, states, LANES), BF16),
            pltpu.VMEM((3 * groups, states, LANES), F32),
            pltpu.VMEM(energy_rows, F32),
            pltpu.VMEM((3 * atoms_here, states, proj_count), BF16),
            pltpu.VMEM(projectors.shape, BF16),
            pltpu.VMEM((bands, *built_shape), BF16),
            pltpu.VMEM(beside_shape, BF16),
            pltpu.VMEM(beside_shape, BF16),
            copies((4,)),
            copies((3 * bands,)),
            copies((bands,)),
        ],
        (
            tile_atom, tile_line, tile_count, xt, core_field, link_early, projectors, energy, mine, from_core,
            from_link, *from_far, gate,
        ),
        micros=8,
    )
    early = swapped(messages, "band")

    later_all, later_pass, late_part = call(
        32,
        functools.partial(later_kernel, bands),
        (),
        [FAR, PINNED, UNREAD],
        [NEAR, FAR, UNREAD],
        [
            ((rest + 1, total_states, cols_z), BF16),
            ((rest // 2, total_states, cols_z), BF16),
            (late_shape, BF16),
        ],
        [copies((bands,)), copies],
        (landed, own_message, late_part),
        aliases={2: 2},
    )
    later_link = lax.ppermute(later_pass, "domain", link_pairs)
    later_core = lax.ppermute(later_pass, "domain", core_pairs)
    link_late = lax.ppermute(late_part, "domain", link_pairs)

    early_all, early_beside, projs, energy_table_here, early_token = call(
        32,
        early_kernel,
        (),
        [NEAR, WHOLE, PINNED] + [FAR] * (bands - 1),
        [NEAR, NEAR, NEAR, NEAR, PINNED],
        [
            ((first + 1, total_states, cols_z), BF16),
            ((first // 2, total_states, cols_z), BF16),
            ((held, total_states, LANES), BF16),
            (energy_rows, F32),
            token,
        ],
        [copies((3 * bands,))],
        (later_all, energy, own_message, *early),
        micros=30,
    )
    (begun,) = call(
        32,
        functools.partial(gram_kernel, first, share),
        (),
        [NEAR, WHOLE, WHOLE, WHOLE, PINNED],
        [NEAR],
        [((2, total_states, total_states), F32)],
        [],
        (later_all, later_core, later_link, pot, early_token),
    )
    parts = domains * bands
    blocks, final_token = call(
        32,
        functools.partial(final_kernel, bands, share),
        (),
        [NEAR, NEAR, WHOLE, NEAR, NEAR, NEAR],
        [WHOLE, PINNED],
        [((parts, states, 2 * total_states // domains), BF16), token],
        [pltpu.VMEM((2, total_states, total_states), F32)],
        (early_all, early_beside, pot, begun, projs, energy_table_here),
    )
    summed = lax.all_to_all(blocks, ("domain", "band"), split_axis=0, concat_axis=0, tiled=True)
    span = 2 * ROWS
    steps = lines // span
    block = pl.BlockSpec((span, states, cols_z), lambda i: (i, 0, 0))
    (applied,) = call(
        62,
        functools.partial(stencil_kernel, share),
        (steps,),
        [
            block,
            pl.BlockSpec((1, states, cols_z), lambda i: (lax.rem(i * span + lines - 1, lines), 0, 0)),
            pl.BlockSpec((1, states, cols_z), lambda i: (lax.rem(i * span + span, lines), 0, 0)),
            block,
            pl.BlockSpec((ahead * bands // steps, states, cols_z), lambda i: (i, 0, 0)),
            pl.BlockSpec((late_lines // steps, states, cols_z), lambda i: (i, 0, 0)),
            block,
            pl.BlockSpec((span, cols_z), lambda i: (i, 0)),
            WHOLE,
            PINNED,
        ],
        [pl.BlockSpec((states, span, cols_z), lambda i: (0, i, 0))],
        [((states, lines, cols_z), BF16)],
        [],
        (
            xt, xt, xt, core_field, link_early, link_late, pltpu.with_memory_space_constraint(added, pltpu.HBM), pot, ring,
            final_token,
        ),
    )

    (subspace,) = call(
        32,
        functools.partial(result_kernel, 1.0 / (lines * cols_z * domains)),
        (),
        [WHOLE],
        [WHOLE],
        [((2, states, total_states // domains), F32)],
        [],
        (summed,),
    )
    return applied.reshape(orbitals.shape), subspace


def solution(mesh):
    in_specs = (
        P("band", ("groups", "domain"), None, None),
        P(("groups", "domain"), None, None),
        P(("groups", "domain"), None, None),
        P(("groups", "domain")),
        P(("groups", "domain")),
        P(("groups", "domain")),
        P("groups", None),
    )
    out_specs = (P("band", ("groups", "domain"), None, None), P(None, ("groups", "band"), "domain"))
    return jax.shard_map(local, mesh=mesh, in_specs=in_specs, out_specs=out_specs, check_vma=False)
```

```python
import functools

import jax
import jax.numpy as jnp
import numpy as np
from jax import lax
from jax.experimental import pallas as pl
from jax.experimental.pallas import tpu as pltpu
from jax.sharding import PartitionSpec as P

F32 = jnp.float32
BF16 = jnp.bfloat16
LANES = 128
ROWS = 16
NT = (((1,), (1,)), ((), ()))
WHOLE = pl.BlockSpec(memory_space=pltpu.VMEM)
NEAR = pl.BlockSpec(memory_space=pltpu.VMEM)
SCALARS = pl.BlockSpec(memory_space=pltpu.SMEM)
FAR = pl.BlockSpec(memory_space=pltpu.HBM)
PINNED = pl.BlockSpec(memory_space=pltpu.HBM)
UNREAD = pl.BlockSpec(memory_space=pl.ANY)
copies = pltpu.SemaphoreType.DMA


def call(room, kernel, grid, in_specs, out_specs, outs, scratch, args, aliases=None, micros=0.001):
    def place(spec):
        return {id(NEAR): pltpu.VMEM, id(PINNED): pltpu.HBM}.get(id(spec))

    args = [
        pltpu.with_memory_space_constraint(arg, place(spec)) if place(spec) else arg
        for spec, arg in zip(in_specs, args)
    ]
    shapes = [(place(spec) or jax.ShapeDtypeStruct)(shape, kind) for spec, (shape, kind) in zip(out_specs, outs)]
    return pl.pallas_call(
        kernel,
        grid=grid,
        out_shape=shapes,
        in_specs=in_specs,
        out_specs=out_specs,
        scratch_shapes=scratch,
        input_output_aliases=aliases or {},
        compiler_params=pltpu.CompilerParams(vmem_limit_bytes=int(room * 2**20)),
        cost_estimate=pl.CostEstimate(flops=int(micros * 1.1e9), bytes_accessed=1 << 10, transcendentals=0),
    )(*args)


def start(copy):
    copy.start()
    return copy


def start_all(pairs, sems):
    return [start(pltpu.make_async_copy(source, target, sems.at[i])) for i, (source, target) in enumerate(pairs)]


def wait_all(started):
    for copy in started:
        copy.wait()


def wait_for(*refs):
    pass


def pack_kernel(first, x_hbm, xt_hbm, early, late, message, x, xt, in_sems, out_sems):
    states, lines, _ = x.shape
    bands = in_sems.shape[0]
    share = lines // bands
    count = share - first
    ahead = early.shape[0] // bands
    loads, sends = [], []
    for c in range(bands):
        where = (slice(None), pl.ds(c * share, share), slice(None))
        loads.append(start(pltpu.make_async_copy(x_hbm.at[where], x.at[where], in_sems.at[c])))

    def send(line, number, target, at):
        copy = pltpu.make_async_copy(
            xt.at[pl.ds(line, number)], target.at[pl.ds(at, number)], out_sems.at[len(sends)]
        )
        sends.append(start(copy))

    for c in range(bands):
        loads[c].wait()
        for y0 in range(c * share, (c + 1) * share, ROWS):
            for s0 in range(0, states, ROWS):
                block = x[s0 : s0 + ROWS, y0 : y0 + ROWS, :]
                xt[y0 : y0 + ROWS, s0 : s0 + ROWS, :] = jnp.swapaxes(block, 0, 1)
        send(c * share, ahead, early, c * ahead)
        send(c * share + ahead, share - ahead, late, c * (share - ahead))
        send(c * share + first, count, message, c * (count + 1))
        send(c * share, 1, message, (c + bands - 1) % bands * (count + 1) + count)
        send(c * share, share, xt_hbm, c * share)
    for copy in sends:
        copy.wait()


def bases(groups):
    domain = lax.axis_index("domain")
    odd, upper = domain & 1, (domain >> 1) & 1
    return [2 * groups * side for side in (1 - odd, odd, 1 - upper, upper)]


def slot_reader(atom_ref, line_ref, count_ref, atoms_here):
    first = (lax.axis_index("domain") - 1) * atoms_here
    live = count_ref[0]

    def slot_at(t):
        return line_ref[t], jnp.clip(atom_ref[t] - first, 0, 3 * atoms_here - 1), t < live

    return slot_at


def energy_table(energy_ref):
    proj_count, atoms = energy_ref.shape
    per_group = LANES // proj_count
    lane = lax.broadcasted_iota(jnp.int32, (proj_count, LANES), 1)
    row = lax.broadcasted_iota(jnp.int32, (proj_count, LANES), 0)
    pick = jnp.where(lane % proj_count == row, 1.0, 0.0).astype(F32)
    spread = jnp.dot(energy_ref[...].T, pick, precision=lax.Precision.HIGHEST, preferred_element_type=F32)
    spread = spread.reshape(atoms // per_group, per_group, LANES)
    lane = lax.broadcasted_iota(jnp.int32, spread.shape, 2)
    atom = lax.broadcasted_iota(jnp.int32, spread.shape, 1)
    return jnp.sum(jnp.where(lane // proj_count == atom, spread, 0.0), axis=1)


def project_kernel(atom_ref, line_ref, count_ref, xt_hbm, p_hbm, mine_hbm, core_hbm, link_hbm, *refs):
    far_hbms, (total, mine_ref, xt_ref, p_ref, sems, out_sems) = refs[:-6], refs[-6:]
    slots, proj_count, _ = p_ref.shape
    groups, states = mine_ref.shape[0] // 3, mine_ref.shape[1]
    per_group = LANES // proj_count
    chunks = sems.shape[0] - 1
    size = slots // chunks
    unroll = 48
    pairs = [(p_hbm.at[pl.ds(c * size, size)], p_ref.at[pl.ds(c * size, size)]) for c in range(chunks)]
    xt_load, *loads = start_all([(xt_hbm, xt_ref), *pairs], sems)

    def clear(i, carry):
        for u in range(per_group):
            total[i * per_group + u] = jnp.zeros_like(total[0])
        return carry

    lax.fori_loop(0, 3 * groups, clear, 0)

    slot_at = slot_reader(atom_ref, line_ref, count_ref, groups * per_group)

    def body(i, carry):
        for u in range(unroll):
            t = i * unroll + u
            line, atom, live = slot_at(t)
            part = lax.dot_general(p_ref[t], xt_ref[line], NT, preferred_element_type=F32)
            total[jnp.where(live, atom, 3 * groups * per_group)] += part
        return carry

    xt_load.wait()
    for c in range(chunks):
        loads[c].wait()
        lax.fori_loop(c * size // unroll, (c + 1) * size // unroll, body, 0)

    for g in range(3 * groups):
        tiles = [total[g * per_group + u] for u in range(per_group)]
        mine_ref[g] = jnp.concatenate(tiles, axis=0).T.astype(BF16)
    sides = bases(groups)
    pairs = [(mine_ref, mine_hbm)]
    for side, far in zip(sides[:2], (core_hbm, link_hbm)):
        pairs.append((mine_ref.at[pl.ds(side, groups)], far.at[pl.ds(0, groups)]))
        pairs.append((mine_ref.at[pl.ds(groups, groups)], far.at[pl.ds(groups, groups)]))
    for side, far in zip(sides[2:], far_hbms):
        pairs.append((mine_ref.at[pl.ds(side, groups)], far))
    wait_all(start_all(pairs, out_sems))


def nonlocal_kernel(
    fars, atom_ref, line_ref, count_ref, xt_hbm, beside_hbm, early_hbm, p_hbm, energy_ref, mine_hbm, core_ref, link_ref, *refs
):
    far_refs, out_hbm, messages, scratch = refs[:fars], refs[fars + 1], refs[fars + 2 : -13], refs[-13:]
    lines_sum, whole_ref, mine_ref, total, table, atoms, p_ref, built, cores, links, sems, in_sems, out_sems = scratch
    lines = xt_hbm.shape[0]
    bands, half = cores.shape[:2]
    share, first = lines // bands, 2 * half
    held = built.shape[1] - first - half
    ahead = early_hbm.shape[0] // bands
    mine = (lax.axis_index("domain") & 1) * half
    pairs = []
    for k in range(bands):
        to = lax.axis_index("band") ^ k
        pairs.append((xt_hbm.at[pl.ds(to * share, first)], built.at[k, pl.ds(0, first)]))
        pairs.append((beside_hbm.at[pl.ds(to * share + mine, half)], cores.at[k]))
        pairs.append((early_hbm.at[pl.ds(to * ahead + mine, half)], links.at[k]))
    brought = start_all(pairs, in_sems)
    slots, proj_count, _ = p_ref.shape
    groups, states = total.shape[0] // 3, total.shape[1]
    per_group = LANES // proj_count
    unroll = 48
    mine_load, load = start_all([(mine_hbm, mine_ref), (p_hbm, p_ref)], sems)
    sends = []

    def clear(i, carry):
        lines_sum[i] = jnp.zeros((states, LANES), F32)
        return carry

    lax.fori_loop(0, lines + 1, clear, 0)
    mine_load.wait()
    total[...] = mine_ref[...].astype(F32)
    sides = bases(groups)
    for g in range(groups):
        total[groups + g] += core_ref[g].astype(F32) + link_ref[g].astype(F32)
        for side, ref in zip(sides[:2], (core_ref, link_ref)):
            total[side + g] += ref[groups + g].astype(F32)
        for side, ref in zip(sides[2:], far_refs):
            total[side + g] += ref[g].astype(F32)
    table[...] = energy_table(energy_ref)
    last = table.shape[0] - 1
    for g in range(3 * groups):
        row = jnp.clip((lax.axis_index("domain") - 1) * groups + g, 0, last)
        tile = (total[g] * table[pl.ds(row, 1), :]).astype(BF16)
        for u in range(per_group):
            atoms[g * per_group + u] = tile[:, u * proj_count : (u + 1) * proj_count]
    for g in range(groups):
        whole_ref[g] = total[groups + g].astype(BF16)
    wait_all(brought)
    for k, message in enumerate(messages):
        to = lax.axis_index("band") ^ k
        for i in range(half):
            built[k, first + i] = (cores[k, i].astype(F32) + links[k, i].astype(F32)).astype(BF16)
        for i in range(held):
            built[k, first + half + i] = whole_ref[to * held + i]
        sends.append(start(pltpu.make_async_copy(built.at[k], message, out_sems.at[k])))
    load.wait()

    slot_at = slot_reader(atom_ref, line_ref, count_ref, groups * per_group)

    def body(i, carry):
        for u in range(unroll):
            t = i * unroll + u
            line, atom, live = slot_at(t)
            part = jnp.dot(atoms[atom], p_ref[t], preferred_element_type=F32)
            lines_sum[jnp.where(live, line, lines)] += part
        return carry

    lax.fori_loop(0, slots // unroll, body, 0)
    sends.append(start(pltpu.make_async_copy(lines_sum.at[pl.ds(0, lines)], out_hbm, sems.at[3])))
    wait_all(sends)


def stencil_kernel(
    share, xt_ref, last_ref, next_ref, core_ref, early_ref, late_ref, added_ref, pot_ref, ring_ref, unread,
    out_ref,
):
    states, here, _ = out_ref.shape

    ahead = early_ref.shape[0] * share // here

    def link(i, rows):
        chunk, at = divmod(i, share)
        if at < ahead:
            return early_ref[chunk * ahead + at, rows, :]
        return late_ref[chunk * (share - ahead) + at - ahead, rows, :]

    def line(i, rows):
        ref, at = (last_ref, 0) if i < 0 else (next_ref, 0) if i == here else (xt_ref, i)
        return ref[at, rows, :]

    for y0 in range(0, here, ROWS):
        for s0 in range(0, states, ROWS):
            rows = slice(s0, s0 + ROWS)
            results = []
            cells = jnp.concatenate([line(y0 + i, rows) for i in range(ROWS)], axis=0)
            along = jnp.dot(cells, ring_ref[...], preferred_element_type=F32)
            before, x = line(y0 - 1, rows).astype(F32), line(y0, rows).astype(F32)
            for i in range(ROWS):
                y = y0 + i
                after = line(y + 1, rows).astype(F32)
                beside = (before + after) + (core_ref[y, rows, :].astype(F32) + link(y, rows).astype(F32))
                value = along[i * ROWS : (i + 1) * ROWS] + pot_ref[y : y + 1, :] * x
                results.append((value + added_ref[y, rows, :] - 0.5 * beside).astype(BF16))
                before, x = x, after
            out_ref[rows, y0 : y0 + ROWS, :] = jnp.swapaxes(jnp.stack(results, axis=0), 0, 1)


def pass_half(all_ref, pass_hbm, sem):
    half = pass_hbm.shape[0]
    copy = start(pltpu.make_async_copy(all_ref.at[pl.ds((1 - (lax.axis_index("domain") & 1)) * half, half)], pass_hbm, sem))
    copy.wait()


def later_kernel(bands, landed, unread, handed, all_ref, pass_hbm, same, sems, pass_sem):
    count, states = all_ref.shape[0], landed.shape[1]
    loads = [
        start(
            pltpu.make_async_copy(
                landed.at[pl.ds(b * count, count)], all_ref.at[:, pl.ds(b * states, states), :], sems.at[b]
            )
        )
        for b in range(bands)
    ]
    for copy in loads:
        copy.wait()
    pass_half(all_ref, pass_hbm, pass_sem)


def early_kernel(after_ref, energy_ref, *refs):
    pieces, (all_ref, beside_ref, projs_ref, table_ref, token, sems) = refs[:-6], refs[-6:]
    states = pieces[0].shape[1]
    count, half, held = all_ref.shape[0] - 1, beside_ref.shape[0], projs_ref.shape[0]
    pairs = []
    for k, piece in enumerate(pieces):
        at = pl.ds(pl.multiple_of((lax.axis_index("band") ^ k) * states, states), states)
        pairs.append((piece.at[pl.ds(0, count)], all_ref.at[pl.ds(0, count), at, :]))
        pairs.append((piece.at[pl.ds(count, half)], beside_ref.at[:, at, :]))
        pairs.append((piece.at[pl.ds(count + half, held)], projs_ref.at[:, at, :]))
    loads = start_all(pairs, sems)
    all_ref[count] = after_ref[0]
    table_ref[...] = energy_table(energy_ref)
    wait_all(loads)


def add_products(row, all_ref, beside_refs, pot_ref, acc):
    half = beside_refs[0].shape[0]
    group = 4
    mine = (lax.axis_index("domain") & 1) * half
    for part, base in ((0, mine), (1, half - mine)):
        for i0 in range(0, half, group):
            xs, ys = [], []
            for i in range(i0, min(i0 + group, half)):
                cell = all_ref[base + i]
                x = cell.astype(F32)
                y = (3.0 + pot_ref[pl.ds(row + base + i, 1), :]) * x - pltpu.roll(x, x.shape[1] - 1, 1)
                y = y - all_ref[base + i + 1].astype(F32)
                if part == 0:
                    for ref in beside_refs:
                        y = y - ref[i].astype(F32)
                xs.append(cell)
                ys.append(y.astype(BF16))
            flat_x = jnp.concatenate(xs, axis=1)
            flat_y = jnp.concatenate(ys, axis=1)
            acc[0] += lax.dot_general(flat_x, flat_x, NT, preferred_element_type=F32)
            acc[1] += lax.dot_general(flat_y, flat_x, NT, preferred_element_type=F32)


def gram_kernel(first, share, all_ref, core_ref, link_ref, pot_ref, unread, acc):
    acc[...] = jnp.zeros_like(acc)
    add_products(lax.axis_index("band") * share + first, all_ref, (core_ref, link_ref), pot_ref, acc)


def final_kernel(bands, share, all_ref, beside_ref, pot_ref, begun_ref, proj_ref, energy_ref, out_ref, token, acc):
    acc[...] = begun_ref[...]
    add_products(lax.axis_index("band") * share, all_ref, (beside_ref,), pot_ref, acc)
    groups = proj_ref.shape[0]
    first = (lax.axis_index("domain") * bands + lax.axis_index("band")) * groups
    for g in range(groups):
        here = proj_ref[g]
        scaled = (here.astype(F32) * energy_ref[pl.ds(first + g, 1), :]).astype(BF16)
        acc[1] += lax.dot_general(scaled, here, NT, preferred_element_type=F32)
    hamil = 0.5 * (acc[1] + acc[1].T)
    domains = out_ref.shape[0] // bands
    rows, cols = out_ref.shape[1], out_ref.shape[2] // 2
    for c in range(domains):
        for r in range(bands):
            r0, c0 = r * rows, c * cols
            out_ref[c * bands + r, :, :cols] = acc[0, r0 : r0 + rows, c0 : c0 + cols].astype(BF16)
            out_ref[c * bands + r, :, cols:] = hamil[r0 : r0 + rows, c0 : c0 + cols].astype(BF16)


def result_kernel(scale, parts_ref, out_ref):
    total = jnp.sum(parts_ref[...].astype(F32), axis=0) * scale
    cols = out_ref.shape[2]
    out_ref[0] = total[:, :cols]
    out_ref[1] = total[:, cols:]


def local(orbitals, potential, projectors, tile_atom, tile_line, tile_count, energies):
    states, _, lines, cols_z = orbitals.shape
    slots, proj_count, _ = projectors.shape
    atom_total = energies.shape[0]
    domains, bands = lax.axis_size("domain"), lax.axis_size("band")
    total_states = states * bands
    atoms_here = atom_total // domains
    per_group = LANES // proj_count
    groups = atoms_here // per_group
    share = lines // bands
    first = 2 * (share * 3 // 32)
    rest = share - first

    core_pairs = [(i, i ^ 1) for i in range(domains) if i ^ 1 < domains]
    link_pairs = [(i, ((i + 1) ^ 1) - 1) for i in range(1, domains) if ((i + 1) ^ 1) - 1 < domains]
    near_far = [(i, i ^ 2) for i in range(domains) if i ^ 2 < domains]
    next = [(i, ((i + 2) ^ 2) - 2) for i in range(2, domains) if ((i + 2) ^ 2) - 2 < domains]
    far_pairs = [pairs for pairs in (near_far, next) if pairs]

    def swapped(values, axis):
        size = lax.axis_size(axis)
        got = {k: lax.ppermute(values[k - 1], axis, [(i, i ^ k) for i in range(size)]) for k in range(size - 1, 0, -1)}
        return [got[k] for k in range(1, size)]

    field = orbitals.reshape(states, lines, cols_z)
    pot = potential.reshape(lines, cols_z)
    energy = energies.T
    energy_rows = (atom_total // per_group, LANES)
    token = ((8, LANES), F32)
    eye = np.eye(cols_z, dtype=np.float32)
    ring = jnp.asarray(3.0 * eye - 0.5 * (np.roll(eye, 1, axis=0) + np.roll(eye, -1, axis=0)), dtype=BF16)

    ahead = share * 5 // 8
    late_lines = lines - ahead * bands
    line_shape, late_shape = (lines, states, cols_z), (late_lines, states, cols_z)
    xt, early_part, late_part, message = call(
        63,
        functools.partial(pack_kernel, first),
        (),
        [FAR],
        [FAR] * 4,
        [
            (line_shape, BF16),
            ((lines - late_lines, states, cols_z), BF16),
            (late_shape, BF16),
            ((bands * (rest + 1), states, cols_z), BF16),
        ],
        [
            pltpu.VMEM((states, lines, cols_z), BF16),
            pltpu.VMEM(line_shape, BF16),
            copies((bands,)),
            copies((5 * bands,)),
        ],
        (field,),
    )
    landed = lax.all_to_all(message, "band", split_axis=0, concat_axis=0, tiled=True)
    link_early = lax.ppermute(early_part, "domain", link_pairs)
    core_field = lax.ppermute(xt, "domain", core_pairs)

    group_shape = (groups, states, LANES)
    mine, to_core, to_link, *to_far = call(
        63,
        project_kernel,
        (),
        [SCALARS] * 3 + [FAR, PINNED],
        [PINNED] + [FAR] * (2 + len(far_pairs)),
        [((3 * groups, states, LANES), BF16)]
        + [((2 * groups, states, LANES), BF16)] * 2
        + [(group_shape, BF16)] * len(far_pairs),
        [
            pltpu.VMEM((3 * atoms_here + 1, proj_count, states), F32),
            pltpu.VMEM((3 * groups, states, LANES), BF16),
            pltpu.VMEM(line_shape, BF16),
            pltpu.VMEM(projectors.shape, BF16),
            copies((5,)),
            copies((5 + len(far_pairs),)),
        ],
        (tile_atom, tile_line, tile_count, xt, projectors),
    )
    from_link = lax.ppermute(to_link, "domain", link_pairs)
    from_far = [lax.ppermute(value, "domain", pairs) for value, pairs in zip(to_far, far_pairs)]
    from_core = lax.ppermute(to_core, "domain", core_pairs)
    (gate,) = call(
        63,
        wait_for,
        (),
        [UNREAD] * (4 + len(far_pairs)),
        [PINNED],
        [token],
        [],
        (from_core, from_link, *from_far, link_early, core_field),
    )
    held = groups // bands
    built_shape = (first + first // 2 + held, states, cols_z)
    beside_shape = (bands, first // 2, states, cols_z)
    added, own_message, *messages = call(
        62,
        functools.partial(nonlocal_kernel, len(far_pairs)),
        (),
        [SCALARS] * 3 + [FAR] * 3 + [PINNED, WHOLE, PINNED, WHOLE, WHOLE] + [WHOLE] * len(far_pairs) + [PINNED],
        [PINNED, PINNED] + [FAR] * (bands - 1),
        [(line_shape, F32)] + [(built_shape, BF16)] * bands,
        [
            pltpu.VMEM((lines + 1, states, cols_z), F32),
            pltpu.VMEM(group_shape, BF16),
            pltpu.VMEM((3 * groups, states, LANES), BF16),
            pltpu.VMEM((3 * groups, states, LANES), F32),
            pltpu.VMEM(energy_rows, F32),
            pltpu.VMEM((3 * atoms_here, states, proj_count), BF16),
            pltpu.VMEM(projectors.shape, BF16),
            pltpu.VMEM((bands, *built_shape), BF16),
            pltpu.VMEM(beside_shape, BF16),
            pltpu.VMEM(beside_shape, BF16),
            copies((4,)),
            copies((3 * bands,)),
            copies((bands,)),
        ],
        (
            tile_atom, tile_line, tile_count, xt, core_field, link_early, projectors, energy, mine, from_core,
            from_link, *from_far, gate,
        ),
        micros=8,
    )
    early = swapped(messages, "band")

    later_all, later_pass, late_part = call(
        32,
        functools.partial(later_kernel, bands),
        (),
        [FAR, PINNED, UNREAD],
        [NEAR, FAR, UNREAD],
        [
            ((rest + 1, total_states, cols_z), BF16),
            ((rest // 2, total_states, cols_z), BF16),
            (late_shape, BF16),
        ],
        [copies((bands,)), copies],
        (landed, own_message, late_part),
        aliases={2: 2},
    )
    later_link = lax.ppermute(later_pass, "domain", link_pairs)
    later_core = lax.ppermute(later_pass, "domain", core_pairs)
    link_late = lax.ppermute(late_part, "domain", link_pairs)

    early_all, early_beside, projs, energy_table_here, early_token = call(
        32,
        early_kernel,
        (),
        [NEAR, WHOLE, PINNED] + [FAR] * (bands - 1),
        [NEAR, NEAR, NEAR, NEAR, PINNED],
        [
            ((first + 1, total_states, cols_z), BF16),
            ((first // 2, total_states, cols_z), BF16),
            ((held, total_states, LANES), BF16),
            (energy_rows, F32),
            token,
        ],
        [copies((3 * bands,))],
        (later_all, energy, own_message, *early),
        micros=30,
    )
    (begun,) = call(
        32,
        functools.partial(gram_kernel, first, share),
        (),
        [NEAR, WHOLE, WHOLE, WHOLE, PINNED],
        [NEAR],
        [((2, total_states, total_states), F32)],
        [],
        (later_all, later_core, later_link, pot, early_token),
    )
    parts = domains * bands
    blocks, final_token = call(
        32,
        functools.partial(final_kernel, bands, share),
        (),
        [NEAR, NEAR, WHOLE, NEAR, NEAR, NEAR],
        [WHOLE, PINNED],
        [((parts, states, 2 * total_states // domains), BF16), token],
        [pltpu.VMEM((2, total_states, total_states), F32)],
        (early_all, early_beside, pot, begun, projs, energy_table_here),
    )
    summed = lax.all_to_all(blocks, ("domain", "band"), split_axis=0, concat_axis=0, tiled=True)
    span = 2 * ROWS
    steps = lines // span
    block = pl.BlockSpec((span, states, cols_z), lambda i: (i, 0, 0))
    (applied,) = call(
        63.5,
        functools.partial(stencil_kernel, share),
        (steps,),
        [
            block,
            pl.BlockSpec((1, states, cols_z), lambda i: (lax.rem(i * span + lines - 1, lines), 0, 0)),
            pl.BlockSpec((1, states, cols_z), lambda i: (lax.rem(i * span + span, lines), 0, 0)),
            block,
            pl.BlockSpec((ahead * bands // steps, states, cols_z), lambda i: (i, 0, 0)),
            pl.BlockSpec((late_lines // steps, states, cols_z), lambda i: (i, 0, 0)),
            block,
            pl.BlockSpec((span, cols_z), lambda i: (i, 0)),
            WHOLE,
            PINNED,
        ],
        [pl.BlockSpec((states, span, cols_z), lambda i: (0, i, 0))],
        [((states, lines, cols_z), BF16)],
        [],
        (
            xt, xt, xt, core_field, link_early, link_late, pltpu.with_memory_space_constraint(added, pltpu.HBM), pot, ring,
            final_token,
        ),
    )

    (subspace,) = call(
        32,
        functools.partial(result_kernel, 1.0 / (lines * cols_z * domains)),
        (),
        [WHOLE],
        [WHOLE],
        [((2, states, total_states // domains), F32)],
        [],
        (summed,),
    )
    return applied.reshape(orbitals.shape), subspace


def solution(mesh):
    in_specs = (
        P("band", ("groups", "domain"), None, None),
        P(("groups", "domain"), None, None),
        P(("groups", "domain"), None, None),
        P(("groups", "domain")),
        P(("groups", "domain")),
        P(("groups", "domain")),
        P("groups", None),
    )
    out_specs = (P("band", ("groups", "domain"), None, None), P(None, ("groups", "band"), "domain"))
    return jax.shard_map(local, mesh=mesh, in_specs=in_specs, out_specs=out_specs, check_vma=False)
```

```python
import functools

import jax
import jax.numpy as jnp
import numpy as np
from jax import lax
from jax.experimental import pallas as pl
from jax.experimental.pallas import tpu as pltpu
from jax.sharding import PartitionSpec as P

F32 = jnp.float32
BF16 = jnp.bfloat16
LANES = 128
ROWS = 16
NT = (((1,), (1,)), ((), ()))
WHOLE = pl.BlockSpec(memory_space=pltpu.VMEM)
NEAR = pl.BlockSpec(memory_space=pltpu.VMEM)
SCALARS = pl.BlockSpec(memory_space=pltpu.SMEM)
FAR = pl.BlockSpec(memory_space=pltpu.HBM)
PINNED = pl.BlockSpec(memory_space=pltpu.HBM)
UNREAD = pl.BlockSpec(memory_space=pl.ANY)
copies = pltpu.SemaphoreType.DMA


def call(room, kernel, grid, in_specs, out_specs, outs, scratch, args, aliases=None, micros=0.001):
    def place(spec):
        return {id(NEAR): pltpu.VMEM, id(PINNED): pltpu.HBM}.get(id(spec))

    args = [
        pltpu.with_memory_space_constraint(arg, place(spec)) if place(spec) else arg
        for spec, arg in zip(in_specs, args)
    ]
    shapes = [(place(spec) or jax.ShapeDtypeStruct)(shape, kind) for spec, (shape, kind) in zip(out_specs, outs)]
    return pl.pallas_call(
        kernel,
        grid=grid,
        out_shape=shapes,
        in_specs=in_specs,
        out_specs=out_specs,
        scratch_shapes=scratch,
        input_output_aliases=aliases or {},
        compiler_params=pltpu.CompilerParams(vmem_limit_bytes=int(room * 2**20)),
        cost_estimate=pl.CostEstimate(flops=int(micros * 1.1e9), bytes_accessed=1 << 10, transcendentals=0),
    )(*args)


def start(copy):
    copy.start()
    return copy


def start_all(pairs, sems):
    return [start(pltpu.make_async_copy(source, target, sems.at[i])) for i, (source, target) in enumerate(pairs)]


def wait_all(started):
    for copy in started:
        copy.wait()


def wait_for(*refs):
    pass


def pack_kernel(first, x_hbm, xt_hbm, early, late, message, x, xt, in_sems, out_sems):
    states, lines, _ = x.shape
    bands = in_sems.shape[0]
    share = lines // bands
    count = share - first
    ahead = early.shape[0] // bands
    loads, sends = [], []
    for c in range(bands):
        where = (slice(None), pl.ds(c * share, share), slice(None))
        loads.append(start(pltpu.make_async_copy(x_hbm.at[where], x.at[where], in_sems.at[c])))

    def send(line, number, target, at):
        copy = pltpu.make_async_copy(
            xt.at[pl.ds(line, number)], target.at[pl.ds(at, number)], out_sems.at[len(sends)]
        )
        sends.append(start(copy))

    for c in range(bands):
        loads[c].wait()
        for y0 in range(c * share, (c + 1) * share, ROWS):
            for s0 in range(0, states, ROWS):
                block = x[s0 : s0 + ROWS, y0 : y0 + ROWS, :]
                xt[y0 : y0 + ROWS, s0 : s0 + ROWS, :] = jnp.swapaxes(block, 0, 1)
        send(c * share, ahead, early, c * ahead)
        send(c * share + ahead, share - ahead, late, c * (share - ahead))
        send(c * share + first, count, message, c * (count + 1))
        send(c * share, 1, message, (c + bands - 1) % bands * (count + 1) + count)
        send(c * share, share, xt_hbm, c * share)
    for copy in sends:
        copy.wait()


def bases(groups):
    domain = lax.axis_index("domain")
    odd, upper = domain & 1, (domain >> 1) & 1
    return [2 * groups * side for side in (1 - odd, odd, 1 - upper, upper)]


def slot_reader(atom_ref, line_ref, count_ref, atoms_here):
    first = (lax.axis_index("domain") - 1) * atoms_here
    live = count_ref[0]

    def slot_at(t):
        return line_ref[t], jnp.clip(atom_ref[t] - first, 0, 3 * atoms_here - 1), t < live

    return slot_at


def energy_table(energy_ref):
    proj_count, atoms = energy_ref.shape
    per_group = LANES // proj_count
    lane = lax.broadcasted_iota(jnp.int32, (proj_count, LANES), 1)
    row = lax.broadcasted_iota(jnp.int32, (proj_count, LANES), 0)
    pick = jnp.where(lane % proj_count == row, 1.0, 0.0).astype(F32)
    spread = jnp.dot(energy_ref[...].T, pick, precision=lax.Precision.HIGHEST, preferred_element_type=F32)
    spread = spread.reshape(atoms // per_group, per_group, LANES)
    lane = lax.broadcasted_iota(jnp.int32, spread.shape, 2)
    atom = lax.broadcasted_iota(jnp.int32, spread.shape, 1)
    return jnp.sum(jnp.where(lane // proj_count == atom, spread, 0.0), axis=1)


def project_kernel(atom_ref, line_ref, count_ref, xt_hbm, p_hbm, mine_hbm, core_hbm, link_hbm, *refs):
    far_hbms, (total, mine_ref, xt_ref, p_ref, sems, out_sems) = refs[:-6], refs[-6:]
    slots, proj_count, _ = p_ref.shape
    groups, states = mine_ref.shape[0] // 3, mine_ref.shape[1]
    per_group = LANES // proj_count
    chunks = sems.shape[0] - 1
    size = slots // chunks
    unroll = 48
    pairs = [(p_hbm.at[pl.ds(c * size, size)], p_ref.at[pl.ds(c * size, size)]) for c in range(chunks)]
    xt_load, *loads = start_all([(xt_hbm, xt_ref), *pairs], sems)

    def clear(i, carry):
        for u in range(per_group):
            total[i * per_group + u] = jnp.zeros_like(total[0])
        return carry

    lax.fori_loop(0, 3 * groups, clear, 0)

    slot_at = slot_reader(atom_ref, line_ref, count_ref, groups * per_group)

    def body(i, carry):
        for u in range(unroll):
            t = i * unroll + u
            line, atom, live = slot_at(t)
            part = lax.dot_general(p_ref[t], xt_ref[line], NT, preferred_element_type=F32)
            total[jnp.where(live, atom, 3 * groups * per_group)] += part
        return carry

    xt_load.wait()
    for c in range(chunks):
        loads[c].wait()
        lax.fori_loop(c * size // unroll, (c + 1) * size // unroll, body, 0)

    for g in range(3 * groups):
        tiles = [total[g * per_group + u] for u in range(per_group)]
        mine_ref[g] = jnp.concatenate(tiles, axis=0).T.astype(BF16)
    sides = bases(groups)
    pairs = [(mine_ref, mine_hbm)]
    for side, far in zip(sides[:2], (core_hbm, link_hbm)):
        pairs.append((mine_ref.at[pl.ds(side, groups)], far.at[pl.ds(0, groups)]))
        pairs.append((mine_ref.at[pl.ds(groups, groups)], far.at[pl.ds(groups, groups)]))
    for side, far in zip(sides[2:], far_hbms):
        pairs.append((mine_ref.at[pl.ds(side, groups)], far))
    wait_all(start_all(pairs, out_sems))


def nonlocal_kernel(
    fars, atom_ref, line_ref, count_ref, xt_hbm, beside_hbm, early_hbm, p_hbm, energy_ref, mine_hbm, core_ref, link_ref, *refs
):
    far_refs, out_hbm, messages, scratch = refs[:fars], refs[fars + 1], refs[fars + 2 : -13], refs[-13:]
    lines_sum, whole_ref, mine_ref, total, table, atoms, p_ref, built, cores, links, sems, in_sems, out_sems = scratch
    lines = xt_hbm.shape[0]
    bands, half = cores.shape[:2]
    share, first = lines // bands, 2 * half
    held = built.shape[1] - first - half
    ahead = early_hbm.shape[0] // bands
    mine = (lax.axis_index("domain") & 1) * half
    pairs = []
    for k in range(bands):
        to = lax.axis_index("band") ^ k
        pairs.append((xt_hbm.at[pl.ds(to * share, first)], built.at[k, pl.ds(0, first)]))
        pairs.append((beside_hbm.at[pl.ds(to * share + mine, half)], cores.at[k]))
        pairs.append((early_hbm.at[pl.ds(to * ahead + mine, half)], links.at[k]))
    brought = start_all(pairs, in_sems)
    slots, proj_count, _ = p_ref.shape
    groups, states = total.shape[0] // 3, total.shape[1]
    per_group = LANES // proj_count
    unroll = 48
    mine_load, load = start_all([(mine_hbm, mine_ref), (p_hbm, p_ref)], sems)
    sends = []

    def clear(i, carry):
        lines_sum[i] = jnp.zeros((states, LANES), F32)
        return carry

    lax.fori_loop(0, lines + 1, clear, 0)
    mine_load.wait()
    total[...] = mine_ref[...].astype(F32)
    sides = bases(groups)
    for g in range(groups):
        total[groups + g] += core_ref[g].astype(F32) + link_ref[g].astype(F32)
        for side, ref in zip(sides[:2], (core_ref, link_ref)):
            total[side + g] += ref[groups + g].astype(F32)
        for side, ref in zip(sides[2:], far_refs):
            total[side + g] += ref[g].astype(F32)
    table[...] = energy_table(energy_ref)
    last = table.shape[0] - 1
    for g in range(3 * groups):
        row = jnp.clip((lax.axis_index("domain") - 1) * groups + g, 0, last)
        tile = (total[g] * table[pl.ds(row, 1), :]).astype(BF16)
        for u in range(per_group):
            atoms[g * per_group + u] = tile[:, u * proj_count : (u + 1) * proj_count]
    for g in range(groups):
        whole_ref[g] = total[groups + g].astype(BF16)
    wait_all(brought)
    for k, message in enumerate(messages):
        to = lax.axis_index("band") ^ k
        for i in range(half):
            built[k, first + i] = (cores[k, i].astype(F32) + links[k, i].astype(F32)).astype(BF16)
        for i in range(held):
            built[k, first + half + i] = whole_ref[to * held + i]
        sends.append(start(pltpu.make_async_copy(built.at[k], message, out_sems.at[k])))
    load.wait()

    slot_at = slot_reader(atom_ref, line_ref, count_ref, groups * per_group)

    def body(i, carry):
        for u in range(unroll):
            t = i * unroll + u
            line, atom, live = slot_at(t)
            part = jnp.dot(atoms[atom], p_ref[t], preferred_element_type=F32)
            lines_sum[jnp.where(live, line, lines)] += part
        return carry

    lax.fori_loop(0, slots // unroll, body, 0)
    sends.append(start(pltpu.make_async_copy(lines_sum.at[pl.ds(0, lines)], out_hbm, sems.at[3])))
    wait_all(sends)


def stencil_kernel(
    share, xt_ref, last_ref, next_ref, core_ref, early_ref, late_ref, added_ref, pot_ref, ring_ref, unread,
    out_ref,
):
    states, here, _ = out_ref.shape

    ahead = early_ref.shape[0] * share // here

    def link(i, rows):
        chunk, at = divmod(i, share)
        if at < ahead:
            return early_ref[chunk * ahead + at, rows, :]
        return late_ref[chunk * (share - ahead) + at - ahead, rows, :]

    def line(i, rows):
        ref, at = (last_ref, 0) if i < 0 else (next_ref, 0) if i == here else (xt_ref, i)
        return ref[at, rows, :]

    for y0 in range(0, here, ROWS):
        for s0 in range(0, states, ROWS):
            rows = slice(s0, s0 + ROWS)
            results = []
            cells = jnp.concatenate([line(y0 + i, rows) for i in range(ROWS)], axis=0)
            along = jnp.dot(cells, ring_ref[...], preferred_element_type=F32)
            before, x = line(y0 - 1, rows).astype(F32), line(y0, rows).astype(F32)
            for i in range(ROWS):
                y = y0 + i
                after = line(y + 1, rows).astype(F32)
                beside = (before + after) + (core_ref[y, rows, :].astype(F32) + link(y, rows).astype(F32))
                value = along[i * ROWS : (i + 1) * ROWS] + pot_ref[y : y + 1, :] * x
                results.append((value + added_ref[y, rows, :] - 0.5 * beside).astype(BF16))
                before, x = x, after
            out_ref[rows, y0 : y0 + ROWS, :] = jnp.swapaxes(jnp.stack(results, axis=0), 0, 1)


def pass_half(all_ref, pass_hbm, sem):
    half = pass_hbm.shape[0]
    copy = start(pltpu.make_async_copy(all_ref.at[pl.ds((1 - (lax.axis_index("domain") & 1)) * half, half)], pass_hbm, sem))
    copy.wait()


def later_kernel(bands, landed, unread, handed, all_ref, pass_hbm, same, sems, pass_sem):
    count, states = all_ref.shape[0], landed.shape[1]
    loads = [
        start(
            pltpu.make_async_copy(
                landed.at[pl.ds(b * count, count)], all_ref.at[:, pl.ds(b * states, states), :], sems.at[b]
            )
        )
        for b in range(bands)
    ]
    for copy in loads:
        copy.wait()
    pass_half(all_ref, pass_hbm, pass_sem)


def add_products(row, all_ref, beside_refs, pot_ref, acc):
    half = beside_refs[0].shape[0]
    group = 4
    mine = (lax.axis_index("domain") & 1) * half
    for part, base in ((0, mine), (1, half - mine)):
        for i0 in range(0, half, group):
            xs, ys = [], []
            for i in range(i0, min(i0 + group, half)):
                cell = all_ref[base + i]
                x = cell.astype(F32)
                y = (3.0 + pot_ref[pl.ds(row + base + i, 1), :]) * x - pltpu.roll(x, x.shape[1] - 1, 1)
                y = y - all_ref[base + i + 1].astype(F32)
                if part == 0:
                    for ref in beside_refs:
                        y = y - ref[i].astype(F32)
                xs.append(cell)
                ys.append(y.astype(BF16))
            flat_x = jnp.concatenate(xs, axis=1)
            flat_y = jnp.concatenate(ys, axis=1)
            acc[0] += lax.dot_general(flat_x, flat_x, NT, preferred_element_type=F32)
            acc[1] += lax.dot_general(flat_y, flat_x, NT, preferred_element_type=F32)


def final_kernel(
    first, share, later_ref, core_ref, link_ref, pot_ref, energy_ref, own_hbm, unread, *refs
):
    pieces, (out_ref, token, lines_ref, beside_ref, projs, table, acc, sems) = refs[:-8], refs[-8:]
    bands, states = len(pieces) + 1, own_hbm.shape[1]
    band = lax.axis_index("band")
    half, held = beside_ref.shape[0], projs.shape[0]
    at = pl.ds(pl.multiple_of(band * states, states), states)
    loads = start_all(
        [
            (own_hbm.at[pl.ds(0, first)], lines_ref.at[pl.ds(0, first), at, :]),
            (own_hbm.at[pl.ds(first, half)], beside_ref.at[:, at, :]),
            (own_hbm.at[pl.ds(first + half, held)], projs.at[:, at, :]),
        ],
        sems,
    )
    acc[...] = jnp.zeros_like(acc)
    add_products(band * share + first, later_ref, (core_ref, link_ref), pot_ref, acc)
    table[...] = energy_table(energy_ref)
    lines_ref[first] = later_ref[0]
    for k, piece in enumerate(pieces, 1):
        at = pl.ds(pl.multiple_of((band ^ k) * states, states), states)
        for i in range(first):
            lines_ref[i, at, :] = piece[i]
        for i in range(half):
            beside_ref[i, at, :] = piece[first + i]
        for i in range(held):
            projs[i, at, :] = piece[first + half + i]
    wait_all(loads)
    add_products(band * share, lines_ref, (beside_ref,), pot_ref, acc)
    row = (lax.axis_index("domain") * bands + band) * held
    for g in range(held):
        here = projs[g]
        scaled = (here.astype(F32) * table[pl.ds(row + g, 1), :]).astype(BF16)
        acc[1] += lax.dot_general(scaled, here, NT, preferred_element_type=F32)
    hamil = 0.5 * (acc[1] + acc[1].T)
    domains = out_ref.shape[0] // bands
    rows, cols = out_ref.shape[1], out_ref.shape[2] // 2
    for c in range(domains):
        for r in range(bands):
            r0, c0 = r * rows, c * cols
            out_ref[c * bands + r, :, :cols] = acc[0, r0 : r0 + rows, c0 : c0 + cols].astype(BF16)
            out_ref[c * bands + r, :, cols:] = hamil[r0 : r0 + rows, c0 : c0 + cols].astype(BF16)


def result_kernel(scale, parts_ref, out_ref):
    total = jnp.sum(parts_ref[...].astype(F32), axis=0) * scale
    cols = out_ref.shape[2]
    out_ref[0] = total[:, :cols]
    out_ref[1] = total[:, cols:]


def local(orbitals, potential, projectors, tile_atom, tile_line, tile_count, energies):
    states, _, lines, cols_z = orbitals.shape
    slots, proj_count, _ = projectors.shape
    atom_total = energies.shape[0]
    domains, bands = lax.axis_size("domain"), lax.axis_size("band")
    total_states = states * bands
    atoms_here = atom_total // domains
    per_group = LANES // proj_count
    groups = atoms_here // per_group
    share = lines // bands
    first = 2 * (share * 3 // 32)
    rest = share - first

    core_pairs = [(i, i ^ 1) for i in range(domains) if i ^ 1 < domains]
    link_pairs = [(i, ((i + 1) ^ 1) - 1) for i in range(1, domains) if ((i + 1) ^ 1) - 1 < domains]
    near_far = [(i, i ^ 2) for i in range(domains) if i ^ 2 < domains]
    next = [(i, ((i + 2) ^ 2) - 2) for i in range(2, domains) if ((i + 2) ^ 2) - 2 < domains]
    far_pairs = [pairs for pairs in (near_far, next) if pairs]

    def swapped(values, axis):
        size = lax.axis_size(axis)
        got = {k: lax.ppermute(values[k - 1], axis, [(i, i ^ k) for i in range(size)]) for k in range(size - 1, 0, -1)}
        return [got[k] for k in range(1, size)]

    field = orbitals.reshape(states, lines, cols_z)
    pot = potential.reshape(lines, cols_z)
    energy = energies.T
    energy_rows = (atom_total // per_group, LANES)
    token = ((8, LANES), F32)
    eye = np.eye(cols_z, dtype=np.float32)
    ring = jnp.asarray(3.0 * eye - 0.5 * (np.roll(eye, 1, axis=0) + np.roll(eye, -1, axis=0)), dtype=BF16)

    ahead = share * 5 // 8
    late_lines = lines - ahead * bands
    line_shape, late_shape = (lines, states, cols_z), (late_lines, states, cols_z)
    xt, early_part, late_part, message = call(
        63,
        functools.partial(pack_kernel, first),
        (),
        [FAR],
        [FAR] * 4,
        [
            (line_shape, BF16),
            ((lines - late_lines, states, cols_z), BF16),
            (late_shape, BF16),
            ((bands * (rest + 1), states, cols_z), BF16),
        ],
        [
            pltpu.VMEM((states, lines, cols_z), BF16),
            pltpu.VMEM(line_shape, BF16),
            copies((bands,)),
            copies((5 * bands,)),
        ],
        (field,),
    )
    landed = lax.all_to_all(message, "band", split_axis=0, concat_axis=0, tiled=True)
    link_early = lax.ppermute(early_part, "domain", link_pairs)
    core_field = lax.ppermute(xt, "domain", core_pairs)

    group_shape = (groups, states, LANES)
    mine, to_core, to_link, *to_far = call(
        63,
        project_kernel,
        (),
        [SCALARS] * 3 + [FAR, PINNED],
        [PINNED] + [FAR] * (2 + len(far_pairs)),
        [((3 * groups, states, LANES), BF16)]
        + [((2 * groups, states, LANES), BF16)] * 2
        + [(group_shape, BF16)] * len(far_pairs),
        [
            pltpu.VMEM((3 * atoms_here + 1, proj_count, states), F32),
            pltpu.VMEM((3 * groups, states, LANES), BF16),
            pltpu.VMEM(line_shape, BF16),
            pltpu.VMEM(projectors.shape, BF16),
            copies((5,)),
            copies((5 + len(far_pairs),)),
        ],
        (tile_atom, tile_line, tile_count, xt, projectors),
    )
    from_link = lax.ppermute(to_link, "domain", link_pairs)
    from_far = [lax.ppermute(value, "domain", pairs) for value, pairs in zip(to_far, far_pairs)]
    from_core = lax.ppermute(to_core, "domain", core_pairs)
    (gate,) = call(
        63,
        wait_for,
        (),
        [UNREAD] * (4 + len(far_pairs)),
        [PINNED],
        [token],
        [],
        (from_core, from_link, *from_far, link_early, core_field),
    )
    held = groups // bands
    built_shape = (first + first // 2 + held, states, cols_z)
    beside_shape = (bands, first // 2, states, cols_z)
    added, own_message, *messages = call(
        62,
        functools.partial(nonlocal_kernel, len(far_pairs)),
        (),
        [SCALARS] * 3 + [FAR] * 3 + [PINNED, WHOLE, PINNED, WHOLE, WHOLE] + [WHOLE] * len(far_pairs) + [PINNED],
        [PINNED, PINNED] + [FAR] * (bands - 1),
        [(line_shape, F32)] + [(built_shape, BF16)] * bands,
        [
            pltpu.VMEM((lines + 1, states, cols_z), F32),
            pltpu.VMEM(group_shape, BF16),
            pltpu.VMEM((3 * groups, states, LANES), BF16),
            pltpu.VMEM((3 * groups, states, LANES), F32),
            pltpu.VMEM(energy_rows, F32),
            pltpu.VMEM((3 * atoms_here, states, proj_count), BF16),
            pltpu.VMEM(projectors.shape, BF16),
            pltpu.VMEM((bands, *built_shape), BF16),
            pltpu.VMEM(beside_shape, BF16),
            pltpu.VMEM(beside_shape, BF16),
            copies((4,)),
            copies((3 * bands,)),
            copies((bands,)),
        ],
        (
            tile_atom, tile_line, tile_count, xt, core_field, link_early, projectors, energy, mine, from_core,
            from_link, *from_far, gate,
        ),
        micros=8,
    )
    early = swapped(messages, "band")

    later_all, later_pass, late_part = call(
        32,
        functools.partial(later_kernel, bands),
        (),
        [FAR, PINNED, UNREAD],
        [NEAR, FAR, UNREAD],
        [
            ((rest + 1, total_states, cols_z), BF16),
            ((rest // 2, total_states, cols_z), BF16),
            (late_shape, BF16),
        ],
        [copies((bands,)), copies],
        (landed, own_message, late_part),
        aliases={2: 2},
    )
    later_link = lax.ppermute(later_pass, "domain", link_pairs)
    later_core = lax.ppermute(later_pass, "domain", core_pairs)
    link_late = lax.ppermute(late_part, "domain", link_pairs)

    (early_token,) = call(
        62.2,
        wait_for,
        (),
        [UNREAD] * (bands - 1),
        [PINNED],
        [token],
        [],
        tuple(early),
        micros=30,
    )
    parts = domains * bands
    blocks, final_token = call(
        32,
        functools.partial(final_kernel, first, share),
        (),
        [NEAR] + [WHOLE] * 4 + [PINNED, PINNED] + [WHOLE] * (bands - 1),
        [WHOLE, PINNED],
        [((parts, states, 2 * total_states // domains), BF16), token],
        [
            pltpu.VMEM((first + 1, total_states, cols_z), BF16),
            pltpu.VMEM((first // 2, total_states, cols_z), BF16),
            pltpu.VMEM((held, total_states, LANES), BF16),
            pltpu.VMEM(energy_rows, F32),
            pltpu.VMEM((2, total_states, total_states), F32),
            copies((3,)),
        ],
        (later_all, later_core, later_link, pot, energy, own_message, early_token, *early),
    )
    summed = lax.all_to_all(blocks, ("domain", "band"), split_axis=0, concat_axis=0, tiled=True)
    span = 2 * ROWS
    steps = lines // span
    block = pl.BlockSpec((span, states, cols_z), lambda i: (i, 0, 0))
    (applied,) = call(
        48,
        functools.partial(stencil_kernel, share),
        (steps,),
        [
            block,
            pl.BlockSpec((1, states, cols_z), lambda i: (lax.rem(i * span + lines - 1, lines), 0, 0)),
            pl.BlockSpec((1, states, cols_z), lambda i: (lax.rem(i * span + span, lines), 0, 0)),
            block,
            pl.BlockSpec((ahead * bands // steps, states, cols_z), lambda i: (i, 0, 0)),
            pl.BlockSpec((late_lines // steps, states, cols_z), lambda i: (i, 0, 0)),
            block,
            pl.BlockSpec((span, cols_z), lambda i: (i, 0)),
            WHOLE,
            PINNED,
        ],
        [pl.BlockSpec((states, span, cols_z), lambda i: (0, i, 0))],
        [((states, lines, cols_z), BF16)],
        [],
        (
            xt, xt, xt, core_field, link_early, link_late, pltpu.with_memory_space_constraint(added, pltpu.HBM), pot, ring,
            final_token,
        ),
    )

    (subspace,) = call(
        32,
        functools.partial(result_kernel, 1.0 / (lines * cols_z * domains)),
        (),
        [WHOLE],
        [WHOLE],
        [((2, states, total_states // domains), F32)],
        [],
        (summed,),
    )
    return applied.reshape(orbitals.shape), subspace


def solution(mesh):
    in_specs = (
        P("band", ("groups", "domain"), None, None),
        P(("groups", "domain"), None, None),
        P(("groups", "domain"), None, None),
        P(("groups", "domain")),
        P(("groups", "domain")),
        P(("groups", "domain")),
        P("groups", None),
    )
    out_specs = (P("band", ("groups", "domain"), None, None), P(None, ("groups", "band"), "domain"))
    return jax.shard_map(local, mesh=mesh, in_specs=in_specs, out_specs=out_specs, check_vma=False)
```

```python
import functools

import jax
import jax.numpy as jnp
import numpy as np
from jax import lax
from jax.experimental import pallas as pl
from jax.experimental.pallas import tpu as pltpu
from jax.sharding import PartitionSpec as P

F32 = jnp.float32
BF16 = jnp.bfloat16
LANES = 128
ROWS = 16
NT = (((1,), (1,)), ((), ()))
WHOLE = pl.BlockSpec(memory_space=pltpu.VMEM)
NEAR = pl.BlockSpec(memory_space=pltpu.VMEM)
SCALARS = pl.BlockSpec(memory_space=pltpu.SMEM)
FAR = pl.BlockSpec(memory_space=pltpu.HBM)
PINNED = pl.BlockSpec(memory_space=pltpu.HBM)
UNREAD = pl.BlockSpec(memory_space=pl.ANY)
copies = pltpu.SemaphoreType.DMA


def call(room, kernel, grid, in_specs, out_specs, outs, scratch, args, aliases=None, micros=0.001):
    def place(spec):
        return {id(NEAR): pltpu.VMEM, id(PINNED): pltpu.HBM}.get(id(spec))

    args = [
        pltpu.with_memory_space_constraint(arg, place(spec)) if place(spec) else arg
        for spec, arg in zip(in_specs, args)
    ]
    shapes = [(place(spec) or jax.ShapeDtypeStruct)(shape, kind) for spec, (shape, kind) in zip(out_specs, outs)]
    return pl.pallas_call(
        kernel,
        grid=grid,
        out_shape=shapes,
        in_specs=in_specs,
        out_specs=out_specs,
        scratch_shapes=scratch,
        input_output_aliases=aliases or {},
        compiler_params=pltpu.CompilerParams(vmem_limit_bytes=int(room * 2**20)),
        cost_estimate=pl.CostEstimate(flops=int(micros * 1.1e9), bytes_accessed=1 << 10, transcendentals=0),
    )(*args)


def start(copy):
    copy.start()
    return copy


def start_all(pairs, sems):
    return [start(pltpu.make_async_copy(source, target, sems.at[i])) for i, (source, target) in enumerate(pairs)]


def wait_all(started):
    for copy in started:
        copy.wait()


def wait_for(*refs):
    pass


def pack_kernel(first, x_hbm, xt_hbm, early, late, message, x, xt, in_sems, out_sems):
    states, lines, _ = x.shape
    bands = in_sems.shape[0]
    share = lines // bands
    count = share - first
    ahead = early.shape[0] // bands
    loads, sends = [], []
    for c in range(bands):
        where = (slice(None), pl.ds(c * share, share), slice(None))
        loads.append(start(pltpu.make_async_copy(x_hbm.at[where], x.at[where], in_sems.at[c])))

    def send(line, number, target, at):
        copy = pltpu.make_async_copy(
            xt.at[pl.ds(line, number)], target.at[pl.ds(at, number)], out_sems.at[len(sends)]
        )
        sends.append(start(copy))

    for c in range(bands):
        loads[c].wait()
        for y0 in range(c * share, (c + 1) * share, ROWS):
            for s0 in range(0, states, ROWS):
                block = x[s0 : s0 + ROWS, y0 : y0 + ROWS, :]
                xt[y0 : y0 + ROWS, s0 : s0 + ROWS, :] = jnp.swapaxes(block, 0, 1)
        send(c * share, ahead, early, c * ahead)
        send(c * share + ahead, share - ahead, late, c * (share - ahead))
        send(c * share + first, count, message, c * (count + 1))
        send(c * share, 1, message, (c + bands - 1) % bands * (count + 1) + count)
        send(c * share, share, xt_hbm, c * share)
    for copy in sends:
        copy.wait()


def bases(groups):
    domain = lax.axis_index("domain")
    odd, upper = domain & 1, (domain >> 1) & 1
    return [2 * groups * side for side in (1 - odd, odd, 1 - upper, upper)]


def slot_reader(atom_ref, line_ref, count_ref, atoms_here):
    first = (lax.axis_index("domain") - 1) * atoms_here
    live = count_ref[0]

    def slot_at(t):
        return line_ref[t], jnp.clip(atom_ref[t] - first, 0, 3 * atoms_here - 1), t < live

    return slot_at


def energy_table(energy_ref):
    proj_count, atoms = energy_ref.shape
    per_group = LANES // proj_count
    lane = lax.broadcasted_iota(jnp.int32, (proj_count, LANES), 1)
    row = lax.broadcasted_iota(jnp.int32, (proj_count, LANES), 0)
    pick = jnp.where(lane % proj_count == row, 1.0, 0.0).astype(F32)
    spread = jnp.dot(energy_ref[...].T, pick, precision=lax.Precision.HIGHEST, preferred_element_type=F32)
    spread = spread.reshape(atoms // per_group, per_group, LANES)
    lane = lax.broadcasted_iota(jnp.int32, spread.shape, 2)
    atom = lax.broadcasted_iota(jnp.int32, spread.shape, 1)
    return jnp.sum(jnp.where(lane // proj_count == atom, spread, 0.0), axis=1)


def project_kernel(atom_ref, line_ref, count_ref, xt_hbm, p_hbm, mine_hbm, core_hbm, link_hbm, *refs):
    far_hbms, (total, mine_ref, xt_ref, p_ref, sems, out_sems) = refs[:-6], refs[-6:]
    slots, proj_count, _ = p_ref.shape
    groups, states = mine_ref.shape[0] // 3, mine_ref.shape[1]
    per_group = LANES // proj_count
    chunks = sems.shape[0] - 1
    size = slots // chunks
    unroll = 48
    pairs = [(p_hbm.at[pl.ds(c * size, size)], p_ref.at[pl.ds(c * size, size)]) for c in range(chunks)]
    xt_load, *loads = start_all([(xt_hbm, xt_ref), *pairs], sems)

    def clear(i, carry):
        for u in range(per_group):
            total[i * per_group + u] = jnp.zeros_like(total[0])
        return carry

    lax.fori_loop(0, 3 * groups, clear, 0)

    slot_at = slot_reader(atom_ref, line_ref, count_ref, groups * per_group)

    def body(i, carry):
        for u in range(unroll):
            t = i * unroll + u
            line, atom, live = slot_at(t)
            part = lax.dot_general(p_ref[t], xt_ref[line], NT, preferred_element_type=F32)
            total[jnp.where(live, atom, 3 * groups * per_group)] += part
        return carry

    xt_load.wait()
    for c in range(chunks):
        loads[c].wait()
        lax.fori_loop(c * size // unroll, (c + 1) * size // unroll, body, 0)

    for g in range(3 * groups):
        tiles = [total[g * per_group + u] for u in range(per_group)]
        mine_ref[g] = jnp.concatenate(tiles, axis=0).T.astype(BF16)
    sides = bases(groups)
    pairs = [(mine_ref, mine_hbm)]
    for side, far in zip(sides[:2], (core_hbm, link_hbm)):
        pairs.append((mine_ref.at[pl.ds(side, groups)], far.at[pl.ds(0, groups)]))
        pairs.append((mine_ref.at[pl.ds(groups, groups)], far.at[pl.ds(groups, groups)]))
    for side, far in zip(sides[2:], far_hbms):
        pairs.append((mine_ref.at[pl.ds(side, groups)], far))
    wait_all(start_all(pairs, out_sems))


def nonlocal_kernel(
    fars, atom_ref, line_ref, count_ref, xt_hbm, beside_hbm, early_hbm, p_hbm, energy_ref, mine_hbm, core_ref, link_ref, *refs
):
    far_refs, out_hbm, messages, scratch = refs[:fars], refs[fars + 1], refs[fars + 2 : -13], refs[-13:]
    lines_sum, whole_ref, mine_ref, total, table, atoms, p_ref, built, cores, links, sems, in_sems, out_sems = scratch
    lines = xt_hbm.shape[0]
    bands, half = cores.shape[:2]
    share, first = lines // bands, 2 * half
    held = built.shape[1] - first - half
    ahead = early_hbm.shape[0] // bands
    mine = (lax.axis_index("domain") & 1) * half
    pairs = []
    for k in range(bands):
        to = lax.axis_index("band") ^ k
        pairs.append((xt_hbm.at[pl.ds(to * share, first)], built.at[k, pl.ds(0, first)]))
        pairs.append((beside_hbm.at[pl.ds(to * share + mine, half)], cores.at[k]))
        pairs.append((early_hbm.at[pl.ds(to * ahead + mine, half)], links.at[k]))
    brought = start_all(pairs, in_sems)
    slots, proj_count, _ = p_ref.shape
    groups, states = total.shape[0] // 3, total.shape[1]
    per_group = LANES // proj_count
    unroll = 48
    mine_load, load = start_all([(mine_hbm, mine_ref), (p_hbm, p_ref)], sems)
    sends = []

    def clear(i, carry):
        lines_sum[i] = jnp.zeros((states, LANES), F32)
        return carry

    lax.fori_loop(0, lines + 1, clear, 0)
    mine_load.wait()
    total[...] = mine_ref[...].astype(F32)
    sides = bases(groups)
    for g in range(groups):
        total[groups + g] += core_ref[g].astype(F32) + link_ref[g].astype(F32)
        for side, ref in zip(sides[:2], (core_ref, link_ref)):
            total[side + g] += ref[groups + g].astype(F32)
        for side, ref in zip(sides[2:], far_refs):
            total[side + g] += ref[g].astype(F32)
    table[...] = energy_table(energy_ref)
    last = table.shape[0] - 1
    for g in range(3 * groups):
        row = jnp.clip((lax.axis_index("domain") - 1) * groups + g, 0, last)
        tile = (total[g] * table[pl.ds(row, 1), :]).astype(BF16)
        for u in range(per_group):
            atoms[g * per_group + u] = tile[:, u * proj_count : (u + 1) * proj_count]
    for g in range(groups):
        whole_ref[g] = total[groups + g].astype(BF16)
    wait_all(brought)
    for k, message in enumerate(messages):
        to = lax.axis_index("band") ^ k
        for i in range(half):
            built[k, first + i] = (cores[k, i].astype(F32) + links[k, i].astype(F32)).astype(BF16)
        for i in range(held):
            built[k, first + half + i] = whole_ref[to * held + i]
        sends.append(start(pltpu.make_async_copy(built.at[k], message, out_sems.at[k])))
    load.wait()

    slot_at = slot_reader(atom_ref, line_ref, count_ref, groups * per_group)

    def body(i, carry):
        for u in range(unroll):
            t = i * unroll + u
            line, atom, live = slot_at(t)
            part = jnp.dot(atoms[atom], p_ref[t], preferred_element_type=F32)
            lines_sum[jnp.where(live, line, lines)] += part
        return carry

    lax.fori_loop(0, slots // unroll, body, 0)
    sends.append(start(pltpu.make_async_copy(lines_sum.at[pl.ds(0, lines)], out_hbm, sems.at[3])))
    wait_all(sends)


def stencil_kernel(
    share, xt_ref, last_ref, next_ref, core_ref, early_ref, late_ref, added_ref, pot_ref, ring_ref, unread,
    out_ref,
):
    states, here, _ = out_ref.shape

    ahead = early_ref.shape[0] * share // here

    def link(i, rows):
        chunk, at = divmod(i, share)
        if at < ahead:
            return early_ref[chunk * ahead + at, rows, :]
        return late_ref[chunk * (share - ahead) + at - ahead, rows, :]

    def line(i, rows):
        ref, at = (last_ref, 0) if i < 0 else (next_ref, 0) if i == here else (xt_ref, i)
        return ref[at, rows, :]

    for y0 in range(0, here, ROWS):
        for s0 in range(0, states, ROWS):
            rows = slice(s0, s0 + ROWS)
            results = []
            cells = jnp.concatenate([line(y0 + i, rows) for i in range(ROWS)], axis=0)
            along = jnp.dot(cells, ring_ref[...], preferred_element_type=F32)
            before, x = line(y0 - 1, rows).astype(F32), line(y0, rows).astype(F32)
            for i in range(ROWS):
                y = y0 + i
                after = line(y + 1, rows).astype(F32)
                beside = (before + after) + (core_ref[y, rows, :].astype(F32) + link(y, rows).astype(F32))
                value = along[i * ROWS : (i + 1) * ROWS] + pot_ref[y : y + 1, :] * x
                results.append((value + added_ref[y, rows, :] - 0.5 * beside).astype(BF16))
                before, x = x, after
            out_ref[rows, y0 : y0 + ROWS, :] = jnp.swapaxes(jnp.stack(results, axis=0), 0, 1)


def pass_half(all_ref, pass_hbm, sem):
    half = pass_hbm.shape[0]
    copy = start(pltpu.make_async_copy(all_ref.at[pl.ds((1 - (lax.axis_index("domain") & 1)) * half, half)], pass_hbm, sem))
    copy.wait()


def later_kernel(bands, landed, unread, handed, all_ref, pass_hbm, same, sems, pass_sem):
    count, states = all_ref.shape[0], landed.shape[1]
    loads = [
        start(
            pltpu.make_async_copy(
                landed.at[pl.ds(b * count, count)], all_ref.at[:, pl.ds(b * states, states), :], sems.at[b]
            )
        )
        for b in range(bands)
    ]
    for copy in loads:
        copy.wait()
    pass_half(all_ref, pass_hbm, pass_sem)


def early_kernel(after_ref, energy_ref, *refs):
    pieces, (all_ref, beside_ref, projs_ref, table_ref, token, sems) = refs[:-6], refs[-6:]
    states = pieces[0].shape[1]
    count, half, held = all_ref.shape[0] - 1, beside_ref.shape[0], projs_ref.shape[0]
    pairs = []
    for k, piece in enumerate(pieces):
        at = pl.ds(pl.multiple_of((lax.axis_index("band") ^ k) * states, states), states)
        pairs.append((piece.at[pl.ds(0, count)], all_ref.at[pl.ds(0, count), at, :]))
        pairs.append((piece.at[pl.ds(count, half)], beside_ref.at[:, at, :]))
        pairs.append((piece.at[pl.ds(count + half, held)], projs_ref.at[:, at, :]))
    loads = start_all(pairs, sems)
    all_ref[count] = after_ref[0]
    table_ref[...] = energy_table(energy_ref)
    wait_all(loads)


def add_products(row, all_ref, beside_refs, pot_ref, acc):
    half = beside_refs[0].shape[0]
    group = 4
    mine = (lax.axis_index("domain") & 1) * half
    for part, base in ((0, mine), (1, half - mine)):
        for i0 in range(0, half, group):
            xs, ys = [], []
            for i in range(i0, min(i0 + group, half)):
                cell = all_ref[base + i]
                x = cell.astype(F32)
                y = (3.0 + pot_ref[pl.ds(row + base + i, 1), :]) * x - pltpu.roll(x, x.shape[1] - 1, 1)
                y = y - all_ref[base + i + 1].astype(F32)
                if part == 0:
                    for ref in beside_refs:
                        y = y - ref[i].astype(F32)
                xs.append(cell)
                ys.append(y.astype(BF16))
            flat_x = jnp.concatenate(xs, axis=1)
            flat_y = jnp.concatenate(ys, axis=1)
            acc[0] += lax.dot_general(flat_x, flat_x, NT, preferred_element_type=F32)
            acc[1] += lax.dot_general(flat_y, flat_x, NT, preferred_element_type=F32)


def gram_kernel(first, share, all_ref, core_ref, link_ref, pot_ref, unread, acc):
    acc[...] = jnp.zeros_like(acc)
    add_products(lax.axis_index("band") * share + first, all_ref, (core_ref, link_ref), pot_ref, acc)


def final_kernel(bands, share, all_ref, beside_ref, pot_ref, begun_ref, proj_ref, energy_ref, out_ref, token, acc):
    acc[...] = begun_ref[...]
    add_products(lax.axis_index("band") * share, all_ref, (beside_ref,), pot_ref, acc)
    groups = proj_ref.shape[0]
    first = (lax.axis_index("domain") * bands + lax.axis_index("band")) * groups
    for g in range(groups):
        here = proj_ref[g]
        scaled = (here.astype(F32) * energy_ref[pl.ds(first + g, 1), :]).astype(BF16)
        acc[1] += lax.dot_general(scaled, here, NT, preferred_element_type=F32)
    hamil = 0.5 * (acc[1] + acc[1].T)
    domains = out_ref.shape[0] // bands
    rows, cols = out_ref.shape[1], out_ref.shape[2] // 2
    for c in range(domains):
        for r in range(bands):
            r0, c0 = r * rows, c * cols
            out_ref[c * bands + r, :, :cols] = acc[0, r0 : r0 + rows, c0 : c0 + cols].astype(BF16)
            out_ref[c * bands + r, :, cols:] = hamil[r0 : r0 + rows, c0 : c0 + cols].astype(BF16)


def result_kernel(scale, parts_ref, out_ref):
    total = jnp.sum(parts_ref[...].astype(F32), axis=0) * scale
    cols = out_ref.shape[2]
    out_ref[0] = total[:, :cols]
    out_ref[1] = total[:, cols:]


def local(orbitals, potential, projectors, tile_atom, tile_line, tile_count, energies):
    states, _, lines, cols_z = orbitals.shape
    slots, proj_count, _ = projectors.shape
    atom_total = energies.shape[0]
    domains, bands = lax.axis_size("domain"), lax.axis_size("band")
    total_states = states * bands
    atoms_here = atom_total // domains
    per_group = LANES // proj_count
    groups = atoms_here // per_group
    share = lines // bands
    first = 2 * (share * 3 // 32)
    rest = share - first

    core_pairs = [(i, i ^ 1) for i in range(domains) if i ^ 1 < domains]
    link_pairs = [(i, ((i + 1) ^ 1) - 1) for i in range(1, domains) if ((i + 1) ^ 1) - 1 < domains]
    near_far = [(i, i ^ 2) for i in range(domains) if i ^ 2 < domains]
    next = [(i, ((i + 2) ^ 2) - 2) for i in range(2, domains) if ((i + 2) ^ 2) - 2 < domains]
    far_pairs = [pairs for pairs in (near_far, next) if pairs]

    def swapped(values, axis):
        size = lax.axis_size(axis)
        got = {k: lax.ppermute(values[k - 1], axis, [(i, i ^ k) for i in range(size)]) for k in range(size - 1, 0, -1)}
        return [got[k] for k in range(1, size)]

    field = orbitals.reshape(states, lines, cols_z)
    pot = potential.reshape(lines, cols_z)
    energy = energies.T
    energy_rows = (atom_total // per_group, LANES)
    token = ((8, LANES), F32)
    eye = np.eye(cols_z, dtype=np.float32)
    ring = jnp.asarray(3.0 * eye - 0.5 * (np.roll(eye, 1, axis=0) + np.roll(eye, -1, axis=0)), dtype=BF16)

    ahead = share * 5 // 8
    late_lines = lines - ahead * bands
    line_shape, late_shape = (lines, states, cols_z), (late_lines, states, cols_z)
    xt, early_part, late_part, message = call(
        63,
        functools.partial(pack_kernel, first),
        (),
        [FAR],
        [FAR] * 4,
        [
            (line_shape, BF16),
            ((lines - late_lines, states, cols_z), BF16),
            (late_shape, BF16),
            ((bands * (rest + 1), states, cols_z), BF16),
        ],
        [
            pltpu.VMEM((states, lines, cols_z), BF16),
            pltpu.VMEM(line_shape, BF16),
            copies((bands,)),
            copies((5 * bands,)),
        ],
        (field,),
    )
    landed = lax.all_to_all(message, "band", split_axis=0, concat_axis=0, tiled=True)
    link_early = lax.ppermute(early_part, "domain", link_pairs)
    core_field = lax.ppermute(xt, "domain", core_pairs)

    group_shape = (groups, states, LANES)
    mine, to_core, to_link, *to_far = call(
        63,
        project_kernel,
        (),
        [SCALARS] * 3 + [FAR, PINNED],
        [PINNED] + [FAR] * (2 + len(far_pairs)),
        [((3 * groups, states, LANES), BF16)]
        + [((2 * groups, states, LANES), BF16)] * 2
        + [(group_shape, BF16)] * len(far_pairs),
        [
            pltpu.VMEM((3 * atoms_here + 1, proj_count, states), F32),
            pltpu.VMEM((3 * groups, states, LANES), BF16),
            pltpu.VMEM(line_shape, BF16),
            pltpu.VMEM(projectors.shape, BF16),
            copies((5,)),
            copies((5 + len(far_pairs),)),
        ],
        (tile_atom, tile_line, tile_count, xt, projectors),
    )
    from_link = lax.ppermute(to_link, "domain", link_pairs)
    from_far = [lax.ppermute(value, "domain", pairs) for value, pairs in zip(to_far, far_pairs)]
    from_core = lax.ppermute(to_core, "domain", core_pairs)
    (gate,) = call(
        63,
        wait_for,
        (),
        [UNREAD] * (4 + len(far_pairs)),
        [PINNED],
        [token],
        [],
        (from_core, from_link, *from_far, link_early, core_field),
    )
    held = groups // bands
    built_shape = (first + first // 2 + held, states, cols_z)
    beside_shape = (bands, first // 2, states, cols_z)
    added, own_message, *messages = call(
        62,
        functools.partial(nonlocal_kernel, len(far_pairs)),
        (),
        [SCALARS] * 3 + [FAR] * 3 + [PINNED, WHOLE, PINNED, WHOLE, WHOLE] + [WHOLE] * len(far_pairs) + [PINNED],
        [PINNED, PINNED] + [FAR] * (bands - 1),
        [(line_shape, F32)] + [(built_shape, BF16)] * bands,
        [
            pltpu.VMEM((lines + 1, states, cols_z), F32),
            pltpu.VMEM(group_shape, BF16),
            pltpu.VMEM((3 * groups, states, LANES), BF16),
            pltpu.VMEM((3 * groups, states, LANES), F32),
            pltpu.VMEM(energy_rows, F32),
            pltpu.VMEM((3 * atoms_here, states, proj_count), BF16),
            pltpu.VMEM(projectors.shape, BF16),
            pltpu.VMEM((bands, *built_shape), BF16),
            pltpu.VMEM(beside_shape, BF16),
            pltpu.VMEM(beside_shape, BF16),
            copies((4,)),
            copies((3 * bands,)),
            copies((bands,)),
        ],
        (
            tile_atom, tile_line, tile_count, xt, core_field, link_early, projectors, energy, mine, from_core,
            from_link, *from_far, gate,
        ),
        micros=8,
    )
    early = swapped(messages, "band")

    later_all, later_pass, late_part = call(
        32,
        functools.partial(later_kernel, bands),
        (),
        [FAR, PINNED, UNREAD],
        [NEAR, FAR, UNREAD],
        [
            ((rest + 1, total_states, cols_z), BF16),
            ((rest // 2, total_states, cols_z), BF16),
            (late_shape, BF16),
        ],
        [copies((bands,)), copies],
        (landed, own_message, late_part),
        aliases={2: 2},
    )
    later_link = lax.ppermute(later_pass, "domain", link_pairs)
    later_core = lax.ppermute(later_pass, "domain", core_pairs)
    link_late = lax.ppermute(late_part, "domain", link_pairs)

    early_all, early_beside, projs, energy_table_here, early_token = call(
        32,
        early_kernel,
        (),
        [NEAR, WHOLE, PINNED] + [FAR] * (bands - 1),
        [NEAR, NEAR, NEAR, NEAR, PINNED],
        [
            ((first + 1, total_states, cols_z), BF16),
            ((first // 2, total_states, cols_z), BF16),
            ((held, total_states, LANES), BF16),
            (energy_rows, F32),
            token,
        ],
        [copies((3 * bands,))],
        (later_all, energy, own_message, *early),
        micros=30,
    )
    (begun,) = call(
        32,
        functools.partial(gram_kernel, first, share),
        (),
        [NEAR, WHOLE, WHOLE, WHOLE, PINNED],
        [NEAR],
        [((2, total_states, total_states), F32)],
        [],
        (later_all, later_core, later_link, pot, early_token),
    )
    parts = domains * bands
    blocks, final_token = call(
        32,
        functools.partial(final_kernel, bands, share),
        (),
        [NEAR, NEAR, WHOLE, NEAR, NEAR, NEAR],
        [WHOLE, PINNED],
        [((parts, states, 2 * total_states // domains), BF16), token],
        [pltpu.VMEM((2, total_states, total_states), F32)],
        (early_all, early_beside, pot, begun, projs, energy_table_here),
    )
    summed = lax.all_to_all(blocks, ("domain", "band"), split_axis=0, concat_axis=0, tiled=True)
    span = 2 * ROWS
    steps = lines // span
    block = pl.BlockSpec((span, states, cols_z), lambda i: (i, 0, 0))
    (applied,) = call(
        48,
        functools.partial(stencil_kernel, share),
        (steps,),
        [
            block,
            pl.BlockSpec((1, states, cols_z), lambda i: (lax.rem(i * span + lines - 1, lines), 0, 0)),
            pl.BlockSpec((1, states, cols_z), lambda i: (lax.rem(i * span + span, lines), 0, 0)),
            block,
            pl.BlockSpec((ahead * bands // steps, states, cols_z), lambda i: (i, 0, 0)),
            pl.BlockSpec((late_lines // steps, states, cols_z), lambda i: (i, 0, 0)),
            block,
            pl.BlockSpec((span, cols_z), lambda i: (i, 0)),
            WHOLE,
            PINNED,
        ],
        [pl.BlockSpec((states, span, cols_z), lambda i: (0, i, 0))],
        [((states, lines, cols_z), BF16)],
        [],
        (
            xt, xt, xt, core_field, link_early, link_late, pltpu.with_memory_space_constraint(added, pltpu.HBM), pot, ring,
            final_token,
        ),
    )

    (subspace,) = call(
        32,
        functools.partial(result_kernel, 1.0 / (lines * cols_z * domains)),
        (),
        [WHOLE],
        [WHOLE],
        [((2, states, total_states // domains), F32)],
        [],
        (summed,),
    )
    return applied.reshape(orbitals.shape), subspace


def solution(mesh):
    in_specs = (
        P("band", ("groups", "domain"), None, None),
        P(("groups", "domain"), None, None),
        P(("groups", "domain"), None, None),
        P(("groups", "domain")),
        P(("groups", "domain")),
        P(("groups", "domain")),
        P("groups", None),
    )
    out_specs = (P("band", ("groups", "domain"), None, None), P(None, ("groups", "band"), "domain"))
    return jax.shard_map(local, mesh=mesh, in_specs=in_specs, out_specs=out_specs, check_vma=False)
```

```python
import functools

import jax
import jax.numpy as jnp
import numpy as np
from jax import lax
from jax.experimental import pallas as pl
from jax.experimental.pallas import tpu as pltpu
from jax.sharding import PartitionSpec as P

F32 = jnp.float32
BF16 = jnp.bfloat16
LANES = 128
ROWS = 16
NT = (((1,), (1,)), ((), ()))
WHOLE = pl.BlockSpec(memory_space=pltpu.VMEM)
NEAR = pl.BlockSpec(memory_space=pltpu.VMEM)
SCALARS = pl.BlockSpec(memory_space=pltpu.SMEM)
FAR = pl.BlockSpec(memory_space=pltpu.HBM)
PINNED = pl.BlockSpec(memory_space=pltpu.HBM)
UNREAD = pl.BlockSpec(memory_space=pl.ANY)
copies = pltpu.SemaphoreType.DMA


def call(room, kernel, grid, in_specs, out_specs, outs, scratch, args, aliases=None, micros=0.001):
    def place(spec):
        return {id(NEAR): pltpu.VMEM, id(PINNED): pltpu.HBM}.get(id(spec))

    args = [
        pltpu.with_memory_space_constraint(arg, place(spec)) if place(spec) else arg
        for spec, arg in zip(in_specs, args)
    ]
    shapes = [(place(spec) or jax.ShapeDtypeStruct)(shape, kind) for spec, (shape, kind) in zip(out_specs, outs)]
    return pl.pallas_call(
        kernel,
        grid=grid,
        out_shape=shapes,
        in_specs=in_specs,
        out_specs=out_specs,
        scratch_shapes=scratch,
        input_output_aliases=aliases or {},
        compiler_params=pltpu.CompilerParams(vmem_limit_bytes=int(room * 2**20)),
        cost_estimate=pl.CostEstimate(flops=int(micros * 1.1e9), bytes_accessed=1 << 10, transcendentals=0),
    )(*args)


def start(copy):
    copy.start()
    return copy


def start_all(pairs, sems):
    return [start(pltpu.make_async_copy(source, target, sems.at[i])) for i, (source, target) in enumerate(pairs)]


def wait_all(started):
    for copy in started:
        copy.wait()


def wait_for(*refs):
    pass


def pack_kernel(first, x_hbm, xt_hbm, early, late, message, x, xt, in_sems, out_sems):
    states, lines, _ = x.shape
    bands = in_sems.shape[0]
    share = lines // bands
    count = share - first
    ahead = early.shape[0] // bands
    loads, sends = [], []
    for c in range(bands):
        where = (slice(None), pl.ds(c * share, share), slice(None))
        loads.append(start(pltpu.make_async_copy(x_hbm.at[where], x.at[where], in_sems.at[c])))

    def send(line, number, target, at):
        copy = pltpu.make_async_copy(
            xt.at[pl.ds(line, number)], target.at[pl.ds(at, number)], out_sems.at[len(sends)]
        )
        sends.append(start(copy))

    for c in range(bands):
        loads[c].wait()
        for y0 in range(c * share, (c + 1) * share, ROWS):
            for s0 in range(0, states, ROWS):
                block = x[s0 : s0 + ROWS, y0 : y0 + ROWS, :]
                xt[y0 : y0 + ROWS, s0 : s0 + ROWS, :] = jnp.swapaxes(block, 0, 1)
        send(c * share, ahead, early, c * ahead)
        send(c * share + ahead, share - ahead, late, c * (share - ahead))
        send(c * share + first, count, message, c * (count + 1))
        send(c * share, 1, message, (c + bands - 1) % bands * (count + 1) + count)
        send(c * share, share, xt_hbm, c * share)
    for copy in sends:
        copy.wait()


def bases(groups):
    domain = lax.axis_index("domain")
    odd, upper = domain & 1, (domain >> 1) & 1
    return [2 * groups * side for side in (1 - odd, odd, 1 - upper, upper)]


def slot_reader(atom_ref, line_ref, count_ref, atoms_here):
    first = (lax.axis_index("domain") - 1) * atoms_here
    live = count_ref[0]

    def slot_at(t):
        return line_ref[t], jnp.clip(atom_ref[t] - first, 0, 3 * atoms_here - 1), t < live

    return slot_at


def energy_table(energy_ref):
    proj_count, atoms = energy_ref.shape
    per_group = LANES // proj_count
    lane = lax.broadcasted_iota(jnp.int32, (proj_count, LANES), 1)
    row = lax.broadcasted_iota(jnp.int32, (proj_count, LANES), 0)
    pick = jnp.where(lane % proj_count == row, 1.0, 0.0).astype(F32)
    spread = jnp.dot(energy_ref[...].T, pick, precision=lax.Precision.HIGHEST, preferred_element_type=F32)
    spread = spread.reshape(atoms // per_group, per_group, LANES)
    lane = lax.broadcasted_iota(jnp.int32, spread.shape, 2)
    atom = lax.broadcasted_iota(jnp.int32, spread.shape, 1)
    return jnp.sum(jnp.where(lane // proj_count == atom, spread, 0.0), axis=1)


def project_kernel(atom_ref, line_ref, count_ref, xt_hbm, p_hbm, mine_hbm, core_hbm, link_hbm, *refs):
    far_hbms, (total, mine_ref, xt_ref, p_ref, sems, out_sems) = refs[:-6], refs[-6:]
    slots, proj_count, _ = p_ref.shape
    groups, states = mine_ref.shape[0] // 3, mine_ref.shape[1]
    per_group = LANES // proj_count
    chunks = sems.shape[0] - 1
    size = slots // chunks
    unroll = 48
    pairs = [(p_hbm.at[pl.ds(c * size, size)], p_ref.at[pl.ds(c * size, size)]) for c in range(chunks)]
    xt_load, *loads = start_all([(xt_hbm, xt_ref), *pairs], sems)

    def clear(i, carry):
        for u in range(per_group):
            total[i * per_group + u] = jnp.zeros_like(total[0])
        return carry

    lax.fori_loop(0, 3 * groups, clear, 0)

    slot_at = slot_reader(atom_ref, line_ref, count_ref, groups * per_group)

    def body(i, carry):
        for u in range(unroll):
            t = i * unroll + u
            line, atom, live = slot_at(t)
            part = lax.dot_general(p_ref[t], xt_ref[line], NT, preferred_element_type=F32)
            total[jnp.where(live, atom, 3 * groups * per_group)] += part
        return carry

    xt_load.wait()
    for c in range(chunks):
        loads[c].wait()
        lax.fori_loop(c * size // unroll, (c + 1) * size // unroll, body, 0)

    for g in range(3 * groups):
        tiles = [total[g * per_group + u] for u in range(per_group)]
        mine_ref[g] = jnp.concatenate(tiles, axis=0).T.astype(BF16)
    sides = bases(groups)
    pairs = [(mine_ref, mine_hbm)]
    for side, far in zip(sides[:2], (core_hbm, link_hbm)):
        pairs.append((mine_ref.at[pl.ds(side, groups)], far.at[pl.ds(0, groups)]))
        pairs.append((mine_ref.at[pl.ds(groups, groups)], far.at[pl.ds(groups, groups)]))
    for side, far in zip(sides[2:], far_hbms):
        pairs.append((mine_ref.at[pl.ds(side, groups)], far))
    wait_all(start_all(pairs, out_sems))


def nonlocal_kernel(
    fars, atom_ref, line_ref, count_ref, xt_hbm, beside_hbm, early_hbm, p_hbm, energy_ref, mine_hbm, core_ref, link_ref, *refs
):
    far_refs, out_hbm, messages, scratch = refs[:fars], refs[fars + 1], refs[fars + 2 : -13], refs[-13:]
    lines_sum, whole_ref, mine_ref, total, table, atoms, p_ref, built, cores, links, sems, in_sems, out_sems = scratch
    lines = xt_hbm.shape[0]
    bands, half = cores.shape[:2]
    share, first = lines // bands, 2 * half
    held = built.shape[1] - first - half
    ahead = early_hbm.shape[0] // bands
    mine = (lax.axis_index("domain") & 1) * half
    pairs = []
    for k in range(bands):
        to = lax.axis_index("band") ^ k
        pairs.append((xt_hbm.at[pl.ds(to * share, first)], built.at[k, pl.ds(0, first)]))
        pairs.append((beside_hbm.at[pl.ds(to * share + mine, half)], cores.at[k]))
        pairs.append((early_hbm.at[pl.ds(to * ahead + mine, half)], links.at[k]))
    brought = start_all(pairs, in_sems)
    slots, proj_count, _ = p_ref.shape
    groups, states = total.shape[0] // 3, total.shape[1]
    per_group = LANES // proj_count
    unroll = 48
    mine_load, load = start_all([(mine_hbm, mine_ref), (p_hbm, p_ref)], sems)
    sends = []

    def clear(i, carry):
        lines_sum[i] = jnp.zeros((states, LANES), F32)
        return carry

    lax.fori_loop(0, lines + 1, clear, 0)
    mine_load.wait()
    total[...] = mine_ref[...].astype(F32)
    sides = bases(groups)
    for g in range(groups):
        total[groups + g] += core_ref[g].astype(F32) + link_ref[g].astype(F32)
        for side, ref in zip(sides[:2], (core_ref, link_ref)):
            total[side + g] += ref[groups + g].astype(F32)
        for side, ref in zip(sides[2:], far_refs):
            total[side + g] += ref[g].astype(F32)
    table[...] = energy_table(energy_ref)
    last = table.shape[0] - 1
    for g in range(3 * groups):
        row = jnp.clip((lax.axis_index("domain") - 1) * groups + g, 0, last)
        tile = (total[g] * table[pl.ds(row, 1), :]).astype(BF16)
        for u in range(per_group):
            atoms[g * per_group + u] = tile[:, u * proj_count : (u + 1) * proj_count]
    for g in range(groups):
        whole_ref[g] = total[groups + g].astype(BF16)
    wait_all(brought)
    for k, message in enumerate(messages):
        to = lax.axis_index("band") ^ k
        for i in range(half):
            built[k, first + i] = (cores[k, i].astype(F32) + links[k, i].astype(F32)).astype(BF16)
        for i in range(held):
            built[k, first + half + i] = whole_ref[to * held + i]
        sends.append(start(pltpu.make_async_copy(built.at[k], message, out_sems.at[k])))
    load.wait()

    slot_at = slot_reader(atom_ref, line_ref, count_ref, groups * per_group)

    def body(i, carry):
        for u in range(unroll):
            t = i * unroll + u
            line, atom, live = slot_at(t)
            part = jnp.dot(atoms[atom], p_ref[t], preferred_element_type=F32)
            lines_sum[jnp.where(live, line, lines)] += part
        return carry

    lax.fori_loop(0, slots // unroll, body, 0)
    sends.append(start(pltpu.make_async_copy(lines_sum.at[pl.ds(0, lines)], out_hbm, sems.at[3])))
    wait_all(sends)


def stencil_kernel(
    share, xt_ref, last_ref, next_ref, core_ref, early_ref, late_ref, added_ref, pot_ref, ring_ref, unread,
    out_ref,
):
    states, here, _ = out_ref.shape

    ahead = early_ref.shape[0] * share // here

    def link(i, rows):
        chunk, at = divmod(i, share)
        if at < ahead:
            return early_ref[chunk * ahead + at, rows, :]
        return late_ref[chunk * (share - ahead) + at - ahead, rows, :]

    def line(i, rows):
        ref, at = (last_ref, 0) if i < 0 else (next_ref, 0) if i == here else (xt_ref, i)
        return ref[at, rows, :]

    for y0 in range(0, here, ROWS):
        for s0 in range(0, states, ROWS):
            rows = slice(s0, s0 + ROWS)
            results = []
            cells = jnp.concatenate([line(y0 + i, rows) for i in range(ROWS)], axis=0)
            along = jnp.dot(cells, ring_ref[...], preferred_element_type=F32)
            before, x = line(y0 - 1, rows).astype(F32), line(y0, rows).astype(F32)
            for i in range(ROWS):
                y = y0 + i
                after = line(y + 1, rows).astype(F32)
                beside = (before + after) + (core_ref[y, rows, :].astype(F32) + link(y, rows).astype(F32))
                value = along[i * ROWS : (i + 1) * ROWS] + pot_ref[y : y + 1, :] * x
                results.append((value + added_ref[y, rows, :] - 0.5 * beside).astype(BF16))
                before, x = x, after
            out_ref[rows, y0 : y0 + ROWS, :] = jnp.swapaxes(jnp.stack(results, axis=0), 0, 1)


def pass_half(all_ref, pass_hbm, sem):
    half = pass_hbm.shape[0]
    copy = start(pltpu.make_async_copy(all_ref.at[pl.ds((1 - (lax.axis_index("domain") & 1)) * half, half)], pass_hbm, sem))
    copy.wait()


def later_kernel(bands, landed, unread, handed, all_ref, pass_hbm, same, sems, pass_sem):
    count, states = all_ref.shape[0], landed.shape[1]
    loads = [
        start(
            pltpu.make_async_copy(
                landed.at[pl.ds(b * count, count)], all_ref.at[:, pl.ds(b * states, states), :], sems.at[b]
            )
        )
        for b in range(bands)
    ]
    for copy in loads:
        copy.wait()
    pass_half(all_ref, pass_hbm, pass_sem)


def add_products(row, all_ref, beside_refs, pot_ref, acc):
    half = beside_refs[0].shape[0]
    group = 4
    mine = (lax.axis_index("domain") & 1) * half
    for part, base in ((0, mine), (1, half - mine)):
        for i0 in range(0, half, group):
            xs, ys = [], []
            for i in range(i0, min(i0 + group, half)):
                cell = all_ref[base + i]
                x = cell.astype(F32)
                y = (3.0 + pot_ref[pl.ds(row + base + i, 1), :]) * x - pltpu.roll(x, x.shape[1] - 1, 1)
                y = y - all_ref[base + i + 1].astype(F32)
                if part == 0:
                    for ref in beside_refs:
                        y = y - ref[i].astype(F32)
                xs.append(cell)
                ys.append(y.astype(BF16))
            flat_x = jnp.concatenate(xs, axis=1)
            flat_y = jnp.concatenate(ys, axis=1)
            acc[0] += lax.dot_general(flat_x, flat_x, NT, preferred_element_type=F32)
            acc[1] += lax.dot_general(flat_y, flat_x, NT, preferred_element_type=F32)


def final_kernel(
    first, share, later_ref, core_ref, link_ref, pot_ref, energy_ref, own_hbm, unread, *refs
):
    pieces, (out_ref, token, lines_ref, beside_ref, projs, table, acc, sems) = refs[:-8], refs[-8:]
    bands, states = len(pieces) + 1, own_hbm.shape[1]
    band = lax.axis_index("band")
    half, held = beside_ref.shape[0], projs.shape[0]
    at = pl.ds(pl.multiple_of(band * states, states), states)
    loads = start_all(
        [
            (own_hbm.at[pl.ds(0, first)], lines_ref.at[pl.ds(0, first), at, :]),
            (own_hbm.at[pl.ds(first, half)], beside_ref.at[:, at, :]),
            (own_hbm.at[pl.ds(first + half, held)], projs.at[:, at, :]),
        ],
        sems,
    )
    acc[...] = jnp.zeros_like(acc)
    add_products(band * share + first, later_ref, (core_ref, link_ref), pot_ref, acc)
    table[...] = energy_table(energy_ref)
    lines_ref[first] = later_ref[0]
    for k, piece in enumerate(pieces, 1):
        at = pl.ds(pl.multiple_of((band ^ k) * states, states), states)
        for i in range(first):
            lines_ref[i, at, :] = piece[i]
        for i in range(half):
            beside_ref[i, at, :] = piece[first + i]
        for i in range(held):
            projs[i, at, :] = piece[first + half + i]
    wait_all(loads)
    add_products(band * share, lines_ref, (beside_ref,), pot_ref, acc)
    row = (lax.axis_index("domain") * bands + band) * held
    for g in range(held):
        here = projs[g]
        scaled = (here.astype(F32) * table[pl.ds(row + g, 1), :]).astype(BF16)
        acc[1] += lax.dot_general(scaled, here, NT, preferred_element_type=F32)
    hamil = 0.5 * (acc[1] + acc[1].T)
    domains = out_ref.shape[0] // bands
    rows, cols = out_ref.shape[1], out_ref.shape[2] // 2
    for c in range(domains):
        for r in range(bands):
            r0, c0 = r * rows, c * cols
            out_ref[c * bands + r, :, :cols] = acc[0, r0 : r0 + rows, c0 : c0 + cols].astype(BF16)
            out_ref[c * bands + r, :, cols:] = hamil[r0 : r0 + rows, c0 : c0 + cols].astype(BF16)


def result_kernel(scale, parts_ref, out_ref):
    total = jnp.sum(parts_ref[...].astype(F32), axis=0) * scale
    cols = out_ref.shape[2]
    out_ref[0] = total[:, :cols]
    out_ref[1] = total[:, cols:]


def local(orbitals, potential, projectors, tile_atom, tile_line, tile_count, energies):
    states, _, lines, cols_z = orbitals.shape
    slots, proj_count, _ = projectors.shape
    atom_total = energies.shape[0]
    domains, bands = lax.axis_size("domain"), lax.axis_size("band")
    total_states = states * bands
    atoms_here = atom_total // domains
    per_group = LANES // proj_count
    groups = atoms_here // per_group
    share = lines // bands
    first = 2 * (share * 3 // 32)
    rest = share - first

    core_pairs = [(i, i ^ 1) for i in range(domains) if i ^ 1 < domains]
    link_pairs = [(i, ((i + 1) ^ 1) - 1) for i in range(1, domains) if ((i + 1) ^ 1) - 1 < domains]
    near_far = [(i, i ^ 2) for i in range(domains) if i ^ 2 < domains]
    next = [(i, ((i + 2) ^ 2) - 2) for i in range(2, domains) if ((i + 2) ^ 2) - 2 < domains]
    far_pairs = [pairs for pairs in (near_far, next) if pairs]

    def swapped(values, axis):
        size = lax.axis_size(axis)
        got = {k: lax.ppermute(values[k - 1], axis, [(i, i ^ k) for i in range(size)]) for k in range(size - 1, 0, -1)}
        return [got[k] for k in range(1, size)]

    field = orbitals.reshape(states, lines, cols_z)
    pot = potential.reshape(lines, cols_z)
    energy = energies.T
    energy_rows = (atom_total // per_group, LANES)
    token = ((8, LANES), F32)
    eye = np.eye(cols_z, dtype=np.float32)
    ring = jnp.asarray(3.0 * eye - 0.5 * (np.roll(eye, 1, axis=0) + np.roll(eye, -1, axis=0)), dtype=BF16)

    ahead = share * 5 // 8
    late_lines = lines - ahead * bands
    line_shape, late_shape = (lines, states, cols_z), (late_lines, states, cols_z)
    xt, early_part, late_part, message = call(
        63,
        functools.partial(pack_kernel, first),
        (),
        [FAR],
        [FAR] * 4,
        [
            (line_shape, BF16),
            ((lines - late_lines, states, cols_z), BF16),
            (late_shape, BF16),
            ((bands * (rest + 1), states, cols_z), BF16),
        ],
        [
            pltpu.VMEM((states, lines, cols_z), BF16),
            pltpu.VMEM(line_shape, BF16),
            copies((bands,)),
            copies((5 * bands,)),
        ],
        (field,),
    )
    landed = lax.all_to_all(message, "band", split_axis=0, concat_axis=0, tiled=True)
    link_early = lax.ppermute(early_part, "domain", link_pairs)
    core_field = lax.ppermute(xt, "domain", core_pairs)

    group_shape = (groups, states, LANES)
    mine, to_core, to_link, *to_far = call(
        63,
        project_kernel,
        (),
        [SCALARS] * 3 + [FAR, PINNED],
        [PINNED] + [FAR] * (2 + len(far_pairs)),
        [((3 * groups, states, LANES), BF16)]
        + [((2 * groups, states, LANES), BF16)] * 2
        + [(group_shape, BF16)] * len(far_pairs),
        [
            pltpu.VMEM((3 * atoms_here + 1, proj_count, states), F32),
            pltpu.VMEM((3 * groups, states, LANES), BF16),
            pltpu.VMEM(line_shape, BF16),
            pltpu.VMEM(projectors.shape, BF16),
            copies((5,)),
            copies((5 + len(far_pairs),)),
        ],
        (tile_atom, tile_line, tile_count, xt, projectors),
    )
    from_link = lax.ppermute(to_link, "domain", link_pairs)
    from_far = [lax.ppermute(value, "domain", pairs) for value, pairs in zip(to_far, far_pairs)]
    from_core = lax.ppermute(to_core, "domain", core_pairs)
    (gate,) = call(
        63,
        wait_for,
        (),
        [UNREAD] * (4 + len(far_pairs)),
        [PINNED],
        [token],
        [],
        (from_core, from_link, *from_far, link_early, core_field),
    )
    held = groups // bands
    built_shape = (first + first // 2 + held, states, cols_z)
    beside_shape = (bands, first // 2, states, cols_z)
    added, own_message, *messages = call(
        62,
        functools.partial(nonlocal_kernel, len(far_pairs)),
        (),
        [SCALARS] * 3 + [FAR] * 3 + [PINNED, WHOLE, PINNED, WHOLE, WHOLE] + [WHOLE] * len(far_pairs) + [PINNED],
        [PINNED, PINNED] + [FAR] * (bands - 1),
        [(line_shape, F32)] + [(built_shape, BF16)] * bands,
        [
            pltpu.VMEM((lines + 1, states, cols_z), F32),
            pltpu.VMEM(group_shape, BF16),
            pltpu.VMEM((3 * groups, states, LANES), BF16),
            pltpu.VMEM((3 * groups, states, LANES), F32),
            pltpu.VMEM(energy_rows, F32),
            pltpu.VMEM((3 * atoms_here, states, proj_count), BF16),
            pltpu.VMEM(projectors.shape, BF16),
            pltpu.VMEM((bands, *built_shape), BF16),
            pltpu.VMEM(beside_shape, BF16),
            pltpu.VMEM(beside_shape, BF16),
            copies((4,)),
            copies((3 * bands,)),
            copies((bands,)),
        ],
        (
            tile_atom, tile_line, tile_count, xt, core_field, link_early, projectors, energy, mine, from_core,
            from_link, *from_far, gate,
        ),
        micros=8,
    )
    early = swapped(messages, "band")

    later_all, later_pass, late_part = call(
        32,
        functools.partial(later_kernel, bands),
        (),
        [FAR, PINNED, UNREAD],
        [NEAR, FAR, UNREAD],
        [
            ((rest + 1, total_states, cols_z), BF16),
            ((rest // 2, total_states, cols_z), BF16),
            (late_shape, BF16),
        ],
        [copies((bands,)), copies],
        (landed, own_message, late_part),
        aliases={2: 2},
    )
    later_link = lax.ppermute(later_pass, "domain", link_pairs)
    later_core = lax.ppermute(later_pass, "domain", core_pairs)
    link_late = lax.ppermute(late_part, "domain", link_pairs)

    (early_token,) = call(
        1,
        wait_for,
        (),
        [UNREAD] * (bands - 1),
        [PINNED],
        [token],
        [],
        tuple(early),
        micros=30,
    )
    parts = domains * bands
    blocks, final_token = call(
        32,
        functools.partial(final_kernel, first, share),
        (),
        [NEAR] + [WHOLE] * 4 + [PINNED, PINNED] + [WHOLE] * (bands - 1),
        [WHOLE, PINNED],
        [((parts, states, 2 * total_states // domains), BF16), token],
        [
            pltpu.VMEM((first + 1, total_states, cols_z), BF16),
            pltpu.VMEM((first // 2, total_states, cols_z), BF16),
            pltpu.VMEM((held, total_states, LANES), BF16),
            pltpu.VMEM(energy_rows, F32),
            pltpu.VMEM((2, total_states, total_states), F32),
            copies((3,)),
        ],
        (later_all, later_core, later_link, pot, energy, own_message, early_token, *early),
    )
    summed = lax.all_to_all(blocks, ("domain", "band"), split_axis=0, concat_axis=0, tiled=True)
    span = 2 * ROWS
    steps = lines // span
    block = pl.BlockSpec((span, states, cols_z), lambda i: (i, 0, 0))
    (applied,) = call(
        48,
        functools.partial(stencil_kernel, share),
        (steps,),
        [
            block,
            pl.BlockSpec((1, states, cols_z), lambda i: (lax.rem(i * span + lines - 1, lines), 0, 0)),
            pl.BlockSpec((1, states, cols_z), lambda i: (lax.rem(i * span + span, lines), 0, 0)),
            block,
            pl.BlockSpec((ahead * bands // steps, states, cols_z), lambda i: (i, 0, 0)),
            pl.BlockSpec((late_lines // steps, states, cols_z), lambda i: (i, 0, 0)),
            block,
            pl.BlockSpec((span, cols_z), lambda i: (i, 0)),
            WHOLE,
            PINNED,
        ],
        [pl.BlockSpec((states, span, cols_z), lambda i: (0, i, 0))],
        [((states, lines, cols_z), BF16)],
        [],
        (
            xt, xt, xt, core_field, link_early, link_late, pltpu.with_memory_space_constraint(added, pltpu.HBM), pot, ring,
            final_token,
        ),
    )

    (subspace,) = call(
        32,
        functools.partial(result_kernel, 1.0 / (lines * cols_z * domains)),
        (),
        [WHOLE],
        [WHOLE],
        [((2, states, total_states // domains), F32)],
        [],
        (summed,),
    )
    return applied.reshape(orbitals.shape), subspace


def solution(mesh):
    in_specs = (
        P("band", ("groups", "domain"), None, None),
        P(("groups", "domain"), None, None),
        P(("groups", "domain"), None, None),
        P(("groups", "domain")),
        P(("groups", "domain")),
        P(("groups", "domain")),
        P("groups", None),
    )
    out_specs = (P("band", ("groups", "domain"), None, None), P(None, ("groups", "band"), "domain"))
    return jax.shard_map(local, mesh=mesh, in_specs=in_specs, out_specs=out_specs, check_vma=False)
```

```python
import functools

import jax
import jax.numpy as jnp
import numpy as np
from jax import lax
from jax.experimental import pallas as pl
from jax.experimental.pallas import tpu as pltpu
from jax.sharding import PartitionSpec as P

F32 = jnp.float32
BF16 = jnp.bfloat16
LANES = 128
ROWS = 16
NT = (((1,), (1,)), ((), ()))
WHOLE = pl.BlockSpec(memory_space=pltpu.VMEM)
NEAR = pl.BlockSpec(memory_space=pltpu.VMEM)
SCALARS = pl.BlockSpec(memory_space=pltpu.SMEM)
FAR = pl.BlockSpec(memory_space=pltpu.HBM)
PINNED = pl.BlockSpec(memory_space=pltpu.HBM)
UNREAD = pl.BlockSpec(memory_space=pl.ANY)
copies = pltpu.SemaphoreType.DMA


def call(room, kernel, grid, in_specs, out_specs, outs, scratch, args, aliases=None, micros=0.001):
    def place(spec):
        return {id(NEAR): pltpu.VMEM, id(PINNED): pltpu.HBM}.get(id(spec))

    args = [
        pltpu.with_memory_space_constraint(arg, place(spec)) if place(spec) else arg
        for spec, arg in zip(in_specs, args)
    ]
    shapes = [(place(spec) or jax.ShapeDtypeStruct)(shape, kind) for spec, (shape, kind) in zip(out_specs, outs)]
    return pl.pallas_call(
        kernel,
        grid=grid,
        out_shape=shapes,
        in_specs=in_specs,
        out_specs=out_specs,
        scratch_shapes=scratch,
        input_output_aliases=aliases or {},
        compiler_params=pltpu.CompilerParams(vmem_limit_bytes=int(room * 2**20)),
        cost_estimate=pl.CostEstimate(flops=int(micros * 1.1e9), bytes_accessed=1 << 10, transcendentals=0),
    )(*args)


def start(copy):
    copy.start()
    return copy


def start_all(pairs, sems):
    return [start(pltpu.make_async_copy(source, target, sems.at[i])) for i, (source, target) in enumerate(pairs)]


def wait_all(started):
    for copy in started:
        copy.wait()


def wait_for(*refs):
    pass


def pack_kernel(first, x_hbm, xt_hbm, early, late, message, x, xt, in_sems, out_sems):
    states, lines, _ = x.shape
    bands = in_sems.shape[0]
    share = lines // bands
    count = share - first
    ahead = early.shape[0] // bands
    loads, sends = [], []
    for c in range(bands):
        where = (slice(None), pl.ds(c * share, share), slice(None))
        loads.append(start(pltpu.make_async_copy(x_hbm.at[where], x.at[where], in_sems.at[c])))

    def send(line, number, target, at):
        copy = pltpu.make_async_copy(
            xt.at[pl.ds(line, number)], target.at[pl.ds(at, number)], out_sems.at[len(sends)]
        )
        sends.append(start(copy))

    for c in range(bands):
        loads[c].wait()
        for y0 in range(c * share, (c + 1) * share, ROWS):
            for s0 in range(0, states, ROWS):
                block = x[s0 : s0 + ROWS, y0 : y0 + ROWS, :]
                xt[y0 : y0 + ROWS, s0 : s0 + ROWS, :] = jnp.swapaxes(block, 0, 1)
        send(c * share, ahead, early, c * ahead)
        send(c * share + ahead, share - ahead, late, c * (share - ahead))
        send(c * share + first, count, message, c * (count + 1))
        send(c * share, 1, message, (c + bands - 1) % bands * (count + 1) + count)
        send(c * share, share, xt_hbm, c * share)
    for copy in sends:
        copy.wait()


def bases(groups):
    domain = lax.axis_index("domain")
    odd, upper = domain & 1, (domain >> 1) & 1
    return [2 * groups * side for side in (1 - odd, odd, 1 - upper, upper)]


def slot_reader(atom_ref, line_ref, count_ref, atoms_here):
    first = (lax.axis_index("domain") - 1) * atoms_here
    live = count_ref[0]

    def slot_at(t):
        return line_ref[t], jnp.clip(atom_ref[t] - first, 0, 3 * atoms_here - 1), t < live

    return slot_at


def energy_table(energy_ref):
    proj_count, atoms = energy_ref.shape
    per_group = LANES // proj_count
    lane = lax.broadcasted_iota(jnp.int32, (proj_count, LANES), 1)
    row = lax.broadcasted_iota(jnp.int32, (proj_count, LANES), 0)
    pick = jnp.where(lane % proj_count == row, 1.0, 0.0).astype(F32)
    spread = jnp.dot(energy_ref[...].T, pick, precision=lax.Precision.HIGHEST, preferred_element_type=F32)
    spread = spread.reshape(atoms // per_group, per_group, LANES)
    lane = lax.broadcasted_iota(jnp.int32, spread.shape, 2)
    atom = lax.broadcasted_iota(jnp.int32, spread.shape, 1)
    return jnp.sum(jnp.where(lane // proj_count == atom, spread, 0.0), axis=1)


def project_kernel(atom_ref, line_ref, count_ref, xt_hbm, p_hbm, mine_hbm, core_hbm, link_hbm, *refs):
    far_hbms, (total, mine_ref, xt_ref, p_ref, sems, out_sems) = refs[:-6], refs[-6:]
    slots, proj_count, _ = p_ref.shape
    groups, states = mine_ref.shape[0] // 3, mine_ref.shape[1]
    per_group = LANES // proj_count
    chunks = sems.shape[0] - 1
    size = slots // chunks
    unroll = 48
    pairs = [(p_hbm.at[pl.ds(c * size, size)], p_ref.at[pl.ds(c * size, size)]) for c in range(chunks)]
    xt_load, *loads = start_all([(xt_hbm, xt_ref), *pairs], sems)

    def clear(i, carry):
        for u in range(per_group):
            total[i * per_group + u] = jnp.zeros_like(total[0])
        return carry

    lax.fori_loop(0, 3 * groups, clear, 0)

    slot_at = slot_reader(atom_ref, line_ref, count_ref, groups * per_group)

    def body(i, carry):
        for u in range(unroll):
            t = i * unroll + u
            line, atom, live = slot_at(t)
            part = lax.dot_general(p_ref[t], xt_ref[line], NT, preferred_element_type=F32)
            total[jnp.where(live, atom, 3 * groups * per_group)] += part
        return carry

    xt_load.wait()
    for c in range(chunks):
        loads[c].wait()
        lax.fori_loop(c * size // unroll, (c + 1) * size // unroll, body, 0)

    for g in range(3 * groups):
        tiles = [total[g * per_group + u] for u in range(per_group)]
        mine_ref[g] = jnp.concatenate(tiles, axis=0).T.astype(BF16)
    sides = bases(groups)
    pairs = [(mine_ref, mine_hbm)]
    for side, far in zip(sides[:2], (core_hbm, link_hbm)):
        pairs.append((mine_ref.at[pl.ds(side, groups)], far.at[pl.ds(0, groups)]))
        pairs.append((mine_ref.at[pl.ds(groups, groups)], far.at[pl.ds(groups, groups)]))
    for side, far in zip(sides[2:], far_hbms):
        pairs.append((mine_ref.at[pl.ds(side, groups)], far))
    wait_all(start_all(pairs, out_sems))


def nonlocal_kernel(
    fars, atom_ref, line_ref, count_ref, xt_hbm, beside_hbm, early_hbm, p_hbm, energy_ref, mine_hbm, core_ref, link_ref, *refs
):
    far_refs, out_hbm, messages, scratch = refs[:fars], refs[fars + 1], refs[fars + 2 : -13], refs[-13:]
    lines_sum, whole_ref, mine_ref, total, table, atoms, p_ref, built, cores, links, sems, in_sems, out_sems = scratch
    lines = xt_hbm.shape[0]
    bands, half = cores.shape[:2]
    share, first = lines // bands, 2 * half
    held = built.shape[1] - first - half
    ahead = early_hbm.shape[0] // bands
    mine = (lax.axis_index("domain") & 1) * half
    pairs = []
    for k in range(bands):
        to = lax.axis_index("band") ^ k
        pairs.append((xt_hbm.at[pl.ds(to * share, first)], built.at[k, pl.ds(0, first)]))
        pairs.append((beside_hbm.at[pl.ds(to * share + mine, half)], cores.at[k]))
        pairs.append((early_hbm.at[pl.ds(to * ahead + mine, half)], links.at[k]))
    brought = start_all(pairs, in_sems)
    slots, proj_count, _ = p_ref.shape
    groups, states = total.shape[0] // 3, total.shape[1]
    per_group = LANES // proj_count
    unroll = 48
    mine_load, load = start_all([(mine_hbm, mine_ref), (p_hbm, p_ref)], sems)
    sends = []

    def clear(i, carry):
        lines_sum[i] = jnp.zeros((states, LANES), F32)
        return carry

    lax.fori_loop(0, lines + 1, clear, 0)
    mine_load.wait()
    total[...] = mine_ref[...].astype(F32)
    sides = bases(groups)
    for g in range(groups):
        total[groups + g] += core_ref[g].astype(F32) + link_ref[g].astype(F32)
        for side, ref in zip(sides[:2], (core_ref, link_ref)):
            total[side + g] += ref[groups + g].astype(F32)
        for side, ref in zip(sides[2:], far_refs):
            total[side + g] += ref[g].astype(F32)
    table[...] = energy_table(energy_ref)
    last = table.shape[0] - 1
    for g in range(3 * groups):
        row = jnp.clip((lax.axis_index("domain") - 1) * groups + g, 0, last)
        tile = (total[g] * table[pl.ds(row, 1), :]).astype(BF16)
        for u in range(per_group):
            atoms[g * per_group + u] = tile[:, u * proj_count : (u + 1) * proj_count]
    for g in range(groups):
        whole_ref[g] = total[groups + g].astype(BF16)
    wait_all(brought)
    for k, message in enumerate(messages):
        to = lax.axis_index("band") ^ k
        for i in range(half):
            built[k, first + i] = (cores[k, i].astype(F32) + links[k, i].astype(F32)).astype(BF16)
        for i in range(held):
            built[k, first + half + i] = whole_ref[to * held + i]
        sends.append(start(pltpu.make_async_copy(built.at[k], message, out_sems.at[k])))
    load.wait()

    slot_at = slot_reader(atom_ref, line_ref, count_ref, groups * per_group)

    def body(i, carry):
        for u in range(unroll):
            t = i * unroll + u
            line, atom, live = slot_at(t)
            part = jnp.dot(atoms[atom], p_ref[t], preferred_element_type=F32)
            lines_sum[jnp.where(live, line, lines)] += part
        return carry

    lax.fori_loop(0, slots // unroll, body, 0)
    sends.append(start(pltpu.make_async_copy(lines_sum.at[pl.ds(0, lines)], out_hbm, sems.at[3])))
    wait_all(sends)


def stencil_kernel(
    share, xt_ref, last_ref, next_ref, core_ref, early_ref, late_ref, added_ref, pot_ref, ring_ref, unread,
    out_ref,
):
    states, here, _ = out_ref.shape

    ahead = early_ref.shape[0] * share // here

    def link(i, rows):
        chunk, at = divmod(i, share)
        if at < ahead:
            return early_ref[chunk * ahead + at, rows, :]
        return late_ref[chunk * (share - ahead) + at - ahead, rows, :]

    def line(i, rows):
        ref, at = (last_ref, 0) if i < 0 else (next_ref, 0) if i == here else (xt_ref, i)
        return ref[at, rows, :]

    for y0 in range(0, here, ROWS):
        for s0 in range(0, states, ROWS):
            rows = slice(s0, s0 + ROWS)
            results = []
            cells = jnp.concatenate([line(y0 + i, rows) for i in range(ROWS)], axis=0)
            along = jnp.dot(cells, ring_ref[...], preferred_element_type=F32)
            before, x = line(y0 - 1, rows).astype(F32), line(y0, rows).astype(F32)
            for i in range(ROWS):
                y = y0 + i
                after = line(y + 1, rows).astype(F32)
                beside = (before + after) + (core_ref[y, rows, :].astype(F32) + link(y, rows).astype(F32))
                value = along[i * ROWS : (i + 1) * ROWS] + pot_ref[y : y + 1, :] * x
                results.append((value + added_ref[y, rows, :] - 0.5 * beside).astype(BF16))
                before, x = x, after
            out_ref[rows, y0 : y0 + ROWS, :] = jnp.swapaxes(jnp.stack(results, axis=0), 0, 1)


def pass_half(all_ref, pass_hbm, sem):
    half = pass_hbm.shape[0]
    copy = start(pltpu.make_async_copy(all_ref.at[pl.ds((1 - (lax.axis_index("domain") & 1)) * half, half)], pass_hbm, sem))
    copy.wait()


def later_kernel(bands, landed, unread, handed, all_ref, pass_hbm, same, sems, pass_sem):
    count, states = all_ref.shape[0], landed.shape[1]
    loads = [
        start(
            pltpu.make_async_copy(
                landed.at[pl.ds(b * count, count)], all_ref.at[:, pl.ds(b * states, states), :], sems.at[b]
            )
        )
        for b in range(bands)
    ]
    for copy in loads:
        copy.wait()
    pass_half(all_ref, pass_hbm, pass_sem)


def early_kernel(after_ref, energy_ref, *refs):
    pieces, (all_ref, beside_ref, projs_ref, table_ref, token, sems) = refs[:-6], refs[-6:]
    states = pieces[0].shape[1]
    count, half, held = all_ref.shape[0] - 1, beside_ref.shape[0], projs_ref.shape[0]
    pairs = []
    for k, piece in enumerate(pieces):
        at = pl.ds(pl.multiple_of((lax.axis_index("band") ^ k) * states, states), states)
        pairs.append((piece.at[pl.ds(0, count)], all_ref.at[pl.ds(0, count), at, :]))
        pairs.append((piece.at[pl.ds(count, half)], beside_ref.at[:, at, :]))
        pairs.append((piece.at[pl.ds(count + half, held)], projs_ref.at[:, at, :]))
    loads = start_all(pairs, sems)
    all_ref[count] = after_ref[0]
    table_ref[...] = energy_table(energy_ref)
    wait_all(loads)


def add_products(row, all_ref, beside_refs, pot_ref, acc):
    half = beside_refs[0].shape[0]
    group = 4
    mine = (lax.axis_index("domain") & 1) * half
    for part, base in ((0, mine), (1, half - mine)):
        for i0 in range(0, half, group):
            xs, ys = [], []
            for i in range(i0, min(i0 + group, half)):
                cell = all_ref[base + i]
                x = cell.astype(F32)
                y = (3.0 + pot_ref[pl.ds(row + base + i, 1), :]) * x - pltpu.roll(x, x.shape[1] - 1, 1)
                y = y - all_ref[base + i + 1].astype(F32)
                if part == 0:
                    for ref in beside_refs:
                        y = y - ref[i].astype(F32)
                xs.append(cell)
                ys.append(y.astype(BF16))
            flat_x = jnp.concatenate(xs, axis=1)
            flat_y = jnp.concatenate(ys, axis=1)
            acc[0] += lax.dot_general(flat_x, flat_x, NT, preferred_element_type=F32)
            acc[1] += lax.dot_general(flat_y, flat_x, NT, preferred_element_type=F32)


def gram_kernel(first, share, all_ref, core_ref, link_ref, pot_ref, unread, acc):
    acc[...] = jnp.zeros_like(acc)
    add_products(lax.axis_index("band") * share + first, all_ref, (core_ref, link_ref), pot_ref, acc)


def final_kernel(bands, share, all_ref, beside_ref, pot_ref, begun_ref, proj_ref, energy_ref, out_ref, token, acc):
    acc[...] = begun_ref[...]
    add_products(lax.axis_index("band") * share, all_ref, (beside_ref,), pot_ref, acc)
    groups = proj_ref.shape[0]
    first = (lax.axis_index("domain") * bands + lax.axis_index("band")) * groups
    for g in range(groups):
        here = proj_ref[g]
        scaled = (here.astype(F32) * energy_ref[pl.ds(first + g, 1), :]).astype(BF16)
        acc[1] += lax.dot_general(scaled, here, NT, preferred_element_type=F32)
    hamil = 0.5 * (acc[1] + acc[1].T)
    domains = out_ref.shape[0] // bands
    rows, cols = out_ref.shape[1], out_ref.shape[2] // 2
    for c in range(domains):
        for r in range(bands):
            r0, c0 = r * rows, c * cols
            out_ref[c * bands + r, :, :cols] = acc[0, r0 : r0 + rows, c0 : c0 + cols].astype(BF16)
            out_ref[c * bands + r, :, cols:] = hamil[r0 : r0 + rows, c0 : c0 + cols].astype(BF16)


def result_kernel(scale, parts_ref, out_ref):
    total = jnp.sum(parts_ref[...].astype(F32), axis=0) * scale
    cols = out_ref.shape[2]
    out_ref[0] = total[:, :cols]
    out_ref[1] = total[:, cols:]


def local(orbitals, potential, projectors, tile_atom, tile_line, tile_count, energies):
    states, _, lines, cols_z = orbitals.shape
    slots, proj_count, _ = projectors.shape
    atom_total = energies.shape[0]
    domains, bands = lax.axis_size("domain"), lax.axis_size("band")
    total_states = states * bands
    atoms_here = atom_total // domains
    per_group = LANES // proj_count
    groups = atoms_here // per_group
    share = lines // bands
    first = 2 * (share // 8)
    rest = share - first

    core_pairs = [(i, i ^ 1) for i in range(domains) if i ^ 1 < domains]
    link_pairs = [(i, ((i + 1) ^ 1) - 1) for i in range(1, domains) if ((i + 1) ^ 1) - 1 < domains]
    near_far = [(i, i ^ 2) for i in range(domains) if i ^ 2 < domains]
    next = [(i, ((i + 2) ^ 2) - 2) for i in range(2, domains) if ((i + 2) ^ 2) - 2 < domains]
    far_pairs = [pairs for pairs in (near_far, next) if pairs]

    def swapped(values, axis):
        size = lax.axis_size(axis)
        got = {k: lax.ppermute(values[k - 1], axis, [(i, i ^ k) for i in range(size)]) for k in range(size - 1, 0, -1)}
        return [got[k] for k in range(1, size)]

    field = orbitals.reshape(states, lines, cols_z)
    pot = potential.reshape(lines, cols_z)
    energy = energies.T
    energy_rows = (atom_total // per_group, LANES)
    token = ((8, LANES), F32)
    eye = np.eye(cols_z, dtype=np.float32)
    ring = jnp.asarray(3.0 * eye - 0.5 * (np.roll(eye, 1, axis=0) + np.roll(eye, -1, axis=0)), dtype=BF16)

    ahead = share * 5 // 8
    late_lines = lines - ahead * bands
    line_shape, late_shape = (lines, states, cols_z), (late_lines, states, cols_z)
    xt, early_part, late_part, message = call(
        63,
        functools.partial(pack_kernel, first),
        (),
        [FAR],
        [FAR] * 4,
        [
            (line_shape, BF16),
            ((lines - late_lines, states, cols_z), BF16),
            (late_shape, BF16),
            ((bands * (rest + 1), states, cols_z), BF16),
        ],
        [
            pltpu.VMEM((states, lines, cols_z), BF16),
            pltpu.VMEM(line_shape, BF16),
            copies((bands,)),
            copies((5 * bands,)),
        ],
        (field,),
    )
    landed = lax.all_to_all(message, "band", split_axis=0, concat_axis=0, tiled=True)
    link_early = lax.ppermute(early_part, "domain", link_pairs)
    core_field = lax.ppermute(xt, "domain", core_pairs)

    group_shape = (groups, states, LANES)
    mine, to_core, to_link, *to_far = call(
        63,
        project_kernel,
        (),
        [SCALARS] * 3 + [FAR, PINNED],
        [PINNED] + [FAR] * (2 + len(far_pairs)),
        [((3 * groups, states, LANES), BF16)]
        + [((2 * groups, states, LANES), BF16)] * 2
        + [(group_shape, BF16)] * len(far_pairs),
        [
            pltpu.VMEM((3 * atoms_here + 1, proj_count, states), F32),
            pltpu.VMEM((3 * groups, states, LANES), BF16),
            pltpu.VMEM(line_shape, BF16),
            pltpu.VMEM(projectors.shape, BF16),
            copies((5,)),
            copies((5 + len(far_pairs),)),
        ],
        (tile_atom, tile_line, tile_count, xt, projectors),
    )
    from_link = lax.ppermute(to_link, "domain", link_pairs)
    from_far = [lax.ppermute(value, "domain", pairs) for value, pairs in zip(to_far, far_pairs)]
    from_core = lax.ppermute(to_core, "domain", core_pairs)
    (gate,) = call(
        63,
        wait_for,
        (),
        [UNREAD] * (4 + len(far_pairs)),
        [PINNED],
        [token],
        [],
        (from_core, from_link, *from_far, link_early, core_field),
    )
    held = groups // bands
    built_shape = (first + first // 2 + held, states, cols_z)
    beside_shape = (bands, first // 2, states, cols_z)
    added, own_message, *messages = call(
        62,
        functools.partial(nonlocal_kernel, len(far_pairs)),
        (),
        [SCALARS] * 3 + [FAR] * 3 + [PINNED, WHOLE, PINNED, WHOLE, WHOLE] + [WHOLE] * len(far_pairs) + [PINNED],
        [PINNED, PINNED] + [FAR] * (bands - 1),
        [(line_shape, F32)] + [(built_shape, BF16)] * bands,
        [
            pltpu.VMEM((lines + 1, states, cols_z), F32),
            pltpu.VMEM(group_shape, BF16),
            pltpu.VMEM((3 * groups, states, LANES), BF16),
            pltpu.VMEM((3 * groups, states, LANES), F32),
            pltpu.VMEM(energy_rows, F32),
            pltpu.VMEM((3 * atoms_here, states, proj_count), BF16),
            pltpu.VMEM(projectors.shape, BF16),
            pltpu.VMEM((bands, *built_shape), BF16),
            pltpu.VMEM(beside_shape, BF16),
            pltpu.VMEM(beside_shape, BF16),
            copies((4,)),
            copies((3 * bands,)),
            copies((bands,)),
        ],
        (
            tile_atom, tile_line, tile_count, xt, core_field, link_early, projectors, energy, mine, from_core,
            from_link, *from_far, gate,
        ),
        micros=8,
    )
    early = swapped(messages, "band")

    later_all, later_pass, late_part = call(
        32,
        functools.partial(later_kernel, bands),
        (),
        [FAR, PINNED, UNREAD],
        [NEAR, FAR, UNREAD],
        [
            ((rest + 1, total_states, cols_z), BF16),
            ((rest // 2, total_states, cols_z), BF16),
            (late_shape, BF16),
        ],
        [copies((bands,)), copies],
        (landed, own_message, late_part),
        aliases={2: 2},
    )
    later_link = lax.ppermute(later_pass, "domain", link_pairs)
    later_core = lax.ppermute(later_pass, "domain", core_pairs)
    link_late = lax.ppermute(late_part, "domain", link_pairs)

    early_all, early_beside, projs, energy_table_here, early_token = call(
        32,
        early_kernel,
        (),
        [NEAR, WHOLE, PINNED] + [FAR] * (bands - 1),
        [NEAR, NEAR, NEAR, NEAR, PINNED],
        [
            ((first + 1, total_states, cols_z), BF16),
            ((first // 2, total_states, cols_z), BF16),
            ((held, total_states, LANES), BF16),
            (energy_rows, F32),
            token,
        ],
        [copies((3 * bands,))],
        (later_all, energy, own_message, *early),
        micros=30,
    )
    (begun,) = call(
        32,
        functools.partial(gram_kernel, first, share),
        (),
        [NEAR, WHOLE, WHOLE, WHOLE, PINNED],
        [NEAR],
        [((2, total_states, total_states), F32)],
        [],
        (later_all, later_core, later_link, pot, early_token),
    )
    parts = domains * bands
    blocks, final_token = call(
        32,
        functools.partial(final_kernel, bands, share),
        (),
        [NEAR, NEAR, WHOLE, NEAR, NEAR, NEAR],
        [WHOLE, PINNED],
        [((parts, states, 2 * total_states // domains), BF16), token],
        [pltpu.VMEM((2, total_states, total_states), F32)],
        (early_all, early_beside, pot, begun, projs, energy_table_here),
    )
    summed = lax.all_to_all(blocks, ("domain", "band"), split_axis=0, concat_axis=0, tiled=True)
    span = 2 * ROWS
    steps = lines // span
    block = pl.BlockSpec((span, states, cols_z), lambda i: (i, 0, 0))
    (applied,) = call(
        48,
        functools.partial(stencil_kernel, share),
        (steps,),
        [
            block,
            pl.BlockSpec((1, states, cols_z), lambda i: (lax.rem(i * span + lines - 1, lines), 0, 0)),
            pl.BlockSpec((1, states, cols_z), lambda i: (lax.rem(i * span + span, lines), 0, 0)),
            block,
            pl.BlockSpec((ahead * bands // steps, states, cols_z), lambda i: (i, 0, 0)),
            pl.BlockSpec((late_lines // steps, states, cols_z), lambda i: (i, 0, 0)),
            block,
            pl.BlockSpec((span, cols_z), lambda i: (i, 0)),
            WHOLE,
            PINNED,
        ],
        [pl.BlockSpec((states, span, cols_z), lambda i: (0, i, 0))],
        [((states, lines, cols_z), BF16)],
        [],
        (
            xt, xt, xt, core_field, link_early, link_late, pltpu.with_memory_space_constraint(added, pltpu.HBM), pot, ring,
            final_token,
        ),
    )

    (subspace,) = call(
        32,
        functools.partial(result_kernel, 1.0 / (lines * cols_z * domains)),
        (),
        [WHOLE],
        [WHOLE],
        [((2, states, total_states // domains), F32)],
        [],
        (summed,),
    )
    return applied.reshape(orbitals.shape), subspace


def solution(mesh):
    in_specs = (
        P("band", ("groups", "domain"), None, None),
        P(("groups", "domain"), None, None),
        P(("groups", "domain"), None, None),
        P(("groups", "domain")),
        P(("groups", "domain")),
        P(("groups", "domain")),
        P("groups", None),
    )
    out_specs = (P("band", ("groups", "domain"), None, None), P(None, ("groups", "band"), "domain"))
    return jax.shard_map(local, mesh=mesh, in_specs=in_specs, out_specs=out_specs, check_vma=False)
```
